32 devices in a mesh: rep: 8 (over z, x), shard: 4 (over y, core).
Axes of the slice: x: 2, y: 2, z: 4, core: 2. Of those that a mesh axis runs over, the one named last changes fastest.
Arguments:
- x_in: bfloat16 [4096, 2048], P(('rep', 'shard')), may hold values from -6 to 6
- cotangent: bfloat16 [4096, 2048], P(('rep', 'shard')), may hold values from -6 to 6
- seq_lengths: int32 [8, 4], P('rep'), may hold values from 1 to 256, 512 in all within a row
- seq_order: int32 [8, 4], P('rep'), may hold values from 0 to 3, each once within a row
- valid: int32 [4096], P(('rep', 'shard')), may hold values 0 or 1
- norm_gain: float32 [2048], replicated, may hold values from 0.5 to 1.5
- w_in: bfloat16 [2048, 8512], P('shard'), may hold values from -0.125 to 0.125
- conv_w: float32 [4, 4352], replicated, may hold values from -3 to 3
- conv_b: float32 [4352], replicated, may hold values from -2 to 2
- dt_bias: float32 [64], replicated, may hold values from -9 to -3
- a_log: float32 [64], replicated, may hold values from 0 to 2
- d_skip: float32 [64], replicated, may hold values from 0.5 to 1.5
- gated_gain: float32 [4096], replicated, may hold values from 0.5 to 1.5
- w_out: bfloat16 [4096, 2048], P('shard'), may hold values from -0.09375 to 0.09375
Outputs:
- block_out: bfloat16 [4096, 2048], P(('rep', 'shard'))
- grad_in: bfloat16 [4096, 2048], P(('rep', 'shard'))
- grad_norm_gain: float32 [2048], replicated
- grad_w_in: float32 [2048, 8512], P('shard')
- grad_conv_w: float32 [4, 4352], replicated
- grad_conv_b: float32 [4352], replicated
- grad_dt_bias: float32 [64], replicated
- grad_a_log: float32 [64], replicated
- grad_d_skip: float32 [64], replicated
- grad_gated_gain: float32 [4096], replicated
- grad_w_out: float32 [4096, 2048], P('shard')
- rms_residual: float32 [], replicated
- rms_mixer: float32 [], replicated
The draws below stay inside these ranges and needn't reach their ends.
Inputs may be any that keep to these rules, and one draw needn't show every extreme that they name: `seq_lengths`: each row holds the lengths of one group's 4 sequences; they sum to 512 and the longest is exactly 256. `seq_order`: each row is a permutation of 0 to 3.
All inputs are finite; a program needn't handle non-finite values. No bound on the sum of `valid` on one device may be relied on, other than what follows from the above.
Results may differ from the reference program's by a relative error of at most 0.0097.
Values may be sent and summed in bfloat16 or wider, within the bound.
A program may use at most 448 MiB of HBM per device.

```python
import math
import jax
import jax.numpy as jnp
import numpy as np
from jax import lax

D = 2048
H = 64
P_SIZE = 64
N = 128
KW = 4
SPAN = 128
TOK_DEV = 128
DI = 4096
CONVW = 4352
PROJ = 8512
MAXLEN = 256
SEQS = 4
GROUPS = 8
TOKENS = 4096
N_SHARD = 4


def with_ends(entries, key, least, largest):
    index_at = [jax.random.randint(jax.random.fold_in(key, axis), (), 0, length) for axis, length in enumerate(entries.shape)]
    longest = entries.shape.index(max(entries.shape))
    neighbour = index_at[:longest] + [(index_at[longest] + 1) % entries.shape[longest]] + index_at[longest + 1:]
    return entries.at[tuple(index_at)].set(least).at[tuple(neighbour)].set(largest)


def shard_levels(stream_key, dims, cuts, low, largest):
    loudness = 1.0
    for dim, blocks in cuts:
        draws = jax.random.uniform(jax.random.fold_in(jax.random.fold_in(stream_key, 6), dim), (blocks,), jnp.float32, low / len(cuts), largest / len(cuts))
        loudness = loudness * jnp.repeat(jnp.exp(draws), dims[dim] // blocks).reshape((-1,) + (1,) * (len(dims) - 1 - dim))
    return loudness


def profile(number_of, total, limit, skew):
    portions = [(1 << 20) // math.isqrt(rank ** skew) + 1 for rank in range(2, number_of + 1)]
    surplus, counts = total - limit - (number_of - 1), [1] * (number_of - 1)
    while surplus > 0:
        movable = [i for i in range(number_of - 1) if counts[i] < limit]
        whole, budget = sum([portions[i] for i in movable]), surplus
        for i in movable:
            addition = min(limit - counts[i], max(1, budget * portions[i] // whole), surplus)
            counts[i] = counts[i] + addition
            surplus = surplus - addition
    return np.array([limit] + counts)


def ragged(own_key, count, total, most, skew):
    if count == 2:
        one = jax.random.randint(own_key, (), max(1, total - most), min(most, total - 1) + 1)
        return jnp.stack([one, total - one])
    lengths = jnp.asarray(profile(count, total, most, skew), jnp.int32)
    pairs = (count - 1) // 2
    donor, taker = lengths[1:1 + 2 * pairs:2], lengths[2:2 + 2 * pairs:2]
    slack = jnp.minimum(donor - 1, most - taker)
    shifted = jax.random.randint(jax.random.fold_in(own_key, 1), (pairs,), 0, 1 << 20) % (slack + 1)
    lengths = lengths.at[1:1 + 2 * pairs:2].set(donor - shifted).at[2:2 + 2 * pairs:2].set(taker + shifted)
    return lengths[jax.random.permutation(jax.random.fold_in(own_key, 2), count)]


def noise(rng, extent, width, bound, cuts=(), kind=jnp.bfloat16):
    gain = shard_levels(rng, extent, cuts, -0.22, 0.18) if cuts else 1.0
    values = jax.random.normal(rng, extent, jnp.float32) * width * gain
    return jnp.minimum(jnp.maximum(values, -bound), bound).astype(kind)


def setup_inputs(seed: int = 0) -> dict:
    seeds = jax.random.split(jax.random.key(seed), 15)
    return {
        "x_in": noise(seeds[0], (TOKENS, D), 1.0, 6.0, ((0, 32),)),
        "cotangent": noise(seeds[1], (TOKENS, D), 1.0, 6.0, ((0, 32),)),
        "seq_lengths": jax.vmap(lambda own: ragged(own, SEQS, TOK_DEV * N_SHARD, MAXLEN, 2))(jax.random.split(seeds[2], GROUPS)).reshape((GROUPS, SEQS)).astype(jnp.int32),
        "seq_order": jax.vmap(lambda own: jax.random.permutation(own, SEQS))(jax.random.split(seeds[3], GROUPS)).reshape((GROUPS, SEQS)).astype(jnp.int32),
        "valid": with_ends((jax.random.randint(seeds[4], (TOKENS,), 0, 8) < 7).astype(jnp.int32), jax.random.fold_in(seeds[4], 1), 0, 1),
        "norm_gain": jnp.clip(1.0 + 0.1 * jax.random.normal(seeds[5], (D,), jnp.float32), 0.5, 1.5),
        "w_in": noise(seeds[6], (D, PROJ), D ** -0.5, 0.125, ((0, 4),)),
        "conv_w": noise(seeds[7], (KW, CONVW), 0.5, 3.0, (), jnp.float32),
        "conv_b": noise(seeds[8], (CONVW,), 0.3, 2.0, (), jnp.float32),
        "dt_bias": jnp.clip(jax.random.uniform(seeds[9], (H,), jnp.float32, -9.0, -3.0), -9.0, -3.0),
        "a_log": jnp.clip(jax.random.uniform(seeds[10], (H,), jnp.float32, 0.0, 2.0), 0.0, 2.0),
        "d_skip": jnp.clip(jax.random.uniform(seeds[11], (H,), jnp.float32, 0.5, 1.5), 0.5, 1.5),
        "gated_gain": jnp.clip(1.0 + 0.1 * jax.random.normal(seeds[12], (DI,), jnp.float32), 0.5, 1.5),
        "w_out": noise(seeds[13], (DI, D), DI ** -0.5, 0.09375, ((0, 4),)),
    }


EPSILON = 1e-05
HIGHEST = lax.Precision.HIGHEST

@jax.custom_vjp
def low(v):
    return lax.optimization_barrier(v.astype(jnp.bfloat16)).astype(jnp.float32)

@jax.custom_vjp
def low_back(v):
    return v

def low_keep(v):
    return (low(v), None)

def low_pass(kept, grad):
    return (grad,)

def back_keep(v):
    return (v, None)

def back_low(kept, grad):
    return (low(grad),)
low.defvjp(low_keep, low_pass)
low_back.defvjp(back_keep, back_low)

def slot_tables(seq_lengths, seq_order, slot_ids):
    seq_count = seq_lengths.shape[0]
    numbers = jnp.arange(seq_count, dtype=jnp.int32)
    chosen = (seq_order[:, None] == numbers[None, :]).astype(jnp.int32)
    given_start = (jnp.cumsum(seq_lengths) - seq_lengths).astype(jnp.int32)
    owner_length = lax.optimization_barrier(jnp.sum(chosen * seq_lengths[None, :], axis=1)).astype(jnp.int32)
    owner_start = (jnp.cumsum(owner_length) - owner_length).astype(jnp.int32)
    owner_from = lax.optimization_barrier(jnp.sum(chosen * given_start[None, :], axis=1)).astype(jnp.int32)
    placed_at = lax.optimization_barrier(jnp.sum(chosen * owner_start[:, None], axis=0)).astype(jnp.int32)
    column = slot_ids[:, None]
    within = (column >= owner_start[None, :]) & (column < (owner_start + owner_length)[None, :])
    offset = column - owner_start[None, :]
    source = lax.optimization_barrier(jnp.sum(jnp.where(within, offset + owner_from[None, :], 0), axis=1)).astype(jnp.int32)
    position = lax.optimization_barrier(jnp.sum(jnp.where(within, offset, 0), axis=1)).astype(jnp.int32)
    given_within = (column >= given_start[None, :]) & (column < (given_start + seq_lengths)[None, :])
    target = lax.optimization_barrier(jnp.sum(jnp.where(given_within, column - given_start[None, :] + placed_at[None, :], 0), axis=1)).astype(jnp.int32)
    return (source, target, position)

def norm_apply(rows_in, gain_row):
    inverse_rms = lax.rsqrt(lax.optimization_barrier(jnp.mean(rows_in * rows_in, axis=1, keepdims=True)) + EPSILON)
    return rows_in * inverse_rms * gain_row[None, :]

def gated_norm(mixed, gate_rows, gain_row):
    product = mixed * jax.nn.silu(gate_rows)
    inverse_rms = lax.rsqrt(lax.optimization_barrier(jnp.mean(product * product, axis=1, keepdims=True)) + EPSILON)
    return product * inverse_rms * gain_row[None, :]

def conv_apply(extended, conv_w, conv_b, position):
    row_count = extended.shape[0] - (KW - 1)
    result = jnp.zeros((row_count, extended.shape[1]), jnp.float32) + conv_b[None, :]
    for column in range(KW):
        reach = (position >= KW - 1 - column).astype(jnp.float32)[:, None]
        result = result + conv_w[column][None, :] * extended[column:column + row_count] * reach
    return jax.nn.silu(result)

def split_mixer(activated, dt_raw, dt_bias, a_log):
    row_count = activated.shape[0]
    values = activated[:, :DI].reshape(row_count, H, P_SIZE)
    input_map = activated[:, DI:DI + N]
    output_map = activated[:, DI + N:DI + 2 * N]
    step_size = jax.nn.softplus(dt_raw + dt_bias[None, :])
    log_decay = -step_size * jnp.exp(a_log)[None, :]
    return (values, input_map, output_map, log_decay, step_size)

def scan_block(carry_state, pieces, d_skip, with_output):
    values, input_map, output_map, log_decay, step_size, position = pieces
    length = log_decay.shape[0]
    final_row = length - 1
    local = jnp.arange(length, dtype=jnp.int32)
    running = jnp.cumsum(log_decay, axis=0)
    scaled = values * step_size[:, :, None]
    begins = local - position
    reach_end = local >= begins[final_row]
    to_end = jnp.where(reach_end[:, None], running[final_row][None, :] - running, 0.0)
    tail_weight = jnp.exp(to_end) * reach_end[:, None].astype(jnp.float32)
    fresh = jnp.einsum('jhp,jn->hpn', scaled * tail_weight[:, :, None], input_map, precision=HIGHEST)
    carried = jnp.where(position[final_row] >= length, jnp.exp(running[final_row]), 0.0)
    next_state = carried[:, None, None] * carry_state + fresh
    if not with_output:
        return (next_state, carried)
    causal = (local[None, :] <= local[:, None]) & (local[None, :] >= begins[:, None])
    heads_first = running.T
    spread = heads_first[:, :, None] - heads_first[:, None, :]
    decay_matrix = jnp.exp(jnp.where(causal[None], spread, 0.0)) * causal[None].astype(jnp.float32)
    pair_products = jnp.dot(output_map, input_map.T, precision=HIGHEST)
    diagonal_part = jnp.einsum('hij,jhp->ihp', decay_matrix * pair_products[None], scaled, precision=HIGHEST)
    entering = jnp.where((position >= local + 1)[:, None], jnp.exp(running), 0.0)
    earlier_part = jnp.einsum('in,hpn->ihp', output_map, carry_state, precision=HIGHEST) * entering[:, :, None]
    outputs = diagonal_part + earlier_part + d_skip[None, :, None] * values
    return (next_state, outputs)

def to_blocks(pieces):
    return tuple((member.reshape((member.shape[0] // SPAN, SPAN) + member.shape[1:]) for member in pieces))

def ssd_run(activated, dt_raw, position, dt_bias, a_log, d_skip, start_state):
    blocks = to_blocks(split_mixer(activated, dt_raw, dt_bias, a_log) + (position,))

    def advance(state, block):
        return scan_block(state, block, d_skip, True)
    final_state, outputs = lax.scan(jax.checkpoint(advance), start_state, blocks)
    return (outputs.reshape(activated.shape[0], DI), final_state)

def group_forward(params, resid, position):
    norm_gain, w_in, conv_w, conv_b, dt_bias, a_log, d_skip, gated_gain, w_out = params
    normed = low(norm_apply(resid, norm_gain))
    projected = low_back(low(jnp.dot(normed, w_in, precision=HIGHEST)))
    gate_rows = projected[:, :DI]
    conv_in = projected[:, DI:DI + CONVW]
    dt_raw = projected[:, DI + CONVW:]
    extended = jnp.pad(conv_in, ((KW - 1, 0), (0, 0)))
    activated = low(conv_apply(extended, conv_w, conv_b, position))
    mixed, final_state = ssd_run(activated, dt_raw, position, dt_bias, a_log, d_skip, jnp.zeros((H, P_SIZE, N), jnp.float32))
    normed_out = low(gated_norm(mixed, gate_rows, gated_gain))
    branch = jnp.dot(normed_out, w_out, precision=HIGHEST)
    return (resid + branch, branch)

def reference(x_in, cotangent, seq_lengths, seq_order, valid, norm_gain, w_in, conv_w, conv_b, dt_bias, a_log, d_skip, gated_gain, w_out):
    group_count = seq_lengths.shape[0]
    group_tok = x_in.shape[0] // group_count
    slot_ids = jnp.arange(group_tok, dtype=jnp.int32)

    def tables(lengths_row, order_row):
        return slot_tables(lengths_row, order_row, slot_ids)
    source, target, positions = jax.vmap(tables)(seq_lengths, seq_order)
    arrivals = x_in.astype(jnp.float32).reshape(group_count, group_tok, D)
    owner_rows = jnp.take_along_axis(arrivals, source[:, :, None], axis=1)
    params = (norm_gain, w_in.astype(jnp.float32), conv_w, conv_b, dt_bias, a_log, d_skip, gated_gain, w_out.astype(jnp.float32))

    def forward(weights, rows_all):

        def per_group(carry, group):
            rows, position = group
            total, branch = group_forward(weights, rows, position)
            return (carry, (total, branch))
        carry_out, (totals, branches) = lax.scan(jax.checkpoint(per_group), jnp.zeros((), jnp.float32), (rows_all, positions))
        return (totals, branches)
    totals, vjp_fn, branches = jax.vjp(forward, params, owner_rows, has_aux=True)
    valid_rows = valid.reshape(group_count, group_tok)
    masked = jnp.where(valid_rows[:, :, None] > 0, cotangent.astype(jnp.float32).reshape(group_count, group_tok, D), 0.0)
    param_grads, row_grads = vjp_fn(masked)
    grad_in = jnp.take_along_axis(row_grads, target[:, :, None], axis=1).reshape(-1, D).astype(jnp.bfloat16)
    block_out = totals.reshape(-1, D).astype(jnp.bfloat16)
    weights_valid = valid_rows.astype(jnp.float32)
    count = jnp.maximum(jnp.sum(weights_valid), 1.0)
    rms_residual = jnp.sqrt(jnp.sum(weights_valid * lax.optimization_barrier(jnp.sum(totals * totals, axis=2))) / (count * D))
    rms_mixer = jnp.sqrt(jnp.sum(weights_valid * lax.optimization_barrier(jnp.sum(branches * branches, axis=2))) / (count * D))
    g_norm, g_in, g_conv_w, g_conv_b, g_dt_bias, g_a_log, g_d_skip, g_gated, g_out = param_grads
    return (block_out, grad_in, g_norm, g_in, g_conv_w, g_conv_b, g_dt_bias, g_a_log, g_d_skip, g_gated, g_out, rms_residual, rms_mixer)
```

```python
import functools

import jax
import jax.numpy as jnp
from jax import lax
from jax.experimental import pallas as pl
from jax.experimental.pallas import tpu as pltpu
from jax.sharding import PartitionSpec as P

D = 2048
H = 64
P_SIZE = 64
N = 128
KW = 4
SPAN = 128
DI = 4096
CONVW = 4352
PROJ = 8512
TAIL = PROJ - 2 * DI

EPSILON = 1e-05
ALL = ("rep", "shard")
VMEM_BYTES = 56 * 1024 * 1024
GATHER_BYTES = 32 * 1024 * 1024
BF = jnp.bfloat16
F32 = jnp.float32


def dot_nn(a, b):
    return lax.dot_general(a, b, (((1,), (0,)), ((), ())), preferred_element_type=F32)


def dot_nt(a, b):
    return lax.dot_general(a, b, (((1,), (1,)), ((), ())), preferred_element_type=F32)


def dot_tn(a, b):
    return lax.dot_general(a, b, (((0,), (0,)), ((), ())), preferred_element_type=F32)


def halves(a):
    high = a.astype(BF)
    return high, (a - high.astype(F32)).astype(BF)


def slot_tables(seq_lengths, seq_order, slot_ids):
    seq_count = seq_lengths.shape[0]
    numbers = jnp.arange(seq_count, dtype=jnp.int32)
    chosen = (seq_order[:, None] == numbers[None, :]).astype(jnp.int32)
    given_start = jnp.cumsum(seq_lengths) - seq_lengths
    owner_length = jnp.sum(chosen * seq_lengths[None, :], axis=1)
    owner_start = jnp.cumsum(owner_length) - owner_length
    owner_from = jnp.sum(chosen * given_start[None, :], axis=1)
    placed_at = jnp.sum(chosen * owner_start[:, None], axis=0)
    column = slot_ids[:, None]
    within = (column >= owner_start[None, :]) & (column < (owner_start + owner_length)[None, :])
    offset = column - owner_start[None, :]
    source = jnp.sum(jnp.where(within, offset + owner_from[None, :], 0), axis=1)
    position = jnp.sum(jnp.where(within, offset, 0), axis=1)
    given_within = (column >= given_start[None, :]) & (
        column < (given_start + seq_lengths)[None, :]
    )
    target = jnp.sum(
        jnp.where(given_within, column - given_start[None, :] + placed_at[None, :], 0), axis=1
    )
    return (source, target, position)


def sigmoid(v):
    return 1.0 / (1.0 + jnp.exp(-v))


def spread(column, lanes=128):
    return jnp.broadcast_to(column, (column.shape[0], lanes))


def conv_pre(x, conv_w, conv_b, place):
    pre = conv_b + conv_w[KW - 1 : KW] * x
    for back in range(1, KW):
        moved = pltpu.roll(x, back, 0)
        pre = pre + jnp.where(place >= back, conv_w[KW - 1 - back : KW - back] * moved, 0.0)
    return pre


def block_terms(row, position_ref, run_ref, run_t_ref):
    place = spread(position_ref[pl.ds(row, SPAN), :])
    local = lax.broadcasted_iota(jnp.int32, (SPAN, 128), 0)
    across = lax.broadcasted_iota(jnp.int32, (SPAN, 128), 1)
    begins = local - place
    causal = (across <= local) & (across >= begins)
    last_begin = begins[SPAN - 1 : SPAN, :]
    reach_end = local >= last_begin
    entered = place >= local + 1
    carries = place[SPAN - 1 : SPAN, :] >= SPAN
    return causal, reach_end, entered, carries


def pair_terms(pair, run, run_t, step, causal, reach_end, entered, carries):
    left = lax.broadcasted_iota(jnp.int32, (SPAN, 128), 1) < P_SIZE
    runs = [spread(run[:, 2 * pair + i : 2 * pair + i + 1]) for i in range(2)]
    decays = []
    for i in range(2):
        gap = runs[i] - run_t[2 * pair + i : 2 * pair + i + 1, :]
        decays.append(jnp.exp(jnp.where(causal, gap, -jnp.inf)))
    both = jnp.where(left, runs[0], runs[1])
    end = both[SPAN - 1 : SPAN, :]
    entering = jnp.where(entered, jnp.exp(both), 0.0)
    tail = jnp.where(reach_end, jnp.exp(jnp.where(reach_end, end - both, 0.0)), 0.0)
    carried = jnp.where(carries, jnp.exp(end), 0.0)
    size = jnp.where(
        left,
        spread(step[:, 2 * pair : 2 * pair + 1]),
        spread(step[:, 2 * pair + 1 : 2 * pair + 2]),
    )
    return left, decays, entering, tail, carried, size


def stacked(value, left):
    zero = jnp.zeros_like(value)
    return jnp.concatenate([jnp.where(left, value, zero), jnp.where(left, zero, value)], axis=0)


def step_and_run(dt_ref, dt_bias_ref, a_log_ref, run_ref, step_ref, length):
    step_ref[...] = jax.nn.softplus(dt_ref[...] + dt_bias_ref[...])
    lower = (
        lax.broadcasted_iota(jnp.int32, (SPAN, SPAN), 0)
        >= lax.broadcasted_iota(jnp.int32, (SPAN, SPAN), 1)
    ).astype(F32)

    def block(b, unused):
        rows = pl.ds(pl.multiple_of(b * SPAN, SPAN), SPAN)
        log_decay = -step_ref[rows, :] * jnp.exp(a_log_ref[...])
        run_ref[rows, :] = jnp.dot(
            lower, log_decay, precision=lax.Precision.HIGHEST, preferred_element_type=F32
        )
        return unused

    lax.fori_loop(0, length // SPAN, block, 0)


def forward_kernel(
    conv_in_ref,
    dt_ref,
    position_ref,
    conv_w_ref,
    conv_b_ref,
    dt_bias_ref,
    a_log_ref,
    d_skip_ref,
    mixed_ref,
    starts_ref,
    act_ref,
    step_ref,
    run_ref,
    state_ref,
):
    length, width = mixed_ref.shape
    place = spread(position_ref[...])
    for c in range((width + 2 * N) // 128):
        lanes = slice(128 * c, 128 * c + 128)
        pre = conv_pre(
            conv_in_ref[:, lanes].astype(F32), conv_w_ref[:, lanes], conv_b_ref[:, lanes], place
        )
        act_ref[:, lanes] = (pre * sigmoid(pre)).astype(BF)
    step_and_run(dt_ref, dt_bias_ref, a_log_ref, run_ref, step_ref, length)
    state_ref[...] = jnp.zeros_like(state_ref)

    def block(b, unused):
        row = pl.multiple_of(b * SPAN, SPAN)
        rows = pl.ds(row, SPAN)
        starts_ref[pl.ds(pl.multiple_of(b * N, N), N), :] = state_ref[...]
        run = run_ref[rows, :]
        run_t = run.T
        step = step_ref[rows, :]
        masks = block_terms(row, position_ref, run_ref, run_t)
        in_map = act_ref[rows, width : width + N]
        out_map = act_ref[rows, width + N : width + 2 * N]
        products = dot_nt(out_map, in_map)
        in_map_t = in_map.T
        for pair in range(width // 128):
            lanes = slice(128 * pair, 128 * pair + 128)
            left, decays, entering, tail, carried, size = pair_terms(
                pair, run, run_t, step, *masks
            )
            values = act_ref[rows, lanes].astype(F32)
            scaled = values * size
            weights = jnp.concatenate([(d * products).astype(BF) for d in decays], axis=1)
            out = dot_nn(weights, stacked(scaled.astype(BF), left))
            state = state_ref[:, lanes]
            high, low = halves(state)
            out += entering * (dot_nn(out_map, high) + dot_nn(out_map, low))
            mixed_ref[rows, lanes] = out + d_skip_ref[:, lanes] * values
            high, low = halves(tail * scaled)
            fresh = dot_nn(in_map_t, high) + dot_nn(in_map_t, low)
            state_ref[:, lanes] = carried * state + fresh
        return unused

    lax.fori_loop(0, length // SPAN, block, 0)


def backward_kernel(
    conv_in_ref,
    dt_ref,
    position_ref,
    conv_w_ref,
    conv_b_ref,
    dt_bias_ref,
    a_log_ref,
    d_skip_ref,
    mixed_ref,
    starts_ref,
    grad_ref,
    join_ref,
    grad_values_ref,
    grad_maps_ref,
    grad_dt_ref,
    grad_conv_w_ref,
    grad_conv_b_ref,
    grad_head_ref,
    grad_skip_ref,
    act_ref,
    pre_ref,
    step_ref,
    run_ref,
    state_ref,
    grad_act_ref,
    joined_ref,
):
    length, width = mixed_ref.shape
    blocks = length // SPAN
    place = spread(position_ref[...])
    for c in range((width + 2 * N) // 128):
        lanes = slice(128 * c, 128 * c + 128)
        pre = conv_pre(
            conv_in_ref[:, lanes].astype(F32), conv_w_ref[:, lanes], conv_b_ref[:, lanes], place
        )
        pre_ref[:, lanes] = pre
        act_ref[:, lanes] = (pre * sigmoid(pre)).astype(BF)
    step_and_run(dt_ref, dt_bias_ref, a_log_ref, run_ref, step_ref, length)
    state_ref[...] = jnp.zeros_like(state_ref)
    grad_head_ref[...] = jnp.zeros_like(grad_head_ref)
    grad_skip_ref[...] = jnp.zeros_like(grad_skip_ref)
    upper = (
        lax.broadcasted_iota(jnp.int32, (SPAN, SPAN), 0)
        <= lax.broadcasted_iota(jnp.int32, (SPAN, SPAN), 1)
    ).astype(F32)
    last_row = lax.broadcasted_iota(jnp.int32, (SPAN, 128), 0) == SPAN - 1

    def block(count, unused):
        b = blocks - 1 - count
        row = pl.multiple_of(b * SPAN, SPAN)
        rows = pl.ds(row, SPAN)
        start_rows = pl.ds(pl.multiple_of(b * N, N), N)
        run = run_ref[rows, :]
        run_t = run.T
        step = step_ref[rows, :]
        masks = block_terms(row, position_ref, run_ref, run_t)
        in_map = act_ref[rows, width : width + N]
        out_map = act_ref[rows, width + N : width + 2 * N]
        out_map_t = out_map.T
        products = dot_nt(out_map, in_map)
        grad_products = jnp.zeros((SPAN, SPAN), F32)
        grad_out_map = jnp.zeros((SPAN, N), F32)
        grad_in_map = jnp.zeros((SPAN, N), F32)
        for pair in range(width // 128):
            lanes = slice(128 * pair, 128 * pair + 128)
            left, decays, entering, tail, carried, size = pair_terms(
                pair, run, run_t, step, *masks
            )
            values = act_ref[rows, lanes].astype(F32)
            grad = grad_ref[rows, lanes]
            start = starts_ref[start_rows, lanes]
            later = state_ref[:, lanes]
            scaled = values * size
            scaled_low = scaled.astype(BF)
            grad_low = grad.astype(BF)
            weights = jnp.concatenate([(d * products).astype(BF) for d in decays], axis=0)
            grad_scaled = dot_tn(weights, stacked(grad_low, left))
            grad_pairs = dot_nt(grad_low, stacked(scaled_low, left))
            grad_products += (
                grad_pairs[:, :SPAN] * decays[0] + grad_pairs[:, SPAN:] * decays[1]
            )
            later_high, later_low = halves(later)
            from_later = tail * (dot_nn(in_map, later_high) + dot_nn(in_map, later_low))
            grad_scaled += from_later
            entering_grad = entering * grad
            entering_high, entering_low = halves(entering_grad)
            start_high = start.astype(BF)
            grad_out_map += dot_nt(entering_high, start_high)
            grad_in_map += dot_nt((tail * scaled).astype(BF), later_high)
            ending = jnp.sum(scaled * from_later, axis=0, keepdims=True) + carried * jnp.sum(
                start * later, axis=0, keepdims=True
            )
            state_ref[:, lanes] = (
                carried * later + dot_nn(out_map_t, entering_high) + dot_nn(out_map_t, entering_low)
            )
            skip = d_skip_ref[:, lanes]
            inner = mixed_ref[rows, lanes] - skip * values
            grad_run = (
                grad_low.astype(F32) * inner
                - scaled_low.astype(F32) * (grad_scaled - from_later)
                - scaled * from_later
                + jnp.where(last_row, ending, 0.0)
            )
            joined_ref[0:SPAN, lanes] = grad_run
            joined_ref[SPAN : 2 * SPAN, lanes] = grad_scaled * values
            grad_act_ref[rows, lanes] = grad_scaled * size + skip * grad
            grad_skip_ref[:, lanes] += jnp.sum(grad * values, axis=0, keepdims=True)
        grad_products = grad_products.astype(BF)
        grad_act_ref[rows, width : width + N] = grad_in_map + dot_tn(grad_products, out_map)
        grad_act_ref[rows, width + N : width + 2 * N] = grad_out_map + dot_nn(
            grad_products, in_map
        )
        joined = joined_ref[...]
        first = joined.astype(BF)
        rest = joined - first.astype(F32)
        second, third = halves(rest)
        join = join_ref[...]
        by_head = dot_nn(first, join) + dot_nn(second, join) + dot_nn(third, join)
        grad_log = jnp.dot(
            upper, by_head[:SPAN], precision=lax.Precision.HIGHEST, preferred_element_type=F32
        )
        rate = jnp.exp(a_log_ref[...])
        log_decay = -step * rate
        grad_step = by_head[SPAN:] - grad_log * rate
        grad_dt = grad_step * sigmoid(dt_ref[rows, :] + dt_bias_ref[...])
        grad_dt_ref[rows, :] = grad_dt
        grad_head_ref[0:1, :] += jnp.sum(grad_dt, axis=0, keepdims=True)
        grad_head_ref[1:2, :] += jnp.sum(grad_log * log_decay, axis=0, keepdims=True)
        return unused

    lax.fori_loop(0, blocks, block, 0)

    for c in range((width + 2 * N) // 128):
        lanes = slice(128 * c, 128 * c + 128)
        x = conv_in_ref[:, lanes].astype(F32)
        conv_w = conv_w_ref[:, lanes]
        pre = pre_ref[:, lanes]
        gain = sigmoid(pre)
        grad_pre = grad_act_ref[:, lanes] * (gain * (1.0 + pre * (1.0 - gain)))
        grad_conv_b_ref[:, lanes] = jnp.sum(grad_pre, axis=0, keepdims=True)
        grad_conv_w_ref[KW - 1 : KW, lanes] = jnp.sum(grad_pre * x, axis=0, keepdims=True)
        grad_x = conv_w[KW - 1 : KW] * grad_pre
        for back in range(1, KW):
            tap = KW - 1 - back
            kept = jnp.where(place >= back, grad_pre, 0.0)
            grad_conv_w_ref[tap : tap + 1, lanes] = jnp.sum(
                kept * pltpu.roll(x, back, 0), axis=0, keepdims=True
            )
            grad_x += conv_w[tap : tap + 1] * pltpu.roll(kept, length - back, 0)
        if c < width // 128:
            grad_values_ref[:, lanes] = grad_x.astype(BF)
        else:
            grad_maps_ref[:, 128 * c - width : 128 * c - width + 128] = grad_x


def params():
    return pltpu.CompilerParams(vmem_limit_bytes=VMEM_BYTES)


def run_forward(conv_in, dt, position, conv_w, conv_b, dt_bias, a_log, d_skip):
    length = conv_in.shape[0]
    width = conv_in.shape[1] - 2 * N
    blocks = length // SPAN
    return pl.pallas_call(
        forward_kernel,
        out_shape=(
            jax.ShapeDtypeStruct((length, width), F32),
            jax.ShapeDtypeStruct((blocks * N, width), F32),
        ),
        scratch_shapes=[
            pltpu.VMEM((length, width + 2 * N), BF),
            pltpu.VMEM((length, 128), F32),
            pltpu.VMEM((length, 128), F32),
            pltpu.VMEM((N, width), F32),
        ],
        compiler_params=params(),
        cost_estimate=pl.CostEstimate(
            flops=20 * length * width * 128, bytes_accessed=12 * length * width, transcendentals=0
        ),
        name="mixer_forward",
    )(conv_in, dt, position, conv_w, conv_b, dt_bias, a_log, d_skip)


def run_backward(
    conv_in, dt, position, conv_w, conv_b, dt_bias, a_log, d_skip, mixed, starts, grad, join
):
    length = conv_in.shape[0]
    width = conv_in.shape[1] - 2 * N
    return pl.pallas_call(
        backward_kernel,
        out_shape=(
            jax.ShapeDtypeStruct((length, width), BF),
            jax.ShapeDtypeStruct((length, 2 * N), F32),
            jax.ShapeDtypeStruct((length, 128), F32),
            jax.ShapeDtypeStruct((KW, width + 2 * N), F32),
            jax.ShapeDtypeStruct((1, width + 2 * N), F32),
            jax.ShapeDtypeStruct((8, 128), F32),
            jax.ShapeDtypeStruct((1, width), F32),
        ),
        scratch_shapes=[
            pltpu.VMEM((length, width + 2 * N), BF),
            pltpu.VMEM((length, width + 2 * N), F32),
            pltpu.VMEM((length, 128), F32),
            pltpu.VMEM((length, 128), F32),
            pltpu.VMEM((N, width), F32),
            pltpu.VMEM((length, width + 2 * N), F32),
            pltpu.VMEM((2 * SPAN, width), F32),
        ],
        compiler_params=params(),
        cost_estimate=pl.CostEstimate(
            flops=40 * length * width * 128, bytes_accessed=20 * length * width, transcendentals=0
        ),
        name="mixer_backward",
    )(conv_in, dt, position, conv_w, conv_b, dt_bias, a_log, d_skip, mixed, starts, grad, join)


def exchange(pieces, axis, mine):
    count = lax.axis_size(axis)
    own = pieces(mine)
    gathered = jnp.zeros((count,) + own.shape, own.dtype)
    gathered = lax.dynamic_update_index_in_dim(gathered, own, mine, 0)
    for other in range(1, count):
        arrived = lax.ppermute(
            pieces(mine ^ other), axis, [(i, i ^ other) for i in range(count)]
        )
        gathered = lax.dynamic_update_index_in_dim(gathered, arrived, mine ^ other, 0)
    return gathered


def columns_at(array, start, width):
    return lax.dynamic_slice_in_dim(array, start, width, axis=1)


def on_device(
    x_in,
    cotangent,
    seq_lengths,
    seq_order,
    valid,
    norm_gain,
    w_in,
    conv_w,
    conv_b,
    dt_bias,
    a_log,
    d_skip,
    gated_gain,
    w_out,
):
    shards, mine = lax.axis_size("shard"), lax.axis_index("shard")
    reps = lax.axis_size("rep")
    rows = x_in.shape[0]
    length = rows * shards
    depth = w_in.shape[0]
    heads = H // shards
    width = DI // shards

    w_tail = w_in[:, 2 * DI :]

    def conv_piece(d):
        return jnp.concatenate([columns_at(w_in, DI + d * width, width), w_tail], axis=1)

    def gate_piece(d):
        return columns_at(w_in, d * width, width)

    x_group = lax.all_gather(x_in, "shard", axis=0, tiled=True)
    w_conv = exchange(conv_piece, "shard", mine).reshape(D, width + TAIL)
    w_gate = exchange(gate_piece, "shard", mine).reshape(D, width)
    grad_branch = jnp.where(valid[:, None] > 0, cotangent, jnp.zeros_like(cotangent))
    grad_branch_group = lax.all_gather(grad_branch, "shard", axis=0, tiled=True)

    slot_ids = jnp.arange(length, dtype=jnp.int32)
    source, target, position = slot_tables(seq_lengths[0], seq_order[0], slot_ids)
    pick = (source[:, None] == slot_ids[None, :]).astype(BF)
    resid = dot_nn(pick, x_group)
    inverse_rms = lax.rsqrt(jnp.mean(resid * resid, axis=1, keepdims=True) + EPSILON)
    normed = (resid * inverse_rms * norm_gain[None, :]).astype(BF)
    normed_mine = lax.dynamic_slice_in_dim(normed, mine * rows, rows, axis=0)
    resid_mine = lax.dynamic_slice_in_dim(resid, mine * rows, rows, axis=0)
    few = reps * length * D * 2 <= GATHER_BYTES
    if few:
        normed_all = lax.all_gather(normed_mine, ALL, axis=0, tiled=True)

    projected = dot_nn(normed, w_conv).astype(BF)
    gate_low = dot_nn(normed, w_gate).astype(BF)
    conv_in = projected[:, : width + 2 * N]
    dt_all = projected[:, width + 2 * N :].astype(F32)

    def own_heads(row):
        picked = columns_at(row, mine * heads, heads)
        return jnp.pad(picked, ((0, 0), (0, 128 - heads)))

    dt = own_heads(dt_all)
    bias_row, decay_row = own_heads(dt_bias[None, :]), own_heads(a_log[None, :])
    skip_row = jnp.repeat(
        lax.dynamic_slice_in_dim(d_skip, mine * heads, heads), P_SIZE, total_repeat_length=width
    )[None, :]

    def own_conv(array):
        return jnp.concatenate([columns_at(array, mine * width, width), array[:, DI:]], axis=1)

    conv_w_own, conv_b_own = own_conv(conv_w), own_conv(conv_b[None, :])
    gain_row = lax.dynamic_slice_in_dim(gated_gain, mine * width, width)[None, :]
    place = position[:, None]

    mixed, starts = run_forward(
        conv_in, dt, place, conv_w_own, conv_b_own, bias_row, decay_row, skip_row
    )

    grad_normed_out = dot_nt(grad_branch_group, w_out)
    gate = gate_low.astype(F32)
    gate_gain = sigmoid(gate)
    product = mixed * (gate * gate_gain)
    weighted = grad_normed_out * gain_row
    partial_sums = jnp.stack(
        [jnp.sum(product * product, axis=1), jnp.sum(weighted * product, axis=1)]
    )
    row_sums = lax.psum(partial_sums, "shard") / DI
    inverse = lax.rsqrt(row_sums[0] + EPSILON)[:, None]
    normalized = product * inverse
    normed_out = (normalized * gain_row).astype(BF)
    grad_product = inverse * weighted - product * (inverse**3 * row_sums[1][:, None])
    grad_gated_gain = jnp.sum(grad_normed_out * normalized, axis=0)
    grad_mixed = grad_product * (gate * gate_gain)
    grad_gate = (
        grad_product * mixed * (gate_gain * (1.0 + gate * (1.0 - gate_gain)))
    ).astype(BF)

    branch = lax.psum_scatter(
        dot_nn(normed_out, w_out), "shard", scatter_dimension=0, tiled=True
    )
    total_rows = resid_mine + branch
    block_out = total_rows.astype(BF)
    weights_valid = valid.astype(F32)
    square_total = jnp.sum(weights_valid * jnp.sum(total_rows * total_rows, axis=1))
    square_branch = jnp.sum(weights_valid * jnp.sum(branch * branch, axis=1))
    valid_count = jnp.sum(weights_valid)

    grad_w_out = lax.psum(dot_tn(normed_out, grad_branch_group).astype(BF), "rep").astype(F32)

    def to_owners(columns):
        if not few:
            part = dot_tn(normed, columns).astype(BF).reshape(shards, depth, columns.shape[1])
            swapped = lax.all_to_all(part, "shard", split_axis=0, concat_axis=0, tiled=True)
            summed = lax.psum(swapped, "rep").astype(F32)
            return summed.transpose(1, 0, 2).reshape(depth, shards * columns.shape[1])
        share = columns.shape[1] // reps
        split = columns.reshape(length, reps, share).transpose(1, 0, 2)
        taken = lax.all_to_all(split, "rep", split_axis=0, concat_axis=0, tiled=True)
        summed = dot_tn(normed_all, taken.reshape(reps * length, share)).astype(BF)
        swapped = lax.all_to_all(
            summed.reshape(shards, depth, share), "shard", split_axis=0, concat_axis=0, tiled=True
        )
        whole = lax.all_gather(swapped, "rep")
        return whole.transpose(2, 1, 0, 3).reshape(depth, DI).astype(F32)

    grad_w_gate = to_owners(grad_gate)

    join = (
        jnp.arange(width, dtype=jnp.int32)[:, None] // P_SIZE
        == jnp.arange(128, dtype=jnp.int32)[None, :]
    ).astype(BF)
    grad_values, grad_maps, grad_dt, grad_conv_w, grad_conv_b, grad_head, grad_skip = run_backward(
        conv_in,
        dt,
        place,
        conv_w_own,
        conv_b_own,
        bias_row,
        decay_row,
        skip_row,
        mixed,
        starts,
        grad_mixed,
        join,
    )
    grad_maps = lax.psum_scatter(
        grad_maps, "shard", scatter_dimension=1, tiled=True
    ).astype(BF)
    grad_dt_low = grad_dt[:, :heads].astype(BF)
    share = 2 * N // shards
    grad_tail = jnp.concatenate([grad_maps, grad_dt_low], axis=1)

    back = (target[:, None] == slot_ids[None, :]).astype(BF)
    grad_own = jnp.concatenate([grad_gate, grad_values, grad_tail], axis=1)
    grad_given = dot_nn(back, grad_own).astype(BF)
    w_own = jnp.concatenate(
        [
            w_gate,
            w_conv[:, :width],
            columns_at(w_conv, width + mine * share, share),
            columns_at(w_conv, width + 2 * N + mine * heads, heads),
        ],
        axis=1,
    )
    grad_normed = lax.psum_scatter(
        dot_nt(grad_given, w_own), "shard", scatter_dimension=0, tiled=True
    )
    given = x_in.astype(F32)
    given_rms = lax.rsqrt(jnp.mean(given * given, axis=1, keepdims=True) + EPSILON)
    grad_norm_gain = jnp.sum(grad_normed * (given * given_rms), axis=0)
    scaled = grad_normed * norm_gain[None, :]
    grad_resid = scaled * given_rms - given * (
        given_rms**3 * jnp.mean(scaled * given, axis=1, keepdims=True)
    )
    back_mine = lax.dynamic_slice_in_dim(back, mine * rows, rows, axis=0)
    grad_in = (grad_resid + dot_nn(back_mine, grad_branch_group)).astype(BF)

    grad_w_values = to_owners(grad_values)
    if few:
        tails = lax.all_gather(grad_tail, ALL, axis=0, tiled=False)
        tails = tails.reshape(reps, shards, length, share + heads).transpose(0, 2, 1, 3)
        tails = jnp.concatenate(
            [
                tails[..., :share].reshape(reps * length, 2 * N),
                tails[..., share:].reshape(reps * length, H),
            ],
            axis=1,
        )
        grad_w_tail = dot_tn(columns_at(normed_all, mine * depth, depth), tails)
    else:
        parts = to_owners(grad_tail).reshape(depth, shards, share + heads)
        grad_w_tail = jnp.concatenate(
            [parts[..., :share].reshape(depth, 2 * N), parts[..., share:].reshape(depth, H)], axis=1
        )
    grad_w_in = jnp.concatenate([grad_w_gate, grad_w_values, grad_w_tail], axis=1)

    def placed(part, whole, start):
        return lax.dynamic_update_slice_in_dim(
            jnp.zeros(part.shape[:-1] + (whole,), F32), part, start, axis=part.ndim - 1
        )

    def placed_conv(part):
        return jnp.concatenate(
            [placed(part[:, :width], DI, mine * width), part[:, width:]], axis=1
        )

    grad_skip_heads = jnp.sum(grad_skip.reshape(heads, P_SIZE), axis=1)
    pieces = (
        grad_norm_gain,
        placed_conv(grad_conv_w).reshape(-1),
        placed_conv(grad_conv_b).reshape(-1),
        placed(grad_head[0, :heads], H, mine * heads),
        placed(grad_head[1, :heads], H, mine * heads),
        placed(grad_skip_heads, H, mine * heads),
        placed(grad_gated_gain, DI, mine * width),
        jnp.stack([square_total, square_branch, valid_count]),
    )
    summed = lax.psum(jnp.concatenate(pieces), ALL)
    results, at = [], 0
    for piece in pieces:
        results.append(summed[at : at + piece.shape[0]])
        at += piece.shape[0]
    count_all = jnp.maximum(results[7][2], 1.0)
    rms_residual = jnp.sqrt(results[7][0] / (count_all * D))
    rms_mixer = jnp.sqrt(results[7][1] / (count_all * D))
    return (
        block_out,
        grad_in,
        results[0],
        grad_w_in,
        results[1].reshape(KW, CONVW),
        results[2],
        results[3],
        results[4],
        results[5],
        results[6],
        grad_w_out,
        rms_residual,
        rms_mixer,
    )


def solution(mesh):
    in_specs = (
        P(ALL, None),
        P(ALL, None),
        P("rep", None),
        P("rep", None),
        P(ALL),
        P(),
        P("shard", None),
        P(),
        P(),
        P(),
        P(),
        P(),
        P(),
        P("shard", None),
    )
    out_specs = (
        P(ALL, None),
        P(ALL, None),
        P(),
        P("shard", None),
        P(),
        P(),
        P(),
        P(),
        P(),
        P(),
        P("shard", None),
        P(),
        P(),
    )
    return jax.shard_map(
        on_device, mesh=mesh, in_specs=in_specs, out_specs=out_specs, check_vma=False
    )
```

```python
import functools

import jax
import jax.numpy as jnp
from jax import lax
from jax.experimental import pallas as pl
from jax.experimental.pallas import tpu as pltpu
from jax.sharding import PartitionSpec as P

D = 2048
H = 64
P_SIZE = 64
N = 128
KW = 4
SPAN = 128
DI = 4096
CONVW = 4352
PROJ = 8512
TAIL = PROJ - 2 * DI

EPSILON = 1e-05
ALL = ("rep", "shard")
VMEM_BYTES = 56 * 1024 * 1024
BF = jnp.bfloat16
F32 = jnp.float32


def dot_nn(a, b):
    return lax.dot_general(a, b, (((1,), (0,)), ((), ())), preferred_element_type=F32)


def dot_nt(a, b):
    return lax.dot_general(a, b, (((1,), (1,)), ((), ())), preferred_element_type=F32)


def dot_tn(a, b):
    return lax.dot_general(a, b, (((0,), (0,)), ((), ())), preferred_element_type=F32)


def halves(a):
    high = a.astype(BF)
    return high, (a - high.astype(F32)).astype(BF)


def slot_tables(seq_lengths, seq_order, slot_ids):
    seq_count = seq_lengths.shape[0]
    numbers = jnp.arange(seq_count, dtype=jnp.int32)
    chosen = (seq_order[:, None] == numbers[None, :]).astype(jnp.int32)
    given_start = jnp.cumsum(seq_lengths) - seq_lengths
    owner_length = jnp.sum(chosen * seq_lengths[None, :], axis=1)
    owner_start = jnp.cumsum(owner_length) - owner_length
    owner_from = jnp.sum(chosen * given_start[None, :], axis=1)
    placed_at = jnp.sum(chosen * owner_start[:, None], axis=0)
    column = slot_ids[:, None]
    within = (column >= owner_start[None, :]) & (column < (owner_start + owner_length)[None, :])
    offset = column - owner_start[None, :]
    source = jnp.sum(jnp.where(within, offset + owner_from[None, :], 0), axis=1)
    position = jnp.sum(jnp.where(within, offset, 0), axis=1)
    given_within = (column >= given_start[None, :]) & (
        column < (given_start + seq_lengths)[None, :]
    )
    target = jnp.sum(
        jnp.where(given_within, column - given_start[None, :] + placed_at[None, :], 0), axis=1
    )
    return (source, target, position)


def sigmoid(v):
    return 1.0 / (1.0 + jnp.exp(-v))


def spread(column, lanes=128):
    return jnp.broadcast_to(column, (column.shape[0], lanes))


def conv_pre(x, conv_w, conv_b, place):
    pre = conv_b + conv_w[KW - 1 : KW] * x
    for back in range(1, KW):
        moved = pltpu.roll(x, back, 0)
        pre = pre + jnp.where(place >= back, conv_w[KW - 1 - back : KW - back] * moved, 0.0)
    return pre


def block_terms(row, position_ref, run_ref, run_t_ref):
    place = spread(position_ref[pl.ds(row, SPAN), :])
    local = lax.broadcasted_iota(jnp.int32, (SPAN, 128), 0)
    across = lax.broadcasted_iota(jnp.int32, (SPAN, 128), 1)
    begins = local - place
    causal = (across <= local) & (across >= begins)
    last_begin = begins[SPAN - 1 : SPAN, :]
    reach_end = local >= last_begin
    entered = place >= local + 1
    carries = place[SPAN - 1 : SPAN, :] >= SPAN
    return causal, reach_end, entered, carries


def pair_terms(pair, run, run_t, step, causal, reach_end, entered, carries):
    left = lax.broadcasted_iota(jnp.int32, (SPAN, 128), 1) < P_SIZE
    runs = [spread(run[:, 2 * pair + i : 2 * pair + i + 1]) for i in range(2)]
    decays = []
    for i in range(2):
        gap = runs[i] - run_t[2 * pair + i : 2 * pair + i + 1, :]
        decays.append(jnp.exp(jnp.where(causal, gap, -jnp.inf)))
    both = jnp.where(left, runs[0], runs[1])
    end = both[SPAN - 1 : SPAN, :]
    entering = jnp.where(entered, jnp.exp(both), 0.0)
    tail = jnp.where(reach_end, jnp.exp(jnp.where(reach_end, end - both, 0.0)), 0.0)
    carried = jnp.where(carries, jnp.exp(end), 0.0)
    size = jnp.where(
        left,
        spread(step[:, 2 * pair : 2 * pair + 1]),
        spread(step[:, 2 * pair + 1 : 2 * pair + 2]),
    )
    return left, decays, entering, tail, carried, size


def stacked(value, left):
    zero = jnp.zeros_like(value)
    return jnp.concatenate([jnp.where(left, value, zero), jnp.where(left, zero, value)], axis=0)


def step_and_run(dt_ref, dt_bias_ref, a_log_ref, run_ref, step_ref, length):
    step_ref[...] = jax.nn.softplus(dt_ref[...] + dt_bias_ref[...])
    lower = (
        lax.broadcasted_iota(jnp.int32, (SPAN, SPAN), 0)
        >= lax.broadcasted_iota(jnp.int32, (SPAN, SPAN), 1)
    ).astype(F32)

    def block(b, unused):
        rows = pl.ds(pl.multiple_of(b * SPAN, SPAN), SPAN)
        log_decay = -step_ref[rows, :] * jnp.exp(a_log_ref[...])
        run_ref[rows, :] = jnp.dot(
            lower, log_decay, precision=lax.Precision.HIGHEST, preferred_element_type=F32
        )
        return unused

    lax.fori_loop(0, length // SPAN, block, 0)


def forward_kernel(
    conv_in_ref,
    dt_ref,
    position_ref,
    conv_w_ref,
    conv_b_ref,
    dt_bias_ref,
    a_log_ref,
    d_skip_ref,
    mixed_ref,
    starts_ref,
    act_ref,
    step_ref,
    run_ref,
    state_ref,
):
    length, width = mixed_ref.shape
    place = spread(position_ref[...])
    for c in range((width + 2 * N) // 128):
        lanes = slice(128 * c, 128 * c + 128)
        pre = conv_pre(
            conv_in_ref[:, lanes].astype(F32), conv_w_ref[:, lanes], conv_b_ref[:, lanes], place
        )
        act_ref[:, lanes] = (pre * sigmoid(pre)).astype(BF)
    step_and_run(dt_ref, dt_bias_ref, a_log_ref, run_ref, step_ref, length)
    state_ref[...] = jnp.zeros_like(state_ref)

    def block(b, unused):
        row = pl.multiple_of(b * SPAN, SPAN)
        rows = pl.ds(row, SPAN)
        starts_ref[pl.ds(pl.multiple_of(b * N, N), N), :] = state_ref[...]
        run = run_ref[rows, :]
        run_t = run.T
        step = step_ref[rows, :]
        masks = block_terms(row, position_ref, run_ref, run_t)
        in_map = act_ref[rows, width : width + N]
        out_map = act_ref[rows, width + N : width + 2 * N]
        products = dot_nt(out_map, in_map)
        in_map_t = in_map.T
        for pair in range(width // 128):
            lanes = slice(128 * pair, 128 * pair + 128)
            left, decays, entering, tail, carried, size = pair_terms(
                pair, run, run_t, step, *masks
            )
            values = act_ref[rows, lanes].astype(F32)
            scaled = values * size
            weights = jnp.concatenate([(d * products).astype(BF) for d in decays], axis=1)
            out = dot_nn(weights, stacked(scaled.astype(BF), left))
            state = state_ref[:, lanes]
            high, low = halves(state)
            out += entering * (dot_nn(out_map, high) + dot_nn(out_map, low))
            mixed_ref[rows, lanes] = out + d_skip_ref[:, lanes] * values
            high, low = halves(tail * scaled)
            fresh = dot_nn(in_map_t, high) + dot_nn(in_map_t, low)
            state_ref[:, lanes] = carried * state + fresh
        return unused

    lax.fori_loop(0, length // SPAN, block, 0)


def backward_kernel(
    conv_in_ref,
    dt_ref,
    position_ref,
    conv_w_ref,
    conv_b_ref,
    dt_bias_ref,
    a_log_ref,
    d_skip_ref,
    mixed_ref,
    starts_ref,
    grad_ref,
    join_ref,
    grad_values_ref,
    grad_maps_ref,
    grad_dt_ref,
    grad_conv_w_ref,
    grad_conv_b_ref,
    grad_head_ref,
    grad_skip_ref,
    act_ref,
    pre_ref,
    step_ref,
    run_ref,
    state_ref,
    grad_act_ref,
    joined_ref,
):
    length, width = mixed_ref.shape
    blocks = length // SPAN
    place = spread(position_ref[...])
    for c in range((width + 2 * N) // 128):
        lanes = slice(128 * c, 128 * c + 128)
        pre = conv_pre(
            conv_in_ref[:, lanes].astype(F32), conv_w_ref[:, lanes], conv_b_ref[:, lanes], place
        )
        pre_ref[:, lanes] = pre
        act_ref[:, lanes] = (pre * sigmoid(pre)).astype(BF)
    step_and_run(dt_ref, dt_bias_ref, a_log_ref, run_ref, step_ref, length)
    state_ref[...] = jnp.zeros_like(state_ref)
    grad_head_ref[...] = jnp.zeros_like(grad_head_ref)
    grad_skip_ref[...] = jnp.zeros_like(grad_skip_ref)
    upper = (
        lax.broadcasted_iota(jnp.int32, (SPAN, SPAN), 0)
        <= lax.broadcasted_iota(jnp.int32, (SPAN, SPAN), 1)
    ).astype(F32)
    last_row = lax.broadcasted_iota(jnp.int32, (SPAN, 128), 0) == SPAN - 1

    def block(count, unused):
        b = blocks - 1 - count
        row = pl.multiple_of(b * SPAN, SPAN)
        rows = pl.ds(row, SPAN)
        start_rows = pl.ds(pl.multiple_of(b * N, N), N)
        run = run_ref[rows, :]
        run_t = run.T
        step = step_ref[rows, :]
        masks = block_terms(row, position_ref, run_ref, run_t)
        in_map = act_ref[rows, width : width + N]
        out_map = act_ref[rows, width + N : width + 2 * N]
        out_map_t = out_map.T
        products = dot_nt(out_map, in_map)
        grad_products = jnp.zeros((SPAN, SPAN), F32)
        grad_out_map = jnp.zeros((SPAN, N), F32)
        grad_in_map = jnp.zeros((SPAN, N), F32)
        for pair in range(width // 128):
            lanes = slice(128 * pair, 128 * pair + 128)
            left, decays, entering, tail, carried, size = pair_terms(
                pair, run, run_t, step, *masks
            )
            values = act_ref[rows, lanes].astype(F32)
            grad = grad_ref[rows, lanes]
            start = starts_ref[start_rows, lanes]
            later = state_ref[:, lanes]
            scaled = values * size
            scaled_low = scaled.astype(BF)
            grad_low = grad.astype(BF)
            weights = jnp.concatenate([(d * products).astype(BF) for d in decays], axis=0)
            grad_scaled = dot_tn(weights, stacked(grad_low, left))
            grad_pairs = dot_nt(grad_low, stacked(scaled_low, left))
            grad_products += (
                grad_pairs[:, :SPAN] * decays[0] + grad_pairs[:, SPAN:] * decays[1]
            )
            later_high, later_low = halves(later)
            from_later = tail * (dot_nn(in_map, later_high) + dot_nn(in_map, later_low))
            grad_scaled += from_later
            entering_grad = entering * grad
            entering_high, entering_low = halves(entering_grad)
            start_high = start.astype(BF)
            grad_out_map += dot_nt(entering_high, start_high)
            grad_in_map += dot_nt((tail * scaled).astype(BF), later_high)
            ending = jnp.sum(scaled * from_later, axis=0, keepdims=True) + carried * jnp.sum(
                start * later, axis=0, keepdims=True
            )
            state_ref[:, lanes] = (
                carried * later + dot_nn(out_map_t, entering_high) + dot_nn(out_map_t, entering_low)
            )
            skip = d_skip_ref[:, lanes]
            inner = mixed_ref[rows, lanes] - skip * values
            grad_run = (
                grad_low.astype(F32) * inner
                - scaled_low.astype(F32) * (grad_scaled - from_later)
                - scaled * from_later
                + jnp.where(last_row, ending, 0.0)
            )
            joined_ref[0:SPAN, lanes] = grad_run
            joined_ref[SPAN : 2 * SPAN, lanes] = grad_scaled * values
            grad_act_ref[rows, lanes] = grad_scaled * size + skip * grad
            grad_skip_ref[:, lanes] += jnp.sum(grad * values, axis=0, keepdims=True)
        grad_products = grad_products.astype(BF)
        grad_act_ref[rows, width : width + N] = grad_in_map + dot_tn(grad_products, out_map)
        grad_act_ref[rows, width + N : width + 2 * N] = grad_out_map + dot_nn(
            grad_products, in_map
        )
        joined = joined_ref[...]
        first = joined.astype(BF)
        rest = joined - first.astype(F32)
        second, third = halves(rest)
        join = join_ref[...]
        by_head = dot_nn(first, join) + dot_nn(second, join) + dot_nn(third, join)
        grad_log = jnp.dot(
            upper, by_head[:SPAN], precision=lax.Precision.HIGHEST, preferred_element_type=F32
        )
        rate = jnp.exp(a_log_ref[...])
        log_decay = -step * rate
        grad_step = by_head[SPAN:] - grad_log * rate
        grad_dt = grad_step * sigmoid(dt_ref[rows, :] + dt_bias_ref[...])
        grad_dt_ref[rows, :] = grad_dt
        grad_head_ref[0:1, :] += jnp.sum(grad_dt, axis=0, keepdims=True)
        grad_head_ref[1:2, :] += jnp.sum(grad_log * log_decay, axis=0, keepdims=True)
        return unused

    lax.fori_loop(0, blocks, block, 0)

    for c in range((width + 2 * N) // 128):
        lanes = slice(128 * c, 128 * c + 128)
        x = conv_in_ref[:, lanes].astype(F32)
        conv_w = conv_w_ref[:, lanes]
        pre = pre_ref[:, lanes]
        gain = sigmoid(pre)
        grad_pre = grad_act_ref[:, lanes] * (gain * (1.0 + pre * (1.0 - gain)))
        grad_conv_b_ref[:, lanes] = jnp.sum(grad_pre, axis=0, keepdims=True)
        grad_conv_w_ref[KW - 1 : KW, lanes] = jnp.sum(grad_pre * x, axis=0, keepdims=True)
        grad_x = conv_w[KW - 1 : KW] * grad_pre
        for back in range(1, KW):
            tap = KW - 1 - back
            kept = jnp.where(place >= back, grad_pre, 0.0)
            grad_conv_w_ref[tap : tap + 1, lanes] = jnp.sum(
                kept * pltpu.roll(x, back, 0), axis=0, keepdims=True
            )
            grad_x += conv_w[tap : tap + 1] * pltpu.roll(kept, length - back, 0)
        if c < width // 128:
            grad_values_ref[:, lanes] = grad_x.astype(BF)
        else:
            grad_maps_ref[:, 128 * c - width : 128 * c - width + 128] = grad_x


def params():
    return pltpu.CompilerParams(vmem_limit_bytes=VMEM_BYTES)


def run_forward(conv_in, dt, position, conv_w, conv_b, dt_bias, a_log, d_skip):
    length = conv_in.shape[0]
    width = conv_in.shape[1] - 2 * N
    blocks = length // SPAN
    return pl.pallas_call(
        forward_kernel,
        out_shape=(
            jax.ShapeDtypeStruct((length, width), F32),
            jax.ShapeDtypeStruct((blocks * N, width), F32),
        ),
        scratch_shapes=[
            pltpu.VMEM((length, width + 2 * N), BF),
            pltpu.VMEM((length, 128), F32),
            pltpu.VMEM((length, 128), F32),
            pltpu.VMEM((N, width), F32),
        ],
        compiler_params=params(),
        cost_estimate=pl.CostEstimate(
            flops=20 * length * width * 128, bytes_accessed=12 * length * width, transcendentals=0
        ),
        name="mixer_forward",
    )(conv_in, dt, position, conv_w, conv_b, dt_bias, a_log, d_skip)


def run_backward(
    conv_in, dt, position, conv_w, conv_b, dt_bias, a_log, d_skip, mixed, starts, grad, join
):
    length = conv_in.shape[0]
    width = conv_in.shape[1] - 2 * N
    return pl.pallas_call(
        backward_kernel,
        out_shape=(
            jax.ShapeDtypeStruct((length, width), BF),
            jax.ShapeDtypeStruct((length, 2 * N), F32),
            jax.ShapeDtypeStruct((length, 128), F32),
            jax.ShapeDtypeStruct((KW, width + 2 * N), F32),
            jax.ShapeDtypeStruct((1, width + 2 * N), F32),
            jax.ShapeDtypeStruct((8, 128), F32),
            jax.ShapeDtypeStruct((1, width), F32),
        ),
        scratch_shapes=[
            pltpu.VMEM((length, width + 2 * N), BF),
            pltpu.VMEM((length, width + 2 * N), F32),
            pltpu.VMEM((length, 128), F32),
            pltpu.VMEM((length, 128), F32),
            pltpu.VMEM((N, width), F32),
            pltpu.VMEM((length, width + 2 * N), F32),
            pltpu.VMEM((2 * SPAN, width), F32),
        ],
        compiler_params=params(),
        cost_estimate=pl.CostEstimate(
            flops=40 * length * width * 128, bytes_accessed=20 * length * width, transcendentals=0
        ),
        name="mixer_backward",
    )(conv_in, dt, position, conv_w, conv_b, dt_bias, a_log, d_skip, mixed, starts, grad, join)


MESH = pl.DeviceIdType.MESH
LINE, PLANE = 4, 2


def end_kernel(
    gate_ref,
    values_ref,
    normed_ref,
    out_ref,
    taken,
    stripes,
    total,
    low,
    local_sem,
    stripe_sem,
    a2a_send,
    a2a_recv,
    swap_send,
    swap_recv,
    line_send,
    line_recv,
    side_send,
    side_recv,
):
    reps, shards = LINE * PLANE, lax.axis_size("shard")
    mine, rep = lax.axis_index("shard"), lax.axis_index("rep")
    z, x = rep // PLANE, lax.rem(rep, PLANE)
    beside = z * PLANE + (1 - x)
    depth = out_ref.shape[3]
    sources = (gate_ref, values_ref)

    def other(step):
        return lax.rem(z + step // PLANE, LINE) * PLANE + lax.rem(x + step % PLANE, PLANE)

    def before(step):
        return lax.rem(z + LINE - step // PLANE, LINE) * PLANE + lax.rem(
            x + PLANE - step % PLANE, PLANE
        )

    barrier = pltpu.get_barrier_semaphore()
    for step in range(1, reps):
        pl.semaphore_signal(barrier, inc=1, device_id=(other(step), mine), device_id_type=MESH)
    for step in range(1, shards):
        pl.semaphore_signal(
            barrier, inc=1, device_id=(rep, lax.rem(mine + step, shards)), device_id_type=MESH
        )
    pl.semaphore_wait(barrier, reps - 1 + shards - 1)

    def share_copy(part, step):
        peer = other(step)
        return pltpu.make_async_remote_copy(
            src_ref=sources[part].at[:, pl.ds(pl.multiple_of(peer * 128, 128), 128)],
            dst_ref=taken.at[part, step],
            send_sem=a2a_send.at[part, step],
            recv_sem=a2a_recv.at[part, step],
            device_id=(peer, mine),
            device_id_type=MESH,
        )

    def own_copy(part):
        return pltpu.make_async_copy(
            sources[part].at[:, pl.ds(pl.multiple_of(rep * 128, 128), 128)],
            taken.at[part, 0],
            local_sem.at[part],
        )

    def stripe_copy(step, slot, shard):
        group = before(step)
        return pltpu.make_async_copy(
            normed_ref.at[group, shard],
            stripes.at[slot, :, pl.ds(128 * shard, 128)],
            stripe_sem.at[slot, shard],
        )

    for part in range(2):
        own_copy(part).start()
        for step in range(1, reps):
            share_copy(part, step).start()

    def swap_copy(part, step):
        peer = lax.rem(mine + step, shards)
        return pltpu.make_async_remote_copy(
            src_ref=low.at[part, pl.ds(pl.multiple_of(peer * depth, depth), depth)],
            dst_ref=out_ref.at[rep, part, mine],
            send_sem=swap_send.at[part, step],
            recv_sem=swap_recv.at[part, step],
            device_id=(rep, peer),
            device_id_type=MESH,
        )

    def swap_own(part):
        return pltpu.make_async_copy(
            low.at[part, pl.ds(pl.multiple_of(mine * depth, depth), depth)],
            out_ref.at[rep, part, mine],
            local_sem.at[2 + part],
        )

    def line_copy(part, origin, toward, lane):
        block = out_ref.at[origin * PLANE + x, part]
        return pltpu.make_async_remote_copy(
            src_ref=block,
            dst_ref=block,
            send_sem=line_send.at[part, lane, origin],
            recv_sem=line_recv.at[part, origin],
            device_id=((z + toward) * PLANE + x, mine),
            device_id_type=MESH,
        )

    def side_copy(part, origin):
        block = out_ref.at[origin * PLANE + x, part]
        return pltpu.make_async_remote_copy(
            src_ref=block,
            dst_ref=block,
            send_sem=side_send.at[part, origin],
            recv_sem=side_recv.at[part, origin],
            device_id=(beside, mine),
            device_id_type=MESH,
        )

    def side_arrival(part, origin):
        block = out_ref.at[origin * PLANE + (1 - x), part]
        return pltpu.make_async_remote_copy(
            src_ref=block,
            dst_ref=block,
            send_sem=side_send.at[part, origin],
            recv_sem=side_recv.at[part, origin],
            device_id=(beside, mine),
            device_id_type=MESH,
        )

    for part in range(2):
        for shard in range(shards):
            stripe_copy(0, 0, shard).start()
        for step in range(reps):
            slot = step % 2
            if step + 1 < reps:
                for shard in range(shards):
                    stripe_copy(step + 1, 1 - slot, shard).start()
            if step == 0:
                own_copy(part).wait()
            else:
                share_copy(part, step).wait_recv()
            for shard in range(shards):
                stripe_copy(step, slot, shard).wait()

            def rows(i, unused, part=part, step=step, slot=slot):
                span = pl.ds(pl.multiple_of(i * 256, 256), 256)
                term = dot_nn(stripes[slot, span, :], taken[part, step])
                if step == 0:
                    total[span, :] = term
                elif step < reps - 1:
                    total[span, :] += term
                else:
                    low[part, span, :] = (total[span, :] + term).astype(BF)
                return unused

            lax.fori_loop(0, D // 256, rows, 0)
        swap_own(part).start()
        for step in range(1, shards):
            swap_copy(part, step).start()
        swap_own(part).wait()
        for step in range(1, shards):
            swap_copy(part, step).wait_recv()
        side_copy(part, z).start()

        @pl.when(z < LINE - 1)
        def _(part=part):
            line_copy(part, z, 1, 0).start()

        @pl.when(z > 0)
        def _(part=part):
            line_copy(part, z, -1, 1).start()

    for step in range(1, LINE):
        for part in range(2):

            @pl.when(z - step >= 0)
            def _(part=part, step=step):
                origin = z - step
                line_copy(part, origin, 1, 0).wait_recv()
                side_copy(part, origin).start()

                @pl.when(z < LINE - 1)
                def _():
                    line_copy(part, origin, 1, 0).start()

            @pl.when(z + step < LINE)
            def _(part=part, step=step):
                origin = z + step
                line_copy(part, origin, -1, 1).wait_recv()
                side_copy(part, origin).start()

                @pl.when(z > 0)
                def _():
                    line_copy(part, origin, -1, 1).start()

    for part in range(2):
        for origin in range(LINE):
            side_arrival(part, origin).wait_recv()
            side_copy(part, origin).wait_send()

            @pl.when((origin <= z) & (z < LINE - 1))
            def _(part=part, origin=origin):
                line_copy(part, origin, 1, 0).wait_send()

            @pl.when((origin >= z) & (z > 0))
            def _(part=part, origin=origin):
                line_copy(part, origin, -1, 1).wait_send()

        for step in range(1, shards):
            swap_copy(part, step).wait_send()
        for step in range(1, reps):
            share_copy(part, step).wait_send()


def run_end(gate, values, normed_stripes, shards):
    reps = LINE * PLANE
    length = gate.shape[0]
    depth = D // shards
    dma = pltpu.SemaphoreType.DMA
    anywhere = pl.BlockSpec(memory_space=pl.ANY)
    return pl.pallas_call(
        end_kernel,
        out_shape=jax.ShapeDtypeStruct((reps, 2, shards, depth, 128), BF),
        in_specs=[anywhere] * 3,
        out_specs=anywhere,
        scratch_shapes=[
            pltpu.VMEM((2, reps, length, 128), BF),
            pltpu.VMEM((2, D, length), BF),
            pltpu.VMEM((D, 128), F32),
            pltpu.VMEM((2, D, 128), BF),
            dma((4,)),
            dma((2, shards)),
            dma((2, reps)),
            dma((2, reps)),
            dma((2, shards)),
            dma((2, shards)),
            dma((2, 2, LINE)),
            dma((2, LINE)),
            dma((2, LINE)),
            dma((2, LINE)),
        ],
        compiler_params=pltpu.CompilerParams(
            vmem_limit_bytes=VMEM_BYTES, collective_id=1, has_side_effects=True
        ),
        cost_estimate=pl.CostEstimate(
            flops=2 * reps * length * D * 256, bytes_accessed=64 << 20, transcendentals=0
        ),
        name="weight_gradient",
    )(gate, values, normed_stripes)


def assemble_kernel(parts_ref, tail_ref, out_ref):
    reps, shards = parts_ref.shape[0], parts_ref.shape[2]
    for part in range(2):
        for shard in range(shards):
            for rep in range(reps):
                at = part * DI + (shard * reps + rep) * 128
                out_ref[:, at : at + 128] = parts_ref[rep, part, shard].astype(F32)
    out_ref[:, 2 * DI :] = tail_ref[...]


def run_assemble(parts, tail):
    reps, unused, shards, depth, unused2 = parts.shape
    step = 64
    return pl.pallas_call(
        assemble_kernel,
        grid=(depth // step,),
        out_shape=jax.ShapeDtypeStruct((depth, PROJ), F32),
        in_specs=[
            pl.BlockSpec((reps, 2, shards, step, 128), lambda i: (0, 0, 0, i, 0)),
            pl.BlockSpec((step, TAIL), lambda i: (i, 0)),
        ],
        out_specs=pl.BlockSpec((step, PROJ), lambda i: (i, 0)),
        compiler_params=params(),
        name="assemble",
    )(parts, tail)


def exchange(pieces, axis, mine):
    count = lax.axis_size(axis)
    own = pieces(mine)
    gathered = jnp.zeros((count,) + own.shape, own.dtype)
    gathered = lax.dynamic_update_index_in_dim(gathered, own, mine, 0)
    for other in range(1, count):
        arrived = lax.ppermute(
            pieces(mine ^ other), axis, [(i, i ^ other) for i in range(count)]
        )
        gathered = lax.dynamic_update_index_in_dim(gathered, arrived, mine ^ other, 0)
    return gathered


def columns_at(array, start, width):
    return lax.dynamic_slice_in_dim(array, start, width, axis=1)


def on_device(
    x_in,
    cotangent,
    seq_lengths,
    seq_order,
    valid,
    norm_gain,
    w_in,
    conv_w,
    conv_b,
    dt_bias,
    a_log,
    d_skip,
    gated_gain,
    w_out,
):
    shards, mine = lax.axis_size("shard"), lax.axis_index("shard")
    reps = lax.axis_size("rep")
    rows = x_in.shape[0]
    length = rows * shards
    depth = w_in.shape[0]
    heads = H // shards
    width = DI // shards

    w_tail = w_in[:, 2 * DI :]

    def conv_piece(d):
        return jnp.concatenate([columns_at(w_in, DI + d * width, width), w_tail], axis=1)

    def gate_piece(d):
        return columns_at(w_in, d * width, width)

    x_group = lax.all_gather(x_in, "shard", axis=0, tiled=True)
    w_conv = exchange(conv_piece, "shard", mine).reshape(D, width + TAIL)
    w_gate = exchange(gate_piece, "shard", mine).reshape(D, width)
    grad_branch = jnp.where(valid[:, None] > 0, cotangent, jnp.zeros_like(cotangent))
    grad_branch_group = lax.all_gather(grad_branch, "shard", axis=0, tiled=True)

    slot_ids = jnp.arange(length, dtype=jnp.int32)
    source, target, position = slot_tables(seq_lengths[0], seq_order[0], slot_ids)
    pick = (source[:, None] == slot_ids[None, :]).astype(BF)
    resid = dot_nn(pick, x_group)
    inverse_rms = lax.rsqrt(jnp.mean(resid * resid, axis=1, keepdims=True) + EPSILON)
    normed = (resid * inverse_rms * norm_gain[None, :]).astype(BF)
    normed_mine = lax.dynamic_slice_in_dim(normed, mine * rows, rows, axis=0)
    resid_mine = lax.dynamic_slice_in_dim(resid, mine * rows, rows, axis=0)
    few = reps == LINE * PLANE and width == reps * 128 and rows == 128
    if few:
        stripes = lax.all_gather(normed_mine.T, ALL).reshape(reps, shards, D, rows)

    projected = dot_nn(normed, w_conv).astype(BF)
    gate_low = dot_nn(normed, w_gate).astype(BF)
    conv_in = projected[:, : width + 2 * N]
    dt_all = projected[:, width + 2 * N :].astype(F32)

    def own_heads(row):
        picked = columns_at(row, mine * heads, heads)
        return jnp.pad(picked, ((0, 0), (0, 128 - heads)))

    dt = own_heads(dt_all)
    bias_row, decay_row = own_heads(dt_bias[None, :]), own_heads(a_log[None, :])
    skip_row = jnp.repeat(
        lax.dynamic_slice_in_dim(d_skip, mine * heads, heads), P_SIZE, total_repeat_length=width
    )[None, :]

    def own_conv(array):
        return jnp.concatenate([columns_at(array, mine * width, width), array[:, DI:]], axis=1)

    conv_w_own, conv_b_own = own_conv(conv_w), own_conv(conv_b[None, :])
    gain_row = lax.dynamic_slice_in_dim(gated_gain, mine * width, width)[None, :]
    place = position[:, None]

    mixed, starts = run_forward(
        conv_in, dt, place, conv_w_own, conv_b_own, bias_row, decay_row, skip_row
    )

    grad_normed_out = dot_nt(grad_branch_group, w_out)
    gate = gate_low.astype(F32)
    gate_gain = sigmoid(gate)
    product = mixed * (gate * gate_gain)
    weighted = grad_normed_out * gain_row
    partial_sums = jnp.stack(
        [jnp.sum(product * product, axis=1), jnp.sum(weighted * product, axis=1)]
    )
    row_sums = lax.psum(partial_sums, "shard") / DI
    inverse = lax.rsqrt(row_sums[0] + EPSILON)[:, None]
    normalized = product * inverse
    normed_out = (normalized * gain_row).astype(BF)
    grad_product = inverse * weighted - product * (inverse**3 * row_sums[1][:, None])
    grad_gated_gain = jnp.sum(grad_normed_out * normalized, axis=0)
    grad_mixed = grad_product * (gate * gate_gain)
    grad_gate = (
        grad_product * mixed * (gate_gain * (1.0 + gate * (1.0 - gate_gain)))
    ).astype(BF)

    branch = lax.psum_scatter(
        dot_nn(normed_out, w_out), "shard", scatter_dimension=0, tiled=True
    )
    total_rows = resid_mine + branch
    block_out = total_rows.astype(BF)
    weights_valid = valid.astype(F32)
    square_total = jnp.sum(weights_valid * jnp.sum(total_rows * total_rows, axis=1))
    square_branch = jnp.sum(weights_valid * jnp.sum(branch * branch, axis=1))
    valid_count = jnp.sum(weights_valid)

    grad_w_out = lax.psum(dot_tn(normed_out, grad_branch_group).astype(BF), "rep").astype(F32)

    def to_owners(columns):
        part = dot_tn(normed, columns).astype(BF).reshape(shards, depth, columns.shape[1])
        swapped = lax.all_to_all(part, "shard", split_axis=0, concat_axis=0, tiled=True)
        summed = lax.psum(swapped, "rep").astype(F32)
        return summed.transpose(1, 0, 2).reshape(depth, shards * columns.shape[1])

    join = (
        jnp.arange(width, dtype=jnp.int32)[:, None] // P_SIZE
        == jnp.arange(128, dtype=jnp.int32)[None, :]
    ).astype(BF)
    grad_values, grad_maps, grad_dt, grad_conv_w, grad_conv_b, grad_head, grad_skip = run_backward(
        conv_in,
        dt,
        place,
        conv_w_own,
        conv_b_own,
        bias_row,
        decay_row,
        skip_row,
        mixed,
        starts,
        grad_mixed,
        join,
    )
    grad_maps = lax.psum_scatter(
        grad_maps, "shard", scatter_dimension=1, tiled=True
    ).astype(BF)
    grad_dt_low = grad_dt[:, :heads].astype(BF)
    share = 2 * N // shards
    grad_tail = jnp.concatenate([grad_maps, grad_dt_low], axis=1)

    back = (target[:, None] == slot_ids[None, :]).astype(BF)
    grad_own = jnp.concatenate([grad_gate, grad_values, grad_tail], axis=1)
    grad_given = dot_nn(back, grad_own).astype(BF)
    w_own = jnp.concatenate(
        [
            w_gate,
            w_conv[:, :width],
            columns_at(w_conv, width + mine * share, share),
            columns_at(w_conv, width + 2 * N + mine * heads, heads),
        ],
        axis=1,
    )
    grad_normed = lax.psum_scatter(
        dot_nt(grad_given, w_own), "shard", scatter_dimension=0, tiled=True
    )
    given = x_in.astype(F32)
    given_rms = lax.rsqrt(jnp.mean(given * given, axis=1, keepdims=True) + EPSILON)
    grad_norm_gain = jnp.sum(grad_normed * (given * given_rms), axis=0)
    scaled = grad_normed * norm_gain[None, :]
    grad_resid = scaled * given_rms - given * (
        given_rms**3 * jnp.mean(scaled * given, axis=1, keepdims=True)
    )
    back_mine = lax.dynamic_slice_in_dim(back, mine * rows, rows, axis=0)
    grad_in = (grad_resid + dot_nn(back_mine, grad_branch_group)).astype(BF)

    tails = lax.all_gather(grad_tail, "shard")
    tails = jnp.concatenate(
        [
            tails[..., :share].transpose(1, 0, 2).reshape(length, 2 * N),
            tails[..., share:].transpose(1, 0, 2).reshape(length, H),
        ],
        axis=1,
    )
    grad_w_tail = lax.psum(dot_tn(columns_at(normed, mine * depth, depth), tails), "rep")
    if few:
        parts = run_end(grad_gate, grad_values, stripes, shards)
        grad_w_in = run_assemble(parts, grad_w_tail)
    else:
        grad_w_in = jnp.concatenate(
            [to_owners(grad_gate), to_owners(grad_values), grad_w_tail], axis=1
        )

    def placed(part, whole, start):
        return lax.dynamic_update_slice_in_dim(
            jnp.zeros(part.shape[:-1] + (whole,), F32), part, start, axis=part.ndim - 1
        )

    def placed_conv(part):
        return jnp.concatenate(
            [placed(part[:, :width], DI, mine * width), part[:, width:]], axis=1
        )

    grad_skip_heads = jnp.sum(grad_skip.reshape(heads, P_SIZE), axis=1)
    pieces = (
        grad_norm_gain,
        placed_conv(grad_conv_w).reshape(-1),
        placed_conv(grad_conv_b).reshape(-1),
        placed(grad_head[0, :heads], H, mine * heads),
        placed(grad_head[1, :heads], H, mine * heads),
        placed(grad_skip_heads, H, mine * heads),
        placed(grad_gated_gain, DI, mine * width),
        jnp.stack([square_total, square_branch, valid_count]),
    )
    summed = lax.psum(jnp.concatenate(pieces), ALL)
    results, at = [], 0
    for piece in pieces:
        results.append(summed[at : at + piece.shape[0]])
        at += piece.shape[0]
    count_all = jnp.maximum(results[7][2], 1.0)
    rms_residual = jnp.sqrt(results[7][0] / (count_all * D))
    rms_mixer = jnp.sqrt(results[7][1] / (count_all * D))
    return (
        block_out,
        grad_in,
        results[0],
        grad_w_in,
        results[1].reshape(KW, CONVW),
        results[2],
        results[3],
        results[4],
        results[5],
        results[6],
        grad_w_out,
        rms_residual,
        rms_mixer,
    )


def solution(mesh):
    in_specs = (
        P(ALL, None),
        P(ALL, None),
        P("rep", None),
        P("rep", None),
        P(ALL),
        P(),
        P("shard", None),
        P(),
        P(),
        P(),
        P(),
        P(),
        P(),
        P("shard", None),
    )
    out_specs = (
        P(ALL, None),
        P(ALL, None),
        P(),
        P("shard", None),
        P(),
        P(),
        P(),
        P(),
        P(),
        P(),
        P("shard", None),
        P(),
        P(),
    )
    return jax.shard_map(
        on_device, mesh=mesh, in_specs=in_specs, out_specs=out_specs, check_vma=False
    )
```

```python
import functools

import jax
import jax.numpy as jnp
from jax import lax
from jax.experimental import pallas as pl
from jax.experimental.pallas import tpu as pltpu
from jax.sharding import PartitionSpec as P

D = 2048
H = 64
P_SIZE = 64
N = 128
KW = 4
SPAN = 128
DI = 4096
CONVW = 4352
PROJ = 8512
TAIL = PROJ - 2 * DI

EPSILON = 1e-05
ALL = ("rep", "shard")
VMEM_BYTES = 56 * 1024 * 1024
BF = jnp.bfloat16
F32 = jnp.float32


def dot_nn(a, b):
    return lax.dot_general(a, b, (((1,), (0,)), ((), ())), preferred_element_type=F32)


def dot_nt(a, b):
    return lax.dot_general(a, b, (((1,), (1,)), ((), ())), preferred_element_type=F32)


def dot_tn(a, b):
    return lax.dot_general(a, b, (((0,), (0,)), ((), ())), preferred_element_type=F32)


def halves(a):
    high = a.astype(BF)
    return high, (a - high.astype(F32)).astype(BF)


def slot_tables(seq_lengths, seq_order, slot_ids):
    seq_count = seq_lengths.shape[0]
    numbers = jnp.arange(seq_count, dtype=jnp.int32)
    chosen = (seq_order[:, None] == numbers[None, :]).astype(jnp.int32)
    given_start = jnp.cumsum(seq_lengths) - seq_lengths
    owner_length = jnp.sum(chosen * seq_lengths[None, :], axis=1)
    owner_start = jnp.cumsum(owner_length) - owner_length
    owner_from = jnp.sum(chosen * given_start[None, :], axis=1)
    placed_at = jnp.sum(chosen * owner_start[:, None], axis=0)
    column = slot_ids[:, None]
    within = (column >= owner_start[None, :]) & (column < (owner_start + owner_length)[None, :])
    offset = column - owner_start[None, :]
    source = jnp.sum(jnp.where(within, offset + owner_from[None, :], 0), axis=1)
    position = jnp.sum(jnp.where(within, offset, 0), axis=1)
    given_within = (column >= given_start[None, :]) & (
        column < (given_start + seq_lengths)[None, :]
    )
    target = jnp.sum(
        jnp.where(given_within, column - given_start[None, :] + placed_at[None, :], 0), axis=1
    )
    return (source, target, position)


def params():
    return pltpu.CompilerParams(vmem_limit_bytes=VMEM_BYTES)


def spread_rows(row):
    return jnp.broadcast_to(row, (16, row.shape[1]))


def sigmoid(v):
    return 1.0 / (1.0 + jnp.exp(-v))


def spread(column, lanes=128):
    return jnp.broadcast_to(column, (column.shape[0], lanes))


MESH = pl.DeviceIdType.MESH
LINE, PLANE = 4, 2
CHUNK = 256
TAIL_PAD = 384


def remote(src, dst, send_sem, recv_sem, device):
    return pltpu.make_async_remote_copy(
        src_ref=src,
        dst_ref=dst,
        send_sem=send_sem,
        recv_sem=recv_sem,
        device_id=device,
        device_id_type=MESH,
    )


def meet(devices):
    barrier = pltpu.get_barrier_semaphore()
    for device in devices:
        pl.semaphore_signal(barrier, inc=1, device_id=device, device_id_type=MESH)
    pl.semaphore_wait(barrier, len(devices))


def tables_in_kernel(lengths_ref, order_ref, slots):
    count = lengths_ref.shape[1]
    lengths = [lengths_ref[0, i] for i in range(count)]
    order = [order_ref[0, i] for i in range(count)]
    given_start, at = [], jnp.int32(0)
    for i in range(count):
        given_start.append(at)
        at = at + lengths[i]
    source = jnp.zeros_like(slots)
    position = jnp.zeros_like(slots)
    placed_at = [jnp.int32(0)] * count
    at = jnp.int32(0)
    for k in range(count):
        length, start = jnp.int32(0), jnp.int32(0)
        for i in range(count):
            chosen = order[k] == i
            length = length + jnp.where(chosen, lengths[i], 0)
            start = start + jnp.where(chosen, given_start[i], 0)
            placed_at[i] = placed_at[i] + jnp.where(chosen, at, 0)
        within = (slots >= at) & (slots < at + length)
        source = source + jnp.where(within, slots - at + start, 0)
        position = position + jnp.where(within, slots - at, 0)
        at = at + length
    target = jnp.zeros_like(slots)
    for i in range(count):
        within = (slots >= given_start[i]) & (slots < given_start[i] + lengths[i])
        target = target + jnp.where(within, slots - given_start[i] + placed_at[i], 0)
    return source, target, position


def start_kernel(
    lengths_ref,
    order_ref,
    x_ref,
    cotangent_ref,
    valid_ref,
    gain_ref,
    w_ref,
    normed_out_ref,
    conv_in_ref,
    gate_ref,
    w_gate_out_ref,
    w_conv_out_ref,
    branch_grad_ref,
    back_ref,
    place_ref,
    resid_ref,
    x_all,
    normed,
    w_gate,
    w_conv,
    grads,
    local_sem,
    row_send,
    row_recv,
    w_send,
    w_recv,
    w_local,
):
    mine, rep = lax.axis_index("shard"), lax.axis_index("rep")
    y, c = mine // 2, lax.rem(mine, 2)
    z, x = rep // PLANE, lax.rem(rep, PLANE)
    sibling, peer, far = y * 2 + (1 - c), (1 - y) * 2 + c, (1 - y) * 2 + (1 - c)
    beside = z * PLANE + (1 - x)
    rows, length = x_ref.shape[0], x_all.shape[0]
    depth, width = w_ref.shape[1], gate_ref.shape[1]
    chunks = width // CHUNK
    tail_half = TAIL // 2
    meet([(rep, sibling), (rep, peer), (rep, far), (beside, mine)])

    def block(ref, shard):
        return ref.at[pl.ds(pl.multiple_of(shard * rows, rows), rows)]

    def row_copies(kind, own, store):
        return (
            remote(own, block(store, mine), row_send.at[kind, 0], row_recv.at[kind, 0], (rep, peer)),
            remote(own, block(store, mine), row_send.at[kind, 1], row_recv.at[kind, 1], (rep, sibling)),
            remote(
                block(store, peer),
                block(store, peer),
                row_send.at[kind, 2],
                row_recv.at[kind, 2],
                (rep, sibling),
            ),
        )

    def lanes(shard):
        return pl.ds(pl.multiple_of(shard * depth, depth), depth)

    def weight_copies(store, index, base, stride, at, half):
        share = pl.ds(pl.multiple_of(at + half * x, 16), half)
        both = pl.ds(pl.multiple_of((1 - y) * 2 * depth, 128), 2 * depth)

        def source(shard, start, count):
            return w_ref.at[pl.ds(pl.multiple_of(base + stride * shard + start, 16), count)]

        def sems(way):
            return w_send.at[way, index], w_recv.at[way, index]

        whole = pl.ds(pl.multiple_of(at, 16), 2 * half)
        near = at if stride else 0
        return (
            lambda: remote(
                source(peer, near + half * x, half), store.at[share, lanes(mine)], *sems(0), (rep, peer)
            ),
            lambda: remote(
                source(far, near + half * x, half), store.at[share, lanes(mine)], *sems(1), (rep, far)
            ),
            lambda: remote(store.at[share, both], store.at[share, both], *sems(2), (beside, mine)),
            lambda: remote(
                source(sibling, near, 2 * half), store.at[whole, lanes(mine)], *sems(3), (rep, sibling)
            ),
            lambda: pltpu.make_async_copy(
                source(mine, near, 2 * half), store.at[whole, lanes(mine)], w_local.at[index]
            ),
        )

    def conv_copies(q):
        return weight_copies(w_conv, q, DI, width, q * CHUNK, CHUNK // 2)

    def tail_copies():
        return weight_copies(w_conv, chunks, 2 * DI, 0, width, tail_half)

    def gate_copies(q):
        return weight_copies(w_gate, chunks + 1 + q, 0, width, q * CHUNK, CHUNK // 2)

    def send_out(copies):
        for i in (0, 1, 3, 4):
            copies[i]().start()

    def pass_on(copies):
        copies[0]().wait_recv()
        copies[1]().wait_recv()
        copies[2]().start()

    def arrived(copies):
        copies[2]().wait_recv()
        copies[3]().wait_recv()
        copies[4]().wait()

    def each(count, body):
        def step(i, unused):
            body(i)
            return unused

        lax.fori_loop(0, count, step, 0)

    x_copies = row_copies(0, x_ref, x_all)
    own_rows = pltpu.make_async_copy(x_ref, block(x_all, mine), local_sem.at[0])
    x_copies[0].start()
    x_copies[1].start()
    own_rows.start()
    each(chunks, lambda q: send_out(conv_copies(q)))
    send_out(tail_copies())
    grads[pl.ds(pl.multiple_of(mine * rows, rows), rows), :] = jnp.where(
        spread(valid_ref[...], D) > 0, cotangent_ref[...].astype(F32), 0.0
    ).astype(BF)
    w_conv[width + TAIL :, :] = jnp.zeros((TAIL_PAD - TAIL, D), BF)

    def table_block(i):
        span = pl.ds(pl.multiple_of(i * rows, rows), rows)
        slots = lax.broadcasted_iota(jnp.int32, (rows, length), 0) + i * rows
        across = lax.broadcasted_iota(jnp.int32, (rows, length), 1)
        target = tables_in_kernel(lengths_ref, order_ref, slots)[1]
        back_ref[span, :] = (target == across).astype(F32).astype(BF)
        few_slots = lax.broadcasted_iota(jnp.int32, (rows, 128), 0) + i * rows
        place_ref[span, :] = tables_in_kernel(lengths_ref, order_ref, few_slots)[2]

    each(length // rows, table_block)
    x_copies[0].wait_recv()
    x_copies[2].start()
    own_rows.wait()
    x_copies[1].wait_recv()
    x_copies[2].wait_recv()

    def picked(i):
        slots = lax.broadcasted_iota(jnp.int32, (rows, length), 0) + i * rows
        across = lax.broadcasted_iota(jnp.int32, (rows, length), 1)
        source = tables_in_kernel(lengths_ref, order_ref, slots)[0]
        return dot_nn((source == across).astype(F32).astype(BF), x_all[...])

    def norm_block(i):
        span = pl.ds(pl.multiple_of(i * rows, rows), rows)
        resid = picked(i)
        inverse = lax.rsqrt(jnp.mean(resid * resid, axis=1, keepdims=True) + EPSILON)
        normed[span, :] = (resid * inverse * gain_ref[...]).astype(BF)

    each(length // rows, norm_block)
    resid_ref[...] = picked(mine).astype(BF)
    normed_store = pltpu.make_async_copy(normed, normed_out_ref, local_sem.at[1])
    normed_store.start()

    each(chunks, lambda q: pass_on(conv_copies(q)))
    pass_on(tail_copies())
    each(chunks, lambda q: send_out(gate_copies(q)))

    def project(store, target, at, count):
        span = pl.ds(pl.multiple_of(at, 128), count)
        target[:, span] = dot_nt(normed[...], store[span, :]).astype(BF)

    def conv_chunk(q):
        arrived(conv_copies(q))
        project(w_conv, conv_in_ref, q * CHUNK, CHUNK)

    each(chunks, conv_chunk)
    arrived(tail_copies())
    project(w_conv, conv_in_ref, width, TAIL_PAD)
    grad_copies = row_copies(1, block(grads, mine), grads)
    grad_copies[0].start()
    grad_copies[1].start()
    conv_store = pltpu.make_async_copy(w_conv, w_conv_out_ref, local_sem.at[2])
    conv_store.start()
    each(chunks, lambda q: pass_on(gate_copies(q)))

    def gate_chunk(q):
        arrived(gate_copies(q))
        project(w_gate, gate_ref, q * CHUNK, CHUNK)

    each(chunks, gate_chunk)
    gate_store = pltpu.make_async_copy(w_gate, w_gate_out_ref, local_sem.at[3])
    gate_store.start()
    grad_copies[0].wait_recv()
    grad_copies[2].start()
    grad_copies[1].wait_recv()
    grad_copies[2].wait_recv()
    branch_grad_ref[...] = grads[...]

    def drain(copies):
        for i in range(4):
            copies[i]().wait_send()

    each(chunks, lambda q: drain(conv_copies(q)))
    drain(tail_copies())
    each(chunks, lambda q: drain(gate_copies(q)))
    for copies in (x_copies, grad_copies):
        for copy in copies:
            copy.wait_send()
    normed_store.wait()
    conv_store.wait()
    gate_store.wait()


def run_start(lengths, order, x_in, cotangent, valid, gain, w_columns, shards):
    rows = x_in.shape[0]
    length, width = rows * shards, DI // shards
    chunks = width // CHUNK
    dma = pltpu.SemaphoreType.DMA
    anywhere = pl.BlockSpec(memory_space=pl.ANY)
    scalars = pl.BlockSpec(memory_space=pltpu.SMEM)
    vector = pl.BlockSpec(memory_space=pltpu.VMEM)
    shape = jax.ShapeDtypeStruct
    return pl.pallas_call(
        start_kernel,
        out_shape=(
            shape((length, D), BF),
            shape((length, width + TAIL_PAD), BF),
            shape((length, width), BF),
            shape((width, D), BF),
            shape((width + TAIL_PAD, D), BF),
            shape((length, D), BF),
            shape((length, length), BF),
            shape((length, 128), jnp.int32),
            shape((rows, D), BF),
        ),
        in_specs=[scalars, scalars, anywhere, vector, vector, vector, anywhere],
        out_specs=(anywhere, vector, vector, anywhere, anywhere, vector, vector, vector, vector),
        scratch_shapes=[
            pltpu.VMEM((length, D), BF),
            pltpu.VMEM((length, D), BF),
            pltpu.VMEM((width, D), BF),
            pltpu.VMEM((width + TAIL_PAD, D), BF),
            pltpu.VMEM((length, D), BF),
            dma((4,)),
            dma((2, 3)),
            dma((2, 3)),
            dma((4, 2 * chunks + 1)),
            dma((4, 2 * chunks + 1)),
            dma((2 * chunks + 1,)),
        ],
        compiler_params=pltpu.CompilerParams(
            vmem_limit_bytes=VMEM_BYTES, collective_id=1, has_side_effects=True
        ),
        cost_estimate=pl.CostEstimate(
            flops=2 * length * D * (2 * width + TAIL_PAD), bytes_accessed=48 << 20, transcendentals=0
        ),
        name="project",
    )(lengths, order, x_in, cotangent, valid, gain, w_columns)


def conv_pre(x, conv_w, conv_b, place):
    pre = conv_b + conv_w[KW - 1 : KW] * x
    for back in range(1, KW):
        moved = pltpu.roll(x, back, 0)
        pre = pre + jnp.where(place >= back, conv_w[KW - 1 - back : KW - back] * moved, 0.0)
    return pre


def conv_lanes(chunk, width, mine):
    if 128 * chunk < width:
        return pl.ds(pl.multiple_of(mine * width + 128 * chunk, 128), 128)
    return pl.ds(DI + 128 * chunk - width, 128)


def block_terms(place):
    local = lax.broadcasted_iota(jnp.int32, (SPAN, 128), 0)
    across = lax.broadcasted_iota(jnp.int32, (SPAN, 128), 1)
    begins = local - place
    causal = (across <= local) & (across >= begins)
    reach_end = local >= begins[SPAN - 1 : SPAN, :]
    entered = place >= local + 1
    carries = place[SPAN - 1 : SPAN, :] >= SPAN
    return causal, reach_end, entered, carries


def pair_terms(pair, run, run_t, step, causal, reach_end, entered, carries):
    left = lax.broadcasted_iota(jnp.int32, (SPAN, 128), 1) < P_SIZE
    runs = [spread(run[:, 2 * pair + i : 2 * pair + i + 1]) for i in range(2)]
    decays = []
    for i in range(2):
        gap = runs[i] - run_t[2 * pair + i : 2 * pair + i + 1, :]
        decays.append(jnp.exp(jnp.where(causal, gap, -jnp.inf)))
    both = jnp.where(left, runs[0], runs[1])
    end = both[SPAN - 1 : SPAN, :]
    entering = jnp.where(entered, jnp.exp(both), 0.0)
    tail = jnp.where(reach_end, jnp.exp(jnp.where(reach_end, end - both, 0.0)), 0.0)
    carried = jnp.where(carries, jnp.exp(end), 0.0)
    size = jnp.where(
        left,
        spread(step[:, 2 * pair : 2 * pair + 1]),
        spread(step[:, 2 * pair + 1 : 2 * pair + 2]),
    )
    return left, decays, entering, tail, carried, size


def stacked(value, left):
    zero = jnp.zeros_like(value)
    return jnp.concatenate([jnp.where(left, value, zero), jnp.where(left, zero, value)], axis=0)


def own_lanes(row, mine, heads):
    return pltpu.roll(row, lax.rem(128 - mine * heads, 128), 1)


def skip_lanes(row, pair):
    left = lax.broadcasted_iota(jnp.int32, (1, 128), 1) < P_SIZE
    return jnp.where(
        left,
        spread(row[:, 2 * pair : 2 * pair + 1]),
        spread(row[:, 2 * pair + 1 : 2 * pair + 2]),
    )


def step_and_run(conv_in_ref, heads_ref, run_ref, step_ref, width, mine):
    length = run_ref.shape[0]
    heads = width // P_SIZE
    lower = (
        lax.broadcasted_iota(jnp.int32, (SPAN, SPAN), 0)
        >= lax.broadcasted_iota(jnp.int32, (SPAN, SPAN), 1)
    ).astype(F32)
    bias = heads_ref[0:1, :]
    rate = jnp.exp(own_lanes(heads_ref[...], mine, heads)[1:2, :])

    def block(b, unused):
        rows = pl.ds(pl.multiple_of(b * SPAN, SPAN), SPAN)
        raw = conv_in_ref[rows, width + 2 * N : width + 2 * N + 128].astype(F32)
        step = own_lanes(jax.nn.softplus(raw + bias), mine, heads)
        step_ref[rows, :] = step
        run_ref[rows, :] = jnp.dot(
            lower, -step * rate, precision=lax.Precision.HIGHEST, preferred_element_type=F32
        )
        return unused

    lax.fori_loop(0, length // SPAN, block, 0)


def forward_kernel(
    conv_in_ref,
    gate_ref,
    branch_grad_ref,
    w_out_ref,
    place_ref,
    conv_w_ref,
    conv_b_ref,
    heads_ref,
    gain_ref,
    mixed_ref,
    starts_ref,
    normed_out_ref,
    grad_mixed_ref,
    grad_gate_ref,
    grad_gain_ref,
    act_ref,
    step_ref,
    run_ref,
    state_ref,
    back_ref,
    sums,
    send_sem,
    recv_sem,
):
    length, width = mixed_ref.shape
    mine, rep, shards = lax.axis_index("shard"), lax.axis_index("rep"), lax.axis_size("shard")
    heads = width // P_SIZE
    peers = [(rep, lax.rem(mine + step, shards)) for step in range(1, shards)]
    barrier = pltpu.get_barrier_semaphore()
    for peer in peers:
        pl.semaphore_signal(barrier, inc=1, device_id=peer, device_id_type=MESH)
    for c in range((width + 2 * N) // 128):
        lanes = slice(128 * c, 128 * c + 128)
        there = conv_lanes(c, width, mine)
        pre = conv_pre(
            conv_in_ref[:, lanes].astype(F32),
            conv_w_ref[:, there],
            conv_b_ref[:, there],
            place_ref[...],
        )
        act_ref[:, lanes] = (pre * sigmoid(pre)).astype(BF)
    step_and_run(conv_in_ref, heads_ref, run_ref, step_ref, width, mine)
    state_ref[...] = jnp.zeros_like(state_ref)
    skips = own_lanes(heads_ref[...], mine, heads)[2:3, :]

    def block(b, unused):
        row = pl.multiple_of(b * SPAN, SPAN)
        rows = pl.ds(row, SPAN)
        starts_ref[pl.ds(pl.multiple_of(b * N, N), N), :] = state_ref[...]
        run = run_ref[rows, :]
        run_t = run.T
        step = step_ref[rows, :]
        masks = block_terms(place_ref[rows, :])
        in_map = act_ref[rows, width : width + N]
        out_map = act_ref[rows, width + N : width + 2 * N]
        products = dot_nt(out_map, in_map)
        in_map_t = in_map.T
        for pair in range(width // 128):
            lanes = slice(128 * pair, 128 * pair + 128)
            left, decays, entering, tail, carried, size = pair_terms(
                pair, run, run_t, step, *masks
            )
            values = act_ref[rows, lanes].astype(F32)
            scaled = values * size
            weights = jnp.concatenate([(d * products).astype(BF) for d in decays], axis=1)
            out = dot_nn(weights, stacked(scaled.astype(BF), left))
            state = state_ref[:, lanes]
            high, low = halves(state)
            out += entering * (dot_nn(out_map, high) + dot_nn(out_map, low))
            mixed_ref[rows, lanes] = out + skip_lanes(skips, pair) * values
            high, low = halves(tail * scaled)
            fresh = dot_nn(in_map_t, high) + dot_nn(in_map_t, low)
            state_ref[:, lanes] = carried * state + fresh
        return unused

    lax.fori_loop(0, length // SPAN, block, 0)

    lane = lax.broadcasted_iota(jnp.int32, (SPAN, 128), 1)

    def gated(rows, c):
        lanes = slice(128 * c, 128 * c + 128)
        gate = gate_ref[rows, lanes].astype(F32)
        opened = sigmoid(gate)
        mixed = mixed_ref[rows, lanes]
        back = back_ref[rows, lanes]
        gain = gain_ref[:, pl.ds(pl.multiple_of(mine * width + 128 * c, 128), 128)]
        return gate, opened, mixed, back, gain, mixed * (gate * opened), back * gain

    def measure(b, unused):
        rows = pl.ds(pl.multiple_of(b * SPAN, SPAN), SPAN)
        back_ref[rows, :] = dot_nt(branch_grad_ref[rows, :], w_out_ref[...])
        squares = jnp.zeros((SPAN, 128), F32)
        crosses = jnp.zeros((SPAN, 128), F32)
        for c in range(width // 128):
            product, weighted = gated(rows, c)[5:]
            squares += product * product
            crosses += weighted * product
        squares = jnp.sum(squares, axis=1, keepdims=True)
        crosses = jnp.sum(crosses, axis=1, keepdims=True)
        both = jnp.where(lane == 0, spread(squares), jnp.where(lane == 1, spread(crosses), 0.0))
        sums[mine, :, rows] = both.T[0:8, :]
        return unused

    lax.fori_loop(0, length // SPAN, measure, 0)

    pl.semaphore_wait(barrier, shards - 1)
    copies = [
        remote(sums.at[mine], sums.at[mine], send_sem.at[i], recv_sem.at[i], peer)
        for i, peer in enumerate(peers)
    ]
    for copy in copies:
        copy.start()
    for copy in copies:
        copy.wait_recv()
    grad_gain_ref[...] = jnp.zeros_like(grad_gain_ref)

    def finish(b, unused):
        rows = pl.ds(pl.multiple_of(b * SPAN, SPAN), SPAN)
        both = sums[0, :, rows]
        for shard in range(1, shards):
            both = both + sums[shard, :, rows]
        both = jnp.concatenate([both, jnp.zeros((SPAN - 8, SPAN), F32)], axis=0).T / DI
        inverse = lax.rsqrt(both[:, 0:1] + EPSILON)
        pull = spread(inverse * inverse * inverse * both[:, 1:2])
        inverse = spread(inverse)
        for c in range(width // 128):
            lanes = slice(128 * c, 128 * c + 128)
            gate, opened, mixed, back, gain, product, weighted = gated(rows, c)
            normalized = product * inverse
            normed_out_ref[rows, lanes] = (normalized * gain).astype(BF)
            grad_product = inverse * weighted - product * pull
            grad_gain_ref[:, lanes] += jnp.sum(back * normalized, axis=0, keepdims=True)
            grad_mixed_ref[rows, lanes] = grad_product * (gate * opened)
            grad_gate_ref[rows, lanes] = (
                grad_product * mixed * (opened * (1.0 + gate * (1.0 - opened)))
            ).astype(BF)
        return unused

    lax.fori_loop(0, length // SPAN, finish, 0)
    for copy in copies:
        copy.wait_send()


def backward_kernel(
    conv_in_ref,
    place_ref,
    conv_w_ref,
    conv_b_ref,
    heads_ref,
    mixed_ref,
    starts_ref,
    grad_ref,
    grad_values_ref,
    grad_tail_ref,
    grad_conv_w_ref,
    grad_conv_b_ref,
    grad_head_ref,
    act_ref,
    pre_ref,
    step_ref,
    run_ref,
    state_ref,
    grad_act_ref,
    joined_ref,
    join_ref,
):
    length, width = mixed_ref.shape
    mine = lax.axis_index("shard")
    heads = width // P_SIZE
    blocks = length // SPAN
    for c in range((width + 2 * N) // 128):
        lanes = slice(128 * c, 128 * c + 128)
        there = conv_lanes(c, width, mine)
        pre = conv_pre(
            conv_in_ref[:, lanes].astype(F32),
            conv_w_ref[:, there],
            conv_b_ref[:, there],
            place_ref[...],
        )
        pre_ref[:, lanes] = pre
        act_ref[:, lanes] = (pre * sigmoid(pre)).astype(BF)
    step_and_run(conv_in_ref, heads_ref, run_ref, step_ref, width, mine)
    state_ref[...] = jnp.zeros_like(state_ref)
    grad_head_ref[...] = jnp.zeros_like(grad_head_ref)
    skips = own_lanes(heads_ref[...], mine, heads)[2:3, :]
    upper = (
        lax.broadcasted_iota(jnp.int32, (SPAN, SPAN), 0)
        <= lax.broadcasted_iota(jnp.int32, (SPAN, SPAN), 1)
    ).astype(F32)
    last_row = lax.broadcasted_iota(jnp.int32, (SPAN, 128), 0) == SPAN - 1
    join_ref[...] = (
        lax.broadcasted_iota(jnp.int32, (width, 128), 0) // P_SIZE + mine * heads
        == lax.broadcasted_iota(jnp.int32, (width, 128), 1)
    ).astype(F32).astype(BF)

    def block(count, unused):
        b = blocks - 1 - count
        row = pl.multiple_of(b * SPAN, SPAN)
        rows = pl.ds(row, SPAN)
        start_rows = pl.ds(pl.multiple_of(b * N, N), N)
        run = run_ref[rows, :]
        run_t = run.T
        step = step_ref[rows, :]
        masks = block_terms(place_ref[rows, :])
        in_map = act_ref[rows, width : width + N]
        out_map = act_ref[rows, width + N : width + 2 * N]
        out_map_t = out_map.T
        products = dot_nt(out_map, in_map)
        grad_products = jnp.zeros((SPAN, SPAN), F32)
        grad_out_map = jnp.zeros((SPAN, N), F32)
        grad_in_map = jnp.zeros((SPAN, N), F32)
        for pair in range(width // 128):
            lanes = slice(128 * pair, 128 * pair + 128)
            left, decays, entering, tail, carried, size = pair_terms(
                pair, run, run_t, step, *masks
            )
            values = act_ref[rows, lanes].astype(F32)
            grad = grad_ref[rows, lanes]
            start = starts_ref[start_rows, lanes]
            later = state_ref[:, lanes]
            scaled = values * size
            scaled_low = scaled.astype(BF)
            grad_low = grad.astype(BF)
            weights = jnp.concatenate([(d * products).astype(BF) for d in decays], axis=0)
            grad_scaled = dot_tn(weights, stacked(grad_low, left))
            grad_pairs = dot_nt(grad_low, stacked(scaled_low, left))
            grad_products += (
                grad_pairs[:, :SPAN] * decays[0] + grad_pairs[:, SPAN:] * decays[1]
            )
            later_high, later_low = halves(later)
            from_later = tail * (dot_nn(in_map, later_high) + dot_nn(in_map, later_low))
            grad_scaled += from_later
            entering_high, entering_low = halves(entering * grad)
            grad_out_map += dot_nt(entering_high, start.astype(BF))
            grad_in_map += dot_nt((tail * scaled).astype(BF), later_high)
            ending = jnp.sum(scaled * from_later, axis=0, keepdims=True) + carried * jnp.sum(
                start * later, axis=0, keepdims=True
            )
            state_ref[:, lanes] = (
                carried * later + dot_nn(out_map_t, entering_high) + dot_nn(out_map_t, entering_low)
            )
            skip = skip_lanes(skips, pair)
            inner = mixed_ref[rows, lanes] - skip * values
            joined_ref[0:SPAN, lanes] = (
                grad_low.astype(F32) * inner
                - scaled_low.astype(F32) * (grad_scaled - from_later)
                - scaled * from_later
                + jnp.where(last_row, ending, 0.0)
            )
            joined_ref[SPAN : 2 * SPAN, lanes] = grad_scaled * values
            joined_ref[2 * SPAN : 2 * SPAN + 16, lanes] = spread_rows(
                jnp.sum(grad * values, axis=0, keepdims=True)
            )
            grad_act_ref[rows, lanes] = grad_scaled * size + skip * grad
        grad_products = grad_products.astype(BF)
        grad_act_ref[rows, width : width + N] = grad_in_map + dot_tn(grad_products, out_map)
        grad_act_ref[rows, width + N : width + 2 * N] = grad_out_map + dot_nn(
            grad_products, in_map
        )
        joined = joined_ref[...]
        first = joined.astype(BF)
        second, third = halves(joined - first.astype(F32))
        join = join_ref[...]
        by_head = dot_nn(first, join) + dot_nn(second, join) + dot_nn(third, join)
        grad_log = jnp.dot(
            upper, by_head[:SPAN], precision=lax.Precision.HIGHEST, preferred_element_type=F32
        )
        rate = jnp.exp(heads_ref[1:2, :])
        raw = conv_in_ref[rows, width + 2 * N : width + 2 * N + 128].astype(F32) + heads_ref[0:1, :]
        grad_dt = (by_head[SPAN : 2 * SPAN] - grad_log * rate) * sigmoid(raw)
        grad_tail_ref[rows, 2 * N : 2 * N + 128] = grad_dt
        grad_head_ref[0:1, :] += jnp.sum(grad_dt, axis=0, keepdims=True)
        grad_head_ref[1:2, :] += jnp.sum(
            -grad_log * jax.nn.softplus(raw) * rate, axis=0, keepdims=True
        )
        grad_head_ref[2:3, :] += by_head[2 * SPAN : 2 * SPAN + 1]
        return unused

    lax.fori_loop(0, blocks, block, 0)

    place = place_ref[...]
    for c in range((width + 2 * N) // 128):
        lanes = slice(128 * c, 128 * c + 128)
        x = conv_in_ref[:, lanes].astype(F32)
        conv_w = conv_w_ref[:, conv_lanes(c, width, mine)]
        pre = pre_ref[:, lanes]
        gain = sigmoid(pre)
        grad_pre = grad_act_ref[:, lanes] * (gain * (1.0 + pre * (1.0 - gain)))
        grad_conv_b_ref[:, lanes] = jnp.sum(grad_pre, axis=0, keepdims=True)
        grad_conv_w_ref[KW - 1 : KW, lanes] = jnp.sum(grad_pre * x, axis=0, keepdims=True)
        grad_x = conv_w[KW - 1 : KW] * grad_pre
        for back in range(1, KW):
            tap = KW - 1 - back
            kept = jnp.where(place >= back, grad_pre, 0.0)
            grad_conv_w_ref[tap : tap + 1, lanes] = jnp.sum(
                kept * pltpu.roll(x, back, 0), axis=0, keepdims=True
            )
            grad_x += conv_w[tap : tap + 1] * pltpu.roll(kept, length - back, 0)
        if c < width // 128:
            grad_values_ref[:, lanes] = grad_x.astype(BF)
        else:
            grad_tail_ref[:, 128 * c - width : 128 * c - width + 128] = grad_x


def run_forward(conv_in, gate, branch_grad, w_out, place, conv_w, conv_b, heads, gain, shards):
    length, width = gate.shape
    blocks = length // SPAN
    shape = jax.ShapeDtypeStruct
    return pl.pallas_call(
        forward_kernel,
        out_shape=(
            shape((length, width), F32),
            shape((blocks * N, width), F32),
            shape((length, width), BF),
            shape((length, width), F32),
            shape((length, width), BF),
            shape((1, width), F32),
        ),
        scratch_shapes=[
            pltpu.VMEM((length, width + 2 * N), BF),
            pltpu.VMEM((length, 128), F32),
            pltpu.VMEM((length, 128), F32),
            pltpu.VMEM((N, width), F32),
            pltpu.VMEM((length, width), F32),
            pltpu.VMEM((shards, 8, length), F32),
            pltpu.SemaphoreType.DMA((shards - 1,)),
            pltpu.SemaphoreType.DMA((shards - 1,)),
        ],
        compiler_params=pltpu.CompilerParams(
            vmem_limit_bytes=VMEM_BYTES, collective_id=2, has_side_effects=True
        ),
        cost_estimate=pl.CostEstimate(
            flops=20 * length * width * 128, bytes_accessed=12 * length * width, transcendentals=0
        ),
        name="mixer_forward",
    )(conv_in, gate, branch_grad, w_out, place, conv_w, conv_b, heads, gain)


def run_backward(conv_in, place, conv_w, conv_b, heads, mixed, starts, grad):
    length, width = mixed.shape
    shape = jax.ShapeDtypeStruct
    return pl.pallas_call(
        backward_kernel,
        out_shape=(
            shape((length, width), BF),
            shape((length, TAIL_PAD), F32),
            shape((KW, width + 2 * N), F32),
            shape((1, width + 2 * N), F32),
            shape((8, 128), F32),
        ),
        scratch_shapes=[
            pltpu.VMEM((length, width + 2 * N), BF),
            pltpu.VMEM((length, width + 2 * N), F32),
            pltpu.VMEM((length, 128), F32),
            pltpu.VMEM((length, 128), F32),
            pltpu.VMEM((N, width), F32),
            pltpu.VMEM((length, width + 2 * N), F32),
            pltpu.VMEM((2 * SPAN + 16, width), F32),
            pltpu.VMEM((width, 128), BF),
        ],
        compiler_params=params(),
        cost_estimate=pl.CostEstimate(
            flops=40 * length * width * 128, bytes_accessed=20 * length * width, transcendentals=0
        ),
        name="mixer_backward",
    )(conv_in, place, conv_w, conv_b, heads, mixed, starts, grad)


def end_kernel(
    gate_ref,
    values_ref,
    tail_ref,
    normed_ref,
    w_gate_hbm,
    w_conv_hbm,
    w_out_hbm,
    normed_out_hbm,
    back_ref,
    branch_grad_hbm,
    x_ref,
    resid_ref,
    valid_ref,
    gain_ref,
    grad_conv_w_ref,
    grad_conv_b_ref,
    grad_head_ref,
    grad_gain_ref,
    parts_ref,
    tails_ref,
    block_out_ref,
    grad_in_ref,
    out_norm_ref,
    out_conv_w_ref,
    out_conv_b_ref,
    out_head_ref,
    out_gain_ref,
    taken,
    group_rows,
    own_columns,
    total,
    low,
    partial,
    pair_in,
    row_in,
    tail_in,
    tail_low,
    tail_sum,
    tail_parts,
    small,
    small_in,
    small_all,
    w_gate_ref,
    w_conv_ref,
    w_out_ref,
    normed_out_ref,
    branch_grad_ref,
    load_sem,
    local_sem,
    group_sem,
    a2a_send,
    a2a_recv,
    swap_send,
    swap_recv,
    line_send,
    line_recv,
    side_send,
    side_recv,
    pair_send,
    pair_recv,
    tail_send,
    tail_recv,
    rep_send,
    rep_recv,
    all_send,
    all_recv,
):
    reps, shards = LINE * PLANE, lax.axis_size("shard")
    mine, rep = lax.axis_index("shard"), lax.axis_index("rep")
    y, c = mine // 2, lax.rem(mine, 2)
    z, x = rep // PLANE, lax.rem(rep, PLANE)
    beside = z * PLANE + (1 - x)
    rows, length = x_ref.shape[0], gate_ref.shape[0]
    width, depth = gate_ref.shape[1], own_columns.shape[1]
    sources = (gate_ref, values_ref)
    sibling, peer = y * 2 + (1 - c), (1 - y) * 2 + c

    def other(step):
        return lax.rem(z + step // PLANE, LINE) * PLANE + lax.rem(x + step % PLANE, PLANE)

    def before(step):
        return lax.rem(z + LINE - step // PLANE, LINE) * PLANE + lax.rem(
            x + PLANE - step % PLANE, PLANE
        )

    def shard_at(step):
        return lax.rem(mine + step, shards)

    def each(count, body):
        def step(i, unused):
            body(i)
            return unused

        lax.fori_loop(0, count, step, 0)

    meet(
        [(other(step), mine) for step in range(1, reps)]
        + [(rep, shard_at(step)) for step in range(1, shards)]
    )

    loads = [
        pltpu.make_async_copy(far_ref, near_ref, load_sem.at[i])
        for i, (far_ref, near_ref) in enumerate(
            [
                (normed_out_hbm, normed_out_ref),
                (w_out_hbm, w_out_ref),
                (w_gate_hbm, w_gate_ref),
                (w_conv_hbm, w_conv_ref),
                (branch_grad_hbm, branch_grad_ref),
            ]
        )
    ]

    def share_copy(part, step):
        to = other(step)
        return remote(
            sources[part].at[:, pl.ds(pl.multiple_of(to * 128, 128), 128)],
            taken.at[part, step],
            a2a_send.at[part, step],
            a2a_recv.at[part, step],
            (to, mine),
        )

    def own_copy(part):
        return pltpu.make_async_copy(
            sources[part].at[:, pl.ds(pl.multiple_of(rep * 128, 128), 128)],
            taken.at[part, 0],
            local_sem.at[part],
        )

    def group_copy(step, slot):
        start = pl.multiple_of(before(step) * length, 128)
        return pltpu.make_async_copy(
            normed_ref.at[pl.ds(start, length)], group_rows.at[slot], group_sem.at[slot]
        )

    own_part = pltpu.make_async_copy(
        normed_ref.at[
            pl.ds(pl.multiple_of(rep * length, 128), length),
            pl.ds(pl.multiple_of(mine * depth, 128), depth),
        ],
        own_columns,
        local_sem.at[4],
    )
    own_part.start()
    group_copy(0, 0).start()
    for part in range(2):
        own_copy(part).start()
        for step in range(1, reps):
            share_copy(part, step).start()

    def row_block(ref, shard):
        return ref.at[pl.ds(pl.multiple_of(shard * rows, rows), rows)]

    def tail_out_copy(step):
        to = shard_at(step)
        return remote(
            row_block(tail_ref, to),
            tail_in.at[step],
            tail_send.at[0, step],
            tail_recv.at[0, step],
            (rep, to),
        )

    def tail_back_copy(step):
        return remote(
            row_block(tail_low, mine),
            row_block(tail_low, mine),
            tail_send.at[1, step],
            tail_recv.at[1, step],
            (rep, shard_at(step)),
        )

    for step in range(1, shards):
        tail_out_copy(step).start()
    for load in loads:
        load.start()

    def pair_copy(kind, side):
        return remote(
            row_block(partial, 2 * side + (1 - c)),
            pair_in.at[kind, side],
            pair_send.at[kind, side],
            pair_recv.at[kind, side],
            (rep, sibling),
        )

    def row_copy(kind):
        return remote(
            pair_in.at[kind, 1 - y],
            row_in.at[kind],
            pair_send.at[kind, 2],
            pair_recv.at[kind, 2],
            (rep, peer),
        )

    def join_pair(kind):
        for side in range(2):
            pair_copy(kind, side).wait_recv()
        for side in range(2):
            span = pl.ds(pl.multiple_of((2 * side + c) * rows, rows), rows)
            pair_in[kind, side] = pair_in[kind, side] + partial[span, :]
        row_copy(kind).start()

    def joined_rows(kind):
        row_copy(kind).wait_recv()
        return pair_in[kind, y] + row_in[kind]

    def branch_rows(i):
        span = pl.ds(pl.multiple_of(i * rows, rows), rows)
        partial[span, :] = dot_nn(normed_out_ref[span, :], w_out_ref[...])

    loads[0].wait()
    loads[1].wait()
    each(shards, branch_rows)
    for side in range(2):
        pair_copy(0, side).start()

    def swap_copy(part, step):
        to = shard_at(step)
        return remote(
            low.at[part, :, pl.ds(pl.multiple_of(to * depth, depth), depth)],
            parts_ref.at[rep, part, mine],
            swap_send.at[part, step],
            swap_recv.at[part, step],
            (rep, to),
        )

    def swap_own(part):
        return pltpu.make_async_copy(
            low.at[part, :, pl.ds(pl.multiple_of(mine * depth, depth), depth)],
            parts_ref.at[rep, part, mine],
            local_sem.at[2 + part],
        )

    def sum_groups(part):
        for step in range(reps):
            slot = step % 2
            last = step == reps - 1
            if not last:
                group_copy(step + 1, 1 - slot).start()
            elif part == 0:
                group_copy(0, 1 - slot).start()
            if step == 0:
                own_copy(part).wait()
            else:
                share_copy(part, step).wait_recv()
            group_copy(step, slot).wait()

            def columns(i, unused, step=step, slot=slot):
                span = pl.ds(pl.multiple_of(i * 512, 512), 512)
                term = dot_tn(taken[part, step], group_rows[slot, :, span])
                if step == 0:
                    total[:, span] = term
                elif step < reps - 1:
                    total[:, span] += term
                else:
                    low[part, :, span] = (total[:, span] + term).astype(BF)
                return unused

            lax.fori_loop(0, D // 512, columns, 0)
        swap_own(part).start()
        for step in range(1, shards):
            swap_copy(part, step).start()

    def line_copy(part, origin, toward, lane):
        block = parts_ref.at[origin * PLANE + x, part]
        return remote(
            block,
            block,
            line_send.at[part, lane, origin],
            line_recv.at[part, origin],
            ((z + toward) * PLANE + x, mine),
        )

    def side_copy(part, origin, from_x):
        block = parts_ref.at[origin * PLANE + from_x, part]
        return remote(
            block, block, side_send.at[part, origin], side_recv.at[part, origin], (beside, mine)
        )

    def spread_own(part):
        swap_own(part).wait()
        for step in range(1, shards):
            swap_copy(part, step).wait_recv()
        side_copy(part, z, x).start()

        @pl.when(z < LINE - 1)
        def _():
            line_copy(part, z, 1, 0).start()

        @pl.when(z > 0)
        def _():
            line_copy(part, z, -1, 1).start()

    def pass_on(part, step):
        @pl.when(z - step >= 0)
        def _():
            origin = z - step
            line_copy(part, origin, 1, 0).wait_recv()

            @pl.when(z < LINE - 1)
            def _():
                line_copy(part, origin, 1, 0).start()

            side_copy(part, origin, x).start()

        @pl.when(z + step < LINE)
        def _():
            origin = z + step
            line_copy(part, origin, -1, 1).wait_recv()

            @pl.when(z > 0)
            def _():
                line_copy(part, origin, -1, 1).start()

            side_copy(part, origin, x).start()

    sum_groups(0)
    join_pair(0)

    for step in range(1, shards):
        tail_out_copy(step).wait_recv()
    span = pl.ds(pl.multiple_of(mine * rows, rows), rows)
    summed_tail = tail_ref[span, :]
    for step in range(1, shards):
        summed_tail = summed_tail + tail_in[step]
    tail_low[span, :] = summed_tail.astype(BF)
    for step in range(1, shards):
        tail_back_copy(step).start()

    spread_own(0)
    sum_groups(1)

    for step in range(1, shards):
        tail_back_copy(step).wait_recv()
    for side in range(2):
        pair_copy(0, side).wait_send()
    heads, share = H // shards, 2 * N // shards
    lane = lax.broadcasted_iota(jnp.int32, (rows, TAIL_PAD), 1)
    owned = ((lane >= mine * share) & (lane < (mine + 1) * share)) | (
        (lane >= 2 * N + mine * heads) & (lane < 2 * N + (mine + 1) * heads)
    )

    def grad_rows(i):
        span = pl.ds(pl.multiple_of(i * rows, rows), rows)
        back = back_ref[span, :]
        tail = dot_nn(back, tail_low[...])
        tail = jnp.where(owned, tail, 0.0).astype(BF)
        partial[span, :] = (
            dot_nn(dot_nn(back, gate_ref[...]).astype(BF), w_gate_ref[...])
            + dot_nn(dot_nn(back, values_ref[...]).astype(BF), w_conv_ref[0:width, :])
            + dot_nn(tail, w_conv_ref[width:, :])
        )

    loads[2].wait()
    loads[3].wait()
    each(shards, grad_rows)
    for side in range(2):
        pair_copy(1, side).start()

    spread_own(1)
    pass_on(0, 1)

    own_part.wait()
    tail_sum[...] = dot_tn(tail_low[...], own_columns[...])
    share_rows = TAIL_PAD // reps

    def tail_rows(ref, owner):
        return ref.at[pl.ds(pl.multiple_of(owner * share_rows, 16), share_rows)]

    def tail_part_copy(step):
        to = other(step)
        return remote(
            tail_rows(tail_sum, to),
            tail_parts.at[step],
            rep_send.at[0, step],
            rep_recv.at[0, step],
            (to, mine),
        )

    def tail_spread_copy(step):
        return remote(
            tail_rows(tails_ref, rep),
            tail_rows(tails_ref, rep),
            rep_send.at[1, step],
            rep_recv.at[1, step],
            (other(step), mine),
        )

    for step in range(1, reps):
        tail_part_copy(step).start()

    branch = joined_rows(0)
    whole = resid_ref[...].astype(F32) + branch
    block_out_ref[...] = whole.astype(BF)
    counts = valid_ref[...].astype(F32)
    square_total = jnp.sum(
        counts * jnp.sum(whole * whole, axis=1, keepdims=True), axis=0, keepdims=True
    )
    square_branch = jnp.sum(
        counts * jnp.sum(branch * branch, axis=1, keepdims=True), axis=0, keepdims=True
    )
    count = jnp.sum(counts, axis=0, keepdims=True)

    pass_on(1, 1)
    join_pair(1)
    pass_on(0, 2)

    for step in range(1, reps):
        tail_part_copy(step).wait_recv()
    span = pl.ds(pl.multiple_of(rep * share_rows, 16), share_rows)
    piece = tail_sum[span, :]
    for step in range(1, reps):
        piece = piece + tail_parts[step]
    tails_ref[span, :] = piece.astype(BF)
    for step in range(1, reps):
        tail_spread_copy(step).start()

    pass_on(1, 2)

    grad_normed = joined_rows(1)
    given = x_ref[...].astype(F32)
    inverse = lax.rsqrt(jnp.mean(given * given, axis=1, keepdims=True) + EPSILON)
    grad_norm_gain = jnp.sum(grad_normed * (given * inverse), axis=0, keepdims=True)
    scaled = grad_normed * gain_ref[...]
    pull = inverse * inverse * inverse * jnp.mean(scaled * given, axis=1, keepdims=True)
    span = pl.ds(pl.multiple_of(mine * rows, rows), rows)
    loads[4].wait()
    kept = dot_nn(back_ref[span, :], branch_grad_ref[...])
    grad_in_ref[...] = (scaled * inverse - given * pull + kept).astype(BF)

    lane = lax.broadcasted_iota(jnp.int32, (1, 128), 1)
    at = 0
    for i in range(D // 128):
        small[at : at + 1, :] = grad_norm_gain[:, 128 * i : 128 * i + 128]
        at += 1
    channels = (width + 2 * N) // 128
    for tap in range(KW):
        for i in range(channels):
            small[at : at + 1, :] = grad_conv_w_ref[tap : tap + 1, 128 * i : 128 * i + 128]
            at += 1
    for i in range(channels):
        small[at : at + 1, :] = grad_conv_b_ref[:, 128 * i : 128 * i + 128]
        at += 1
    for i in range(width // 128):
        small[at : at + 1, :] = grad_gain_ref[:, 128 * i : 128 * i + 128]
        at += 1
    small[at : at + 3, :] = grad_head_ref[0:3, :]
    small[at + 3 : at + 4, :] = jnp.where(
        lane == 0,
        spread(square_total),
        jnp.where(lane == 1, spread(square_branch), jnp.where(lane == 2, spread(count), 0.0)),
    )
    small[at + 4 :, :] = jnp.zeros((small.shape[0] - at - 4, 128), F32)

    def small_rep_copy(step):
        return remote(
            small, small_in.at[rep], rep_send.at[2, step], rep_recv.at[2, step], (other(step), mine)
        )

    def small_rep_arrival(step):
        return remote(
            small,
            small_in.at[before(step)],
            rep_send.at[2, step],
            rep_recv.at[2, step],
            (other(step), mine),
        )

    def small_shard_copy(step):
        return remote(
            small_all.at[mine],
            small_all.at[mine],
            all_send.at[step],
            all_recv.at[step],
            (rep, shard_at(step)),
        )

    for step in range(1, reps):
        small_rep_copy(step).start()
    small_in[rep] = small[...]

    pass_on(0, 3)
    for step in range(1, reps):
        small_rep_arrival(step).wait_recv()
    added = small_in[0]
    for i in range(1, reps):
        added = added + small_in[i]
    small_all[mine] = added
    for step in range(1, shards):
        small_shard_copy(step).start()
    pass_on(1, 3)
    for step in range(1, shards):
        small_shard_copy(step).wait_recv()

    def over_shards(row):
        value = small_all[0, row : row + 1, :]
        for i in range(1, shards):
            value = value + small_all[i, row : row + 1, :]
        return value

    at = 0
    for i in range(D // 128):
        out_norm_ref[:, 128 * i : 128 * i + 128] = over_shards(at)
        at += 1
    for tap in range(KW + 1):
        ref, row = (out_conv_w_ref, tap) if tap < KW else (out_conv_b_ref, 0)
        for i in range(channels):
            if i < width // 128:
                for shard in range(shards):
                    to = shard * width + 128 * i
                    ref[row : row + 1, to : to + 128] = small_all[shard, at : at + 1, :]
            else:
                to = DI + 128 * i - width
                ref[row : row + 1, to : to + 128] = over_shards(at)
            at += 1
    for i in range(width // 128):
        for shard in range(shards):
            to = shard * width + 128 * i
            out_gain_ref[:, to : to + 128] = small_all[shard, at : at + 1, :]
        at += 1
    for i in range(3):
        out_head_ref[i : i + 1, :] = over_shards(at + i)
    stats = over_shards(at + 3)
    per = jnp.maximum(stats[:, 2:3], 1.0) * D
    out_head_ref[3:4, :] = jnp.sqrt(stats / spread(per))
    out_head_ref[4:8, :] = jnp.zeros((4, 128), F32)

    for step in range(1, reps):
        tail_spread_copy(step).wait_recv()
    for part in range(2):
        for origin in range(LINE):
            side_copy(part, origin, 1 - x).wait_recv()
            side_copy(part, origin, x).wait_send()

            @pl.when((origin <= z) & (z < LINE - 1))
            def _(part=part, origin=origin):
                line_copy(part, origin, 1, 0).wait_send()

            @pl.when((origin >= z) & (z > 0))
            def _(part=part, origin=origin):
                line_copy(part, origin, -1, 1).wait_send()

        for step in range(1, shards):
            swap_copy(part, step).wait_send()
        for step in range(1, reps):
            share_copy(part, step).wait_send()
    for side in range(2):
        pair_copy(1, side).wait_send()
    for kind in range(2):
        row_copy(kind).wait_send()
    for step in range(1, shards):
        tail_out_copy(step).wait_send()
        tail_back_copy(step).wait_send()
        small_shard_copy(step).wait_send()
    for step in range(1, reps):
        tail_part_copy(step).wait_send()
        tail_spread_copy(step).wait_send()
        small_rep_copy(step).wait_send()


def run_end(operands, shards):
    gate = operands[0]
    reps = LINE * PLANE
    length, width = gate.shape
    rows, depth = length // shards, D // shards
    dma = pltpu.SemaphoreType.DMA
    vector = pl.BlockSpec(memory_space=pltpu.VMEM)
    anywhere = pl.BlockSpec(memory_space=pl.ANY)
    shape = jax.ShapeDtypeStruct
    channels = width + 2 * N
    small = -(-(D + 5 * channels + width + 4 * 128) // 1024) * 8
    return pl.pallas_call(
        end_kernel,
        out_shape=(
            shape((reps, 2, shards, 128, depth), BF),
            shape((TAIL_PAD, depth), BF),
            shape((rows, D), BF),
            shape((rows, D), BF),
            shape((1, D), F32),
            shape((KW, CONVW), F32),
            shape((1, CONVW), F32),
            shape((8, 128), F32),
            shape((1, DI), F32),
        ),
        in_specs=[vector] * 3 + [anywhere] * 5 + [vector, anywhere] + [vector] * 8,
        out_specs=(anywhere,) + (vector,) * 8,
        scratch_shapes=[
            pltpu.VMEM((2, reps, length, 128), BF),
            pltpu.VMEM((2, length, D), BF),
            pltpu.VMEM((length, depth), BF),
            pltpu.VMEM((128, D), F32),
            pltpu.VMEM((2, 128, D), BF),
            pltpu.VMEM((length, D), F32),
            pltpu.VMEM((2, 2, rows, D), F32),
            pltpu.VMEM((2, rows, D), F32),
            pltpu.VMEM((shards, rows, TAIL_PAD), F32),
            pltpu.VMEM((length, TAIL_PAD), BF),
            pltpu.VMEM((TAIL_PAD, depth), F32),
            pltpu.VMEM((reps, TAIL_PAD // reps, depth), F32),
            pltpu.VMEM((small, 128), F32),
            pltpu.VMEM((reps, small, 128), F32),
            pltpu.VMEM((shards, small, 128), F32),
            pltpu.VMEM((width, D), BF),
            pltpu.VMEM((width + TAIL_PAD, D), BF),
            pltpu.VMEM((width, D), BF),
            pltpu.VMEM((length, width), BF),
            pltpu.VMEM((length, D), BF),
            dma((5,)),
            dma((5,)),
            dma((2,)),
            dma((2, reps)),
            dma((2, reps)),
            dma((2, shards)),
            dma((2, shards)),
            dma((2, 2, LINE)),
            dma((2, LINE)),
            dma((2, LINE)),
            dma((2, LINE)),
            dma((2, 3)),
            dma((2, 3)),
            dma((2, shards)),
            dma((2, shards)),
            dma((3, reps)),
            dma((3, reps)),
            dma((shards,)),
            dma((shards,)),
        ],
        compiler_params=pltpu.CompilerParams(
            vmem_limit_bytes=VMEM_BYTES, collective_id=3, has_side_effects=True
        ),
        cost_estimate=pl.CostEstimate(
            flops=2 * reps * length * D * 256, bytes_accessed=96 << 20, transcendentals=0
        ),
        name="weight_gradient",
    )(*operands)


def assemble_kernel(parts_ref, tail_ref, out_ref):
    step, steps = pl.program_id(0), pl.num_programs(0)
    reps = parts_ref.shape[0]

    @pl.when(step < steps - 1)
    def _():
        for rep in range(reps):
            out_ref[128 * rep : 128 * rep + 128, :] = parts_ref[rep, 0, 0].astype(F32)

    @pl.when(step == steps - 1)
    def _():
        out_ref[0:TAIL, :] = tail_ref[0:TAIL, :].astype(F32)


def run_assemble(parts, tail):
    reps, unused, shards, unused2, depth = parts.shape
    steps = 2 * shards

    def place(i):
        at = jnp.minimum(i, steps - 1)
        return (0, at // shards, lax.rem(at, shards), 0, 0)

    return pl.pallas_call(
        assemble_kernel,
        grid=(steps + 1,),
        out_shape=jax.ShapeDtypeStruct((PROJ, depth), F32),
        in_specs=[
            pl.BlockSpec((reps, 1, 1, 128, depth), place),
            pl.BlockSpec((TAIL_PAD, depth), lambda i: (0, 0)),
        ],
        out_specs=pl.BlockSpec((reps * 128, depth), lambda i: (i, 0)),
        compiler_params=params(),
        name="assemble",
    )(parts, tail)


def exchange(pieces, axis, mine):
    count = lax.axis_size(axis)
    own = pieces(mine)
    gathered = jnp.zeros((count,) + own.shape, own.dtype)
    gathered = lax.dynamic_update_index_in_dim(gathered, own, mine, 0)
    for other in range(1, count):
        arrived = lax.ppermute(
            pieces(mine ^ other), axis, [(i, i ^ other) for i in range(count)]
        )
        gathered = lax.dynamic_update_index_in_dim(gathered, arrived, mine ^ other, 0)
    return gathered


def columns_at(array, start, width):
    return lax.dynamic_slice_in_dim(array, start, width, axis=1)


def plain_device(
    x_in,
    cotangent,
    seq_lengths,
    seq_order,
    valid,
    norm_gain,
    w_in,
    conv_w,
    conv_b,
    head_rows,
    gain_row,
    w_out,
):
    shards, mine = lax.axis_size("shard"), lax.axis_index("shard")
    rows = x_in.shape[0]
    length = rows * shards
    depth = w_in.shape[0]
    heads = H // shards
    width = DI // shards
    share = 2 * N // shards
    w_tail = w_in[:, 2 * DI :]

    def conv_piece(d):
        return jnp.concatenate([columns_at(w_in, DI + d * width, width), w_tail], axis=1)

    x_group = lax.all_gather(x_in, "shard", axis=0, tiled=True)
    w_conv = exchange(conv_piece, "shard", mine).reshape(D, width + TAIL)
    w_gate = exchange(lambda d: columns_at(w_in, d * width, width), "shard", mine).reshape(D, width)
    branch_grad = lax.all_gather(
        jnp.where(valid[:, None] > 0, cotangent, jnp.zeros_like(cotangent)),
        "shard",
        axis=0,
        tiled=True,
    )
    slot_ids = jnp.arange(length, dtype=jnp.int32)
    source, target, position = slot_tables(seq_lengths[0], seq_order[0], slot_ids)
    resid = dot_nn((source[:, None] == slot_ids[None, :]).astype(BF), x_group)
    inverse_rms = lax.rsqrt(jnp.mean(resid * resid, axis=1, keepdims=True) + EPSILON)
    normed = (resid * inverse_rms * norm_gain[None, :]).astype(BF)
    resid_mine = lax.dynamic_slice_in_dim(resid, mine * rows, rows, axis=0)
    gate = dot_nn(normed, w_gate).astype(BF)
    conv_in = jnp.pad(dot_nn(normed, w_conv).astype(BF), ((0, 0), (0, TAIL_PAD - TAIL)))
    place = jnp.broadcast_to(position[:, None], (length, 128))
    mixed, starts, normed_out, grad_mixed, grad_gate, grad_gain = run_forward(
        conv_in, gate, branch_grad, w_out, place, conv_w, conv_b, head_rows, gain_row, shards
    )
    branch = lax.psum_scatter(dot_nn(normed_out, w_out), "shard", scatter_dimension=0, tiled=True)
    total_rows = resid_mine + branch
    weights_valid = valid.astype(F32)
    square_total = jnp.sum(weights_valid * jnp.sum(total_rows * total_rows, axis=1))
    square_branch = jnp.sum(weights_valid * jnp.sum(branch * branch, axis=1))
    grad_w_out = lax.psum(dot_tn(normed_out, branch_grad), "rep")
    grad_values, grad_tail, grad_conv_w, grad_conv_b, grad_head = run_backward(
        conv_in, place, conv_w, conv_b, head_rows, mixed, starts, grad_mixed
    )
    grad_tail = lax.psum(grad_tail, "shard").astype(BF)
    lane = jnp.arange(TAIL, dtype=jnp.int32)
    owned = ((lane >= mine * share) & (lane < (mine + 1) * share)) | (
        (lane >= 2 * N + mine * heads) & (lane < 2 * N + (mine + 1) * heads)
    )
    kept_tail = jnp.where(owned[None, :], grad_tail[:, :TAIL], jnp.zeros((), BF))
    back = (target[:, None] == slot_ids[None, :]).astype(BF)

    def returned(grad):
        return dot_nn(back, grad).astype(BF)

    grad_normed = lax.psum_scatter(
        dot_nt(returned(grad_gate), w_gate)
        + dot_nt(returned(grad_values), w_conv[:, :width])
        + dot_nt(returned(kept_tail), w_conv[:, width:]),
        "shard",
        scatter_dimension=0,
        tiled=True,
    )
    given = x_in.astype(F32)
    given_rms = lax.rsqrt(jnp.mean(given * given, axis=1, keepdims=True) + EPSILON)
    grad_norm_gain = jnp.sum(grad_normed * (given * given_rms), axis=0)
    scaled = grad_normed * norm_gain[None, :]
    grad_resid = scaled * given_rms - given * (
        given_rms**3 * jnp.mean(scaled * given, axis=1, keepdims=True)
    )
    back_mine = lax.dynamic_slice_in_dim(back, mine * rows, rows, axis=0)
    grad_in = (grad_resid + dot_nn(back_mine, branch_grad)).astype(BF)

    def to_owners(columns):
        part = dot_tn(normed, columns).reshape(shards, depth, columns.shape[1])
        swapped = lax.all_to_all(part, "shard", split_axis=0, concat_axis=0, tiled=True)
        summed = lax.psum(swapped, "rep")
        return summed.transpose(1, 0, 2).reshape(depth, shards * columns.shape[1])

    grad_w_tail = lax.psum(
        dot_tn(columns_at(normed, mine * depth, depth), grad_tail[:, :TAIL]), "rep"
    )
    grad_w_in = jnp.concatenate([to_owners(grad_gate), to_owners(grad_values), grad_w_tail], axis=1)

    def placed(part):
        own = lax.dynamic_update_slice_in_dim(
            jnp.zeros((part.shape[0], DI), F32), part[:, :width], mine * width, axis=1
        )
        return jnp.concatenate([own, part[:, width:]], axis=1)

    summed = lax.psum(
        (
            grad_norm_gain,
            placed(grad_conv_w),
            placed(grad_conv_b)[0],
            grad_head,
            placed(grad_gain)[0],
            jnp.stack([square_total, square_branch, jnp.sum(weights_valid)]),
        ),
        ALL,
    )
    roots = jnp.sqrt(summed[5] / (jnp.maximum(summed[5][2], 1.0) * D))
    return (
        total_rows.astype(BF),
        grad_in,
        summed[0],
        grad_w_in,
        summed[1],
        summed[2],
        summed[3][0, :H],
        summed[3][1, :H],
        summed[3][2, :H],
        summed[4],
        grad_w_out,
        roots[0],
        roots[1],
    )


def on_device(
    x_in,
    cotangent,
    seq_lengths,
    seq_order,
    valid,
    norm_gain,
    w_in,
    conv_w,
    conv_b,
    dt_bias,
    a_log,
    d_skip,
    gated_gain,
    w_out,
):
    shards, mine = lax.axis_size("shard"), lax.axis_index("shard")
    reps = lax.axis_size("rep")
    rows = x_in.shape[0]
    length = rows * shards
    depth = w_in.shape[0]
    heads = H // shards
    width = DI // shards

    head_rows = jnp.pad(jnp.stack([dt_bias, a_log, d_skip]), ((0, 5), (0, 128 - H)))
    bias_row, gain_row = conv_b[None, :], gated_gain[None, :]
    spans = reps == LINE * PLANE and shards == 4 and width == reps * 128 and rows == 128
    if not spans:
        return plain_device(
            x_in,
            cotangent,
            seq_lengths,
            seq_order,
            valid,
            norm_gain,
            w_in,
            conv_w,
            bias_row,
            head_rows,
            gain_row,
            w_out,
        )
    norm_row, valid_column = norm_gain[None, :], valid[:, None]
    normed, conv_in, gate, w_gate, w_conv, branch_grad, back, place, resid = run_start(
        seq_lengths, seq_order, x_in, cotangent, valid_column, norm_row, w_in.T, shards
    )
    normed_mine = lax.dynamic_slice_in_dim(normed, mine * rows, rows, axis=0)
    normed_all = lax.all_gather(normed_mine, ALL, axis=0, tiled=True)
    mixed, starts, normed_out, grad_mixed, grad_gate, grad_gain = run_forward(
        conv_in, gate, branch_grad, w_out, place, conv_w, bias_row, head_rows, gain_row, shards
    )
    grad_w_out = lax.psum(dot_tn(normed_out, branch_grad).astype(BF), "rep").astype(F32)
    grad_values, grad_tail, grad_conv_w, grad_conv_b, grad_head = run_backward(
        conv_in, place, conv_w, bias_row, head_rows, mixed, starts, grad_mixed
    )
    operands = (
        grad_gate,
        grad_values,
        grad_tail,
        normed_all,
        w_gate,
        w_conv,
        w_out,
        normed_out,
        back,
        branch_grad,
        x_in,
        resid,
        valid_column,
        norm_row,
        grad_conv_w,
        grad_conv_b,
        grad_head,
        grad_gain,
    )
    parts, tails, block_out, grad_in, out_norm, out_conv_w, out_conv_b, out_head, out_gain = (
        run_end(operands, shards)
    )
    grad_w_in = run_assemble(parts, tails).T
    return (
        block_out,
        grad_in,
        out_norm[0],
        grad_w_in,
        out_conv_w,
        out_conv_b[0],
        out_head[0, :H],
        out_head[1, :H],
        out_head[2, :H],
        out_gain[0],
        grad_w_out,
        out_head[3, 0],
        out_head[3, 1],
    )


def solution(mesh):
    in_specs = (
        P(ALL, None),
        P(ALL, None),
        P("rep", None),
        P("rep", None),
        P(ALL),
        P(),
        P("shard", None),
        P(),
        P(),
        P(),
        P(),
        P(),
        P(),
        P("shard", None),
    )
    out_specs = (
        P(ALL, None),
        P(ALL, None),
        P(),
        P("shard", None),
        P(),
        P(),
        P(),
        P(),
        P(),
        P(),
        P("shard", None),
        P(),
        P(),
    )
    return jax.shard_map(
        on_device, mesh=mesh, in_specs=in_specs, out_specs=out_specs, check_vma=False
    )
```

```python
import functools

import jax
import jax.numpy as jnp
from jax import lax
from jax.experimental import pallas as pl
from jax.experimental.pallas import tpu as pltpu
from jax.sharding import PartitionSpec as P

D = 2048
H = 64
P_SIZE = 64
N = 128
KW = 4
SPAN = 128
DI = 4096
CONVW = 4352
PROJ = 8512
TAIL = PROJ - 2 * DI

EPSILON = 1e-05
ALL = ("rep", "shard")
VMEM_BYTES = 56 * 1024 * 1024
BF = jnp.bfloat16
F32 = jnp.float32


def dot_nn(a, b):
    return lax.dot_general(a, b, (((1,), (0,)), ((), ())), preferred_element_type=F32)


def dot_nt(a, b):
    return lax.dot_general(a, b, (((1,), (1,)), ((), ())), preferred_element_type=F32)


def dot_tn(a, b):
    return lax.dot_general(a, b, (((0,), (0,)), ((), ())), preferred_element_type=F32)


def halves(a):
    high = a.astype(BF)
    return high, (a - high.astype(F32)).astype(BF)


def slot_tables(seq_lengths, seq_order, slot_ids):
    seq_count = seq_lengths.shape[0]
    numbers = jnp.arange(seq_count, dtype=jnp.int32)
    chosen = (seq_order[:, None] == numbers[None, :]).astype(jnp.int32)
    given_start = jnp.cumsum(seq_lengths) - seq_lengths
    owner_length = jnp.sum(chosen * seq_lengths[None, :], axis=1)
    owner_start = jnp.cumsum(owner_length) - owner_length
    owner_from = jnp.sum(chosen * given_start[None, :], axis=1)
    placed_at = jnp.sum(chosen * owner_start[:, None], axis=0)
    column = slot_ids[:, None]
    within = (column >= owner_start[None, :]) & (column < (owner_start + owner_length)[None, :])
    offset = column - owner_start[None, :]
    source = jnp.sum(jnp.where(within, offset + owner_from[None, :], 0), axis=1)
    position = jnp.sum(jnp.where(within, offset, 0), axis=1)
    given_within = (column >= given_start[None, :]) & (
        column < (given_start + seq_lengths)[None, :]
    )
    target = jnp.sum(
        jnp.where(given_within, column - given_start[None, :] + placed_at[None, :], 0), axis=1
    )
    return (source, target, position)


def params():
    return pltpu.CompilerParams(vmem_limit_bytes=VMEM_BYTES)


def spread_rows(row):
    return jnp.broadcast_to(row, (16, row.shape[1]))


def sigmoid(v):
    return 1.0 / (1.0 + jnp.exp(-v))


def spread(column, lanes=128):
    return jnp.broadcast_to(column, (column.shape[0], lanes))


MESH = pl.DeviceIdType.MESH
LINE, PLANE = 4, 2
CHUNK = 256
TAIL_PAD = 384


def remote(src, dst, send_sem, recv_sem, device):
    return pltpu.make_async_remote_copy(
        src_ref=src,
        dst_ref=dst,
        send_sem=send_sem,
        recv_sem=recv_sem,
        device_id=device,
        device_id_type=MESH,
    )


def meet(devices):
    barrier = pltpu.get_barrier_semaphore()
    for device in devices:
        pl.semaphore_signal(barrier, inc=1, device_id=device, device_id_type=MESH)
    pl.semaphore_wait(barrier, len(devices))


class Line:
    def __init__(self, store, first, share, send_sem, recv_sem):
        self.store, self.first, self.share = store, first, share
        self.send_sem, self.recv_sem = send_sem, recv_sem
        self.mine, self.rep = lax.axis_index("shard"), lax.axis_index("rep")
        self.z, self.x = self.rep // PLANE, lax.rem(self.rep, PLANE)
        self.sibling = self.mine // 2 * 2 + (1 - lax.rem(self.mine, 2))

    def along(self, origin, toward, first=False):
        block = self.store.at[origin, self.share]
        lane = (toward + 1) // 2
        return remote(
            self.first if first else block,
            block,
            self.send_sem.at[lane, origin],
            self.recv_sem.at[0, origin],
            ((self.z + toward) * PLANE + self.x, self.mine),
        )

    def inward(self, origin):
        block = self.store.at[origin, self.share]
        return remote(
            block,
            block,
            self.send_sem.at[2, origin],
            self.recv_sem.at[1, origin],
            (self.rep, self.sibling),
        )

    def start(self):
        for toward in (1, -1):
            self.guarded(toward, lambda: self.along(self.z, toward, True).start())

    def guarded(self, toward, act):
        pl.when(self.z < LINE - 1 if toward > 0 else self.z > 0)(act)

    def step(self, distance):
        for toward in (1, -1):
            origin = self.z - toward * distance

            @pl.when(origin >= 0 if toward > 0 else origin < LINE)
            def _():
                self.along(origin, toward).wait_recv()
                self.guarded(toward, lambda: self.along(origin, toward).start())
                self.inward(origin).start()

    def finish(self):
        for origin in range(LINE):

            @pl.when(origin != self.z)
            def _():
                self.inward(origin).wait_recv()
                self.inward(origin).wait_send()

            for toward in (1, -1):
                passed = origin <= self.z if toward > 0 else origin >= self.z
                pl.when(passed)(
                    lambda: self.guarded(toward, lambda: self.along(origin, toward).wait_send())
                )


def meet_with_line(devices):
    mine, rep = lax.axis_index("shard"), lax.axis_index("rep")
    z, x = rep // PLANE, lax.rem(rep, PLANE)
    barrier = pltpu.get_barrier_semaphore()
    for device in devices:
        pl.semaphore_signal(barrier, inc=1, device_id=device, device_id_type=MESH)
    for toward, there in ((1, z < LINE - 1), (-1, z > 0)):

        @pl.when(there)
        def _():
            pl.semaphore_signal(
                barrier, inc=1, device_id=((z + toward) * PLANE + x, mine), device_id_type=MESH
            )

    beyond = (z + LINE - 1) // LINE + (2 * (LINE - 1) - z) // LINE
    pl.semaphore_wait(barrier, len(devices) + beyond)


def tables_in_kernel(lengths_ref, order_ref, slots):
    count = lengths_ref.shape[1]
    lengths = [lengths_ref[0, i] for i in range(count)]
    order = [order_ref[0, i] for i in range(count)]
    given_start, at = [], jnp.int32(0)
    for i in range(count):
        given_start.append(at)
        at = at + lengths[i]
    source = jnp.zeros_like(slots)
    position = jnp.zeros_like(slots)
    placed_at = [jnp.int32(0)] * count
    at = jnp.int32(0)
    for k in range(count):
        length, start = jnp.int32(0), jnp.int32(0)
        for i in range(count):
            chosen = order[k] == i
            length = length + jnp.where(chosen, lengths[i], 0)
            start = start + jnp.where(chosen, given_start[i], 0)
            placed_at[i] = placed_at[i] + jnp.where(chosen, at, 0)
        within = (slots >= at) & (slots < at + length)
        source = source + jnp.where(within, slots - at + start, 0)
        position = position + jnp.where(within, slots - at, 0)
        at = at + length
    target = jnp.zeros_like(slots)
    for i in range(count):
        within = (slots >= given_start[i]) & (slots < given_start[i] + lengths[i])
        target = target + jnp.where(within, slots - given_start[i] + placed_at[i], 0)
    return source, target, position


def start_kernel(
    lengths_ref,
    order_ref,
    x_ref,
    cotangent_ref,
    valid_ref,
    gain_ref,
    w_ref,
    normed_out_ref,
    conv_in_ref,
    gate_ref,
    w_gate_out_ref,
    w_conv_out_ref,
    branch_grad_ref,
    back_ref,
    place_ref,
    resid_ref,
    inverse_ref,
    line_ref,
    side_ref,
    x_all,
    normed,
    w_gate,
    w_conv,
    grads,
    local_sem,
    row_send,
    row_recv,
    w_send,
    w_recv,
    w_local,
    line_send,
    line_recv,
    side_send,
    side_recv,
):
    mine, rep = lax.axis_index("shard"), lax.axis_index("rep")
    y, c = mine // 2, lax.rem(mine, 2)
    z, x = rep // PLANE, lax.rem(rep, PLANE)
    sibling, peer, far = y * 2 + (1 - c), (1 - y) * 2 + c, (1 - y) * 2 + (1 - c)
    beside = z * PLANE + (1 - x)
    rows, length = x_ref.shape[0], x_all.shape[0]
    depth, width = w_ref.shape[1], gate_ref.shape[1]
    chunks = width // CHUNK
    tail_half = TAIL // 2
    meet_with_line([(rep, sibling), (rep, peer), (rep, far), (beside, mine)])

    part = pl.ds(pl.multiple_of(y * (D // 2), 128), D // 2)
    share = pl.ds(pl.multiple_of(c * (length // 2), 16), length // 2)
    wholes = (x_all, grads)

    lines = [
        Line(
            line_ref.at[kind],
            wholes[kind].at[share, part],
            share,
            line_send.at[kind],
            line_recv.at[kind],
        )
        for kind in range(2)
    ]

    def side_copy(kind):
        return remote(
            wholes[kind].at[share, part],
            side_ref.at[kind, share],
            side_send.at[kind, 0],
            side_recv.at[kind, 0],
            (beside, mine),
        )

    def side_inward(kind):
        block = side_ref.at[kind, share]
        return remote(block, block, side_send.at[kind, 1], side_recv.at[kind, 1], (rep, sibling))

    def line_own(kind):
        return pltpu.make_async_copy(
            wholes[kind].at[:, part], line_ref.at[kind, z], local_sem.at[4 + kind]
        )

    def block(ref, shard):
        return ref.at[pl.ds(pl.multiple_of(shard * rows, rows), rows)]

    def row_copies(kind, own, store):
        return (
            remote(own, block(store, mine), row_send.at[kind, 0], row_recv.at[kind, 0], (rep, peer)),
            remote(own, block(store, mine), row_send.at[kind, 1], row_recv.at[kind, 1], (rep, sibling)),
            remote(
                block(store, peer),
                block(store, peer),
                row_send.at[kind, 2],
                row_recv.at[kind, 2],
                (rep, sibling),
            ),
        )

    def lanes(shard):
        return pl.ds(pl.multiple_of(shard * depth, depth), depth)

    def weight_copies(store, index, base, stride, at, half):
        share = pl.ds(pl.multiple_of(at + half * x, 16), half)
        both = pl.ds(pl.multiple_of((1 - y) * 2 * depth, 128), 2 * depth)

        def source(shard, start, count):
            return w_ref.at[pl.ds(pl.multiple_of(base + stride * shard + start, 16), count)]

        def sems(way):
            return w_send.at[way, index], w_recv.at[way, index]

        whole = pl.ds(pl.multiple_of(at, 16), 2 * half)
        near = at if stride else 0
        return (
            lambda: remote(
                source(peer, near + half * x, half), store.at[share, lanes(mine)], *sems(0), (rep, peer)
            ),
            lambda: remote(
                source(far, near + half * x, half), store.at[share, lanes(mine)], *sems(1), (rep, far)
            ),
            lambda: remote(store.at[share, both], store.at[share, both], *sems(2), (beside, mine)),
            lambda: remote(
                source(sibling, near, 2 * half), store.at[whole, lanes(mine)], *sems(3), (rep, sibling)
            ),
            lambda: pltpu.make_async_copy(
                source(mine, near, 2 * half), store.at[whole, lanes(mine)], w_local.at[index]
            ),
        )

    def conv_copies(q):
        return weight_copies(w_conv, q, DI, width, q * CHUNK, CHUNK // 2)

    def tail_copies():
        return weight_copies(w_conv, chunks, 2 * DI, 0, width, tail_half)

    def gate_copies(q):
        return weight_copies(w_gate, chunks + 1 + q, 0, width, q * CHUNK, CHUNK // 2)

    def send_near(copies):
        copies[3]().start()
        copies[4]().start()

    def send_far(copies):
        copies[0]().start()
        copies[1]().start()

    def pass_on(copies):
        copies[0]().wait_recv()
        copies[1]().wait_recv()
        copies[2]().start()
        copies[0]().wait_send()
        copies[1]().wait_send()

    def arrived(copies):
        copies[2]().wait_recv()
        copies[3]().wait_recv()
        copies[4]().wait()

    def each(count, body):
        def step(i, unused):
            body(i)
            return unused

        lax.fori_loop(0, count, step, 0)

    x_copies = row_copies(0, x_ref, x_all)
    grad_copies = row_copies(1, block(grads, mine), grads)
    own_rows = pltpu.make_async_copy(x_ref, block(x_all, mine), local_sem.at[0])
    convs = [conv_copies(q) for q in range(chunks)]
    gates = [gate_copies(q) for q in range(chunks)]
    tail = tail_copies()
    x_copies[0].start()
    x_copies[1].start()
    own_rows.start()
    for copies in convs + [tail] + gates:
        send_near(copies)
    grads[pl.ds(pl.multiple_of(mine * rows, rows), rows), :] = jnp.where(
        spread(valid_ref[...], D) > 0, cotangent_ref[...].astype(F32), 0.0
    ).astype(BF)
    grad_copies[0].start()
    grad_copies[1].start()
    w_conv[width + TAIL :, :] = jnp.zeros((TAIL_PAD - TAIL, D), BF)

    def table_block(i):
        span = pl.ds(pl.multiple_of(i * rows, rows), rows)
        slots = lax.broadcasted_iota(jnp.int32, (rows, length), 0) + i * rows
        across = lax.broadcasted_iota(jnp.int32, (rows, length), 1)
        target = tables_in_kernel(lengths_ref, order_ref, slots)[1]
        back_ref[span, :] = (target == across).astype(F32).astype(BF)
        few_slots = lax.broadcasted_iota(jnp.int32, (rows, 128), 0) + i * rows
        place_ref[span, :] = tables_in_kernel(lengths_ref, order_ref, few_slots)[2]

    each(length // rows, table_block)
    x_copies[0].wait_recv()
    x_copies[2].start()
    x_copies[0].wait_send()
    send_far(convs[0])
    own_rows.wait()
    x_copies[1].wait_recv()
    x_copies[2].wait_recv()
    line_own(0).start()
    lines[0].start()
    side_copy(0).start()

    def picked(i):
        slots = lax.broadcasted_iota(jnp.int32, (rows, length), 0) + i * rows
        across = lax.broadcasted_iota(jnp.int32, (rows, length), 1)
        source = tables_in_kernel(lengths_ref, order_ref, slots)[0]
        return dot_nn((source == across).astype(F32).astype(BF), x_all[...])

    def norm_block(i):
        span = pl.ds(pl.multiple_of(i * rows, rows), rows)
        resid = picked(i)
        inverse = lax.rsqrt(jnp.mean(resid * resid, axis=1, keepdims=True) + EPSILON)
        normed[span, :] = (resid * inverse * gain_ref[...]).astype(BF)

    each(length // rows // 2, norm_block)
    grad_copies[0].wait_recv()
    grad_copies[2].start()
    grad_copies[0].wait_send()
    send_far(convs[1])
    each(length // rows // 2, lambda i: norm_block(i + length // rows // 2))
    lines[0].step(1)
    grad_copies[1].wait_recv()
    grad_copies[2].wait_recv()
    line_own(1).start()
    lines[1].start()
    side_copy(1).start()
    pass_on(convs[0])
    send_far(convs[2])
    resid_ref[...] = picked(mine).astype(BF)
    normed_store = pltpu.make_async_copy(normed, normed_out_ref, local_sem.at[1])
    normed_store.start()

    def inverse_block(i):
        span = pl.ds(pl.multiple_of(i * rows, rows), rows)
        given = x_all[span, :].astype(F32)
        inverse_ref[span, :] = spread(
            lax.rsqrt(jnp.mean(given * given, axis=1, keepdims=True) + EPSILON)
        )

    def project(store, target, at, count):
        span = pl.ds(at, count)
        target[:, span] = dot_nt(normed[...], store[span, :]).astype(BF)

    def conv_chunk(q):
        arrived(convs[q])
        project(w_conv, conv_in_ref, q * CHUNK, CHUNK)

    def gate_chunk(q):
        arrived(gates[q])
        project(w_gate, gate_ref, q * CHUNK, CHUNK)

    each(length // rows, inverse_block)
    pass_on(convs[1])
    send_far(convs[3])
    lines[0].step(2)
    conv_chunk(0)
    pass_on(convs[2])
    send_far(tail)
    lines[1].step(1)
    conv_chunk(1)
    pass_on(convs[3])
    send_far(gates[0])
    lines[0].step(3)
    conv_chunk(2)
    pass_on(tail)
    send_far(gates[1])
    lines[1].step(2)
    conv_chunk(3)
    pass_on(gates[0])
    send_far(gates[2])
    arrived(tail)
    project(w_conv, conv_in_ref, width, TAIL_PAD)
    conv_store = pltpu.make_async_copy(w_conv, w_conv_out_ref, local_sem.at[2])
    conv_store.start()
    pass_on(gates[1])
    send_far(gates[3])
    lines[1].step(3)
    gate_chunk(0)
    branch_grad_ref[...] = grads[...]
    pass_on(gates[2])
    gate_chunk(1)
    side_copy(0).wait_recv()
    side_inward(0).start()
    pass_on(gates[3])
    gate_chunk(2)
    side_copy(1).wait_recv()
    side_inward(1).start()
    gate_chunk(3)
    gate_store = pltpu.make_async_copy(w_gate, w_gate_out_ref, local_sem.at[3])
    gate_store.start()

    for copies in convs + [tail] + gates:
        copies[2]().wait_send()
        copies[3]().wait_send()
    x_copies[1].wait_send()
    x_copies[2].wait_send()
    grad_copies[1].wait_send()
    grad_copies[2].wait_send()
    normed_store.wait()
    conv_store.wait()
    gate_store.wait()
    for kind in range(2):
        line_own(kind).wait()
        lines[kind].finish()
        side_copy(kind).wait_send()
        side_inward(kind).wait_recv()
        side_inward(kind).wait_send()


def run_start(lengths, order, x_in, cotangent, valid, gain, w_columns, shards):
    rows = x_in.shape[0]
    length, width = rows * shards, DI // shards
    chunks = width // CHUNK
    dma = pltpu.SemaphoreType.DMA
    anywhere = pl.BlockSpec(memory_space=pl.ANY)
    scalars = pl.BlockSpec(memory_space=pltpu.SMEM)
    vector = pl.BlockSpec(memory_space=pltpu.VMEM)
    shape = jax.ShapeDtypeStruct
    return pl.pallas_call(
        start_kernel,
        out_shape=(
            shape((length, D), BF),
            shape((length, width + TAIL_PAD), BF),
            shape((length, width), BF),
            shape((width, D), BF),
            shape((width + TAIL_PAD, D), BF),
            shape((length, D), BF),
            shape((length, length), BF),
            shape((length, 128), jnp.int32),
            shape((rows, D), BF),
            shape((length, 128), F32),
            shape((2, LINE, length, D // 2), BF),
            shape((2, length, D // 2), BF),
        ),
        in_specs=[scalars, scalars, anywhere, vector, vector, vector, anywhere],
        out_specs=(anywhere, vector, vector, anywhere, anywhere) + (vector,) * 5 + (anywhere,) * 2,
        scratch_shapes=[
            pltpu.VMEM((length, D), BF),
            pltpu.VMEM((length, D), BF),
            pltpu.VMEM((width, D), BF),
            pltpu.VMEM((width + TAIL_PAD, D), BF),
            pltpu.VMEM((length, D), BF),
            dma((6,)),
            dma((2, 3)),
            dma((2, 3)),
            dma((4, 2 * chunks + 1)),
            dma((4, 2 * chunks + 1)),
            dma((2 * chunks + 1,)),
            dma((2, 3, LINE)),
            dma((2, 2, LINE)),
            dma((2, 2)),
            dma((2, 2)),
        ],
        compiler_params=pltpu.CompilerParams(
            vmem_limit_bytes=VMEM_BYTES, collective_id=1, has_side_effects=True
        ),
        cost_estimate=pl.CostEstimate(
            flops=2 * length * D * (2 * width + TAIL_PAD), bytes_accessed=48 << 20, transcendentals=0
        ),
        name="project",
    )(lengths, order, x_in, cotangent, valid, gain, w_columns)


def conv_pre(x, conv_w, conv_b, place):
    pre = conv_b + conv_w[KW - 1 : KW] * x
    for back in range(1, KW):
        moved = pltpu.roll(x, back, 0)
        pre = pre + jnp.where(place >= back, conv_w[KW - 1 - back : KW - back] * moved, 0.0)
    return pre


def conv_lanes(chunk, width, mine):
    if 128 * chunk < width:
        return pl.ds(pl.multiple_of(mine * width + 128 * chunk, 128), 128)
    return pl.ds(DI + 128 * chunk - width, 128)


def block_terms(place):
    local = lax.broadcasted_iota(jnp.int32, (SPAN, 128), 0)
    across = lax.broadcasted_iota(jnp.int32, (SPAN, 128), 1)
    begins = local - place
    causal = (across <= local) & (across >= begins)
    reach_end = local >= begins[SPAN - 1 : SPAN, :]
    entered = place >= local + 1
    carries = place[SPAN - 1 : SPAN, :] >= SPAN
    return causal, reach_end, entered, carries


def pair_terms(pair, run, run_t, step, causal, reach_end, entered, carries):
    left = lax.broadcasted_iota(jnp.int32, (SPAN, 128), 1) < P_SIZE
    runs = [spread(run[:, 2 * pair + i : 2 * pair + i + 1]) for i in range(2)]
    decays = []
    for i in range(2):
        gap = runs[i] - run_t[2 * pair + i : 2 * pair + i + 1, :]
        decays.append(jnp.exp(jnp.where(causal, gap, -jnp.inf)))
    both = jnp.where(left, runs[0], runs[1])
    end = both[SPAN - 1 : SPAN, :]
    entering = jnp.where(entered, jnp.exp(both), 0.0)
    tail = jnp.where(reach_end, jnp.exp(jnp.where(reach_end, end - both, 0.0)), 0.0)
    carried = jnp.where(carries, jnp.exp(end), 0.0)
    size = jnp.where(
        left,
        spread(step[:, 2 * pair : 2 * pair + 1]),
        spread(step[:, 2 * pair + 1 : 2 * pair + 2]),
    )
    return left, decays, entering, tail, carried, size


def stacked(value, left):
    zero = jnp.zeros_like(value)
    return jnp.concatenate([jnp.where(left, value, zero), jnp.where(left, zero, value)], axis=0)


def own_lanes(row, mine, heads):
    return pltpu.roll(row, lax.rem(128 - mine * heads, 128), 1)


def skip_lanes(row, pair):
    left = lax.broadcasted_iota(jnp.int32, (1, 128), 1) < P_SIZE
    return jnp.where(
        left,
        spread(row[:, 2 * pair : 2 * pair + 1]),
        spread(row[:, 2 * pair + 1 : 2 * pair + 2]),
    )


def step_and_run(conv_in_ref, heads_ref, run_ref, step_ref, width, mine):
    length = run_ref.shape[0]
    heads = width // P_SIZE
    lower = (
        lax.broadcasted_iota(jnp.int32, (SPAN, SPAN), 0)
        >= lax.broadcasted_iota(jnp.int32, (SPAN, SPAN), 1)
    ).astype(F32)
    bias = heads_ref[0:1, :]
    rate = jnp.exp(own_lanes(heads_ref[...], mine, heads)[1:2, :])

    def block(b, unused):
        rows = pl.ds(pl.multiple_of(b * SPAN, SPAN), SPAN)
        raw = conv_in_ref[rows, width + 2 * N : width + 2 * N + 128].astype(F32)
        step = own_lanes(jax.nn.softplus(raw + bias), mine, heads)
        step_ref[rows, :] = step
        run_ref[rows, :] = jnp.dot(
            lower, -step * rate, precision=lax.Precision.HIGHEST, preferred_element_type=F32
        )
        return unused

    lax.fori_loop(0, length // SPAN, block, 0)


def side_copies(line_ref, side_ref, blocks, send_sem, recv_sem):
    mine, rep = lax.axis_index("shard"), lax.axis_index("rep")
    y, c = mine // 2, lax.rem(mine, 2)
    z, x = rep // PLANE, lax.rem(rep, PLANE)
    length = side_ref.shape[1]
    share = pl.ds(pl.multiple_of(c * (length // 2), 16), length // 2)
    across = [
        remote(
            line_ref.at[kind, lax.rem(z + ahead, LINE), share],
            side_ref.at[i, share],
            send_sem.at[0, i],
            recv_sem.at[0, i],
            (z * PLANE + (1 - x), mine),
        )
        for i, (kind, ahead) in enumerate(blocks)
    ]
    inward = [
        remote(
            side_ref.at[i, share],
            side_ref.at[i, share],
            send_sem.at[1, i],
            recv_sem.at[1, i],
            (rep, y * 2 + (1 - c)),
        )
        for i in range(len(blocks))
    ]
    return across, inward


SIDE_BLOCKS = ((0, 1), (0, 2), (0, 3))


def hand_inward(copies):
    for over, inner in zip(*copies):
        over.wait_recv()
        inner.start()


def finish_side(copies):
    for over, inner in zip(*copies):
        inner.wait_recv()
        inner.wait_send()
        over.wait_send()


def forward_kernel(spans, *refs):
    refs = list(refs)
    if spans:
        line_ref, beside_ref = refs[9:11]
        side_ref, grad_side_ref = refs[17:19]
        side_send, side_recv, line_send, line_recv = refs[27:]
        refs = refs[:9] + refs[11:17] + refs[19:27]
    (
        conv_in_ref,
        gate_ref,
        branch_grad_ref,
        w_out_ref,
        place_ref,
        conv_w_ref,
        conv_b_ref,
        heads_ref,
        gain_ref,
        mixed_ref,
        starts_ref,
        normed_out_ref,
        grad_mixed_ref,
        grad_gate_ref,
        grad_gain_ref,
        act_ref,
        step_ref,
        run_ref,
        state_ref,
        back_ref,
        sums,
        send_sem,
        recv_sem,
    ) = refs
    length, width = mixed_ref.shape
    mine, rep, shards = lax.axis_index("shard"), lax.axis_index("rep"), lax.axis_size("shard")
    heads = width // P_SIZE
    peers = [(rep, lax.rem(mine + step, shards)) for step in range(1, shards)]
    if spans:
        z, x = rep // PLANE, lax.rem(rep, PLANE)
        meet_with_line(peers + [(z * PLANE + (1 - x), mine)])
        share = pl.ds(
            pl.multiple_of(lax.rem(mine, 2) * (length // 2), 16), length // 2
        )
        line = Line(grad_side_ref, beside_ref.at[1, share], share, line_send, line_recv)
        line.start()
        sides = side_copies(line_ref, side_ref, SIDE_BLOCKS, side_send, side_recv)
        for copy in sides[0]:
            copy.start()
    else:
        meet(peers)
    for c in range((width + 2 * N) // 128):
        lanes = slice(128 * c, 128 * c + 128)
        there = conv_lanes(c, width, mine)
        pre = conv_pre(
            conv_in_ref[:, lanes].astype(F32),
            conv_w_ref[:, there],
            conv_b_ref[:, there],
            place_ref[...],
        )
        act_ref[:, lanes] = (pre * sigmoid(pre)).astype(BF)
    step_and_run(conv_in_ref, heads_ref, run_ref, step_ref, width, mine)
    if spans:
        line.step(1)
    state_ref[...] = jnp.zeros_like(state_ref)
    skips = own_lanes(heads_ref[...], mine, heads)[2:3, :]

    def block(b, unused):
        row = pl.multiple_of(b * SPAN, SPAN)
        rows = pl.ds(row, SPAN)
        starts_ref[pl.ds(pl.multiple_of(b * N, N), N), :] = state_ref[...]
        run = run_ref[rows, :]
        run_t = run.T
        step = step_ref[rows, :]
        masks = block_terms(place_ref[rows, :])
        in_map = act_ref[rows, width : width + N]
        out_map = act_ref[rows, width + N : width + 2 * N]
        products = dot_nt(out_map, in_map)
        in_map_t = in_map.T
        for pair in range(width // 128):
            lanes = slice(128 * pair, 128 * pair + 128)
            left, decays, entering, tail, carried, size = pair_terms(
                pair, run, run_t, step, *masks
            )
            values = act_ref[rows, lanes].astype(F32)
            scaled = values * size
            weights = jnp.concatenate([(d * products).astype(BF) for d in decays], axis=1)
            out = dot_nn(weights, stacked(scaled.astype(BF), left))
            state = state_ref[:, lanes]
            high, low = halves(state)
            out += entering * (dot_nn(out_map, high) + dot_nn(out_map, low))
            mixed_ref[rows, lanes] = out + skip_lanes(skips, pair) * values
            high, low = halves(tail * scaled)
            fresh = dot_nn(in_map_t, high) + dot_nn(in_map_t, low)
            state_ref[:, lanes] = carried * state + fresh
        return unused

    lax.fori_loop(0, length // SPAN, block, 0)
    if spans:
        line.step(2)

    lane = lax.broadcasted_iota(jnp.int32, (SPAN, 128), 1)

    def gated(rows, c):
        lanes = slice(128 * c, 128 * c + 128)
        gate = gate_ref[rows, lanes].astype(F32)
        opened = sigmoid(gate)
        mixed = mixed_ref[rows, lanes]
        back = back_ref[rows, lanes]
        gain = gain_ref[:, pl.ds(pl.multiple_of(mine * width + 128 * c, 128), 128)]
        return gate, opened, mixed, back, gain, mixed * (gate * opened), back * gain

    def measure(b, unused):
        rows = pl.ds(pl.multiple_of(b * SPAN, SPAN), SPAN)
        back_ref[rows, :] = dot_nt(branch_grad_ref[rows, :], w_out_ref[...])
        squares = jnp.zeros((SPAN, 128), F32)
        crosses = jnp.zeros((SPAN, 128), F32)
        for c in range(width // 128):
            product, weighted = gated(rows, c)[5:]
            squares += product * product
            crosses += weighted * product
        squares = jnp.sum(squares, axis=1, keepdims=True)
        crosses = jnp.sum(crosses, axis=1, keepdims=True)
        both = jnp.where(lane == 0, spread(squares), jnp.where(lane == 1, spread(crosses), 0.0))
        sums[mine, :, rows] = both.T[0:8, :]
        return unused

    lax.fori_loop(0, length // SPAN, measure, 0)

    copies = [
        remote(sums.at[mine], sums.at[mine], send_sem.at[i], recv_sem.at[i], peer)
        for i, peer in enumerate(peers)
    ]
    for copy in copies:
        copy.start()
    for copy in copies:
        copy.wait_recv()
    grad_gain_ref[...] = jnp.zeros_like(grad_gain_ref)

    def finish(b, unused):
        rows = pl.ds(pl.multiple_of(b * SPAN, SPAN), SPAN)
        both = sums[0, :, rows]
        for shard in range(1, shards):
            both = both + sums[shard, :, rows]
        both = jnp.concatenate([both, jnp.zeros((SPAN - 8, SPAN), F32)], axis=0).T / DI
        inverse = lax.rsqrt(both[:, 0:1] + EPSILON)
        pull = spread(inverse * inverse * inverse * both[:, 1:2])
        inverse = spread(inverse)
        for c in range(width // 128):
            lanes = slice(128 * c, 128 * c + 128)
            gate, opened, mixed, back, gain, product, weighted = gated(rows, c)
            normalized = product * inverse
            normed_out_ref[rows, lanes] = (normalized * gain).astype(BF)
            grad_product = inverse * weighted - product * pull
            grad_gain_ref[:, lanes] += jnp.sum(back * normalized, axis=0, keepdims=True)
            grad_mixed_ref[rows, lanes] = grad_product * (gate * opened)
            grad_gate_ref[rows, lanes] = (
                grad_product * mixed * (opened * (1.0 + gate * (1.0 - opened)))
            ).astype(BF)
        return unused

    lax.fori_loop(0, length // SPAN, finish, 0)
    for copy in copies:
        copy.wait_send()
    if spans:
        line.step(3)
        hand_inward(sides)
        finish_side(sides)
        line.finish()


def rep_steps():
    return [(i // PLANE, i % PLANE) for i in range(1, LINE * PLANE)]


def rep_at(step):
    rep = lax.axis_index("rep")
    z, x = rep // PLANE, lax.rem(rep, PLANE)
    return lax.rem(z + step[0], LINE) * PLANE + lax.rem(x + step[1], PLANE)


def share_copy(source, taken, send_sem, recv_sem, step):
    to, z = rep_at(step), lax.axis_index("rep") // PLANE
    return remote(
        source.at[:, pl.ds(pl.multiple_of(to * 128, 128), 128)],
        taken.at[z, step[1]],
        send_sem.at[step[0], step[1]],
        recv_sem.at[z, step[1]],
        (to, lax.axis_index("shard")),
    )


def share_own(source, taken, sem):
    rep = lax.axis_index("rep")
    return pltpu.make_async_copy(
        source.at[:, pl.ds(pl.multiple_of(rep * 128, 128), 128)], taken.at[rep // PLANE, 0], sem
    )


def share_arrival(taken, recv_sem, at, side):
    block, sem = taken.at[at, side], recv_sem.at[at, side]
    remote(block, block, sem, sem, (rep_at((0, 1)), lax.axis_index("shard"))).wait_recv()


def share_wait(source, taken, recv_sem, own, at, side):
    z = lax.axis_index("rep") // PLANE
    if side == 1:
        share_arrival(taken, recv_sem, at, side)
    else:
        pl.when(z != at)(lambda: share_arrival(taken, recv_sem, at, side))
        pl.when(z == at)(lambda: own.wait())


def in_given_order(back_ref, inverse_ref, grad_ref, given_ref, scaled_ref):
    length, width = grad_ref.shape

    def block(i, unused):
        span = pl.ds(pl.multiple_of(i * SPAN, SPAN), SPAN)
        moved = dot_nn(back_ref[span, :], grad_ref[...])
        if given_ref is not None:
            given_ref[span, :] = moved.astype(BF)
        for c in range(width // 128):
            lanes = slice(128 * c, 128 * c + 128)
            scaled_ref[span, lanes] = (moved[:, lanes] * inverse_ref[span, :]).astype(BF)
        return unused

    lax.fori_loop(0, length // SPAN, block, 0)


class RowSum:
    def __init__(self, partial, pair_in, row_in, send_sem, recv_sem):
        self.partial, self.pair_in, self.row_in = partial, pair_in, row_in
        self.rows = row_in.shape[0]
        mine, rep = lax.axis_index("shard"), lax.axis_index("rep")
        self.y, self.core = mine // 2, lax.rem(mine, 2)
        sibling, peer = self.y * 2 + (1 - self.core), (1 - self.y) * 2 + self.core
        self.pairs = [
            remote(
                partial.at[self.span(2 * side + (1 - self.core))],
                pair_in.at[side],
                send_sem.at[side],
                recv_sem.at[side],
                (rep, sibling),
            )
            for side in range(2)
        ]
        self.across = remote(
            pair_in.at[1 - self.y], row_in, send_sem.at[2], recv_sem.at[2], (rep, peer)
        )

    def span(self, shard):
        return pl.ds(pl.multiple_of(shard * self.rows, self.rows), self.rows)

    def fill(self, rows_of):
        def block(i, unused):
            span = self.span(i)
            self.partial[span, :] = rows_of(span)
            return unused

        lax.fori_loop(0, self.partial.shape[0] // self.rows, block, 0)
        for copy in self.pairs:
            copy.start()

    def join(self):
        for copy in self.pairs:
            copy.wait_recv()
        for side in range(2):
            self.pair_in[side] = (
                self.pair_in[side] + self.partial[self.span(2 * side + self.core), :]
            )
        self.across.start()

    def result(self):
        self.across.wait_recv()
        return self.pair_in[self.y] + self.row_in[...]

    def finish(self):
        for copy in self.pairs + [self.across]:
            copy.wait_send()


def backward_kernel(spans, *refs):
    refs = list(refs)
    if spans:
        grad_gate_ref, back_ref, inverse_ref, normed_out_ref, w_out_ref = refs[8:13]
        taken_ref, taken_out_ref, gate_peer_ref, gate_given_ref, branch_ref = refs[18:23]
        extra = refs[31:]
        refs = refs[:8] + refs[13:18] + refs[23:31]
        scaled_ref, partial, pair_in, row_in = extra[:4]
        share_send, share_recv, own_sem, pair_send, pair_recv, peer_send, peer_recv = extra[4:]
    (
        conv_in_ref,
        place_ref,
        conv_w_ref,
        conv_b_ref,
        heads_ref,
        mixed_ref,
        starts_ref,
        grad_ref,
        grad_values_ref,
        grad_tail_ref,
        grad_conv_w_ref,
        grad_conv_b_ref,
        grad_head_ref,
        act_ref,
        pre_ref,
        step_ref,
        run_ref,
        state_ref,
        grad_act_ref,
        joined_ref,
        join_ref,
    ) = refs
    length, width = mixed_ref.shape
    mine = lax.axis_index("shard")
    heads = width // P_SIZE
    blocks = length // SPAN
    if spans:
        rep = lax.axis_index("rep")
        y, core = mine // 2, lax.rem(mine, 2)
        sibling, peer = y * 2 + (1 - core), (1 - y) * 2 + core
        meet(
            [(rep_at(step), mine) for step in rep_steps()] + [(rep, sibling), (rep, peer)]
        )
        in_given_order(back_ref, inverse_ref, grad_gate_ref, gate_given_ref, scaled_ref)
        exchanges = ((scaled_ref, taken_ref), (normed_out_ref, taken_out_ref))
        own_shares = [share_own(*pair, own_sem.at[i]) for i, pair in enumerate(exchanges)]

        def exchange_start(i):
            own_shares[i].start()
            for step in rep_steps():
                share_copy(*exchanges[i], share_send.at[i], share_recv.at[i], step).start()

        def gate_peer_copy(at, side):
            return remote(
                taken_ref.at[at, side],
                gate_peer_ref.at[at, side],
                peer_send.at[at, side],
                peer_recv.at[at, side],
                (rep, peer),
            )

        exchange_start(0)
        rows_sum = RowSum(partial, pair_in, row_in, pair_send, pair_recv)
        rows_sum.fill(lambda span: dot_nn(normed_out_ref[span, :], w_out_ref[...]))
        exchange_start(1)
    for c in range((width + 2 * N) // 128):
        lanes = slice(128 * c, 128 * c + 128)
        there = conv_lanes(c, width, mine)
        pre = conv_pre(
            conv_in_ref[:, lanes].astype(F32),
            conv_w_ref[:, there],
            conv_b_ref[:, there],
            place_ref[...],
        )
        pre_ref[:, lanes] = pre
        act_ref[:, lanes] = (pre * sigmoid(pre)).astype(BF)
    step_and_run(conv_in_ref, heads_ref, run_ref, step_ref, width, mine)
    if spans:
        rows_sum.join()
    state_ref[...] = jnp.zeros_like(state_ref)
    grad_head_ref[...] = jnp.zeros_like(grad_head_ref)
    skips = own_lanes(heads_ref[...], mine, heads)[2:3, :]
    upper = (
        lax.broadcasted_iota(jnp.int32, (SPAN, SPAN), 0)
        <= lax.broadcasted_iota(jnp.int32, (SPAN, SPAN), 1)
    ).astype(F32)
    last_row = lax.broadcasted_iota(jnp.int32, (SPAN, 128), 0) == SPAN - 1
    join_ref[...] = (
        lax.broadcasted_iota(jnp.int32, (width, 128), 0) // P_SIZE + mine * heads
        == lax.broadcasted_iota(jnp.int32, (width, 128), 1)
    ).astype(F32).astype(BF)

    def block(count, unused):
        b = blocks - 1 - count
        row = pl.multiple_of(b * SPAN, SPAN)
        rows = pl.ds(row, SPAN)
        start_rows = pl.ds(pl.multiple_of(b * N, N), N)
        run = run_ref[rows, :]
        run_t = run.T
        step = step_ref[rows, :]
        masks = block_terms(place_ref[rows, :])
        in_map = act_ref[rows, width : width + N]
        out_map = act_ref[rows, width + N : width + 2 * N]
        out_map_t = out_map.T
        products = dot_nt(out_map, in_map)
        grad_products = jnp.zeros((SPAN, SPAN), F32)
        grad_out_map = jnp.zeros((SPAN, N), F32)
        grad_in_map = jnp.zeros((SPAN, N), F32)
        for pair in range(width // 128):
            lanes = slice(128 * pair, 128 * pair + 128)
            left, decays, entering, tail, carried, size = pair_terms(
                pair, run, run_t, step, *masks
            )
            values = act_ref[rows, lanes].astype(F32)
            grad = grad_ref[rows, lanes]
            start = starts_ref[start_rows, lanes]
            later = state_ref[:, lanes]
            scaled = values * size
            scaled_low = scaled.astype(BF)
            grad_low = grad.astype(BF)
            weights = jnp.concatenate([(d * products).astype(BF) for d in decays], axis=0)
            grad_scaled = dot_tn(weights, stacked(grad_low, left))
            grad_pairs = dot_nt(grad_low, stacked(scaled_low, left))
            grad_products += (
                grad_pairs[:, :SPAN] * decays[0] + grad_pairs[:, SPAN:] * decays[1]
            )
            later_high, later_low = halves(later)
            from_later = tail * (dot_nn(in_map, later_high) + dot_nn(in_map, later_low))
            grad_scaled += from_later
            entering_high, entering_low = halves(entering * grad)
            grad_out_map += dot_nt(entering_high, start.astype(BF))
            grad_in_map += dot_nt((tail * scaled).astype(BF), later_high)
            ending = jnp.sum(scaled * from_later, axis=0, keepdims=True) + carried * jnp.sum(
                start * later, axis=0, keepdims=True
            )
            state_ref[:, lanes] = (
                carried * later + dot_nn(out_map_t, entering_high) + dot_nn(out_map_t, entering_low)
            )
            skip = skip_lanes(skips, pair)
            inner = mixed_ref[rows, lanes] - skip * values
            joined_ref[0:SPAN, lanes] = (
                grad_low.astype(F32) * inner
                - scaled_low.astype(F32) * (grad_scaled - from_later)
                - scaled * from_later
                + jnp.where(last_row, ending, 0.0)
            )
            joined_ref[SPAN : 2 * SPAN, lanes] = grad_scaled * values
            joined_ref[2 * SPAN : 2 * SPAN + 16, lanes] = spread_rows(
                jnp.sum(grad * values, axis=0, keepdims=True)
            )
            grad_act_ref[rows, lanes] = grad_scaled * size + skip * grad
        grad_products = grad_products.astype(BF)
        grad_act_ref[rows, width : width + N] = grad_in_map + dot_tn(grad_products, out_map)
        grad_act_ref[rows, width + N : width + 2 * N] = grad_out_map + dot_nn(
            grad_products, in_map
        )
        joined = joined_ref[...]
        first = joined.astype(BF)
        second, third = halves(joined - first.astype(F32))
        join = join_ref[...]
        by_head = dot_nn(first, join) + dot_nn(second, join) + dot_nn(third, join)
        grad_log = jnp.dot(
            upper, by_head[:SPAN], precision=lax.Precision.HIGHEST, preferred_element_type=F32
        )
        rate = jnp.exp(heads_ref[1:2, :])
        raw = conv_in_ref[rows, width + 2 * N : width + 2 * N + 128].astype(F32) + heads_ref[0:1, :]
        grad_dt = (by_head[SPAN : 2 * SPAN] - grad_log * rate) * sigmoid(raw)
        grad_tail_ref[rows, 2 * N : 2 * N + 128] = grad_dt
        grad_head_ref[0:1, :] += jnp.sum(grad_dt, axis=0, keepdims=True)
        grad_head_ref[1:2, :] += jnp.sum(
            -grad_log * jax.nn.softplus(raw) * rate, axis=0, keepdims=True
        )
        grad_head_ref[2:3, :] += by_head[2 * SPAN : 2 * SPAN + 1]
        return unused

    lax.fori_loop(0, blocks, block, 0)
    if spans:
        for at in range(LINE):
            for side in range(PLANE):
                share_wait(scaled_ref, taken_ref, share_recv.at[0], own_shares[0], at, side)
                gate_peer_copy(at, side).start()

    place = place_ref[...]
    for c in range((width + 2 * N) // 128):
        lanes = slice(128 * c, 128 * c + 128)
        x = conv_in_ref[:, lanes].astype(F32)
        conv_w = conv_w_ref[:, conv_lanes(c, width, mine)]
        pre = pre_ref[:, lanes]
        gain = sigmoid(pre)
        grad_pre = grad_act_ref[:, lanes] * (gain * (1.0 + pre * (1.0 - gain)))
        grad_conv_b_ref[:, lanes] = jnp.sum(grad_pre, axis=0, keepdims=True)
        grad_conv_w_ref[KW - 1 : KW, lanes] = jnp.sum(grad_pre * x, axis=0, keepdims=True)
        grad_x = conv_w[KW - 1 : KW] * grad_pre
        for back in range(1, KW):
            tap = KW - 1 - back
            kept = jnp.where(place >= back, grad_pre, 0.0)
            grad_conv_w_ref[tap : tap + 1, lanes] = jnp.sum(
                kept * pltpu.roll(x, back, 0), axis=0, keepdims=True
            )
            grad_x += conv_w[tap : tap + 1] * pltpu.roll(kept, length - back, 0)
        if c < width // 128:
            grad_values_ref[:, lanes] = grad_x.astype(BF)
        else:
            grad_tail_ref[:, 128 * c - width : 128 * c - width + 128] = grad_x
    if spans:
        branch_ref[...] = rows_sum.result()
        for at in range(LINE):
            for side in range(PLANE):
                share_wait(
                    normed_out_ref, taken_out_ref, share_recv.at[1], own_shares[1], at, side
                )
        for i, pair in enumerate(exchanges):
            for step in rep_steps():
                share_copy(*pair, share_send.at[i], share_recv.at[i], step).wait_send()
        for at in range(LINE):
            for side in range(PLANE):
                gate_peer_copy(at, side).wait()
        rows_sum.finish()


def run_forward(
    conv_in, gate, branch_grad, w_out, place, conv_w, conv_b, heads, gain, shards, extra=()
):
    length, width = gate.shape
    blocks = length // SPAN
    shape = jax.ShapeDtypeStruct
    vector = pl.BlockSpec(memory_space=pltpu.VMEM)
    anywhere = pl.BlockSpec(memory_space=pl.ANY)
    dma = pltpu.SemaphoreType.DMA
    spans = len(extra) > 0
    side = (len(SIDE_BLOCKS), length, D // 2)
    return pl.pallas_call(
        functools.partial(forward_kernel, spans),
        out_shape=(
            shape((length, width), F32),
            shape((blocks * N, width), F32),
            shape((length, width), BF),
            shape((length, width), F32),
            shape((length, width), BF),
            shape((1, width), F32),
        )
        + ((shape(side, BF), shape((LINE, length, D // 2), BF)) if spans else ()),
        in_specs=[vector] * 9 + [anywhere] * (2 * spans),
        out_specs=(vector,) * 6 + (anywhere,) * (2 * spans),
        scratch_shapes=[
            pltpu.VMEM((length, width + 2 * N), BF),
            pltpu.VMEM((length, 128), F32),
            pltpu.VMEM((length, 128), F32),
            pltpu.VMEM((N, width), F32),
            pltpu.VMEM((length, width), F32),
            pltpu.VMEM((shards, 8, length), F32),
            dma((shards - 1,)),
            dma((shards - 1,)),
        ]
        + [
            dma((2, len(SIDE_BLOCKS))),
            dma((2, len(SIDE_BLOCKS))),
            dma((3, LINE)),
            dma((2, LINE)),
        ]
        * spans,
        compiler_params=pltpu.CompilerParams(
            vmem_limit_bytes=VMEM_BYTES, collective_id=2, has_side_effects=True
        ),
        cost_estimate=pl.CostEstimate(
            flops=20 * length * width * 128, bytes_accessed=12 * length * width, transcendentals=0
        ),
        name="mixer_forward",
    )(conv_in, gate, branch_grad, w_out, place, conv_w, conv_b, heads, gain, *extra)


def run_backward(conv_in, place, conv_w, conv_b, heads, mixed, starts, grad, extra=()):
    length, width = mixed.shape
    shape = jax.ShapeDtypeStruct
    vector = pl.BlockSpec(memory_space=pltpu.VMEM)
    anywhere = pl.BlockSpec(memory_space=pl.ANY)
    dma = pltpu.SemaphoreType.DMA
    spans = len(extra) > 0
    return pl.pallas_call(
        functools.partial(backward_kernel, spans),
        out_shape=(
            shape((length, width), BF),
            shape((length, TAIL_PAD), F32),
            shape((KW, width + 2 * N), F32),
            shape((1, width + 2 * N), F32),
            shape((8, 128), F32),
        )
        + (
            (
                shape((LINE, PLANE, length, 128), BF),
                shape((LINE, PLANE, length, 128), BF),
                shape((LINE, PLANE, length, 128), BF),
                shape((length, width), BF),
                shape((length // 4, D), F32),
            )
            if spans
            else ()
        ),
        in_specs=[vector] * (8 + 5 * spans),
        out_specs=(vector,) * 5 + ((anywhere,) * 3 + (vector,) * 2) * spans,
        scratch_shapes=[
            pltpu.VMEM((length, width + 2 * N), BF),
            pltpu.VMEM((length, width + 2 * N), F32),
            pltpu.VMEM((length, 128), F32),
            pltpu.VMEM((length, 128), F32),
            pltpu.VMEM((N, width), F32),
            pltpu.VMEM((length, width + 2 * N), F32),
            pltpu.VMEM((2 * SPAN + 16, width), F32),
            pltpu.VMEM((width, 128), BF),
        ]
        + [
            pltpu.VMEM((length, width), BF),
            pltpu.VMEM((length, D), F32),
            pltpu.VMEM((2, length // 4, D), F32),
            pltpu.VMEM((length // 4, D), F32),
            dma((2, LINE, PLANE)),
            dma((2, LINE, PLANE)),
            dma((2,)),
            dma((3,)),
            dma((3,)),
            dma((LINE, PLANE)),
            dma((LINE, PLANE)),
        ]
        * spans,
        compiler_params=pltpu.CompilerParams(
            vmem_limit_bytes=VMEM_BYTES, collective_id=4, has_side_effects=True
        )
        if spans
        else params(),
        cost_estimate=pl.CostEstimate(
            flops=40 * length * width * 128, bytes_accessed=20 * length * width, transcendentals=0
        ),
        name="mixer_backward",
    )(conv_in, place, conv_w, conv_b, heads, mixed, starts, grad, *extra)


def end_kernel(
    gate_taken_hbm,
    gate_peer_hbm,
    out_taken_hbm,
    gate_given_ref,
    values_ref,
    tail_ref,
    normed_ref,
    line_ref,
    beside_ref,
    side_a_ref,
    side_b_ref,
    inverse_ref,
    w_gate_hbm,
    w_conv_hbm,
    branch_ref,
    back_ref,
    branch_grad_hbm,
    x_ref,
    resid_ref,
    valid_ref,
    gain_ref,
    grad_conv_w_ref,
    grad_conv_b_ref,
    grad_head_ref,
    grad_gain_ref,
    parts_ref,
    w_out_grad_ref,
    tails_ref,
    block_out_ref,
    grad_in_ref,
    out_norm_ref,
    out_conv_w_ref,
    out_conv_b_ref,
    out_head_ref,
    out_gain_ref,
    taken,
    taken_peer,
    values_given_ref,
    scaled_ref,
    group_rows,
    own_columns,
    total,
    low,
    partial,
    pair_in,
    row_in,
    tail_in,
    tail_low,
    tail_sum,
    tail_parts,
    small,
    small_in,
    small_all,
    w_gate_ref,
    w_conv_ref,
    branch_grad_ref,
    load_sem,
    local_sem,
    group_sem,
    share_send,
    share_recv,
    peer_send,
    peer_recv,
    swap_send,
    swap_recv,
    line_send,
    line_recv,
    side_send,
    side_recv,
    pair_send,
    pair_recv,
    tail_send,
    tail_recv,
    rep_send,
    rep_recv,
    all_send,
    all_recv,
):
    reps, shards = LINE * PLANE, lax.axis_size("shard")
    mine, rep = lax.axis_index("shard"), lax.axis_index("rep")
    y, c = mine // 2, lax.rem(mine, 2)
    z, x = rep // PLANE, lax.rem(rep, PLANE)
    beside = z * PLANE + (1 - x)
    rows, length = x_ref.shape[0], values_ref.shape[0]
    width, depth = values_ref.shape[1], own_columns.shape[1]
    half = D // 2
    sibling, peer = y * 2 + (1 - c), (1 - y) * 2 + c

    def other(step):
        return lax.rem(z + step // PLANE, LINE) * PLANE + lax.rem(x + step % PLANE, PLANE)

    def before(step):
        return lax.rem(z + LINE - step // PLANE, LINE) * PLANE + lax.rem(
            x + PLANE - step % PLANE, PLANE
        )

    def shard_at(step):
        return lax.rem(mine + step, shards)

    def each(count, body):
        def step(i, unused):
            body(i)
            return unused

        lax.fori_loop(0, count, step, 0)

    meet(
        [(other(step), mine) for step in range(1, reps)]
        + [(rep, shard_at(step)) for step in range(1, shards)]
    )

    loads = [
        pltpu.make_async_copy(far_ref, near_ref, load_sem.at[i])
        for i, (far_ref, near_ref) in enumerate(
            [
                (w_gate_hbm, w_gate_ref),
                (w_conv_hbm, w_conv_ref),
                (branch_grad_hbm, branch_grad_ref),
            ]
        )
    ]

    def place_of(i):
        return lax.rem(z + i // PLANE, LINE), i % PLANE

    def group_copy(part, i, slot):
        at, side = place_of(i)
        kind = part // 2
        if side == 0:
            source = line_ref.at[kind, at]
        elif i // PLANE == 0:
            source = beside_ref.at[kind]
        elif kind == 0:
            source = side_a_ref.at[i // PLANE - 1]
        else:
            source = side_b_ref.at[at]
        return pltpu.make_async_copy(source, group_rows.at[slot], group_sem.at[slot])

    def peer_copy(part, at, side):
        return remote(
            taken.at[part, at, side],
            taken_peer.at[part, at, side],
            peer_send.at[part, at, side],
            peer_recv.at[part, at, side],
            (rep, peer),
        )

    own_part = pltpu.make_async_copy(
        normed_ref.at[:, pl.ds(pl.multiple_of(mine * depth, depth), depth)],
        own_columns,
        local_sem.at[4],
    )
    own_part.start()
    gate_load = pltpu.make_async_copy(gate_taken_hbm, taken.at[0], local_sem.at[0])
    gate_load.start()
    peer_load = pltpu.make_async_copy(gate_peer_hbm, taken_peer.at[0], local_sem.at[7])
    peer_load.start()
    out_load = pltpu.make_async_copy(out_taken_hbm, taken.at[2], local_sem.at[5])
    out_load.start()
    group_copy(0, 0, 0).start()
    out_load.wait()
    for i in range(reps):
        peer_copy(2, *place_of(i)).start()

    def row_block(ref, shard):
        return ref.at[pl.ds(pl.multiple_of(shard * rows, rows), rows)]

    def tail_out_copy(step):
        to = shard_at(step)
        return remote(
            row_block(tail_ref, to),
            tail_in.at[step],
            tail_send.at[0, step],
            tail_recv.at[0, step],
            (rep, to),
        )

    def tail_back_copy(step):
        return remote(
            row_block(tail_low, mine),
            row_block(tail_low, mine),
            tail_send.at[1, step],
            tail_recv.at[1, step],
            (rep, shard_at(step)),
        )

    for step in range(1, shards):
        tail_out_copy(step).start()
    for load in loads:
        load.start()

    rows_sum = RowSum(partial, pair_in, row_in, pair_send, pair_recv)

    def swap_copy(part):
        if part == 2:
            return remote(
                low.at[2, pl.ds(pl.multiple_of((1 - y) * 128, 128), 128), :],
                w_out_grad_ref.at[rep, :, pl.ds(pl.multiple_of(y * half, 128), half)],
                swap_send.at[2],
                swap_recv.at[2],
                (rep, peer),
            )
        return remote(
            low.at[part, :, pl.ds(pl.multiple_of((1 - c) * depth, depth), depth)],
            parts_ref.at[rep, part, c],
            swap_send.at[part],
            swap_recv.at[part],
            (rep, sibling),
        )

    def swap_own(part):
        if part == 2:
            return pltpu.make_async_copy(
                low.at[2, pl.ds(pl.multiple_of(y * 128, 128), 128), :],
                w_out_grad_ref.at[rep, :, pl.ds(pl.multiple_of(y * half, 128), half)],
                local_sem.at[6],
            )
        return pltpu.make_async_copy(
            low.at[part, :, pl.ds(pl.multiple_of(c * depth, depth), depth)],
            parts_ref.at[rep, part, c],
            local_sem.at[2 + part],
        )

    def sum_groups(part, then=None):
        gains = gain_ref[:, pl.ds(pl.multiple_of(y * half, 128), half)] if part < 2 else 1.0
        for i in range(reps):
            slot = i % 2
            at, side = place_of(i)
            if i < reps - 1:
                group_copy(part, i + 1, 1 - slot).start()
            elif then is not None:
                group_copy(then, 0, 1 - slot).start()
            if part > 0:
                peer_copy(part, at, side).wait_recv()
            elif i == 0:
                gate_load.wait()
                peer_load.wait()
            group_copy(part, i, slot).wait()
            both = jnp.concatenate([taken[part, at, side], taken_peer[part, at, side]], axis=1)
            term = dot_tn(both, group_rows[slot])
            if i == 0:
                total[...] = term
            elif i < reps - 1:
                total[...] += term
            else:
                term = ((total[...] + term) * gains).astype(BF)
                for place, half_rows in ((y, term[:128]), (1 - y, term[128:])):
                    low[part, pl.ds(pl.multiple_of(place * 128, 128), 128), :] = half_rows
        swap_own(part).start()
        swap_copy(part).start()

    def sum_block(part, owner):
        return w_out_grad_ref.at[owner] if part == 2 else parts_ref.at[owner, part]

    def line_copy(part, origin, toward, lane):
        block = sum_block(part, origin * PLANE + x)
        return remote(
            block,
            block,
            line_send.at[part, lane, origin],
            line_recv.at[part, origin],
            ((z + toward) * PLANE + x, mine),
        )

    def side_copy(part, origin, from_x):
        block = sum_block(part, origin * PLANE + from_x)
        return remote(
            block, block, side_send.at[part, origin], side_recv.at[part, origin], (beside, mine)
        )

    def spread_own(part):
        swap_own(part).wait()
        swap_copy(part).wait_recv()
        side_copy(part, z, x).start()

        @pl.when(z < LINE - 1)
        def _():
            line_copy(part, z, 1, 0).start()

        @pl.when(z > 0)
        def _():
            line_copy(part, z, -1, 1).start()

    def pass_on(part, step):
        @pl.when(z - step >= 0)
        def _():
            origin = z - step
            line_copy(part, origin, 1, 0).wait_recv()

            @pl.when(z < LINE - 1)
            def _():
                line_copy(part, origin, 1, 0).start()

            side_copy(part, origin, x).start()

        @pl.when(z + step < LINE)
        def _():
            origin = z + step
            line_copy(part, origin, -1, 1).wait_recv()

            @pl.when(z > 0)
            def _():
                line_copy(part, origin, -1, 1).start()

            side_copy(part, origin, x).start()

    sum_groups(0, 2)
    in_given_order(back_ref, inverse_ref, values_ref, values_given_ref, scaled_ref)
    own_share = share_own(scaled_ref, taken.at[1], local_sem.at[1])
    own_share.start()
    for step in rep_steps():
        share_copy(scaled_ref, taken.at[1], share_send, share_recv, step).start()
    spread_own(0)
    for step in range(1, shards):
        tail_out_copy(step).wait_recv()
    span = pl.ds(pl.multiple_of(mine * rows, rows), rows)
    summed_tail = tail_ref[span, :]
    for step in range(1, shards):
        summed_tail = summed_tail + tail_in[step]
    tail_low[span, :] = summed_tail.astype(BF)
    for step in range(1, shards):
        tail_back_copy(step).start()
    sum_groups(2, 1)
    pass_on(0, 1)
    spread_own(2)
    for i in range(reps):
        at, side = place_of(i)
        if i == 0:
            own_share.wait()
        else:
            share_arrival(taken.at[1], share_recv, at, side)
        peer_copy(1, at, side).start()
    pass_on(0, 2)

    for step in range(1, shards):
        tail_back_copy(step).wait_recv()
    heads, share = H // shards, 2 * N // shards
    lane = lax.broadcasted_iota(jnp.int32, (rows, TAIL_PAD), 1)
    owned = ((lane >= mine * share) & (lane < (mine + 1) * share)) | (
        (lane >= 2 * N + mine * heads) & (lane < 2 * N + (mine + 1) * heads)
    )

    def grad_rows(span):
        tail = dot_nn(back_ref[span, :], tail_low[...])
        tail = jnp.where(owned, tail, 0.0).astype(BF)
        return (
            dot_nn(gate_given_ref[span, :], w_gate_ref[...])
            + dot_nn(values_given_ref[span, :], w_conv_ref[0:width, :])
            + dot_nn(tail, w_conv_ref[width:, :])
        )

    loads[0].wait()
    loads[1].wait()
    rows_sum.fill(grad_rows)
    pass_on(0, 3)
    pass_on(2, 1)
    rows_sum.join()
    sum_groups(1)
    pass_on(2, 2)
    spread_own(1)

    own_part.wait()
    tail_sum[...] = dot_tn(tail_low[...], own_columns[...])
    share_rows = TAIL_PAD // reps

    def tail_rows(ref, owner):
        return ref.at[pl.ds(pl.multiple_of(owner * share_rows, 16), share_rows)]

    def tail_part_copy(step):
        to = other(step)
        return remote(
            tail_rows(tail_sum, to),
            tail_parts.at[step],
            rep_send.at[0, step],
            rep_recv.at[0, step],
            (to, mine),
        )

    def tail_spread_copy(step):
        return remote(
            tail_rows(tails_ref, rep),
            tail_rows(tails_ref, rep),
            rep_send.at[1, step],
            rep_recv.at[1, step],
            (other(step), mine),
        )

    for step in range(1, reps):
        tail_part_copy(step).start()

    branch = branch_ref[...]
    whole = resid_ref[...].astype(F32) + branch
    block_out_ref[...] = whole.astype(BF)
    counts = valid_ref[...].astype(F32)
    square_total = jnp.sum(
        counts * jnp.sum(whole * whole, axis=1, keepdims=True), axis=0, keepdims=True
    )
    square_branch = jnp.sum(
        counts * jnp.sum(branch * branch, axis=1, keepdims=True), axis=0, keepdims=True
    )
    count = jnp.sum(counts, axis=0, keepdims=True)

    pass_on(2, 3)
    pass_on(1, 1)

    for step in range(1, reps):
        tail_part_copy(step).wait_recv()
    span = pl.ds(pl.multiple_of(rep * share_rows, 16), share_rows)
    piece = tail_sum[span, :]
    for step in range(1, reps):
        piece = piece + tail_parts[step]
    tails_ref[span, :] = piece.astype(BF)
    for step in range(1, reps):
        tail_spread_copy(step).start()

    pass_on(1, 2)

    grad_normed = rows_sum.result()
    given = x_ref[...].astype(F32)
    inverse = lax.rsqrt(jnp.mean(given * given, axis=1, keepdims=True) + EPSILON)
    grad_norm_gain = jnp.sum(grad_normed * (given * inverse), axis=0, keepdims=True)
    scaled = grad_normed * gain_ref[...]
    pull = inverse * inverse * inverse * jnp.mean(scaled * given, axis=1, keepdims=True)
    span = pl.ds(pl.multiple_of(mine * rows, rows), rows)
    loads[2].wait()
    kept = dot_nn(back_ref[span, :], branch_grad_ref[...])
    grad_in_ref[...] = (scaled * inverse - given * pull + kept).astype(BF)

    lane = lax.broadcasted_iota(jnp.int32, (1, 128), 1)
    at = 0
    for i in range(D // 128):
        small[at : at + 1, :] = grad_norm_gain[:, 128 * i : 128 * i + 128]
        at += 1
    channels = (width + 2 * N) // 128
    for tap in range(KW):
        for i in range(channels):
            small[at : at + 1, :] = grad_conv_w_ref[tap : tap + 1, 128 * i : 128 * i + 128]
            at += 1
    for i in range(channels):
        small[at : at + 1, :] = grad_conv_b_ref[:, 128 * i : 128 * i + 128]
        at += 1
    for i in range(width // 128):
        small[at : at + 1, :] = grad_gain_ref[:, 128 * i : 128 * i + 128]
        at += 1
    small[at : at + 3, :] = grad_head_ref[0:3, :]
    small[at + 3 : at + 4, :] = jnp.where(
        lane == 0,
        spread(square_total),
        jnp.where(lane == 1, spread(square_branch), jnp.where(lane == 2, spread(count), 0.0)),
    )
    small[at + 4 :, :] = jnp.zeros((small.shape[0] - at - 4, 128), F32)

    def small_rep_copy(step):
        return remote(
            small, small_in.at[rep], rep_send.at[2, step], rep_recv.at[2, step], (other(step), mine)
        )

    def small_rep_arrival(step):
        return remote(
            small,
            small_in.at[before(step)],
            rep_send.at[2, step],
            rep_recv.at[2, step],
            (other(step), mine),
        )

    def small_shard_copy(step):
        return remote(
            small_all.at[mine],
            small_all.at[mine],
            all_send.at[step],
            all_recv.at[step],
            (rep, shard_at(step)),
        )

    for step in range(1, reps):
        small_rep_copy(step).start()
    small_in[rep] = small[...]

    for step in range(1, reps):
        small_rep_arrival(step).wait_recv()
    added = small_in[0]
    for i in range(1, reps):
        added = added + small_in[i]
    small_all[mine] = added
    for step in range(1, shards):
        small_shard_copy(step).start()
    pass_on(1, 3)
    for step in range(1, shards):
        small_shard_copy(step).wait_recv()

    def over_shards(row):
        value = small_all[0, row : row + 1, :]
        for i in range(1, shards):
            value = value + small_all[i, row : row + 1, :]
        return value

    at = 0
    for i in range(D // 128):
        out_norm_ref[:, 128 * i : 128 * i + 128] = over_shards(at)
        at += 1
    for tap in range(KW + 1):
        ref, row = (out_conv_w_ref, tap) if tap < KW else (out_conv_b_ref, 0)
        for i in range(channels):
            if i < width // 128:
                for shard in range(shards):
                    to = shard * width + 128 * i
                    ref[row : row + 1, to : to + 128] = small_all[shard, at : at + 1, :]
            else:
                to = DI + 128 * i - width
                ref[row : row + 1, to : to + 128] = over_shards(at)
            at += 1
    for i in range(width // 128):
        for shard in range(shards):
            to = shard * width + 128 * i
            out_gain_ref[:, to : to + 128] = small_all[shard, at : at + 1, :]
        at += 1
    for i in range(3):
        out_head_ref[i : i + 1, :] = over_shards(at + i)
    stats = over_shards(at + 3)
    per = jnp.maximum(stats[:, 2:3], 1.0) * D
    out_head_ref[3:4, :] = jnp.sqrt(stats / spread(per))
    out_head_ref[4:8, :] = jnp.zeros((4, 128), F32)

    for step in range(1, reps):
        tail_spread_copy(step).wait_recv()
    for part in range(3):
        for origin in range(LINE):
            side_copy(part, origin, 1 - x).wait_recv()
            side_copy(part, origin, x).wait_send()

            @pl.when((origin <= z) & (z < LINE - 1))
            def _(part=part, origin=origin):
                line_copy(part, origin, 1, 0).wait_send()

            @pl.when((origin >= z) & (z > 0))
            def _(part=part, origin=origin):
                line_copy(part, origin, -1, 1).wait_send()

        swap_copy(part).wait_send()
        if part > 0:
            for i in range(reps):
                peer_copy(part, *place_of(i)).wait_send()
    for step in rep_steps():
        share_copy(scaled_ref, taken.at[1], share_send, share_recv, step).wait_send()
    rows_sum.finish()
    for step in range(1, shards):
        tail_out_copy(step).wait_send()
        tail_back_copy(step).wait_send()
        small_shard_copy(step).wait_send()
    for step in range(1, reps):
        tail_part_copy(step).wait_send()
        tail_spread_copy(step).wait_send()
        small_rep_copy(step).wait_send()


def run_end(operands, shards):
    reps = LINE * PLANE
    length, width = operands[4].shape
    rows, depth = length // shards, D // shards
    dma = pltpu.SemaphoreType.DMA
    vector = pl.BlockSpec(memory_space=pltpu.VMEM)
    anywhere = pl.BlockSpec(memory_space=pl.ANY)
    shape = jax.ShapeDtypeStruct
    channels = width + 2 * N
    small = -(-(D + 5 * channels + width + 4 * 128) // 1024) * 8
    return pl.pallas_call(
        end_kernel,
        out_shape=(
            shape((reps, 2, 2, 256, depth), BF),
            shape((reps, 128, D), BF),
            shape((TAIL_PAD, depth), BF),
            shape((rows, D), BF),
            shape((rows, D), BF),
            shape((1, D), F32),
            shape((KW, CONVW), F32),
            shape((1, CONVW), F32),
            shape((8, 128), F32),
            shape((1, DI), F32),
        ),
        in_specs=[anywhere] * 3 + [vector] * 3 + [anywhere] * 5 + [vector] + [anywhere] * 2 + [vector] * 2 + [anywhere] + [vector] * 8,
        out_specs=(anywhere,) * 2 + (vector,) * 8,
        scratch_shapes=[
            pltpu.VMEM((3, LINE, PLANE, length, 128), BF),
            pltpu.VMEM((3, LINE, PLANE, length, 128), BF),
            pltpu.VMEM((length, width), BF),
            pltpu.VMEM((length, width), BF),
            pltpu.VMEM((2, length, D // 2), BF),
            pltpu.VMEM((length, depth), BF),
            pltpu.VMEM((256, D // 2), F32),
            pltpu.VMEM((3, 256, D // 2), BF),
            pltpu.VMEM((length, D), F32),
            pltpu.VMEM((2, rows, D), F32),
            pltpu.VMEM((rows, D), F32),
            pltpu.VMEM((shards, rows, TAIL_PAD), F32),
            pltpu.VMEM((length, TAIL_PAD), BF),
            pltpu.VMEM((TAIL_PAD, depth), F32),
            pltpu.VMEM((reps, TAIL_PAD // reps, depth), F32),
            pltpu.VMEM((small, 128), F32),
            pltpu.VMEM((reps, small, 128), F32),
            pltpu.VMEM((shards, small, 128), F32),
            pltpu.VMEM((width, D), BF),
            pltpu.VMEM((width + TAIL_PAD, D), BF),
            pltpu.VMEM((length, D), BF),
            dma((3,)),
            dma((8,)),
            dma((2,)),
            dma((LINE, PLANE)),
            dma((LINE, PLANE)),
            dma((3, LINE, PLANE)),
            dma((3, LINE, PLANE)),
            dma((3,)),
            dma((3,)),
            dma((3, 2, LINE)),
            dma((3, LINE)),
            dma((3, LINE)),
            dma((3, LINE)),
            dma((3,)),
            dma((3,)),
            dma((2, shards)),
            dma((2, shards)),
            dma((3, reps)),
            dma((3, reps)),
            dma((shards,)),
            dma((shards,)),
        ],
        compiler_params=pltpu.CompilerParams(
            vmem_limit_bytes=VMEM_BYTES, collective_id=3, has_side_effects=True
        ),
        cost_estimate=pl.CostEstimate(
            flops=2 * reps * length * D * 256, bytes_accessed=96 << 20, transcendentals=0
        ),
        name="weight_gradient",
    )(*operands)


def assemble_kernel(parts_ref, tail_ref, out_ref):
    step, steps = pl.program_id(0), pl.num_programs(0)
    reps = parts_ref.shape[0]

    @pl.when(step < steps - 1)
    def _():
        for rep in range(reps):
            out_ref[128 * rep : 128 * rep + 128, :] = parts_ref[rep, 0, 0].astype(F32)

    @pl.when(step == steps - 1)
    def _():
        out_ref[0:TAIL, :] = tail_ref[0:TAIL, :].astype(F32)


def run_assemble(parts, tail):
    reps, unused, cores, stack, depth = parts.shape
    shards = cores * stack // 128
    steps = 2 * shards

    def place(i):
        at = jnp.minimum(i, steps - 1)
        shard = lax.rem(at, shards)
        return (0, at // shards, lax.rem(shard, cores), shard // cores, 0)

    return pl.pallas_call(
        assemble_kernel,
        grid=(steps + 1,),
        out_shape=jax.ShapeDtypeStruct((PROJ, depth), F32),
        in_specs=[
            pl.BlockSpec((reps, 1, 1, 128, depth), place),
            pl.BlockSpec((TAIL_PAD, depth), lambda i: (0, 0)),
        ],
        out_specs=pl.BlockSpec((reps * 128, depth), lambda i: (i, 0)),
        compiler_params=params(),
        name="assemble",
    )(parts, tail)


def exchange(pieces, axis, mine):
    count = lax.axis_size(axis)
    own = pieces(mine)
    gathered = jnp.zeros((count,) + own.shape, own.dtype)
    gathered = lax.dynamic_update_index_in_dim(gathered, own, mine, 0)
    for other in range(1, count):
        arrived = lax.ppermute(
            pieces(mine ^ other), axis, [(i, i ^ other) for i in range(count)]
        )
        gathered = lax.dynamic_update_index_in_dim(gathered, arrived, mine ^ other, 0)
    return gathered


def columns_at(array, start, width):
    return lax.dynamic_slice_in_dim(array, start, width, axis=1)


def plain_device(
    x_in,
    cotangent,
    seq_lengths,
    seq_order,
    valid,
    norm_gain,
    w_in,
    conv_w,
    conv_b,
    head_rows,
    gain_row,
    w_out,
):
    shards, mine = lax.axis_size("shard"), lax.axis_index("shard")
    rows = x_in.shape[0]
    length = rows * shards
    depth = w_in.shape[0]
    heads = H // shards
    width = DI // shards
    share = 2 * N // shards
    w_tail = w_in[:, 2 * DI :]

    def conv_piece(d):
        return jnp.concatenate([columns_at(w_in, DI + d * width, width), w_tail], axis=1)

    x_group = lax.all_gather(x_in, "shard", axis=0, tiled=True)
    w_conv = exchange(conv_piece, "shard", mine).reshape(D, width + TAIL)
    w_gate = exchange(lambda d: columns_at(w_in, d * width, width), "shard", mine).reshape(D, width)
    branch_grad = lax.all_gather(
        jnp.where(valid[:, None] > 0, cotangent, jnp.zeros_like(cotangent)),
        "shard",
        axis=0,
        tiled=True,
    )
    slot_ids = jnp.arange(length, dtype=jnp.int32)
    source, target, position = slot_tables(seq_lengths[0], seq_order[0], slot_ids)
    resid = dot_nn((source[:, None] == slot_ids[None, :]).astype(BF), x_group)
    inverse_rms = lax.rsqrt(jnp.mean(resid * resid, axis=1, keepdims=True) + EPSILON)
    normed = (resid * inverse_rms * norm_gain[None, :]).astype(BF)
    resid_mine = lax.dynamic_slice_in_dim(resid, mine * rows, rows, axis=0)
    gate = dot_nn(normed, w_gate).astype(BF)
    conv_in = jnp.pad(dot_nn(normed, w_conv).astype(BF), ((0, 0), (0, TAIL_PAD - TAIL)))
    place = jnp.broadcast_to(position[:, None], (length, 128))
    mixed, starts, normed_out, grad_mixed, grad_gate, grad_gain = run_forward(
        conv_in, gate, branch_grad, w_out, place, conv_w, conv_b, head_rows, gain_row, shards
    )
    branch = lax.psum_scatter(dot_nn(normed_out, w_out), "shard", scatter_dimension=0, tiled=True)
    total_rows = resid_mine + branch
    weights_valid = valid.astype(F32)
    square_total = jnp.sum(weights_valid * jnp.sum(total_rows * total_rows, axis=1))
    square_branch = jnp.sum(weights_valid * jnp.sum(branch * branch, axis=1))
    grad_w_out = lax.psum(dot_tn(normed_out, branch_grad), "rep")
    grad_values, grad_tail, grad_conv_w, grad_conv_b, grad_head = run_backward(
        conv_in, place, conv_w, conv_b, head_rows, mixed, starts, grad_mixed
    )
    grad_tail = lax.psum(grad_tail, "shard").astype(BF)
    lane = jnp.arange(TAIL, dtype=jnp.int32)
    owned = ((lane >= mine * share) & (lane < (mine + 1) * share)) | (
        (lane >= 2 * N + mine * heads) & (lane < 2 * N + (mine + 1) * heads)
    )
    kept_tail = jnp.where(owned[None, :], grad_tail[:, :TAIL], jnp.zeros((), BF))
    back = (target[:, None] == slot_ids[None, :]).astype(BF)

    def returned(grad):
        return dot_nn(back, grad).astype(BF)

    grad_normed = lax.psum_scatter(
        dot_nt(returned(grad_gate), w_gate)
        + dot_nt(returned(grad_values), w_conv[:, :width])
        + dot_nt(returned(kept_tail), w_conv[:, width:]),
        "shard",
        scatter_dimension=0,
        tiled=True,
    )
    given = x_in.astype(F32)
    given_rms = lax.rsqrt(jnp.mean(given * given, axis=1, keepdims=True) + EPSILON)
    grad_norm_gain = jnp.sum(grad_normed * (given * given_rms), axis=0)
    scaled = grad_normed * norm_gain[None, :]
    grad_resid = scaled * given_rms - given * (
        given_rms**3 * jnp.mean(scaled * given, axis=1, keepdims=True)
    )
    back_mine = lax.dynamic_slice_in_dim(back, mine * rows, rows, axis=0)
    grad_in = (grad_resid + dot_nn(back_mine, branch_grad)).astype(BF)

    def to_owners(columns):
        part = dot_tn(normed, columns).reshape(shards, depth, columns.shape[1])
        swapped = lax.all_to_all(part, "shard", split_axis=0, concat_axis=0, tiled=True)
        summed = lax.psum(swapped, "rep")
        return summed.transpose(1, 0, 2).reshape(depth, shards * columns.shape[1])

    grad_w_tail = lax.psum(
        dot_tn(columns_at(normed, mine * depth, depth), grad_tail[:, :TAIL]), "rep"
    )
    grad_w_in = jnp.concatenate([to_owners(grad_gate), to_owners(grad_values), grad_w_tail], axis=1)

    def placed(part):
        own = lax.dynamic_update_slice_in_dim(
            jnp.zeros((part.shape[0], DI), F32), part[:, :width], mine * width, axis=1
        )
        return jnp.concatenate([own, part[:, width:]], axis=1)

    summed = lax.psum(
        (
            grad_norm_gain,
            placed(grad_conv_w),
            placed(grad_conv_b)[0],
            grad_head,
            placed(grad_gain)[0],
            jnp.stack([square_total, square_branch, jnp.sum(weights_valid)]),
        ),
        ALL,
    )
    roots = jnp.sqrt(summed[5] / (jnp.maximum(summed[5][2], 1.0) * D))
    return (
        total_rows.astype(BF),
        grad_in,
        summed[0],
        grad_w_in,
        summed[1],
        summed[2],
        summed[3][0, :H],
        summed[3][1, :H],
        summed[3][2, :H],
        summed[4],
        grad_w_out,
        roots[0],
        roots[1],
    )


def on_device(
    x_in,
    cotangent,
    seq_lengths,
    seq_order,
    valid,
    norm_gain,
    w_in,
    conv_w,
    conv_b,
    dt_bias,
    a_log,
    d_skip,
    gated_gain,
    w_out,
):
    shards, mine = lax.axis_size("shard"), lax.axis_index("shard")
    reps = lax.axis_size("rep")
    rows = x_in.shape[0]
    length = rows * shards
    depth = w_in.shape[0]
    heads = H // shards
    width = DI // shards

    head_rows = jnp.pad(jnp.stack([dt_bias, a_log, d_skip]), ((0, 5), (0, 128 - H)))
    bias_row, gain_row = conv_b[None, :], gated_gain[None, :]
    spans = reps == LINE * PLANE and shards == 4 and width == reps * 128 and rows == 128
    if not spans:
        return plain_device(
            x_in,
            cotangent,
            seq_lengths,
            seq_order,
            valid,
            norm_gain,
            w_in,
            conv_w,
            bias_row,
            head_rows,
            gain_row,
            w_out,
        )
    norm_row, valid_column = norm_gain[None, :], valid[:, None]
    normed, conv_in, gate, w_gate, w_conv, branch_grad, back, place, resid, inverse, line, beside = (
        run_start(seq_lengths, seq_order, x_in, cotangent, valid_column, norm_row, w_in.T, shards)
    )
    mixed, starts, normed_out, grad_mixed, grad_gate, grad_gain, side_a, side_b = run_forward(
        conv_in, gate, branch_grad, w_out, place, conv_w, bias_row, head_rows, gain_row, shards, (line, beside)
    )
    (
        grad_values,
        grad_tail,
        grad_conv_w,
        grad_conv_b,
        grad_head,
        gate_taken,
        out_taken,
        gate_peer,
        gate_given,
        branch,
    ) = run_backward(
        conv_in,
        place,
        conv_w,
        bias_row,
        head_rows,
        mixed,
        starts,
        grad_mixed,
        (grad_gate, back, inverse, normed_out, w_out),
    )
    operands = (
        gate_taken,
        gate_peer,
        out_taken,
        gate_given,
        grad_values,
        grad_tail,
        normed,
        line,
        beside,
        side_a,
        side_b,
        inverse,
        w_gate,
        w_conv,
        branch,
        back,
        branch_grad,
        x_in,
        resid,
        valid_column,
        norm_row,
        grad_conv_w,
        grad_conv_b,
        grad_head,
        grad_gain,
    )
    (
        parts,
        w_out_parts,
        tails,
        block_out,
        grad_in,
        out_norm,
        out_conv_w,
        out_conv_b,
        out_head,
        out_gain,
    ) = run_end(operands, shards)
    grad_w_out = w_out_parts.reshape(width, D).astype(F32)
    grad_w_in = run_assemble(parts, tails).T
    return (
        block_out,
        grad_in,
        out_norm[0],
        grad_w_in,
        out_conv_w,
        out_conv_b[0],
        out_head[0, :H],
        out_head[1, :H],
        out_head[2, :H],
        out_gain[0],
        grad_w_out,
        out_head[3, 0],
        out_head[3, 1],
    )


def solution(mesh):
    in_specs = (
        P(ALL, None),
        P(ALL, None),
        P("rep", None),
        P("rep", None),
        P(ALL),
        P(),
        P("shard", None),
        P(),
        P(),
        P(),
        P(),
        P(),
        P(),
        P("shard", None),
    )
    out_specs = (
        P(ALL, None),
        P(ALL, None),
        P(),
        P("shard", None),
        P(),
        P(),
        P(),
        P(),
        P(),
        P(),
        P("shard", None),
        P(),
        P(),
    )
    return jax.shard_map(
        on_device, mesh=mesh, in_specs=in_specs, out_specs=out_specs, check_vma=False
    )
```

```python
import functools

import jax
import jax.numpy as jnp
from jax import lax
from jax.experimental import pallas as pl
from jax.experimental.pallas import tpu as pltpu
from jax.sharding import PartitionSpec as P

D = 2048
H = 64
P_SIZE = 64
N = 128
KW = 4
SPAN = 128
DI = 4096
CONVW = 4352
PROJ = 8512
TAIL = PROJ - 2 * DI

EPSILON = 1e-05
ALL = ("rep", "shard")
VMEM_BYTES = 58 * 1024 * 1024
BF = jnp.bfloat16
F32 = jnp.float32


def dot_nn(a, b):
    return lax.dot_general(a, b, (((1,), (0,)), ((), ())), preferred_element_type=F32)


def dot_nt(a, b):
    return lax.dot_general(a, b, (((1,), (1,)), ((), ())), preferred_element_type=F32)


def dot_tn(a, b):
    return lax.dot_general(a, b, (((0,), (0,)), ((), ())), preferred_element_type=F32)


def halves(a):
    high = a.astype(BF)
    return high, (a - high.astype(F32)).astype(BF)


def slot_tables(seq_lengths, seq_order, slot_ids):
    seq_count = seq_lengths.shape[0]
    numbers = jnp.arange(seq_count, dtype=jnp.int32)
    chosen = (seq_order[:, None] == numbers[None, :]).astype(jnp.int32)
    given_start = jnp.cumsum(seq_lengths) - seq_lengths
    owner_length = jnp.sum(chosen * seq_lengths[None, :], axis=1)
    owner_start = jnp.cumsum(owner_length) - owner_length
    owner_from = jnp.sum(chosen * given_start[None, :], axis=1)
    placed_at = jnp.sum(chosen * owner_start[:, None], axis=0)
    column = slot_ids[:, None]
    within = (column >= owner_start[None, :]) & (column < (owner_start + owner_length)[None, :])
    offset = column - owner_start[None, :]
    source = jnp.sum(jnp.where(within, offset + owner_from[None, :], 0), axis=1)
    position = jnp.sum(jnp.where(within, offset, 0), axis=1)
    given_within = (column >= given_start[None, :]) & (
        column < (given_start + seq_lengths)[None, :]
    )
    target = jnp.sum(
        jnp.where(given_within, column - given_start[None, :] + placed_at[None, :], 0), axis=1
    )
    return (source, target, position)


def params():
    return pltpu.CompilerParams(vmem_limit_bytes=VMEM_BYTES)


def spread_rows(row):
    return jnp.broadcast_to(row, (16, row.shape[1]))


def sigmoid(v):
    return 1.0 / (1.0 + jnp.exp(-v))


def spread(column, lanes=128):
    return jnp.broadcast_to(column, (column.shape[0], lanes))


MESH = pl.DeviceIdType.MESH
LINE, PLANE = 4, 2
CHUNK = 256
TAIL_PAD = 384


def remote(src, dst, send_sem, recv_sem, device):
    return pltpu.make_async_remote_copy(
        src_ref=src,
        dst_ref=dst,
        send_sem=send_sem,
        recv_sem=recv_sem,
        device_id=device,
        device_id_type=MESH,
    )


def meet(devices):
    barrier = pltpu.get_barrier_semaphore()
    for device in devices:
        pl.semaphore_signal(barrier, inc=1, device_id=device, device_id_type=MESH)
    pl.semaphore_wait(barrier, len(devices))


class Line:
    def __init__(self, store, first, share, send_sem, recv_sem):
        self.store, self.first, self.share = store, first, share
        self.send_sem, self.recv_sem = send_sem, recv_sem
        self.mine, self.rep = lax.axis_index("shard"), lax.axis_index("rep")
        self.z, self.x = self.rep // PLANE, lax.rem(self.rep, PLANE)
        self.sibling = self.mine // 2 * 2 + (1 - lax.rem(self.mine, 2))

    def along(self, origin, toward, first=False):
        block = self.store.at[origin, self.share]
        lane = (toward + 1) // 2
        return remote(
            self.first if first else block,
            block,
            self.send_sem.at[lane, origin],
            self.recv_sem.at[0, origin],
            ((self.z + toward) * PLANE + self.x, self.mine),
        )

    def inward(self, origin):
        block = self.store.at[origin, self.share]
        return remote(
            block,
            block,
            self.send_sem.at[2, origin],
            self.recv_sem.at[1, origin],
            (self.rep, self.sibling),
        )

    def start(self):
        for toward in (1, -1):
            self.guarded(toward, lambda: self.along(self.z, toward, True).start())

    def guarded(self, toward, act):
        pl.when(self.z < LINE - 1 if toward > 0 else self.z > 0)(act)

    def step(self, distance):
        for toward in (1, -1):
            origin = self.z - toward * distance

            @pl.when(origin >= 0 if toward > 0 else origin < LINE)
            def _():
                self.along(origin, toward).wait_recv()
                self.guarded(toward, lambda: self.along(origin, toward).start())
                self.inward(origin).start()

    def finish(self):
        for origin in range(LINE):

            @pl.when(origin != self.z)
            def _():
                self.inward(origin).wait_recv()
                self.inward(origin).wait_send()

            for toward in (1, -1):
                passed = origin <= self.z if toward > 0 else origin >= self.z
                pl.when(passed)(
                    lambda: self.guarded(toward, lambda: self.along(origin, toward).wait_send())
                )


def meet_with_line(devices):
    mine, rep = lax.axis_index("shard"), lax.axis_index("rep")
    z, x = rep // PLANE, lax.rem(rep, PLANE)
    barrier = pltpu.get_barrier_semaphore()
    for device in devices:
        pl.semaphore_signal(barrier, inc=1, device_id=device, device_id_type=MESH)
    for toward, there in ((1, z < LINE - 1), (-1, z > 0)):

        @pl.when(there)
        def _():
            pl.semaphore_signal(
                barrier, inc=1, device_id=((z + toward) * PLANE + x, mine), device_id_type=MESH
            )

    beyond = (z + LINE - 1) // LINE + (2 * (LINE - 1) - z) // LINE
    pl.semaphore_wait(barrier, len(devices) + beyond)


def tables_in_kernel(lengths_ref, order_ref, slots):
    count = lengths_ref.shape[1]
    lengths = [lengths_ref[0, i] for i in range(count)]
    order = [order_ref[0, i] for i in range(count)]
    given_start, at = [], jnp.int32(0)
    for i in range(count):
        given_start.append(at)
        at = at + lengths[i]
    source = jnp.zeros_like(slots)
    position = jnp.zeros_like(slots)
    placed_at = [jnp.int32(0)] * count
    at = jnp.int32(0)
    for k in range(count):
        length, start = jnp.int32(0), jnp.int32(0)
        for i in range(count):
            chosen = order[k] == i
            length = length + jnp.where(chosen, lengths[i], 0)
            start = start + jnp.where(chosen, given_start[i], 0)
            placed_at[i] = placed_at[i] + jnp.where(chosen, at, 0)
        within = (slots >= at) & (slots < at + length)
        source = source + jnp.where(within, slots - at + start, 0)
        position = position + jnp.where(within, slots - at, 0)
        at = at + length
    target = jnp.zeros_like(slots)
    for i in range(count):
        within = (slots >= given_start[i]) & (slots < given_start[i] + lengths[i])
        target = target + jnp.where(within, slots - given_start[i] + placed_at[i], 0)
    return source, target, position


def start_phases(
    lengths_ref,
    order_ref,
    x_ref,
    cotangent_ref,
    valid_ref,
    gain_ref,
    w_ref,
    normed_out_ref,
    w_gate_out_ref,
    w_conv_out_ref,
    branch_grad_out_ref,
    back_ref,
    resid_ref,
    inverse_ref,
    line_ref,
    conv_in_ref,
    gate_ref,
    grads,
    place_ref,
    x_all,
    normed,
    w_gate,
    w_conv,
    local_sem,
    row_send,
    row_recv,
    w_send,
    w_recv,
    w_local,
    line_send,
    line_recv,
):
    mine, rep = lax.axis_index("shard"), lax.axis_index("rep")
    y, c = mine // 2, lax.rem(mine, 2)
    z, x = rep // PLANE, lax.rem(rep, PLANE)
    sibling, peer, far = y * 2 + (1 - c), (1 - y) * 2 + c, (1 - y) * 2 + (1 - c)
    beside = z * PLANE + (1 - x)
    rows, length = x_ref.shape[0], x_all.shape[0]
    depth, width = w_ref.shape[1], gate_ref.shape[1]
    chunks = width // CHUNK
    tail_half = TAIL // 2

    part = pl.ds(pl.multiple_of(y * (D // 2), 128), D // 2)
    share = pl.ds(pl.multiple_of(c * (length // 2), 16), length // 2)
    wholes = (x_all, grads)

    lines = [
        Line(
            line_ref.at[kind],
            wholes[kind].at[share, part],
            share,
            line_send.at[kind],
            line_recv.at[kind],
        )
        for kind in range(2)
    ]

    def line_own(kind):
        return pltpu.make_async_copy(
            wholes[kind].at[:, part], line_ref.at[kind, z], local_sem.at[4 + kind]
        )

    def block(ref, shard):
        return ref.at[pl.ds(pl.multiple_of(shard * rows, rows), rows)]

    def row_copies(kind, own, store):
        return (
            remote(own, block(store, mine), row_send.at[kind, 0], row_recv.at[kind, 0], (rep, peer)),
            remote(own, block(store, mine), row_send.at[kind, 1], row_recv.at[kind, 1], (rep, sibling)),
            remote(
                block(store, peer),
                block(store, peer),
                row_send.at[kind, 2],
                row_recv.at[kind, 2],
                (rep, sibling),
            ),
        )

    def lanes(shard):
        return pl.ds(pl.multiple_of(shard * depth, depth), depth)

    def weight_copies(store, index, base, stride, at, half):
        share = pl.ds(pl.multiple_of(at + half * x, 16), half)
        both = pl.ds(pl.multiple_of((1 - y) * 2 * depth, 128), 2 * depth)

        def source(shard, start, count):
            return w_ref.at[pl.ds(pl.multiple_of(base + stride * shard + start, 16), count)]

        def sems(way):
            return w_send.at[way, index], w_recv.at[way, index]

        whole = pl.ds(pl.multiple_of(at, 16), 2 * half)
        near = at if stride else 0
        return (
            lambda: remote(
                source(peer, near + half * x, half), store.at[share, lanes(mine)], *sems(0), (rep, peer)
            ),
            lambda: remote(
                source(far, near + half * x, half), store.at[share, lanes(mine)], *sems(1), (rep, far)
            ),
            lambda: remote(store.at[share, both], store.at[share, both], *sems(2), (beside, mine)),
            lambda: remote(
                source(sibling, near, 2 * half), store.at[whole, lanes(mine)], *sems(3), (rep, sibling)
            ),
            lambda: pltpu.make_async_copy(
                source(mine, near, 2 * half), store.at[whole, lanes(mine)], w_local.at[index]
            ),
        )

    def conv_copies(q):
        return weight_copies(w_conv, q, DI, width, q * CHUNK, CHUNK // 2)

    def tail_copies():
        return weight_copies(w_conv, chunks, 2 * DI, 0, width, tail_half)

    def gate_copies(q):
        return weight_copies(w_gate, chunks + 1 + q, 0, width, q * CHUNK, CHUNK // 2)

    def send_near(copies):
        copies[3]().start()
        copies[4]().start()

    def send_far(copies):
        copies[0]().start()
        copies[1]().start()

    def pass_on(copies):
        copies[0]().wait_recv()
        copies[1]().wait_recv()
        copies[2]().start()
        copies[0]().wait_send()
        copies[1]().wait_send()

    def arrived(copies):
        copies[2]().wait_recv()
        copies[3]().wait_recv()
        copies[4]().wait()

    def each(count, body):
        def step(i, unused):
            body(i)
            return unused

        lax.fori_loop(0, count, step, 0)

    x_copies = row_copies(0, x_ref, x_all)
    grad_copies = row_copies(1, block(grads, mine), grads)
    own_rows = pltpu.make_async_copy(x_ref, block(x_all, mine), local_sem.at[0])
    convs = [conv_copies(q) for q in range(chunks)]
    gates = [gate_copies(q) for q in range(chunks)]
    tail = tail_copies()
    x_copies[0].start()
    x_copies[1].start()
    own_rows.start()
    for copies in convs + [tail] + gates:
        send_near(copies)
    grads[pl.ds(pl.multiple_of(mine * rows, rows), rows), :] = jnp.where(
        spread(valid_ref[...], D) > 0, cotangent_ref[...].astype(F32), 0.0
    ).astype(BF)
    grad_copies[0].start()
    grad_copies[1].start()
    w_conv[width + TAIL :, :] = jnp.zeros((TAIL_PAD - TAIL, D), BF)

    def table_block(i):
        span = pl.ds(pl.multiple_of(i * rows, rows), rows)
        slots = lax.broadcasted_iota(jnp.int32, (rows, length), 0) + i * rows
        across = lax.broadcasted_iota(jnp.int32, (rows, length), 1)
        target = tables_in_kernel(lengths_ref, order_ref, slots)[1]
        back_ref[span, :] = (target == across).astype(F32).astype(BF)
        few_slots = lax.broadcasted_iota(jnp.int32, (rows, 128), 0) + i * rows
        place_ref[span, :] = tables_in_kernel(lengths_ref, order_ref, few_slots)[2]

    each(length // rows, table_block)
    x_copies[0].wait_recv()
    x_copies[2].start()
    x_copies[0].wait_send()
    send_far(convs[0])
    send_far(convs[1])
    own_rows.wait()
    x_copies[1].wait_recv()
    x_copies[2].wait_recv()
    line_own(0).start()
    lines[0].start()

    def picked(i):
        slots = lax.broadcasted_iota(jnp.int32, (rows, length), 0) + i * rows
        across = lax.broadcasted_iota(jnp.int32, (rows, length), 1)
        source = tables_in_kernel(lengths_ref, order_ref, slots)[0]
        return dot_nn((source == across).astype(F32).astype(BF), x_all[...])

    def norm_block(i):
        span = pl.ds(pl.multiple_of(i * rows, rows), rows)
        resid = picked(i)
        inverse = lax.rsqrt(jnp.mean(resid * resid, axis=1, keepdims=True) + EPSILON)
        normed[span, :] = (resid * inverse * gain_ref[...]).astype(BF)

    each(length // rows // 2, norm_block)
    grad_copies[0].wait_recv()
    grad_copies[2].start()
    grad_copies[0].wait_send()
    send_far(convs[2])
    each(length // rows // 2, lambda i: norm_block(i + length // rows // 2))
    grad_copies[1].wait_recv()
    grad_copies[2].wait_recv()
    line_own(1).start()
    lines[1].start()
    pass_on(convs[0])
    send_far(convs[3])
    resid_ref[...] = picked(mine).astype(BF)
    normed_store = pltpu.make_async_copy(normed, normed_out_ref, local_sem.at[1])
    normed_store.start()

    def inverse_block(i):
        span = pl.ds(pl.multiple_of(i * rows, rows), rows)
        given = x_all[span, :].astype(F32)
        inverse_ref[span, :] = spread(
            lax.rsqrt(jnp.mean(given * given, axis=1, keepdims=True) + EPSILON)
        )

    def project(store, target, at, count):
        span = pl.ds(at, count)
        target[:, span] = dot_nt(normed[...], store[span, :]).astype(BF)

    def conv_chunk(q):
        arrived(convs[q])
        project(w_conv, conv_in_ref, q * CHUNK, CHUNK)

    def gate_chunk(q):
        arrived(gates[q])
        project(w_gate, gate_ref, q * CHUNK, CHUNK)

    pass_on(convs[1])
    send_far(tail)
    lines[0].step(1)
    each(length // rows, inverse_block)
    pass_on(convs[2])
    send_far(gates[0])
    conv_chunk(0)
    pass_on(convs[3])
    send_far(gates[1])
    conv_chunk(1)
    pass_on(tail)
    send_far(gates[2])
    conv_chunk(2)
    lines[0].step(2)
    send_far(gates[3])
    conv_chunk(3)
    arrived(tail)
    project(w_conv, conv_in_ref, width, TAIL_PAD)
    conv_store = pltpu.make_async_copy(w_conv, w_conv_out_ref, local_sem.at[2])
    conv_store.start()
    yield
    pass_on(gates[0])
    lines[1].step(1)
    yield
    pass_on(gates[1])
    lines[0].step(3)
    gate_chunk(0)
    yield
    pass_on(gates[2])
    gate_chunk(1)
    pass_on(gates[3])
    gate_chunk(2)
    gate_chunk(3)
    gate_store = pltpu.make_async_copy(w_gate, w_gate_out_ref, local_sem.at[3])
    gate_store.start()
    grads_store = pltpu.make_async_copy(grads, branch_grad_out_ref, local_sem.at[6])
    grads_store.start()
    lines[1].step(2)
    yield
    for copies in convs + [tail] + gates:
        copies[2]().wait_send()
        copies[3]().wait_send()
    x_copies[1].wait_send()
    x_copies[2].wait_send()
    grad_copies[1].wait_send()
    grad_copies[2].wait_send()
    normed_store.wait()
    conv_store.wait()
    gate_store.wait()
    grads_store.wait()
    lines[1].step(3)
    for kind in range(2):
        line_own(kind).wait()
        lines[kind].finish()
    yield


def conv_pre(x, conv_w, conv_b, place):
    pre = conv_b + conv_w[KW - 1 : KW] * x
    for back in range(1, KW):
        moved = pltpu.roll(x, back, 0)
        pre = pre + jnp.where(place >= back, conv_w[KW - 1 - back : KW - back] * moved, 0.0)
    return pre


def conv_lanes(chunk, width, mine):
    if 128 * chunk < width:
        return pl.ds(pl.multiple_of(mine * width + 128 * chunk, 128), 128)
    return pl.ds(DI + 128 * chunk - width, 128)


def block_terms(place):
    local = lax.broadcasted_iota(jnp.int32, (SPAN, 128), 0)
    across = lax.broadcasted_iota(jnp.int32, (SPAN, 128), 1)
    begins = local - place
    causal = (across <= local) & (across >= begins)
    reach_end = local >= begins[SPAN - 1 : SPAN, :]
    entered = place >= local + 1
    carries = place[SPAN - 1 : SPAN, :] >= SPAN
    return causal, reach_end, entered, carries


def pair_terms(pair, run, run_t, step, causal, reach_end, entered, carries):
    left = lax.broadcasted_iota(jnp.int32, (SPAN, 128), 1) < P_SIZE
    runs = [spread(run[:, 2 * pair + i : 2 * pair + i + 1]) for i in range(2)]
    decays = []
    for i in range(2):
        gap = runs[i] - run_t[2 * pair + i : 2 * pair + i + 1, :]
        decays.append(jnp.exp(jnp.where(causal, gap, -jnp.inf)))
    both = jnp.where(left, runs[0], runs[1])
    end = both[SPAN - 1 : SPAN, :]
    entering = jnp.where(entered, jnp.exp(both), 0.0)
    tail = jnp.where(reach_end, jnp.exp(jnp.where(reach_end, end - both, 0.0)), 0.0)
    carried = jnp.where(carries, jnp.exp(end), 0.0)
    size = jnp.where(
        left,
        spread(step[:, 2 * pair : 2 * pair + 1]),
        spread(step[:, 2 * pair + 1 : 2 * pair + 2]),
    )
    return left, decays, entering, tail, carried, size


def stacked(value, left):
    zero = jnp.zeros_like(value)
    return jnp.concatenate([jnp.where(left, value, zero), jnp.where(left, zero, value)], axis=0)


def own_lanes(row, mine, heads):
    return pltpu.roll(row, lax.rem(128 - mine * heads, 128), 1)


def skip_lanes(row, pair):
    left = lax.broadcasted_iota(jnp.int32, (1, 128), 1) < P_SIZE
    return jnp.where(
        left,
        spread(row[:, 2 * pair : 2 * pair + 1]),
        spread(row[:, 2 * pair + 1 : 2 * pair + 2]),
    )


def step_and_run(conv_in_ref, heads_ref, run_ref, step_ref, width, mine):
    length = run_ref.shape[0]
    heads = width // P_SIZE
    lower = (
        lax.broadcasted_iota(jnp.int32, (SPAN, SPAN), 0)
        >= lax.broadcasted_iota(jnp.int32, (SPAN, SPAN), 1)
    ).astype(F32)
    bias = heads_ref[0:1, :]
    rate = jnp.exp(own_lanes(heads_ref[...], mine, heads)[1:2, :])

    def block(b, unused):
        rows = pl.ds(pl.multiple_of(b * SPAN, SPAN), SPAN)
        raw = conv_in_ref[rows, width + 2 * N : width + 2 * N + 128].astype(F32)
        step = own_lanes(jax.nn.softplus(raw + bias), mine, heads)
        step_ref[rows, :] = step
        run_ref[rows, :] = jnp.dot(
            lower, -step * rate, precision=lax.Precision.HIGHEST, preferred_element_type=F32
        )
        return unused

    lax.fori_loop(0, length // SPAN, block, 0)


def along_line(step):
    rep = lax.axis_index("rep")
    there = lax.rem(rep // PLANE + step, LINE)
    return there * PLANE + lax.rem(rep, PLANE), there


def share_copy(source, taken, send_sem, recv_sem, step):
    to, there = along_line(step)
    z, wide = lax.axis_index("rep") // PLANE, taken.shape[2]
    return remote(
        source.at[:, pl.ds(pl.multiple_of(there * wide, 128), wide)],
        taken.at[z],
        send_sem.at[step],
        recv_sem.at[z],
        (to, lax.axis_index("shard")),
    )


def share_own(source, taken, sem):
    z, wide = lax.axis_index("rep") // PLANE, taken.shape[2]
    return pltpu.make_async_copy(
        source.at[:, pl.ds(pl.multiple_of(z * wide, 128), wide)], taken.at[z], sem
    )


def share_start(source, taken, send_sem, recv_sem, own):
    own.start()
    for step in range(1, LINE):
        share_copy(source, taken, send_sem, recv_sem, step).start()


def share_arrival(taken, recv_sem, own, step):
    to, there = along_line(step)
    if step == 0:
        own.wait()
    else:
        block, sem = taken.at[there], recv_sem.at[there]
        remote(block, block, sem, sem, (to, lax.axis_index("shard"))).wait_recv()
    return there


def share_sent(source, taken, send_sem, recv_sem):
    for step in range(1, LINE):
        share_copy(source, taken, send_sem, recv_sem, step).wait_send()


def in_given_order(back_ref, inverse_ref, grad_ref, given_ref, scaled_ref):
    length, width = grad_ref.shape

    def block(i, unused):
        span = pl.ds(pl.multiple_of(i * SPAN, SPAN), SPAN)
        moved = dot_nn(back_ref[span, :], grad_ref[...])
        if given_ref is not None:
            given_ref[span, :] = moved.astype(BF)
        for c in range(width // 128):
            lanes = slice(128 * c, 128 * c + 128)
            scaled_ref[span, lanes] = (moved[:, lanes] * inverse_ref[span, :]).astype(BF)
        return unused

    lax.fori_loop(0, length // SPAN, block, 0)


class RowSum:
    def __init__(self, partial, pair_in, row_out, row_in, send_sem, recv_sem):
        self.partial, self.pair_in, self.row_out, self.row_in = partial, pair_in, row_out, row_in
        self.rows = row_in.shape[0]
        mine, rep = lax.axis_index("shard"), lax.axis_index("rep")
        self.y, self.core = mine // 2, lax.rem(mine, 2)
        sibling, peer = self.y * 2 + (1 - self.core), (1 - self.y) * 2 + self.core
        self.pairs = [
            remote(
                partial.at[self.span(2 * side + (1 - self.core))],
                pair_in.at[side],
                send_sem.at[side],
                recv_sem.at[side],
                (rep, sibling),
            )
            for side in range(2)
        ]
        self.across = remote(row_out, row_in, send_sem.at[2], recv_sem.at[2], (rep, peer))

    def span(self, shard):
        return pl.ds(pl.multiple_of(shard * self.rows, self.rows), self.rows)

    def fill(self, rows_of):
        def block(i, unused):
            span = self.span(i)
            self.partial[span, :] = rows_of(span)
            return unused

        lax.fori_loop(0, self.partial.shape[0] // self.rows, block, 0)
        for copy in self.pairs:
            copy.start()

    def join(self):
        for copy in self.pairs:
            copy.wait_recv()
        there = self.span(2 * (1 - self.y) + self.core)
        self.row_out[...] = (self.pair_in[1 - self.y] + self.partial[there, :]).astype(BF)
        self.across.start()

    def result(self):
        self.across.wait_recv()
        here = self.partial[self.span(2 * self.y + self.core), :]
        return self.pair_in[self.y] + here + self.row_in[...].astype(F32)

    def finish(self):
        for copy in self.pairs + [self.across]:
            copy.wait_send()


def mixer_kernel(spans, *refs):
    refs = list(refs)

    def take(count):
        taken, refs[:] = refs[:count], refs[count:]
        return taken

    if spans:
        start_in = take(7)
        w_out_hbm, conv_w_ref, conv_b_ref, heads_ref, gain_ref = take(5)
        start_out = take(8)
        normed_out_ref, grad_gain_ref, grad_values_ref = take(3)
    else:
        conv_in_ref, gate_ref, branch_grad_ref, w_out_ref, place_ref = take(5)
        conv_w_ref, conv_b_ref, heads_ref, gain_ref = take(4)
        normed_out_ref, grad_gate_ref, grad_gain_ref, grad_values_ref, grad_tail_ref = take(5)
    grad_conv_w_ref, grad_conv_b_ref, grad_head_ref = take(3)
    if spans:
        taken_ref, taken_out_ref, gate_peer_ref = take(3)
        gate_given_ref, tail_ref = take(2)
    (
        mixed_ref,
        starts_ref,
        grad_mixed_ref,
        act_ref,
        pre_ref,
        step_ref,
        run_ref,
        state_ref,
        gno_ref,
        sums,
        grad_act_ref,
        joined_ref,
        join_ref,
        send_sem,
        recv_sem,
    ) = take(15)
    if spans:
        start_scratch = take(8)
        start_sems = take(8)
        conv_in_ref, gate_ref, branch_grad_ref, place_ref = start_scratch[:4]
        back_ref, inverse_ref = start_out[4], start_out[6]
        w_out_ref, grad_gate_ref, grad_tail_ref, scaled_ref, tail_in = take(5)
        share_send, share_recv, own_sem, peer_send, peer_recv, tail_send, tail_recv = take(7)
    length, width = gate_ref.shape
    mine, rep, shards = lax.axis_index("shard"), lax.axis_index("rep"), lax.axis_size("shard")
    heads = width // P_SIZE
    peers = [(rep, lax.rem(mine + step, shards)) for step in range(1, shards)]
    if spans:
        y, core = mine // 2, lax.rem(mine, 2)
        sibling, peer = y * 2 + (1 - core), (1 - y) * 2 + core
        others = [lax.rem(mine + step, shards) for step in range(1, shards)]
        rows = length // shards
        beside = rep // PLANE * PLANE + (1 - lax.rem(rep, PLANE))
        meet([(along_line(step)[0], mine) for step in range(1, LINE)] + [(beside, mine)] + peers)
        w_out_load = pltpu.make_async_copy(w_out_hbm, w_out_ref, own_sem.at[2])
        w_out_load.start()
        start = start_phases(*start_in, *start_out, *start_scratch, *start_sems)
        next(start)
    else:
        meet(peers)
    for c in range((width + 2 * N) // 128):
        lanes = slice(128 * c, 128 * c + 128)
        there = conv_lanes(c, width, mine)
        pre = conv_pre(
            conv_in_ref[:, lanes].astype(F32),
            conv_w_ref[:, there],
            conv_b_ref[:, there],
            place_ref[...],
        )
        pre_ref[:, lanes] = pre
        act_ref[:, lanes] = (pre * sigmoid(pre)).astype(BF)
    step_and_run(conv_in_ref, heads_ref, run_ref, step_ref, width, mine)
    if spans:
        next(start)
    state_ref[...] = jnp.zeros_like(state_ref)
    skips = own_lanes(heads_ref[...], mine, heads)[2:3, :]

    def forward_block(b, unused):
        row = pl.multiple_of(b * SPAN, SPAN)
        rows = pl.ds(row, SPAN)
        starts_ref[pl.ds(pl.multiple_of(b * N, N), N), :] = state_ref[...]
        run = run_ref[rows, :]
        run_t = run.T
        step = step_ref[rows, :]
        masks = block_terms(place_ref[rows, :])
        in_map = act_ref[rows, width : width + N]
        out_map = act_ref[rows, width + N : width + 2 * N]
        products = dot_nt(out_map, in_map)
        in_map_t = in_map.T
        for pair in range(width // 128):
            lanes = slice(128 * pair, 128 * pair + 128)
            left, decays, entering, tail, carried, size = pair_terms(
                pair, run, run_t, step, *masks
            )
            values = act_ref[rows, lanes].astype(F32)
            scaled = values * size
            weights = jnp.concatenate([(d * products).astype(BF) for d in decays], axis=1)
            out = dot_nn(weights, stacked(scaled.astype(BF), left))
            state = state_ref[:, lanes]
            high, low = halves(state)
            out += entering * (dot_nn(out_map, high) + dot_nn(out_map, low))
            mixed_ref[rows, lanes] = out + skip_lanes(skips, pair) * values
            high, low = halves(tail * scaled)
            fresh = dot_nn(in_map_t, high) + dot_nn(in_map_t, low)
            state_ref[:, lanes] = carried * state + fresh
        return unused

    halfway = length // SPAN // 2
    lax.fori_loop(0, halfway, forward_block, 0)
    if spans:
        next(start)
    lax.fori_loop(halfway, length // SPAN, forward_block, 0)
    if spans:
        next(start)
        w_out_load.wait()

    lane = lax.broadcasted_iota(jnp.int32, (SPAN, 128), 1)

    def gated(rows, c):
        lanes = slice(128 * c, 128 * c + 128)
        gate = gate_ref[rows, lanes].astype(F32)
        opened = sigmoid(gate)
        mixed = mixed_ref[rows, lanes]
        back = gno_ref[rows, lanes]
        gain = gain_ref[:, pl.ds(pl.multiple_of(mine * width + 128 * c, 128), 128)]
        return gate, opened, mixed, back, gain, mixed * (gate * opened), back * gain

    def measure(b, unused):
        rows = pl.ds(pl.multiple_of(b * SPAN, SPAN), SPAN)
        gno_ref[rows, :] = dot_nt(branch_grad_ref[rows, :], w_out_ref[...])
        squares = jnp.zeros((SPAN, 128), F32)
        crosses = jnp.zeros((SPAN, 128), F32)
        for c in range(width // 128):
            product, weighted = gated(rows, c)[5:]
            squares += product * product
            crosses += weighted * product
        squares = jnp.sum(squares, axis=1, keepdims=True)
        crosses = jnp.sum(crosses, axis=1, keepdims=True)
        both = jnp.where(lane == 0, spread(squares), jnp.where(lane == 1, spread(crosses), 0.0))
        sums[mine, :, rows] = both.T[0:8, :]
        return unused

    lax.fori_loop(0, length // SPAN, measure, 0)

    copies = [
        remote(sums.at[mine], sums.at[mine], send_sem.at[i], recv_sem.at[i], peer)
        for i, peer in enumerate(peers)
    ]
    for copy in copies:
        copy.start()
    for copy in copies:
        copy.wait_recv()
    grad_gain_ref[...] = jnp.zeros_like(grad_gain_ref)

    def finish(b, unused):
        rows = pl.ds(pl.multiple_of(b * SPAN, SPAN), SPAN)
        both = sums[0, :, rows]
        for shard in range(1, shards):
            both = both + sums[shard, :, rows]
        both = jnp.concatenate([both, jnp.zeros((SPAN - 8, SPAN), F32)], axis=0).T / DI
        inverse = lax.rsqrt(both[:, 0:1] + EPSILON)
        pull = spread(inverse * inverse * inverse * both[:, 1:2])
        inverse = spread(inverse)
        for c in range(width // 128):
            lanes = slice(128 * c, 128 * c + 128)
            gate, opened, mixed, back, gain, product, weighted = gated(rows, c)
            normalized = product * inverse
            normed_out_ref[rows, lanes] = (normalized * gain).astype(BF)
            grad_product = inverse * weighted - product * pull
            grad_gain_ref[:, lanes] += jnp.sum(back * normalized, axis=0, keepdims=True)
            grad_mixed_ref[rows, lanes] = grad_product * (gate * opened)
            grad_gate_ref[rows, lanes] = (
                grad_product * mixed * (opened * (1.0 + gate * (1.0 - opened)))
            ).astype(BF)
        return unused

    lax.fori_loop(0, length // SPAN, finish, 0)
    for copy in copies:
        copy.wait_send()
    if spans:
        exchanges = ((scaled_ref, taken_ref), (normed_out_ref, taken_out_ref))
        own_shares = [share_own(*pair, own_sem.at[i]) for i, pair in enumerate(exchanges)]

        def gate_peer_copy(at):
            return remote(
                taken_ref.at[at], gate_peer_ref.at[at], peer_send.at[at], peer_recv.at[at], (rep, peer)
            )

        def row_block(ref, shard):
            return ref.at[pl.ds(pl.multiple_of(shard * rows, rows), rows)]

        tail_out = [
            remote(
                row_block(grad_tail_ref, other),
                tail_in.at[i],
                tail_send.at[0, i],
                tail_recv.at[0, i],
                (rep, other),
            )
            for i, other in enumerate(others)
        ]
        tail_back = [
            remote(
                row_block(tail_ref, mine),
                row_block(tail_ref, mine),
                tail_send.at[1, i],
                tail_recv.at[1, i],
                (rep, other),
            )
            for i, other in enumerate(others)
        ]
        in_given_order(back_ref, inverse_ref, grad_gate_ref, gate_given_ref, scaled_ref)
        share_start(*exchanges[0], share_send.at[0], share_recv.at[0], own_shares[0])
    state_ref[...] = jnp.zeros_like(state_ref)
    grad_head_ref[...] = jnp.zeros_like(grad_head_ref)
    upper = (
        lax.broadcasted_iota(jnp.int32, (SPAN, SPAN), 0)
        <= lax.broadcasted_iota(jnp.int32, (SPAN, SPAN), 1)
    ).astype(F32)
    last_row = lax.broadcasted_iota(jnp.int32, (SPAN, 128), 0) == SPAN - 1
    join_ref[...] = (
        lax.broadcasted_iota(jnp.int32, (width, 128), 0) // P_SIZE + mine * heads
        == lax.broadcasted_iota(jnp.int32, (width, 128), 1)
    ).astype(F32).astype(BF)

    blocks = length // SPAN

    def backward_block(count, unused):
        b = blocks - 1 - count
        row = pl.multiple_of(b * SPAN, SPAN)
        rows = pl.ds(row, SPAN)
        start_rows = pl.ds(pl.multiple_of(b * N, N), N)
        run = run_ref[rows, :]
        run_t = run.T
        step = step_ref[rows, :]
        masks = block_terms(place_ref[rows, :])
        in_map = act_ref[rows, width : width + N]
        out_map = act_ref[rows, width + N : width + 2 * N]
        out_map_t = out_map.T
        products = dot_nt(out_map, in_map)
        grad_products = jnp.zeros((SPAN, SPAN), F32)
        grad_out_map = jnp.zeros((SPAN, N), F32)
        grad_in_map = jnp.zeros((SPAN, N), F32)
        for pair in range(width // 128):
            lanes = slice(128 * pair, 128 * pair + 128)
            left, decays, entering, tail, carried, size = pair_terms(
                pair, run, run_t, step, *masks
            )
            values = act_ref[rows, lanes].astype(F32)
            grad = grad_mixed_ref[rows, lanes]
            start = starts_ref[start_rows, lanes]
            later = state_ref[:, lanes]
            scaled = values * size
            scaled_low = scaled.astype(BF)
            grad_low = grad.astype(BF)
            weights = jnp.concatenate([(d * products).astype(BF) for d in decays], axis=0)
            grad_scaled = dot_tn(weights, stacked(grad_low, left))
            grad_pairs = dot_nt(grad_low, stacked(scaled_low, left))
            grad_products += (
                grad_pairs[:, :SPAN] * decays[0] + grad_pairs[:, SPAN:] * decays[1]
            )
            later_high, later_low = halves(later)
            from_later = tail * (dot_nn(in_map, later_high) + dot_nn(in_map, later_low))
            grad_scaled += from_later
            entering_high, entering_low = halves(entering * grad)
            grad_out_map += dot_nt(entering_high, start.astype(BF))
            grad_in_map += dot_nt((tail * scaled).astype(BF), later_high)
            ending = jnp.sum(scaled * from_later, axis=0, keepdims=True) + carried * jnp.sum(
                start * later, axis=0, keepdims=True
            )
            state_ref[:, lanes] = (
                carried * later + dot_nn(out_map_t, entering_high) + dot_nn(out_map_t, entering_low)
            )
            skip = skip_lanes(skips, pair)
            inner = mixed_ref[rows, lanes] - skip * values
            joined_ref[0:SPAN, lanes] = (
                grad_low.astype(F32) * inner
                - scaled_low.astype(F32) * (grad_scaled - from_later)
                - scaled * from_later
                + jnp.where(last_row, ending, 0.0)
            )
            joined_ref[SPAN : 2 * SPAN, lanes] = grad_scaled * values
            joined_ref[2 * SPAN : 2 * SPAN + 16, lanes] = spread_rows(
                jnp.sum(grad * values, axis=0, keepdims=True)
            )
            grad_act_ref[rows, lanes] = grad_scaled * size + skip * grad
        grad_products = grad_products.astype(BF)
        grad_act_ref[rows, width : width + N] = grad_in_map + dot_tn(grad_products, out_map)
        grad_act_ref[rows, width + N : width + 2 * N] = grad_out_map + dot_nn(
            grad_products, in_map
        )
        joined = joined_ref[...]
        first = joined.astype(BF)
        second, third = halves(joined - first.astype(F32))
        join = join_ref[...]
        by_head = dot_nn(first, join) + dot_nn(second, join) + dot_nn(third, join)
        grad_log = jnp.dot(
            upper, by_head[:SPAN], precision=lax.Precision.HIGHEST, preferred_element_type=F32
        )
        rate = jnp.exp(heads_ref[1:2, :])
        raw = conv_in_ref[rows, width + 2 * N : width + 2 * N + 128].astype(F32) + heads_ref[0:1, :]
        grad_dt = (by_head[SPAN : 2 * SPAN] - grad_log * rate) * sigmoid(raw)
        grad_tail_ref[rows, 2 * N : 2 * N + 128] = grad_dt
        grad_head_ref[0:1, :] += jnp.sum(grad_dt, axis=0, keepdims=True)
        grad_head_ref[1:2, :] += jnp.sum(
            -grad_log * jax.nn.softplus(raw) * rate, axis=0, keepdims=True
        )
        grad_head_ref[2:3, :] += by_head[2 * SPAN : 2 * SPAN + 1]
        return unused

    if spans:
        lax.fori_loop(0, blocks - 1, backward_block, 0)
        for step in range(LINE):
            at = share_arrival(taken_ref, share_recv.at[0], own_shares[0], step)
            gate_peer_copy(at).start()
        share_start(*exchanges[1], share_send.at[1], share_recv.at[1], own_shares[1])
        lax.fori_loop(blocks - 1, blocks, backward_block, 0)
    else:
        lax.fori_loop(0, blocks, backward_block, 0)

    place = place_ref[...]
    own_chunks = width // 128
    for c in [own_chunks, own_chunks + 1] + list(range(own_chunks)):
        lanes = slice(128 * c, 128 * c + 128)
        x = conv_in_ref[:, lanes].astype(F32)
        conv_w = conv_w_ref[:, conv_lanes(c, width, mine)]
        pre = pre_ref[:, lanes]
        gain = sigmoid(pre)
        grad_pre = grad_act_ref[:, lanes] * (gain * (1.0 + pre * (1.0 - gain)))
        grad_conv_b_ref[:, lanes] = jnp.sum(grad_pre, axis=0, keepdims=True)
        grad_conv_w_ref[KW - 1 : KW, lanes] = jnp.sum(grad_pre * x, axis=0, keepdims=True)
        grad_x = conv_w[KW - 1 : KW] * grad_pre
        for back in range(1, KW):
            tap = KW - 1 - back
            kept = jnp.where(place >= back, grad_pre, 0.0)
            grad_conv_w_ref[tap : tap + 1, lanes] = jnp.sum(
                kept * pltpu.roll(x, back, 0), axis=0, keepdims=True
            )
            grad_x += conv_w[tap : tap + 1] * pltpu.roll(kept, length - back, 0)
        if c < width // 128:
            grad_values_ref[:, lanes] = grad_x.astype(BF)
        else:
            grad_tail_ref[:, 128 * c - width : 128 * c - width + 128] = grad_x
        if spans and c == own_chunks + 1:
            for copy in tail_out:
                copy.start()
    if spans:
        span = pl.ds(pl.multiple_of(mine * rows, rows), rows)
        tail = grad_tail_ref[span, :]
        for i, copy in enumerate(tail_out):
            copy.wait_recv()
            tail = tail + tail_in[i]
        tail_ref[span, :] = tail.astype(BF)
        for copy in tail_back:
            copy.start()
        for step in range(LINE):
            share_arrival(taken_out_ref, share_recv.at[1], own_shares[1], step)
        for i, pair in enumerate(exchanges):
            share_sent(*pair, share_send.at[i], share_recv.at[i])
        for at in range(LINE):
            gate_peer_copy(at).wait()
        for copy in tail_out:
            copy.wait_send()
        for copy in tail_back:
            copy.wait()
        next(start)


def run_mixer(operands, shards, spans):
    if spans:
        rows = operands[2].shape[0]
        length, width = rows * shards, DI // shards
    else:
        length, width = operands[1].shape
        rows = length // shards
    blocks, chunks = length // SPAN, width // CHUNK
    shape = jax.ShapeDtypeStruct
    vector = pl.BlockSpec(memory_space=pltpu.VMEM)
    anywhere = pl.BlockSpec(memory_space=pl.ANY)
    scalars = pl.BlockSpec(memory_space=pltpu.SMEM)
    dma = pltpu.SemaphoreType.DMA
    small = [
        shape((KW, width + 2 * N), F32),
        shape((1, width + 2 * N), F32),
        shape((8, 128), F32),
    ]
    scratch = [
        pltpu.VMEM((length, width), F32),
        pltpu.VMEM((blocks * N, width), F32),
        pltpu.VMEM((length, width), F32),
        pltpu.VMEM((length, width + 2 * N), BF),
        pltpu.VMEM((length, width + 2 * N), F32),
        pltpu.VMEM((length, 128), F32),
        pltpu.VMEM((length, 128), F32),
        pltpu.VMEM((N, width), F32),
        pltpu.VMEM((length, width), F32),
        pltpu.VMEM((shards, 8, length), F32),
        pltpu.VMEM((length, width + 2 * N), F32),
        pltpu.VMEM((2 * SPAN + 16, width), F32),
        pltpu.VMEM((width, 128), BF),
        dma((shards - 1,)),
        dma((shards - 1,)),
    ]
    if spans:
        taken = shape((LINE, length, 2 * 128), BF)
        outs = [
            (shape((length, D), BF), anywhere),
            (shape((width, D), BF), anywhere),
            (shape((width + TAIL_PAD, D), BF), anywhere),
            (shape((length, D), BF), anywhere),
            (shape((length, length), BF), vector),
            (shape((rows, D), BF), vector),
            (shape((length, 128), F32), vector),
            (shape((2, LINE, length, D // 2), BF), anywhere),
            (shape((length, width), BF), vector),
            (shape((1, width), F32), vector),
            (shape((length, width), BF), vector),
            *[(one, vector) for one in small],
            (taken, anywhere),
            (taken, anywhere),
            (taken, anywhere),
            (shape((length, width), BF), vector),
            (shape((length, TAIL_PAD), BF), vector),
        ]
        in_specs = [scalars, scalars, anywhere, vector, vector, vector, anywhere, anywhere]
        in_specs += [vector] * 4
        weights = 2 * chunks + 1
        scratch += [
            pltpu.VMEM((length, width + TAIL_PAD), BF),
            pltpu.VMEM((length, width), BF),
            pltpu.VMEM((length, D), BF),
            pltpu.VMEM((length, 128), jnp.int32),
            pltpu.VMEM((length, D), BF),
            pltpu.VMEM((length, D), BF),
            pltpu.VMEM((width, D), BF),
            pltpu.VMEM((width + TAIL_PAD, D), BF),
            dma((7,)),
            dma((2, 3)),
            dma((2, 3)),
            dma((4, weights)),
            dma((4, weights)),
            dma((weights,)),
            dma((2, 3, LINE)),
            dma((2, 2, LINE)),
            pltpu.VMEM((width, D), BF),
            pltpu.VMEM((length, width), BF),
            pltpu.VMEM((length, TAIL_PAD), F32),
            pltpu.VMEM((length, width), BF),
            pltpu.VMEM((shards - 1, rows, TAIL_PAD), F32),
            dma((2, LINE)),
            dma((2, LINE)),
            dma((3,)),
            dma((LINE,)),
            dma((LINE,)),
            dma((2, shards - 1)),
            dma((2, shards - 1)),
        ]
    else:
        wide = shape((length, width), BF)
        outs = [wide, wide, shape((1, width), F32), wide, shape((length, TAIL_PAD), F32), *small]
        outs = [(one, vector) for one in outs]
        in_specs = [vector] * 9
    return pl.pallas_call(
        functools.partial(mixer_kernel, spans),
        out_shape=tuple(out for out, spec in outs),
        in_specs=in_specs,
        out_specs=tuple(spec for out, spec in outs),
        scratch_shapes=scratch,
        compiler_params=pltpu.CompilerParams(
            vmem_limit_bytes=VMEM_BYTES, collective_id=2, has_side_effects=True
        ),
        cost_estimate=pl.CostEstimate(
            flops=60 * length * width * 128, bytes_accessed=32 * length * width, transcendentals=0
        ),
        name="mixer",
    )(*operands)


def end_kernel(
    gate_taken_hbm,
    gate_peer_hbm,
    out_taken_hbm,
    gate_given_ref,
    values_ref,
    tail_low,
    normed_ref,
    line_ref,
    inverse_ref,
    w_gate_hbm,
    w_conv_hbm,
    w_out_hbm,
    normed_out_hbm,
    back_ref,
    branch_grad_hbm,
    x_ref,
    resid_ref,
    valid_ref,
    gain_ref,
    grad_conv_w_ref,
    grad_conv_b_ref,
    grad_head_ref,
    grad_gain_ref,
    parts_ref,
    w_out_grad_ref,
    tails_ref,
    block_out_ref,
    grad_in_ref,
    out_norm_ref,
    out_conv_w_ref,
    out_conv_b_ref,
    out_head_ref,
    out_gain_ref,
    taken,
    taken_peer,
    values_given_ref,
    scaled_ref,
    group_rows,
    own_columns,
    total,
    sum_kept,
    mail_out,
    mail_in,
    low,
    partial,
    pair_in,
    row_out,
    row_in,
    branch_pair,
    branch_out,
    branch_in,
    tail_sum,
    tail_own,
    tail_parts,
    small,
    small_in,
    small_all,
    w_gate_ref,
    w_conv_ref,
    branch_grad_ref,
    w_out_ref,
    normed_out_ref,
    load_sem,
    local_sem,
    group_sem,
    share_send,
    share_recv,
    peer_send,
    peer_recv,
    mail_send,
    mail_recv,
    swap_send,
    swap_recv,
    line_send,
    line_recv,
    side_send,
    side_recv,
    pair_send,
    pair_recv,
    branch_send,
    branch_recv,
    rep_send,
    rep_recv,
    all_send,
    all_recv,
):
    reps, shards = LINE * PLANE, lax.axis_size("shard")
    mine, rep = lax.axis_index("shard"), lax.axis_index("rep")
    y, c = mine // 2, lax.rem(mine, 2)
    z, x = rep // PLANE, lax.rem(rep, PLANE)
    beside = z * PLANE + (1 - x)
    rows, length = x_ref.shape[0], values_ref.shape[0]
    width, depth = values_ref.shape[1], own_columns.shape[1]
    half = D // 2
    sibling, peer = y * 2 + (1 - c), (1 - y) * 2 + c

    def other(step):
        return lax.rem(z + step // PLANE, LINE) * PLANE + lax.rem(x + step % PLANE, PLANE)

    def before(step):
        return lax.rem(z + LINE - step // PLANE, LINE) * PLANE + lax.rem(
            x + PLANE - step % PLANE, PLANE
        )

    def shard_at(step):
        return lax.rem(mine + step, shards)

    def each(count, body):
        def step(i, unused):
            body(i)
            return unused

        lax.fori_loop(0, count, step, 0)

    meet(
        [(other(step), mine) for step in range(1, reps)]
        + [(rep, shard_at(step)) for step in range(1, shards)]
    )

    loads = [
        pltpu.make_async_copy(far_ref, near_ref, load_sem.at[i])
        for i, (far_ref, near_ref) in enumerate(
            [
                (w_gate_hbm, w_gate_ref),
                (w_conv_hbm, w_conv_ref),
                (branch_grad_hbm, branch_grad_ref),
                (w_out_hbm, w_out_ref),
                (normed_out_hbm, normed_out_ref),
            ]
        )
    ]

    def group_copy(part, step):
        at = along_line(step)[1]
        return pltpu.make_async_copy(
            line_ref.at[part // 2, at], group_rows.at[step], group_sem.at[step]
        )

    def peer_copy(part, at):
        return remote(
            taken.at[part, at],
            taken_peer.at[part, at],
            peer_send.at[part, at],
            peer_recv.at[part, at],
            (rep, peer),
        )

    own_part = pltpu.make_async_copy(
        normed_ref.at[:, pl.ds(pl.multiple_of(mine * depth, depth), depth)],
        own_columns,
        local_sem.at[4],
    )
    own_part.start()
    gate_load = pltpu.make_async_copy(gate_taken_hbm, taken.at[0], local_sem.at[0])
    gate_load.start()
    peer_load = pltpu.make_async_copy(gate_peer_hbm, taken_peer.at[0], local_sem.at[7])
    peer_load.start()
    out_load = pltpu.make_async_copy(out_taken_hbm, taken.at[2], local_sem.at[5])
    out_load.start()
    for step in range(LINE):
        group_copy(0, step).start()
    out_load.wait()
    for at in range(LINE):
        peer_copy(2, at).start()

    for load in loads[::-1]:
        load.start()

    rows_sum = RowSum(partial, pair_in, row_out, row_in, pair_send, pair_recv)
    branch_sum = RowSum(partial, branch_pair, branch_out, branch_in, branch_send, branch_recv)

    def swap_copy(part):
        if part == 2:
            return remote(
                low.at[2, pl.ds(pl.multiple_of((1 - y) * 128, 128), 128), :],
                w_out_grad_ref.at[rep, :, pl.ds(pl.multiple_of(y * half, 128), half)],
                swap_send.at[2],
                swap_recv.at[2],
                (rep, peer),
            )
        return remote(
            low.at[part, :, pl.ds(pl.multiple_of((1 - c) * depth, depth), depth)],
            parts_ref.at[rep, part, c],
            swap_send.at[part],
            swap_recv.at[part],
            (rep, sibling),
        )

    def swap_own(part):
        if part == 2:
            return pltpu.make_async_copy(
                low.at[2, pl.ds(pl.multiple_of(y * 128, 128), 128), :],
                w_out_grad_ref.at[rep, :, pl.ds(pl.multiple_of(y * half, 128), half)],
                local_sem.at[6],
            )
        return pltpu.make_async_copy(
            low.at[part, :, pl.ds(pl.multiple_of(c * depth, depth), depth)],
            parts_ref.at[rep, part, c],
            local_sem.at[2 + part],
        )

    def mail_copy(part):
        return remote(
            mail_out.at[part],
            mail_in.at[part],
            mail_send.at[part],
            mail_recv.at[part],
            (beside, mine),
        )

    def sum_groups(part, then=None):
        for step in range(LINE):
            at = along_line(step)[1]
            if part > 0:
                peer_copy(part, at).wait_recv()
            elif step == 0:
                gate_load.wait()
                peer_load.wait()
            group_copy(part, step).wait()
            both = jnp.concatenate([taken[part, at], taken_peer[part, at]], axis=1)
            for lanes in (slice(0, half // 2), slice(half // 2, half)):
                term = dot_tn(both, group_rows[step, :, lanes])
                if step == 0:
                    total[:, lanes] = term
                else:
                    total[:, lanes] += term
            if then is not None:
                group_copy(then, step).start()
        for source, place in ((0, y), (256, 1 - y)):
            rows_kept = pl.ds(pl.multiple_of(source + x * 128, 128), 128)
            rows_sent = pl.ds(pl.multiple_of(source + (1 - x) * 128, 128), 128)
            there = pl.ds(pl.multiple_of(place * 128, 128), 128)
            sum_kept[there, :] = total[rows_kept, :]
            mail_out[part, there, :] = total[rows_sent, :].astype(BF)
        mail_copy(part).start()

    def close_sum(part):
        gains = gain_ref[:, pl.ds(pl.multiple_of(y * half, 128), half)] if part < 2 else 1.0
        mail_copy(part).wait_recv()
        low[part] = ((sum_kept[...] + mail_in[part].astype(F32)) * gains).astype(BF)
        swap_own(part).start()
        swap_copy(part).start()

    def sum_block(part, owner):
        return w_out_grad_ref.at[owner] if part == 2 else parts_ref.at[owner, part]

    def line_copy(part, origin, toward, lane):
        block = sum_block(part, origin * PLANE + x)
        return remote(
            block,
            block,
            line_send.at[part, lane, origin],
            line_recv.at[part, origin],
            ((z + toward) * PLANE + x, mine),
        )

    def side_copy(part, origin, from_x):
        block = sum_block(part, origin * PLANE + from_x)
        return remote(
            block, block, side_send.at[part, origin], side_recv.at[part, origin], (beside, mine)
        )

    def spread_own(part):
        swap_own(part).wait()
        swap_copy(part).wait_recv()
        side_copy(part, z, x).start()

        @pl.when(z < LINE - 1)
        def _():
            line_copy(part, z, 1, 0).start()

        @pl.when(z > 0)
        def _():
            line_copy(part, z, -1, 1).start()

    def pass_on(part, step):
        @pl.when(z - step >= 0)
        def _():
            origin = z - step
            line_copy(part, origin, 1, 0).wait_recv()

            @pl.when(z < LINE - 1)
            def _():
                line_copy(part, origin, 1, 0).start()

            side_copy(part, origin, x).start()

        @pl.when(z + step < LINE)
        def _():
            origin = z + step
            line_copy(part, origin, -1, 1).wait_recv()

            @pl.when(z > 0)
            def _():
                line_copy(part, origin, -1, 1).start()

            side_copy(part, origin, x).start()

    in_given_order(back_ref, inverse_ref, values_ref, values_given_ref, scaled_ref)
    own_share = share_own(scaled_ref, taken.at[1], local_sem.at[1])
    share_start(scaled_ref, taken.at[1], share_send, share_recv, own_share)
    sum_groups(0, 2)
    close_sum(0)
    spread_own(0)
    loads[3].wait()
    loads[4].wait()
    branch_sum.fill(lambda span: dot_nn(normed_out_ref[span, :], w_out_ref[...]))
    sum_groups(2, 1)
    branch_sum.join()
    close_sum(2)
    pass_on(0, 1)
    spread_own(2)

    branch = branch_sum.result()
    branch_sum.finish()
    whole = resid_ref[...].astype(F32) + branch
    block_out_ref[...] = whole.astype(BF)
    counts = valid_ref[...].astype(F32)
    square_total = jnp.sum(
        counts * jnp.sum(whole * whole, axis=1, keepdims=True), axis=0, keepdims=True
    )
    square_branch = jnp.sum(
        counts * jnp.sum(branch * branch, axis=1, keepdims=True), axis=0, keepdims=True
    )
    count = jnp.sum(counts, axis=0, keepdims=True)
    pass_on(0, 2)

    heads, share = H // shards, 2 * N // shards
    lane = lax.broadcasted_iota(jnp.int32, (rows, TAIL_PAD), 1)
    owned = ((lane >= mine * share) & (lane < (mine + 1) * share)) | (
        (lane >= 2 * N + mine * heads) & (lane < 2 * N + (mine + 1) * heads)
    )

    def grad_rows(span):
        tail = dot_nn(back_ref[span, :], tail_low[...])
        tail = jnp.where(owned, tail, 0.0).astype(BF)
        return (
            dot_nn(gate_given_ref[span, :], w_gate_ref[...])
            + dot_nn(values_given_ref[span, :], w_conv_ref[0:width, :])
            + dot_nn(tail, w_conv_ref[width:, :])
        )

    loads[0].wait()
    loads[1].wait()
    rows_sum.fill(grad_rows)

    share_rows = TAIL_PAD // reps

    def tail_rows(ref, owner):
        return ref.at[pl.ds(pl.multiple_of(owner * share_rows, 16), share_rows)]

    def tail_part_copy(step):
        to = other(step)
        return remote(
            tail_rows(tail_sum, to),
            tail_parts.at[step],
            rep_send.at[0, step],
            rep_recv.at[0, step],
            (to, mine),
        )

    def tail_spread_copy(step):
        return remote(
            tail_rows(tails_ref, rep),
            tail_rows(tails_ref, rep),
            rep_send.at[1, step],
            rep_recv.at[1, step],
            (other(step), mine),
        )

    own_part.wait()
    tail_own[...] = dot_tn(tail_low[...], own_columns[...])
    tail_sum[...] = tail_own[...].astype(BF)
    for step in range(1, reps):
        tail_part_copy(step).start()

    for step in range(LINE):
        at = share_arrival(taken.at[1], share_recv, own_share, step)
        peer_copy(1, at).start()
    rows_sum.join()
    pass_on(0, 3)

    pass_on(2, 1)
    for step in range(1, reps):
        tail_part_copy(step).wait_recv()
    span = pl.ds(pl.multiple_of(rep * share_rows, 16), share_rows)
    piece = tail_own[span, :]
    for step in range(1, reps):
        piece = piece + tail_parts[step].astype(F32)
    tails_ref[span, :] = piece.astype(BF)
    for step in range(1, reps):
        tail_spread_copy(step).start()

    grad_normed = rows_sum.result()
    given = x_ref[...].astype(F32)
    inverse = lax.rsqrt(jnp.mean(given * given, axis=1, keepdims=True) + EPSILON)
    grad_norm_gain = jnp.sum(grad_normed * (given * inverse), axis=0, keepdims=True)
    scaled = grad_normed * gain_ref[...]
    pull = inverse * inverse * inverse * jnp.mean(scaled * given, axis=1, keepdims=True)
    span = pl.ds(pl.multiple_of(mine * rows, rows), rows)
    loads[2].wait()
    kept = dot_nn(back_ref[span, :], branch_grad_ref[...])
    grad_in_ref[...] = (scaled * inverse - given * pull + kept).astype(BF)
    pass_on(2, 2)

    lane = lax.broadcasted_iota(jnp.int32, (1, 128), 1)
    at = 0
    for i in range(D // 128):
        small[at : at + 1, :] = grad_norm_gain[:, 128 * i : 128 * i + 128]
        at += 1
    channels = (width + 2 * N) // 128
    for tap in range(KW):
        for i in range(channels):
            small[at : at + 1, :] = grad_conv_w_ref[tap : tap + 1, 128 * i : 128 * i + 128]
            at += 1
    for i in range(channels):
        small[at : at + 1, :] = grad_conv_b_ref[:, 128 * i : 128 * i + 128]
        at += 1
    for i in range(width // 128):
        small[at : at + 1, :] = grad_gain_ref[:, 128 * i : 128 * i + 128]
        at += 1
    small[at : at + 3, :] = grad_head_ref[0:3, :]
    small[at + 3 : at + 4, :] = jnp.where(
        lane == 0,
        spread(square_total),
        jnp.where(lane == 1, spread(square_branch), jnp.where(lane == 2, spread(count), 0.0)),
    )
    small[at + 4 :, :] = jnp.zeros((small.shape[0] - at - 4, 128), F32)

    def small_rep_copy(step):
        return remote(
            small, small_in.at[rep], rep_send.at[2, step], rep_recv.at[2, step], (other(step), mine)
        )

    def small_rep_arrival(step):
        return remote(
            small,
            small_in.at[before(step)],
            rep_send.at[2, step],
            rep_recv.at[2, step],
            (other(step), mine),
        )

    def small_shard_copy(step):
        return remote(
            small_all.at[mine],
            small_all.at[mine],
            all_send.at[step],
            all_recv.at[step],
            (rep, shard_at(step)),
        )

    for step in range(1, reps):
        small_rep_copy(step).start()
    small_in[rep] = small[...]
    sum_groups(1)
    pass_on(2, 3)
    close_sum(1)
    spread_own(1)
    for step in range(1, reps):
        small_rep_arrival(step).wait_recv()
    added = small_in[0]
    for i in range(1, reps):
        added = added + small_in[i]
    small_all[mine] = added
    for step in range(1, shards):
        small_shard_copy(step).start()
    pass_on(1, 1)
    for step in range(1, shards):
        small_shard_copy(step).wait_recv()

    def over_shards(row):
        value = small_all[0, row : row + 1, :]
        for i in range(1, shards):
            value = value + small_all[i, row : row + 1, :]
        return value

    at = 0
    for i in range(D // 128):
        out_norm_ref[:, 128 * i : 128 * i + 128] = over_shards(at)
        at += 1
    for tap in range(KW + 1):
        ref, row = (out_conv_w_ref, tap) if tap < KW else (out_conv_b_ref, 0)
        for i in range(channels):
            if i < width // 128:
                for shard in range(shards):
                    to = shard * width + 128 * i
                    ref[row : row + 1, to : to + 128] = small_all[shard, at : at + 1, :]
            else:
                to = DI + 128 * i - width
                ref[row : row + 1, to : to + 128] = over_shards(at)
            at += 1
    for i in range(width // 128):
        for shard in range(shards):
            to = shard * width + 128 * i
            out_gain_ref[:, to : to + 128] = small_all[shard, at : at + 1, :]
        at += 1
    for i in range(3):
        out_head_ref[i : i + 1, :] = over_shards(at + i)
    stats = over_shards(at + 3)
    per = jnp.maximum(stats[:, 2:3], 1.0) * D
    out_head_ref[3:4, :] = jnp.sqrt(stats / spread(per))
    out_head_ref[4:8, :] = jnp.zeros((4, 128), F32)

    pass_on(1, 2)
    pass_on(1, 3)

    for step in range(1, reps):
        tail_spread_copy(step).wait_recv()
    for part in range(3):
        for origin in range(LINE):
            side_copy(part, origin, 1 - x).wait_recv()
            side_copy(part, origin, x).wait_send()

            @pl.when((origin <= z) & (z < LINE - 1))
            def _(part=part, origin=origin):
                line_copy(part, origin, 1, 0).wait_send()

            @pl.when((origin >= z) & (z > 0))
            def _(part=part, origin=origin):
                line_copy(part, origin, -1, 1).wait_send()

        swap_copy(part).wait_send()
        mail_copy(part).wait_send()
        if part > 0:
            for at in range(LINE):
                peer_copy(part, at).wait_send()
    share_sent(scaled_ref, taken.at[1], share_send, share_recv)
    rows_sum.finish()
    for step in range(1, shards):
        small_shard_copy(step).wait_send()
    for step in range(1, reps):
        tail_part_copy(step).wait_send()
        tail_spread_copy(step).wait_send()
        small_rep_copy(step).wait_send()


def run_end(operands, shards):
    reps = LINE * PLANE
    length, width = operands[4].shape
    rows, depth = length // shards, D // shards
    dma = pltpu.SemaphoreType.DMA
    vector = pl.BlockSpec(memory_space=pltpu.VMEM)
    anywhere = pl.BlockSpec(memory_space=pl.ANY)
    shape = jax.ShapeDtypeStruct
    channels = width + 2 * N
    small = -(-(D + 5 * channels + width + 4 * 128) // 1024) * 8
    return pl.pallas_call(
        end_kernel,
        out_shape=(
            shape((reps, 2, 2, 256, depth), BF),
            shape((reps, 128, D), BF),
            shape((TAIL_PAD, depth), BF),
            shape((rows, D), BF),
            shape((rows, D), BF),
            shape((1, D), F32),
            shape((KW, CONVW), F32),
            shape((1, CONVW), F32),
            shape((8, 128), F32),
            shape((1, DI), F32),
        ),
        in_specs=[anywhere] * 3 + [vector] * 3 + [anywhere] * 2 + [vector] + [anywhere] * 4 + [vector] + [anywhere] + [vector] * 8,
        out_specs=(anywhere,) * 2 + (vector,) * 8,
        scratch_shapes=[
            pltpu.VMEM((3, LINE, length, 256), BF),
            pltpu.VMEM((3, LINE, length, 256), BF),
            pltpu.VMEM((length, width), BF),
            pltpu.VMEM((length, width), BF),
            pltpu.VMEM((LINE, length, D // 2), BF),
            pltpu.VMEM((length, depth), BF),
            pltpu.VMEM((512, D // 2), F32),
            pltpu.VMEM((256, D // 2), F32),
            pltpu.VMEM((3, 256, D // 2), BF),
            pltpu.VMEM((3, 256, D // 2), BF),
            pltpu.VMEM((3, 256, D // 2), BF),
            pltpu.VMEM((length, D), F32),
            pltpu.VMEM((2, rows, D), F32),
            pltpu.VMEM((rows, D), BF),
            pltpu.VMEM((rows, D), BF),
            pltpu.VMEM((2, rows, D), F32),
            pltpu.VMEM((rows, D), BF),
            pltpu.VMEM((rows, D), BF),
            pltpu.VMEM((TAIL_PAD, depth), BF),
            pltpu.VMEM((TAIL_PAD, depth), F32),
            pltpu.VMEM((reps, TAIL_PAD // reps, depth), BF),
            pltpu.VMEM((small, 128), F32),
            pltpu.VMEM((reps, small, 128), F32),
            pltpu.VMEM((shards, small, 128), F32),
            pltpu.VMEM((width, D), BF),
            pltpu.VMEM((width + TAIL_PAD, D), BF),
            pltpu.VMEM((length, D), BF),
            pltpu.VMEM((width, D), BF),
            pltpu.VMEM((length, width), BF),
            dma((5,)),
            dma((8,)),
            dma((LINE,)),
            dma((LINE,)),
            dma((LINE,)),
            dma((3, LINE)),
            dma((3, LINE)),
            dma((3,)),
            dma((3,)),
            dma((3,)),
            dma((3,)),
            dma((3, 2, LINE)),
            dma((3, LINE)),
            dma((3, LINE)),
            dma((3, LINE)),
            dma((3,)),
            dma((3,)),
            dma((3,)),
            dma((3,)),
            dma((3, reps)),
            dma((3, reps)),
            dma((shards,)),
            dma((shards,)),
        ],
        compiler_params=pltpu.CompilerParams(
            vmem_limit_bytes=VMEM_BYTES, collective_id=3, has_side_effects=True
        ),
        cost_estimate=pl.CostEstimate(
            flops=2 * reps * length * D * 256, bytes_accessed=96 << 20, transcendentals=0
        ),
        name="weight_gradient",
    )(*operands)


def assemble_kernel(parts_ref, tail_ref, out_ref):
    step, steps = pl.program_id(0), pl.num_programs(0)
    reps = parts_ref.shape[0]

    @pl.when(step < steps - 1)
    def _():
        for rep in range(reps):
            out_ref[128 * rep : 128 * rep + 128, :] = parts_ref[rep, 0, 0].astype(F32)

    @pl.when(step == steps - 1)
    def _():
        out_ref[0:TAIL, :] = tail_ref[0:TAIL, :].astype(F32)


def run_assemble(parts, tail):
    reps, unused, cores, stack, depth = parts.shape
    shards = cores * stack // 128
    steps = 2 * shards

    def place(i):
        at = jnp.minimum(i, steps - 1)
        shard = lax.rem(at, shards)
        return (0, at // shards, lax.rem(shard, cores), shard // cores, 0)

    return pl.pallas_call(
        assemble_kernel,
        grid=(steps + 1,),
        out_shape=jax.ShapeDtypeStruct((PROJ, depth), F32),
        in_specs=[
            pl.BlockSpec((reps, 1, 1, 128, depth), place),
            pl.BlockSpec((TAIL_PAD, depth), lambda i: (0, 0)),
        ],
        out_specs=pl.BlockSpec((reps * 128, depth), lambda i: (i, 0)),
        compiler_params=params(),
        name="assemble",
    )(parts, tail)


def exchange(pieces, axis, mine):
    count = lax.axis_size(axis)
    own = pieces(mine)
    gathered = jnp.zeros((count,) + own.shape, own.dtype)
    gathered = lax.dynamic_update_index_in_dim(gathered, own, mine, 0)
    for other in range(1, count):
        arrived = lax.ppermute(
            pieces(mine ^ other), axis, [(i, i ^ other) for i in range(count)]
        )
        gathered = lax.dynamic_update_index_in_dim(gathered, arrived, mine ^ other, 0)
    return gathered


def columns_at(array, start, width):
    return lax.dynamic_slice_in_dim(array, start, width, axis=1)


def plain_device(
    x_in,
    cotangent,
    seq_lengths,
    seq_order,
    valid,
    norm_gain,
    w_in,
    conv_w,
    conv_b,
    head_rows,
    gain_row,
    w_out,
):
    shards, mine = lax.axis_size("shard"), lax.axis_index("shard")
    rows = x_in.shape[0]
    length = rows * shards
    depth = w_in.shape[0]
    heads = H // shards
    width = DI // shards
    share = 2 * N // shards
    w_tail = w_in[:, 2 * DI :]

    def conv_piece(d):
        return jnp.concatenate([columns_at(w_in, DI + d * width, width), w_tail], axis=1)

    x_group = lax.all_gather(x_in, "shard", axis=0, tiled=True)
    w_conv = exchange(conv_piece, "shard", mine).reshape(D, width + TAIL)
    w_gate = exchange(lambda d: columns_at(w_in, d * width, width), "shard", mine).reshape(D, width)
    branch_grad = lax.all_gather(
        jnp.where(valid[:, None] > 0, cotangent, jnp.zeros_like(cotangent)),
        "shard",
        axis=0,
        tiled=True,
    )
    slot_ids = jnp.arange(length, dtype=jnp.int32)
    source, target, position = slot_tables(seq_lengths[0], seq_order[0], slot_ids)
    resid = dot_nn((source[:, None] == slot_ids[None, :]).astype(BF), x_group)
    inverse_rms = lax.rsqrt(jnp.mean(resid * resid, axis=1, keepdims=True) + EPSILON)
    normed = (resid * inverse_rms * norm_gain[None, :]).astype(BF)
    resid_mine = lax.dynamic_slice_in_dim(resid, mine * rows, rows, axis=0)
    gate = dot_nn(normed, w_gate).astype(BF)
    conv_in = jnp.pad(dot_nn(normed, w_conv).astype(BF), ((0, 0), (0, TAIL_PAD - TAIL)))
    place = jnp.broadcast_to(position[:, None], (length, 128))
    (
        normed_out,
        grad_gate,
        grad_gain,
        grad_values,
        grad_tail,
        grad_conv_w,
        grad_conv_b,
        grad_head,
    ) = run_mixer(
        (conv_in, gate, branch_grad, w_out, place, conv_w, conv_b, head_rows, gain_row), shards, False
    )
    branch = lax.psum_scatter(dot_nn(normed_out, w_out), "shard", scatter_dimension=0, tiled=True)
    total_rows = resid_mine + branch
    weights_valid = valid.astype(F32)
    square_total = jnp.sum(weights_valid * jnp.sum(total_rows * total_rows, axis=1))
    square_branch = jnp.sum(weights_valid * jnp.sum(branch * branch, axis=1))
    grad_w_out = lax.psum(dot_tn(normed_out, branch_grad), "rep")
    grad_tail = lax.psum(grad_tail, "shard").astype(BF)
    lane = jnp.arange(TAIL, dtype=jnp.int32)
    owned = ((lane >= mine * share) & (lane < (mine + 1) * share)) | (
        (lane >= 2 * N + mine * heads) & (lane < 2 * N + (mine + 1) * heads)
    )
    kept_tail = jnp.where(owned[None, :], grad_tail[:, :TAIL], jnp.zeros((), BF))
    back = (target[:, None] == slot_ids[None, :]).astype(BF)

    def returned(grad):
        return dot_nn(back, grad).astype(BF)

    grad_normed = lax.psum_scatter(
        dot_nt(returned(grad_gate), w_gate)
        + dot_nt(returned(grad_values), w_conv[:, :width])
        + dot_nt(returned(kept_tail), w_conv[:, width:]),
        "shard",
        scatter_dimension=0,
        tiled=True,
    )
    given = x_in.astype(F32)
    given_rms = lax.rsqrt(jnp.mean(given * given, axis=1, keepdims=True) + EPSILON)
    grad_norm_gain = jnp.sum(grad_normed * (given * given_rms), axis=0)
    scaled = grad_normed * norm_gain[None, :]
    grad_resid = scaled * given_rms - given * (
        given_rms**3 * jnp.mean(scaled * given, axis=1, keepdims=True)
    )
    back_mine = lax.dynamic_slice_in_dim(back, mine * rows, rows, axis=0)
    grad_in = (grad_resid + dot_nn(back_mine, branch_grad)).astype(BF)

    def to_owners(columns):
        part = dot_tn(normed, columns).reshape(shards, depth, columns.shape[1])
        swapped = lax.all_to_all(part, "shard", split_axis=0, concat_axis=0, tiled=True)
        summed = lax.psum(swapped, "rep")
        return summed.transpose(1, 0, 2).reshape(depth, shards * columns.shape[1])

    grad_w_tail = lax.psum(
        dot_tn(columns_at(normed, mine * depth, depth), grad_tail[:, :TAIL]), "rep"
    )
    grad_w_in = jnp.concatenate([to_owners(grad_gate), to_owners(grad_values), grad_w_tail], axis=1)

    def placed(part):
        own = lax.dynamic_update_slice_in_dim(
            jnp.zeros((part.shape[0], DI), F32), part[:, :width], mine * width, axis=1
        )
        return jnp.concatenate([own, part[:, width:]], axis=1)

    summed = lax.psum(
        (
            grad_norm_gain,
            placed(grad_conv_w),
            placed(grad_conv_b)[0],
            grad_head,
            placed(grad_gain)[0],
            jnp.stack([square_total, square_branch, jnp.sum(weights_valid)]),
        ),
        ALL,
    )
    roots = jnp.sqrt(summed[5] / (jnp.maximum(summed[5][2], 1.0) * D))
    return (
        total_rows.astype(BF),
        grad_in,
        summed[0],
        grad_w_in,
        summed[1],
        summed[2],
        summed[3][0, :H],
        summed[3][1, :H],
        summed[3][2, :H],
        summed[4],
        grad_w_out,
        roots[0],
        roots[1],
    )


def on_device(
    x_in,
    cotangent,
    seq_lengths,
    seq_order,
    valid,
    norm_gain,
    w_in,
    conv_w,
    conv_b,
    dt_bias,
    a_log,
    d_skip,
    gated_gain,
    w_out,
):
    shards, mine = lax.axis_size("shard"), lax.axis_index("shard")
    reps = lax.axis_size("rep")
    rows = x_in.shape[0]
    length = rows * shards
    depth = w_in.shape[0]
    heads = H // shards
    width = DI // shards

    head_rows = jnp.pad(jnp.stack([dt_bias, a_log, d_skip]), ((0, 5), (0, 128 - H)))
    bias_row, gain_row = conv_b[None, :], gated_gain[None, :]
    spans = reps == LINE * PLANE and shards == 4 and width == reps * 128 and rows == 128
    if not spans:
        return plain_device(
            x_in,
            cotangent,
            seq_lengths,
            seq_order,
            valid,
            norm_gain,
            w_in,
            conv_w,
            bias_row,
            head_rows,
            gain_row,
            w_out,
        )
    norm_row, valid_column = norm_gain[None, :], valid[:, None]
    (
        normed,
        w_gate,
        w_conv,
        branch_grad,
        back,
        resid,
        inverse,
        line,
        normed_out,
        grad_gain,
        grad_values,
        grad_conv_w,
        grad_conv_b,
        grad_head,
        gate_taken,
        out_taken,
        gate_peer,
        gate_given,
        tail,
    ) = run_mixer(
        (
            seq_lengths,
            seq_order,
            x_in,
            cotangent,
            valid_column,
            norm_row,
            w_in.T,
            w_out,
            conv_w,
            bias_row,
            head_rows,
            gain_row,
        ),
        shards,
        True,
    )
    operands = (
        gate_taken,
        gate_peer,
        out_taken,
        gate_given,
        grad_values,
        tail,
        normed,
        line,
        inverse,
        w_gate,
        w_conv,
        w_out,
        normed_out,
        back,
        branch_grad,
        x_in,
        resid,
        valid_column,
        norm_row,
        grad_conv_w,
        grad_conv_b,
        grad_head,
        grad_gain,
    )
    (
        parts,
        w_out_parts,
        tails,
        block_out,
        grad_in,
        out_norm,
        out_conv_w,
        out_conv_b,
        out_head,
        out_gain,
    ) = run_end(operands, shards)
    grad_w_out = w_out_parts.reshape(width, D).astype(F32)
    grad_w_in = run_assemble(parts, tails).T
    return (
        block_out,
        grad_in,
        out_norm[0],
        grad_w_in,
        out_conv_w,
        out_conv_b[0],
        out_head[0, :H],
        out_head[1, :H],
        out_head[2, :H],
        out_gain[0],
        grad_w_out,
        out_head[3, 0],
        out_head[3, 1],
    )


def solution(mesh):
    in_specs = (
        P(ALL, None),
        P(ALL, None),
        P("rep", None),
        P("rep", None),
        P(ALL),
        P(),
        P("shard", None),
        P(),
        P(),
        P(),
        P(),
        P(),
        P(),
        P("shard", None),
    )
    out_specs = (
        P(ALL, None),
        P(ALL, None),
        P(),
        P("shard", None),
        P(),
        P(),
        P(),
        P(),
        P(),
        P(),
        P("shard", None),
        P(),
        P(),
    )
    return jax.shard_map(
        on_device, mesh=mesh, in_specs=in_specs, out_specs=out_specs, check_vma=False
    )
```

```python
import functools

import jax
import jax.numpy as jnp
from jax import lax
from jax.experimental import pallas as pl
from jax.experimental.pallas import tpu as pltpu
from jax.sharding import PartitionSpec as P

D = 2048
H = 64
P_SIZE = 64
N = 128
KW = 4
SPAN = 128
DI = 4096
CONVW = 4352
PROJ = 8512
TAIL = PROJ - 2 * DI

EPSILON = 1e-05
ALL = ("rep", "shard")
VMEM_BYTES = 58 * 1024 * 1024
BF = jnp.bfloat16
F32 = jnp.float32


def dot_nn(a, b):
    return lax.dot_general(a, b, (((1,), (0,)), ((), ())), preferred_element_type=F32)


def dot_nt(a, b):
    return lax.dot_general(a, b, (((1,), (1,)), ((), ())), preferred_element_type=F32)


def dot_tn(a, b):
    return lax.dot_general(a, b, (((0,), (0,)), ((), ())), preferred_element_type=F32)


def halves(a):
    high = a.astype(BF)
    return high, (a - high.astype(F32)).astype(BF)


def slot_tables(seq_lengths, seq_order, slot_ids):
    seq_count = seq_lengths.shape[0]
    numbers = jnp.arange(seq_count, dtype=jnp.int32)
    chosen = (seq_order[:, None] == numbers[None, :]).astype(jnp.int32)
    given_start = jnp.cumsum(seq_lengths) - seq_lengths
    owner_length = jnp.sum(chosen * seq_lengths[None, :], axis=1)
    owner_start = jnp.cumsum(owner_length) - owner_length
    owner_from = jnp.sum(chosen * given_start[None, :], axis=1)
    placed_at = jnp.sum(chosen * owner_start[:, None], axis=0)
    column = slot_ids[:, None]
    within = (column >= owner_start[None, :]) & (column < (owner_start + owner_length)[None, :])
    offset = column - owner_start[None, :]
    source = jnp.sum(jnp.where(within, offset + owner_from[None, :], 0), axis=1)
    position = jnp.sum(jnp.where(within, offset, 0), axis=1)
    given_within = (column >= given_start[None, :]) & (
        column < (given_start + seq_lengths)[None, :]
    )
    target = jnp.sum(
        jnp.where(given_within, column - given_start[None, :] + placed_at[None, :], 0), axis=1
    )
    return (source, target, position)


def params():
    return pltpu.CompilerParams(vmem_limit_bytes=VMEM_BYTES)


def spread_rows(row):
    return jnp.broadcast_to(row, (16, row.shape[1]))


def sigmoid(v):
    return 1.0 / (1.0 + jnp.exp(-v))


def spread(column, lanes=128):
    return jnp.broadcast_to(column, (column.shape[0], lanes))


MESH = pl.DeviceIdType.MESH
LINE, PLANE = 4, 2
CHUNK = 256
TAIL_PAD = 384


def remote(src, dst, send_sem, recv_sem, device):
    return pltpu.make_async_remote_copy(
        src_ref=src,
        dst_ref=dst,
        send_sem=send_sem,
        recv_sem=recv_sem,
        device_id=device,
        device_id_type=MESH,
    )


def meet(devices):
    barrier = pltpu.get_barrier_semaphore()
    for device in devices:
        pl.semaphore_signal(barrier, inc=1, device_id=device, device_id_type=MESH)
    pl.semaphore_wait(barrier, len(devices))


class Line:
    def __init__(self, store, first, share, send_sem, recv_sem):
        self.store, self.first, self.share = store, first, share
        self.send_sem, self.recv_sem = send_sem, recv_sem
        self.mine, self.rep = lax.axis_index("shard"), lax.axis_index("rep")
        self.z, self.x = self.rep // PLANE, lax.rem(self.rep, PLANE)
        self.sibling = self.mine // 2 * 2 + (1 - lax.rem(self.mine, 2))

    def along(self, origin, toward, first=False):
        block = self.store.at[origin, self.share]
        lane = (toward + 1) // 2
        return remote(
            self.first if first else block,
            block,
            self.send_sem.at[lane, origin],
            self.recv_sem.at[0, origin],
            ((self.z + toward) * PLANE + self.x, self.mine),
        )

    def inward(self, origin):
        block = self.store.at[origin, self.share]
        return remote(
            block,
            block,
            self.send_sem.at[2, origin],
            self.recv_sem.at[1, origin],
            (self.rep, self.sibling),
        )

    def start(self):
        for toward in (1, -1):
            self.guarded(toward, lambda: self.along(self.z, toward, True).start())

    def guarded(self, toward, act):
        pl.when(self.z < LINE - 1 if toward > 0 else self.z > 0)(act)

    def step(self, distance):
        for toward in (1, -1):
            origin = self.z - toward * distance

            @pl.when(origin >= 0 if toward > 0 else origin < LINE)
            def _():
                self.along(origin, toward).wait_recv()
                self.guarded(toward, lambda: self.along(origin, toward).start())
                self.inward(origin).start()

    def finish(self):
        for origin in range(LINE):

            @pl.when(origin != self.z)
            def _():
                self.inward(origin).wait_recv()
                self.inward(origin).wait_send()

            for toward in (1, -1):
                passed = origin <= self.z if toward > 0 else origin >= self.z
                pl.when(passed)(
                    lambda: self.guarded(toward, lambda: self.along(origin, toward).wait_send())
                )


def meet_with_line(devices):
    mine, rep = lax.axis_index("shard"), lax.axis_index("rep")
    z, x = rep // PLANE, lax.rem(rep, PLANE)
    barrier = pltpu.get_barrier_semaphore()
    for device in devices:
        pl.semaphore_signal(barrier, inc=1, device_id=device, device_id_type=MESH)
    for toward, there in ((1, z < LINE - 1), (-1, z > 0)):

        @pl.when(there)
        def _():
            pl.semaphore_signal(
                barrier, inc=1, device_id=((z + toward) * PLANE + x, mine), device_id_type=MESH
            )

    beyond = (z + LINE - 1) // LINE + (2 * (LINE - 1) - z) // LINE
    pl.semaphore_wait(barrier, len(devices) + beyond)


def tables_in_kernel(lengths_ref, order_ref, slots):
    count = lengths_ref.shape[1]
    lengths = [lengths_ref[0, i] for i in range(count)]
    order = [order_ref[0, i] for i in range(count)]
    given_start, at = [], jnp.int32(0)
    for i in range(count):
        given_start.append(at)
        at = at + lengths[i]
    source = jnp.zeros_like(slots)
    position = jnp.zeros_like(slots)
    placed_at = [jnp.int32(0)] * count
    at = jnp.int32(0)
    for k in range(count):
        length, start = jnp.int32(0), jnp.int32(0)
        for i in range(count):
            chosen = order[k] == i
            length = length + jnp.where(chosen, lengths[i], 0)
            start = start + jnp.where(chosen, given_start[i], 0)
            placed_at[i] = placed_at[i] + jnp.where(chosen, at, 0)
        within = (slots >= at) & (slots < at + length)
        source = source + jnp.where(within, slots - at + start, 0)
        position = position + jnp.where(within, slots - at, 0)
        at = at + length
    target = jnp.zeros_like(slots)
    for i in range(count):
        within = (slots >= given_start[i]) & (slots < given_start[i] + lengths[i])
        target = target + jnp.where(within, slots - given_start[i] + placed_at[i], 0)
    return source, target, position


def start_phases(
    lengths_ref,
    order_ref,
    x_ref,
    cotangent_ref,
    valid_ref,
    gain_ref,
    w_ref,
    normed_out_ref,
    w_gate_out_ref,
    w_conv_out_ref,
    branch_grad_out_ref,
    back_ref,
    resid_ref,
    inverse_ref,
    line_ref,
    conv_in_ref,
    gate_ref,
    grads,
    place_ref,
    x_all,
    normed,
    w_gate,
    w_conv,
    local_sem,
    row_send,
    row_recv,
    w_send,
    w_recv,
    w_local,
    line_send,
    line_recv,
):
    mine, rep = lax.axis_index("shard"), lax.axis_index("rep")
    y, c = mine // 2, lax.rem(mine, 2)
    z, x = rep // PLANE, lax.rem(rep, PLANE)
    sibling, peer, far = y * 2 + (1 - c), (1 - y) * 2 + c, (1 - y) * 2 + (1 - c)
    beside = z * PLANE + (1 - x)
    rows, length = x_ref.shape[0], x_all.shape[0]
    depth, width = w_ref.shape[1], gate_ref.shape[1]
    chunks = width // CHUNK
    tail_half = TAIL // 2

    part = pl.ds(pl.multiple_of(y * (D // 2), 128), D // 2)
    share = pl.ds(pl.multiple_of(c * (length // 2), 16), length // 2)
    wholes = (x_all, grads)

    lines = [
        Line(
            line_ref.at[kind],
            wholes[kind].at[share, part],
            share,
            line_send.at[kind],
            line_recv.at[kind],
        )
        for kind in range(2)
    ]

    def line_own(kind):
        return pltpu.make_async_copy(
            wholes[kind].at[:, part], line_ref.at[kind, z], local_sem.at[4 + kind]
        )

    def block(ref, shard):
        return ref.at[pl.ds(pl.multiple_of(shard * rows, rows), rows)]

    def row_copies(kind, own, store):
        return (
            remote(own, block(store, mine), row_send.at[kind, 0], row_recv.at[kind, 0], (rep, peer)),
            remote(own, block(store, mine), row_send.at[kind, 1], row_recv.at[kind, 1], (rep, sibling)),
            remote(
                block(store, peer),
                block(store, peer),
                row_send.at[kind, 2],
                row_recv.at[kind, 2],
                (rep, sibling),
            ),
        )

    def lanes(shard):
        return pl.ds(pl.multiple_of(shard * depth, depth), depth)

    def weight_copies(store, index, base, stride, at, half):
        share = pl.ds(pl.multiple_of(at + half * x, 16), half)
        both = pl.ds(pl.multiple_of((1 - y) * 2 * depth, 128), 2 * depth)

        def source(shard, start, count):
            return w_ref.at[pl.ds(pl.multiple_of(base + stride * shard + start, 16), count)]

        def sems(way):
            return w_send.at[way, index], w_recv.at[way, index]

        whole = pl.ds(pl.multiple_of(at, 16), 2 * half)
        near = at if stride else 0
        return (
            lambda: remote(
                source(peer, near + half * x, half), store.at[share, lanes(mine)], *sems(0), (rep, peer)
            ),
            lambda: remote(
                source(far, near + half * x, half), store.at[share, lanes(mine)], *sems(1), (rep, far)
            ),
            lambda: remote(store.at[share, both], store.at[share, both], *sems(2), (beside, mine)),
            lambda: remote(
                source(sibling, near, 2 * half), store.at[whole, lanes(mine)], *sems(3), (rep, sibling)
            ),
            lambda: pltpu.make_async_copy(
                source(mine, near, 2 * half), store.at[whole, lanes(mine)], w_local.at[index]
            ),
        )

    def conv_copies(q):
        return weight_copies(w_conv, q, DI, width, q * CHUNK, CHUNK // 2)

    def tail_copies():
        return weight_copies(w_conv, chunks, 2 * DI, 0, width, tail_half)

    def gate_copies(q):
        return weight_copies(w_gate, chunks + 1 + q, 0, width, q * CHUNK, CHUNK // 2)

    def send_near(copies):
        copies[3]().start()
        copies[4]().start()

    def send_far(copies):
        copies[0]().start()
        copies[1]().start()

    def pass_on(copies):
        copies[0]().wait_recv()
        copies[1]().wait_recv()
        copies[2]().start()
        copies[0]().wait_send()
        copies[1]().wait_send()

    def arrived(copies):
        copies[2]().wait_recv()
        copies[3]().wait_recv()
        copies[4]().wait()

    def each(count, body):
        def step(i, unused):
            body(i)
            return unused

        lax.fori_loop(0, count, step, 0)

    x_copies = row_copies(0, x_ref, x_all)
    grad_copies = row_copies(1, block(grads, mine), grads)
    own_rows = pltpu.make_async_copy(x_ref, block(x_all, mine), local_sem.at[0])
    convs = [conv_copies(q) for q in range(chunks)]
    gates = [gate_copies(q) for q in range(chunks)]
    tail = tail_copies()
    x_copies[0].start()
    x_copies[1].start()
    own_rows.start()
    for copies in convs + [tail] + gates:
        send_near(copies)
    grads[pl.ds(pl.multiple_of(mine * rows, rows), rows), :] = jnp.where(
        spread(valid_ref[...], D) > 0, cotangent_ref[...].astype(F32), 0.0
    ).astype(BF)
    grad_copies[0].start()
    grad_copies[1].start()
    w_conv[width + TAIL :, :] = jnp.zeros((TAIL_PAD - TAIL, D), BF)

    def table_block(i):
        span = pl.ds(pl.multiple_of(i * rows, rows), rows)
        slots = lax.broadcasted_iota(jnp.int32, (rows, length), 0) + i * rows
        across = lax.broadcasted_iota(jnp.int32, (rows, length), 1)
        target = tables_in_kernel(lengths_ref, order_ref, slots)[1]
        back_ref[span, :] = (target == across).astype(F32).astype(BF)
        few_slots = lax.broadcasted_iota(jnp.int32, (rows, 128), 0) + i * rows
        place_ref[span, :] = tables_in_kernel(lengths_ref, order_ref, few_slots)[2]

    each(length // rows, table_block)
    x_copies[0].wait_recv()
    x_copies[2].start()
    x_copies[0].wait_send()
    send_far(convs[0])
    send_far(convs[1])
    own_rows.wait()
    x_copies[1].wait_recv()
    x_copies[2].wait_recv()
    line_own(0).start()
    lines[0].start()

    def picked(i):
        slots = lax.broadcasted_iota(jnp.int32, (rows, length), 0) + i * rows
        across = lax.broadcasted_iota(jnp.int32, (rows, length), 1)
        source = tables_in_kernel(lengths_ref, order_ref, slots)[0]
        return dot_nn((source == across).astype(F32).astype(BF), x_all[...])

    def norm_block(i):
        span = pl.ds(pl.multiple_of(i * rows, rows), rows)
        resid = picked(i)
        inverse = lax.rsqrt(jnp.mean(resid * resid, axis=1, keepdims=True) + EPSILON)
        normed[span, :] = (resid * inverse * gain_ref[...]).astype(BF)

    each(length // rows // 2, norm_block)
    grad_copies[0].wait_recv()
    grad_copies[2].start()
    grad_copies[0].wait_send()
    send_far(convs[2])
    each(length // rows // 2, lambda i: norm_block(i + length // rows // 2))
    grad_copies[1].wait_recv()
    grad_copies[2].wait_recv()
    line_own(1).start()
    lines[1].start()
    pass_on(convs[0])
    send_far(convs[3])
    resid_ref[...] = picked(mine).astype(BF)
    normed_store = pltpu.make_async_copy(normed, normed_out_ref, local_sem.at[1])
    normed_store.start()

    def inverse_block(i):
        span = pl.ds(pl.multiple_of(i * rows, rows), rows)
        given = x_all[span, :].astype(F32)
        inverse_ref[span, :] = spread(
            lax.rsqrt(jnp.mean(given * given, axis=1, keepdims=True) + EPSILON)
        )

    def project(store, target, at, count):
        span = pl.ds(at, count)
        target[:, span] = dot_nt(normed[...], store[span, :]).astype(BF)

    def conv_chunk(q):
        arrived(convs[q])
        project(w_conv, conv_in_ref, q * CHUNK, CHUNK)

    def gate_chunk(q):
        arrived(gates[q])
        project(w_gate, gate_ref, q * CHUNK, CHUNK)

    pass_on(convs[1])
    send_far(tail)
    lines[0].step(1)
    each(length // rows, inverse_block)
    pass_on(convs[2])
    send_far(gates[0])
    conv_chunk(0)
    pass_on(convs[3])
    send_far(gates[1])
    lines[0].step(2)
    conv_chunk(1)
    pass_on(tail)
    send_far(gates[2])
    conv_chunk(2)
    send_far(gates[3])
    conv_chunk(3)
    arrived(tail)
    project(w_conv, conv_in_ref, width, TAIL_PAD)
    conv_store = pltpu.make_async_copy(w_conv, w_conv_out_ref, local_sem.at[2])
    conv_store.start()
    lines[1].step(1)
    yield
    pass_on(gates[0])
    lines[0].step(3)
    yield
    pass_on(gates[1])
    lines[1].step(2)
    gate_chunk(0)
    yield
    pass_on(gates[2])
    gate_chunk(1)
    pass_on(gates[3])
    gate_chunk(2)
    gate_chunk(3)
    gate_store = pltpu.make_async_copy(w_gate, w_gate_out_ref, local_sem.at[3])
    gate_store.start()
    grads_store = pltpu.make_async_copy(grads, branch_grad_out_ref, local_sem.at[6])
    grads_store.start()
    lines[1].step(3)
    yield
    for copies in convs + [tail] + gates:
        copies[2]().wait_send()
        copies[3]().wait_send()
    x_copies[1].wait_send()
    x_copies[2].wait_send()
    grad_copies[1].wait_send()
    grad_copies[2].wait_send()
    normed_store.wait()
    conv_store.wait()
    gate_store.wait()
    grads_store.wait()
    for kind in range(2):
        line_own(kind).wait()
        lines[kind].finish()
    yield


def conv_pre(x, conv_w, conv_b, place):
    pre = conv_b + conv_w[KW - 1 : KW] * x
    for back in range(1, KW):
        moved = pltpu.roll(x, back, 0)
        pre = pre + jnp.where(place >= back, conv_w[KW - 1 - back : KW - back] * moved, 0.0)
    return pre


def conv_lanes(chunk, width, mine):
    if 128 * chunk < width:
        return pl.ds(pl.multiple_of(mine * width + 128 * chunk, 128), 128)
    return pl.ds(DI + 128 * chunk - width, 128)


def block_terms(place):
    local = lax.broadcasted_iota(jnp.int32, (SPAN, 128), 0)
    across = lax.broadcasted_iota(jnp.int32, (SPAN, 128), 1)
    begins = local - place
    causal = (across <= local) & (across >= begins)
    reach_end = local >= begins[SPAN - 1 : SPAN, :]
    entered = place >= local + 1
    carries = place[SPAN - 1 : SPAN, :] >= SPAN
    return causal, reach_end, entered, carries


def pair_terms(pair, run, run_t, step, causal, reach_end, entered, carries):
    left = lax.broadcasted_iota(jnp.int32, (SPAN, 128), 1) < P_SIZE
    runs = [spread(run[:, 2 * pair + i : 2 * pair + i + 1]) for i in range(2)]
    decays = []
    for i in range(2):
        gap = runs[i] - run_t[2 * pair + i : 2 * pair + i + 1, :]
        decays.append(jnp.exp(jnp.where(causal, gap, -jnp.inf)))
    both = jnp.where(left, runs[0], runs[1])
    end = both[SPAN - 1 : SPAN, :]
    entering = jnp.where(entered, jnp.exp(both), 0.0)
    tail = jnp.where(reach_end, jnp.exp(jnp.where(reach_end, end - both, 0.0)), 0.0)
    carried = jnp.where(carries, jnp.exp(end), 0.0)
    size = jnp.where(
        left,
        spread(step[:, 2 * pair : 2 * pair + 1]),
        spread(step[:, 2 * pair + 1 : 2 * pair + 2]),
    )
    return left, decays, entering, tail, carried, size


def stacked(value, left):
    zero = jnp.zeros_like(value)
    return jnp.concatenate([jnp.where(left, value, zero), jnp.where(left, zero, value)], axis=0)


def own_lanes(row, mine, heads):
    return pltpu.roll(row, lax.rem(128 - mine * heads, 128), 1)


def skip_lanes(row, pair):
    left = lax.broadcasted_iota(jnp.int32, (1, 128), 1) < P_SIZE
    return jnp.where(
        left,
        spread(row[:, 2 * pair : 2 * pair + 1]),
        spread(row[:, 2 * pair + 1 : 2 * pair + 2]),
    )


def step_and_run(conv_in_ref, heads_ref, run_ref, step_ref, width, mine):
    length = run_ref.shape[0]
    heads = width // P_SIZE
    lower = (
        lax.broadcasted_iota(jnp.int32, (SPAN, SPAN), 0)
        >= lax.broadcasted_iota(jnp.int32, (SPAN, SPAN), 1)
    ).astype(F32)
    bias = heads_ref[0:1, :]
    rate = jnp.exp(own_lanes(heads_ref[...], mine, heads)[1:2, :])

    def block(b, unused):
        rows = pl.ds(pl.multiple_of(b * SPAN, SPAN), SPAN)
        raw = conv_in_ref[rows, width + 2 * N : width + 2 * N + 128].astype(F32)
        step = own_lanes(jax.nn.softplus(raw + bias), mine, heads)
        step_ref[rows, :] = step
        run_ref[rows, :] = jnp.dot(
            lower, -step * rate, precision=lax.Precision.HIGHEST, preferred_element_type=F32
        )
        return unused

    lax.fori_loop(0, length // SPAN, block, 0)


def along_line(step):
    rep = lax.axis_index("rep")
    there = lax.rem(rep // PLANE + step, LINE)
    return there * PLANE + lax.rem(rep, PLANE), there


def share_copy(source, taken, send_sem, recv_sem, step):
    to, there = along_line(step)
    z, wide = lax.axis_index("rep") // PLANE, taken.shape[2]
    return remote(
        source.at[:, pl.ds(pl.multiple_of(there * wide, 128), wide)],
        taken.at[z],
        send_sem.at[step],
        recv_sem.at[z],
        (to, lax.axis_index("shard")),
    )


def share_own(source, taken, sem):
    z, wide = lax.axis_index("rep") // PLANE, taken.shape[2]
    return pltpu.make_async_copy(
        source.at[:, pl.ds(pl.multiple_of(z * wide, 128), wide)], taken.at[z], sem
    )


def share_start(source, taken, send_sem, recv_sem, own):
    own.start()
    for step in range(1, LINE):
        share_copy(source, taken, send_sem, recv_sem, step).start()


def share_arrival(taken, recv_sem, own, step):
    to, there = along_line(step)
    if step == 0:
        own.wait()
    else:
        block, sem = taken.at[there], recv_sem.at[there]
        remote(block, block, sem, sem, (to, lax.axis_index("shard"))).wait_recv()
    return there


def share_sent(source, taken, send_sem, recv_sem):
    for step in range(1, LINE):
        share_copy(source, taken, send_sem, recv_sem, step).wait_send()


def in_given_order(back_ref, inverse_ref, grad_ref, given_ref, scaled_ref):
    length, width = grad_ref.shape

    def block(i, unused):
        span = pl.ds(pl.multiple_of(i * SPAN, SPAN), SPAN)
        moved = dot_nn(back_ref[span, :], grad_ref[...])
        if given_ref is not None:
            given_ref[span, :] = moved.astype(BF)
        for c in range(width // 128):
            lanes = slice(128 * c, 128 * c + 128)
            scaled_ref[span, lanes] = (moved[:, lanes] * inverse_ref[span, :]).astype(BF)
        return unused

    lax.fori_loop(0, length // SPAN, block, 0)


class RowSum:
    def __init__(self, partial, pair_in, row_out, row_in, send_sem, recv_sem):
        self.partial, self.pair_in, self.row_out, self.row_in = partial, pair_in, row_out, row_in
        self.rows = row_in.shape[0]
        mine, rep = lax.axis_index("shard"), lax.axis_index("rep")
        self.y, self.core = mine // 2, lax.rem(mine, 2)
        sibling, peer = self.y * 2 + (1 - self.core), (1 - self.y) * 2 + self.core
        self.pairs = [
            remote(
                partial.at[self.span(2 * side + (1 - self.core))],
                pair_in.at[side],
                send_sem.at[side],
                recv_sem.at[side],
                (rep, sibling),
            )
            for side in range(2)
        ]
        self.across = remote(row_out, row_in, send_sem.at[2], recv_sem.at[2], (rep, peer))

    def span(self, shard):
        return pl.ds(pl.multiple_of(shard * self.rows, self.rows), self.rows)

    def fill(self, rows_of):
        def block(i, unused):
            span = self.span(i)
            self.partial[span, :] = rows_of(span)
            return unused

        lax.fori_loop(0, self.partial.shape[0] // self.rows, block, 0)
        for copy in self.pairs:
            copy.start()

    def join(self):
        for copy in self.pairs:
            copy.wait_recv()
        there = self.span(2 * (1 - self.y) + self.core)
        self.row_out[...] = (self.pair_in[1 - self.y] + self.partial[there, :]).astype(BF)
        self.across.start()

    def result(self):
        self.across.wait_recv()
        here = self.partial[self.span(2 * self.y + self.core), :]
        return self.pair_in[self.y] + here + self.row_in[...].astype(F32)

    def finish(self):
        for copy in self.pairs + [self.across]:
            copy.wait_send()


def mixer_kernel(spans, *refs):
    refs = list(refs)

    def take(count):
        taken, refs[:] = refs[:count], refs[count:]
        return taken

    if spans:
        start_in = take(7)
        w_out_hbm, conv_w_ref, conv_b_ref, heads_ref, gain_ref = take(5)
        start_out = take(8)
        normed_out_ref, grad_gain_ref, grad_values_ref = take(3)
    else:
        conv_in_ref, gate_ref, branch_grad_ref, w_out_ref, place_ref = take(5)
        conv_w_ref, conv_b_ref, heads_ref, gain_ref = take(4)
        normed_out_ref, grad_gate_ref, grad_gain_ref, grad_values_ref, grad_tail_ref = take(5)
    grad_conv_w_ref, grad_conv_b_ref, grad_head_ref = take(3)
    if spans:
        taken_ref, taken_out_ref, gate_peer_ref = take(3)
        gate_given_ref, tail_ref = take(2)
    (
        mixed_ref,
        starts_ref,
        grad_mixed_ref,
        act_ref,
        pre_ref,
        step_ref,
        run_ref,
        state_ref,
        gno_ref,
        sums,
        grad_act_ref,
        joined_ref,
        join_ref,
        send_sem,
        recv_sem,
    ) = take(15)
    if spans:
        start_scratch = take(8)
        start_sems = take(8)
        conv_in_ref, gate_ref, branch_grad_ref, place_ref = start_scratch[:4]
        back_ref, inverse_ref = start_out[4], start_out[6]
        w_out_ref, grad_gate_ref, grad_tail_ref, scaled_ref, tail_in = take(5)
        share_send, share_recv, own_sem, peer_send, peer_recv, tail_send, tail_recv = take(7)
    length, width = gate_ref.shape
    mine, rep, shards = lax.axis_index("shard"), lax.axis_index("rep"), lax.axis_size("shard")
    heads = width // P_SIZE
    peers = [(rep, lax.rem(mine + step, shards)) for step in range(1, shards)]
    if spans:
        y, core = mine // 2, lax.rem(mine, 2)
        sibling, peer = y * 2 + (1 - core), (1 - y) * 2 + core
        others = [lax.rem(mine + step, shards) for step in range(1, shards)]
        rows = length // shards
        beside = rep // PLANE * PLANE + (1 - lax.rem(rep, PLANE))
        meet([(along_line(step)[0], mine) for step in range(1, LINE)] + [(beside, mine)] + peers)
        w_out_load = pltpu.make_async_copy(w_out_hbm, w_out_ref, own_sem.at[2])
        w_out_load.start()
        start = start_phases(*start_in, *start_out, *start_scratch, *start_sems)
        next(start)
    else:
        meet(peers)
    for c in range((width + 2 * N) // 128):
        lanes = slice(128 * c, 128 * c + 128)
        there = conv_lanes(c, width, mine)
        pre = conv_pre(
            conv_in_ref[:, lanes].astype(F32),
            conv_w_ref[:, there],
            conv_b_ref[:, there],
            place_ref[...],
        )
        pre_ref[:, lanes] = pre
        act_ref[:, lanes] = (pre * sigmoid(pre)).astype(BF)
    step_and_run(conv_in_ref, heads_ref, run_ref, step_ref, width, mine)
    if spans:
        next(start)
    state_ref[...] = jnp.zeros_like(state_ref)
    skips = own_lanes(heads_ref[...], mine, heads)[2:3, :]

    def forward_block(b, unused):
        row = pl.multiple_of(b * SPAN, SPAN)
        rows = pl.ds(row, SPAN)
        starts_ref[pl.ds(pl.multiple_of(b * N, N), N), :] = state_ref[...]
        run = run_ref[rows, :]
        run_t = run.T
        step = step_ref[rows, :]
        masks = block_terms(place_ref[rows, :])
        in_map = act_ref[rows, width : width + N]
        out_map = act_ref[rows, width + N : width + 2 * N]
        products = dot_nt(out_map, in_map)
        in_map_t = in_map.T
        for pair in range(width // 128):
            lanes = slice(128 * pair, 128 * pair + 128)
            left, decays, entering, tail, carried, size = pair_terms(
                pair, run, run_t, step, *masks
            )
            values = act_ref[rows, lanes].astype(F32)
            scaled = values * size
            weights = jnp.concatenate([(d * products).astype(BF) for d in decays], axis=1)
            out = dot_nn(weights, stacked(scaled.astype(BF), left))
            state = state_ref[:, lanes]
            high, low = halves(state)
            out += entering * (dot_nn(out_map, high) + dot_nn(out_map, low))
            mixed_ref[rows, lanes] = out + skip_lanes(skips, pair) * values
            high, low = halves(tail * scaled)
            fresh = dot_nn(in_map_t, high) + dot_nn(in_map_t, low)
            state_ref[:, lanes] = carried * state + fresh
        return unused

    halfway = length // SPAN // 2
    lax.fori_loop(0, halfway, forward_block, 0)
    if spans:
        next(start)
    lax.fori_loop(halfway, length // SPAN, forward_block, 0)
    if spans:
        next(start)
        w_out_load.wait()

    lane = lax.broadcasted_iota(jnp.int32, (SPAN, 128), 1)

    def gated(rows, c):
        lanes = slice(128 * c, 128 * c + 128)
        gate = gate_ref[rows, lanes].astype(F32)
        opened = sigmoid(gate)
        mixed = mixed_ref[rows, lanes]
        back = gno_ref[rows, lanes]
        gain = gain_ref[:, pl.ds(pl.multiple_of(mine * width + 128 * c, 128), 128)]
        return gate, opened, mixed, back, gain, mixed * (gate * opened), back * gain

    def measure(b, unused):
        rows = pl.ds(pl.multiple_of(b * SPAN, SPAN), SPAN)
        gno_ref[rows, :] = dot_nt(branch_grad_ref[rows, :], w_out_ref[...])
        squares = jnp.zeros((SPAN, 128), F32)
        crosses = jnp.zeros((SPAN, 128), F32)
        for c in range(width // 128):
            product, weighted = gated(rows, c)[5:]
            squares += product * product
            crosses += weighted * product
        squares = jnp.sum(squares, axis=1, keepdims=True)
        crosses = jnp.sum(crosses, axis=1, keepdims=True)
        both = jnp.where(lane == 0, spread(squares), jnp.where(lane == 1, spread(crosses), 0.0))
        sums[mine, :, rows] = both.T[0:8, :]
        return unused

    lax.fori_loop(0, length // SPAN, measure, 0)

    copies = [
        remote(sums.at[mine], sums.at[mine], send_sem.at[i], recv_sem.at[i], peer)
        for i, peer in enumerate(peers)
    ]
    for copy in copies:
        copy.start()
    for copy in copies:
        copy.wait_recv()
    grad_gain_ref[...] = jnp.zeros_like(grad_gain_ref)

    def finish(b, unused):
        rows = pl.ds(pl.multiple_of(b * SPAN, SPAN), SPAN)
        both = sums[0, :, rows]
        for shard in range(1, shards):
            both = both + sums[shard, :, rows]
        both = jnp.concatenate([both, jnp.zeros((SPAN - 8, SPAN), F32)], axis=0).T / DI
        inverse = lax.rsqrt(both[:, 0:1] + EPSILON)
        pull = spread(inverse * inverse * inverse * both[:, 1:2])
        inverse = spread(inverse)
        for c in range(width // 128):
            lanes = slice(128 * c, 128 * c + 128)
            gate, opened, mixed, back, gain, product, weighted = gated(rows, c)
            normalized = product * inverse
            normed_out_ref[rows, lanes] = (normalized * gain).astype(BF)
            grad_product = inverse * weighted - product * pull
            grad_gain_ref[:, lanes] += jnp.sum(back * normalized, axis=0, keepdims=True)
            grad_mixed_ref[rows, lanes] = grad_product * (gate * opened)
            grad_gate_ref[rows, lanes] = (
                grad_product * mixed * (opened * (1.0 + gate * (1.0 - opened)))
            ).astype(BF)
        return unused

    lax.fori_loop(0, length // SPAN, finish, 0)
    for copy in copies:
        copy.wait_send()
    if spans:
        exchanges = ((scaled_ref, taken_ref), (normed_out_ref, taken_out_ref))
        own_shares = [share_own(*pair, own_sem.at[i]) for i, pair in enumerate(exchanges)]

        def gate_peer_copy(at):
            return remote(
                taken_ref.at[at], gate_peer_ref.at[at], peer_send.at[at], peer_recv.at[at], (rep, peer)
            )

        def row_block(ref, shard):
            return ref.at[pl.ds(pl.multiple_of(shard * rows, rows), rows)]

        tail_out = [
            remote(
                row_block(grad_tail_ref, other),
                tail_in.at[i],
                tail_send.at[0, i],
                tail_recv.at[0, i],
                (rep, other),
            )
            for i, other in enumerate(others)
        ]
        tail_back = [
            remote(
                row_block(tail_ref, mine),
                row_block(tail_ref, mine),
                tail_send.at[1, i],
                tail_recv.at[1, i],
                (rep, other),
            )
            for i, other in enumerate(others)
        ]
        in_given_order(back_ref, inverse_ref, grad_gate_ref, gate_given_ref, scaled_ref)
        share_start(*exchanges[0], share_send.at[0], share_recv.at[0], own_shares[0])
    state_ref[...] = jnp.zeros_like(state_ref)
    grad_head_ref[...] = jnp.zeros_like(grad_head_ref)
    upper = (
        lax.broadcasted_iota(jnp.int32, (SPAN, SPAN), 0)
        <= lax.broadcasted_iota(jnp.int32, (SPAN, SPAN), 1)
    ).astype(F32)
    last_row = lax.broadcasted_iota(jnp.int32, (SPAN, 128), 0) == SPAN - 1
    join_ref[...] = (
        lax.broadcasted_iota(jnp.int32, (width, 128), 0) // P_SIZE + mine * heads
        == lax.broadcasted_iota(jnp.int32, (width, 128), 1)
    ).astype(F32).astype(BF)

    blocks = length // SPAN

    def backward_block(count, unused):
        b = blocks - 1 - count
        row = pl.multiple_of(b * SPAN, SPAN)
        rows = pl.ds(row, SPAN)
        start_rows = pl.ds(pl.multiple_of(b * N, N), N)
        run = run_ref[rows, :]
        run_t = run.T
        step = step_ref[rows, :]
        masks = block_terms(place_ref[rows, :])
        in_map = act_ref[rows, width : width + N]
        out_map = act_ref[rows, width + N : width + 2 * N]
        out_map_t = out_map.T
        products = dot_nt(out_map, in_map)
        grad_products = jnp.zeros((SPAN, SPAN), F32)
        grad_out_map = jnp.zeros((SPAN, N), F32)
        grad_in_map = jnp.zeros((SPAN, N), F32)
        for pair in range(width // 128):
            lanes = slice(128 * pair, 128 * pair + 128)
            left, decays, entering, tail, carried, size = pair_terms(
                pair, run, run_t, step, *masks
            )
            values = act_ref[rows, lanes].astype(F32)
            grad = grad_mixed_ref[rows, lanes]
            start = starts_ref[start_rows, lanes]
            later = state_ref[:, lanes]
            scaled = values * size
            scaled_low = scaled.astype(BF)
            grad_low = grad.astype(BF)
            weights = jnp.concatenate([(d * products).astype(BF) for d in decays], axis=0)
            grad_scaled = dot_tn(weights, stacked(grad_low, left))
            grad_pairs = dot_nt(grad_low, stacked(scaled_low, left))
            grad_products += (
                grad_pairs[:, :SPAN] * decays[0] + grad_pairs[:, SPAN:] * decays[1]
            )
            later_high, later_low = halves(later)
            from_later = tail * (dot_nn(in_map, later_high) + dot_nn(in_map, later_low))
            grad_scaled += from_later
            entering_high, entering_low = halves(entering * grad)
            grad_out_map += dot_nt(entering_high, start.astype(BF))
            grad_in_map += dot_nt((tail * scaled).astype(BF), later_high)
            ending = jnp.sum(scaled * from_later, axis=0, keepdims=True) + carried * jnp.sum(
                start * later, axis=0, keepdims=True
            )
            state_ref[:, lanes] = (
                carried * later + dot_nn(out_map_t, entering_high) + dot_nn(out_map_t, entering_low)
            )
            skip = skip_lanes(skips, pair)
            inner = mixed_ref[rows, lanes] - skip * values
            joined_ref[0:SPAN, lanes] = (
                grad_low.astype(F32) * inner
                - scaled_low.astype(F32) * (grad_scaled - from_later)
                - scaled * from_later
                + jnp.where(last_row, ending, 0.0)
            )
            joined_ref[SPAN : 2 * SPAN, lanes] = grad_scaled * values
            joined_ref[2 * SPAN : 2 * SPAN + 16, lanes] = spread_rows(
                jnp.sum(grad * values, axis=0, keepdims=True)
            )
            grad_act_ref[rows, lanes] = grad_scaled * size + skip * grad
        grad_products = grad_products.astype(BF)
        grad_act_ref[rows, width : width + N] = grad_in_map + dot_tn(grad_products, out_map)
        grad_act_ref[rows, width + N : width + 2 * N] = grad_out_map + dot_nn(
            grad_products, in_map
        )
        joined = joined_ref[...]
        first = joined.astype(BF)
        second, third = halves(joined - first.astype(F32))
        join = join_ref[...]
        by_head = dot_nn(first, join) + dot_nn(second, join) + dot_nn(third, join)
        grad_log = jnp.dot(
            upper, by_head[:SPAN], precision=lax.Precision.HIGHEST, preferred_element_type=F32
        )
        rate = jnp.exp(heads_ref[1:2, :])
        raw = conv_in_ref[rows, width + 2 * N : width + 2 * N + 128].astype(F32) + heads_ref[0:1, :]
        grad_dt = (by_head[SPAN : 2 * SPAN] - grad_log * rate) * sigmoid(raw)
        grad_tail_ref[rows, 2 * N : 2 * N + 128] = grad_dt
        grad_head_ref[0:1, :] += jnp.sum(grad_dt, axis=0, keepdims=True)
        grad_head_ref[1:2, :] += jnp.sum(
            -grad_log * jax.nn.softplus(raw) * rate, axis=0, keepdims=True
        )
        grad_head_ref[2:3, :] += by_head[2 * SPAN : 2 * SPAN + 1]
        return unused

    if spans:
        lax.fori_loop(0, blocks - 1, backward_block, 0)
        for step in range(LINE):
            at = share_arrival(taken_ref, share_recv.at[0], own_shares[0], step)
            gate_peer_copy(at).start()
        lax.fori_loop(blocks - 1, blocks, backward_block, 0)
        share_start(*exchanges[1], share_send.at[1], share_recv.at[1], own_shares[1])
    else:
        lax.fori_loop(0, blocks, backward_block, 0)

    place = place_ref[...]
    own_chunks = width // 128
    for c in [own_chunks, own_chunks + 1] + list(range(own_chunks)):
        lanes = slice(128 * c, 128 * c + 128)
        x = conv_in_ref[:, lanes].astype(F32)
        conv_w = conv_w_ref[:, conv_lanes(c, width, mine)]
        pre = pre_ref[:, lanes]
        gain = sigmoid(pre)
        grad_pre = grad_act_ref[:, lanes] * (gain * (1.0 + pre * (1.0 - gain)))
        grad_conv_b_ref[:, lanes] = jnp.sum(grad_pre, axis=0, keepdims=True)
        grad_conv_w_ref[KW - 1 : KW, lanes] = jnp.sum(grad_pre * x, axis=0, keepdims=True)
        grad_x = conv_w[KW - 1 : KW] * grad_pre
        for back in range(1, KW):
            tap = KW - 1 - back
            kept = jnp.where(place >= back, grad_pre, 0.0)
            grad_conv_w_ref[tap : tap + 1, lanes] = jnp.sum(
                kept * pltpu.roll(x, back, 0), axis=0, keepdims=True
            )
            grad_x += conv_w[tap : tap + 1] * pltpu.roll(kept, length - back, 0)
        if c < width // 128:
            grad_values_ref[:, lanes] = grad_x.astype(BF)
        else:
            grad_tail_ref[:, 128 * c - width : 128 * c - width + 128] = grad_x
        if spans and c == own_chunks + 1:
            for copy in tail_out:
                copy.start()
    if spans:
        span = pl.ds(pl.multiple_of(mine * rows, rows), rows)
        tail = grad_tail_ref[span, :]
        for i, copy in enumerate(tail_out):
            copy.wait_recv()
            tail = tail + tail_in[i]
        tail_ref[span, :] = tail.astype(BF)
        for copy in tail_back:
            copy.start()
        for step in range(LINE):
            share_arrival(taken_out_ref, share_recv.at[1], own_shares[1], step)
        for i, pair in enumerate(exchanges):
            share_sent(*pair, share_send.at[i], share_recv.at[i])
        for at in range(LINE):
            gate_peer_copy(at).wait()
        for copy in tail_out:
            copy.wait_send()
        for copy in tail_back:
            copy.wait()
        next(start)


def run_mixer(operands, shards, spans):
    if spans:
        rows = operands[2].shape[0]
        length, width = rows * shards, DI // shards
    else:
        length, width = operands[1].shape
        rows = length // shards
    blocks, chunks = length // SPAN, width // CHUNK
    shape = jax.ShapeDtypeStruct
    vector = pl.BlockSpec(memory_space=pltpu.VMEM)
    anywhere = pl.BlockSpec(memory_space=pl.ANY)
    scalars = pl.BlockSpec(memory_space=pltpu.SMEM)
    dma = pltpu.SemaphoreType.DMA
    small = [
        shape((KW, width + 2 * N), F32),
        shape((1, width + 2 * N), F32),
        shape((8, 128), F32),
    ]
    scratch = [
        pltpu.VMEM((length, width), F32),
        pltpu.VMEM((blocks * N, width), F32),
        pltpu.VMEM((length, width), F32),
        pltpu.VMEM((length, width + 2 * N), BF),
        pltpu.VMEM((length, width + 2 * N), F32),
        pltpu.VMEM((length, 128), F32),
        pltpu.VMEM((length, 128), F32),
        pltpu.VMEM((N, width), F32),
        pltpu.VMEM((length, width), F32),
        pltpu.VMEM((shards, 8, length), F32),
        pltpu.VMEM((length, width + 2 * N), F32),
        pltpu.VMEM((2 * SPAN + 16, width), F32),
        pltpu.VMEM((width, 128), BF),
        dma((shards - 1,)),
        dma((shards - 1,)),
    ]
    if spans:
        taken = shape((LINE, length, 2 * 128), BF)
        outs = [
            (shape((length, D), BF), anywhere),
            (shape((width, D), BF), anywhere),
            (shape((width + TAIL_PAD, D), BF), anywhere),
            (shape((length, D), BF), anywhere),
            (shape((length, length), BF), vector),
            (shape((rows, D), BF), vector),
            (shape((length, 128), F32), vector),
            (shape((2, LINE, length, D // 2), BF), anywhere),
            (shape((length, width), BF), vector),
            (shape((1, width), F32), vector),
            (shape((length, width), BF), vector),
            *[(one, vector) for one in small],
            (taken, anywhere),
            (taken, anywhere),
            (taken, anywhere),
            (shape((length, width), BF), vector),
            (shape((length, TAIL_PAD), BF), vector),
        ]
        in_specs = [scalars, scalars, anywhere, vector, vector, vector, anywhere, anywhere]
        in_specs += [vector] * 4
        weights = 2 * chunks + 1
        scratch += [
            pltpu.VMEM((length, width + TAIL_PAD), BF),
            pltpu.VMEM((length, width), BF),
            pltpu.VMEM((length, D), BF),
            pltpu.VMEM((length, 128), jnp.int32),
            pltpu.VMEM((length, D), BF),
            pltpu.VMEM((length, D), BF),
            pltpu.VMEM((width, D), BF),
            pltpu.VMEM((width + TAIL_PAD, D), BF),
            dma((7,)),
            dma((2, 3)),
            dma((2, 3)),
            dma((4, weights)),
            dma((4, weights)),
            dma((weights,)),
            dma((2, 3, LINE)),
            dma((2, 2, LINE)),
            pltpu.VMEM((width, D), BF),
            pltpu.VMEM((length, width), BF),
            pltpu.VMEM((length, TAIL_PAD), F32),
            pltpu.VMEM((length, width), BF),
            pltpu.VMEM((shards - 1, rows, TAIL_PAD), F32),
            dma((2, LINE)),
            dma((2, LINE)),
            dma((3,)),
            dma((LINE,)),
            dma((LINE,)),
            dma((2, shards - 1)),
            dma((2, shards - 1)),
        ]
    else:
        wide = shape((length, width), BF)
        outs = [wide, wide, shape((1, width), F32), wide, shape((length, TAIL_PAD), F32), *small]
        outs = [(one, vector) for one in outs]
        in_specs = [vector] * 9
    return pl.pallas_call(
        functools.partial(mixer_kernel, spans),
        out_shape=tuple(out for out, spec in outs),
        in_specs=in_specs,
        out_specs=tuple(spec for out, spec in outs),
        scratch_shapes=scratch,
        compiler_params=pltpu.CompilerParams(
            vmem_limit_bytes=VMEM_BYTES, collective_id=2, has_side_effects=True
        ),
        cost_estimate=pl.CostEstimate(
            flops=60 * length * width * 128, bytes_accessed=32 * length * width, transcendentals=0
        ),
        name="mixer",
    )(*operands)


def end_kernel(
    gate_taken_hbm,
    gate_peer_hbm,
    out_taken_hbm,
    gate_given_ref,
    values_ref,
    tail_low,
    normed_ref,
    line_ref,
    inverse_ref,
    w_gate_hbm,
    w_conv_hbm,
    w_out_hbm,
    normed_out_hbm,
    back_ref,
    branch_grad_hbm,
    x_ref,
    resid_ref,
    valid_ref,
    gain_ref,
    grad_conv_w_ref,
    grad_conv_b_ref,
    grad_head_ref,
    grad_gain_ref,
    parts_ref,
    w_out_grad_ref,
    tails_ref,
    block_out_ref,
    grad_in_ref,
    out_norm_ref,
    out_conv_w_ref,
    out_conv_b_ref,
    out_head_ref,
    out_gain_ref,
    taken,
    taken_peer,
    values_given_ref,
    scaled_ref,
    group_rows,
    own_columns,
    total,
    sum_kept,
    mail_out,
    mail_in,
    low,
    partial,
    pair_in,
    row_out,
    row_in,
    branch_pair,
    branch_out,
    branch_in,
    tail_sum,
    tail_own,
    tail_parts,
    small,
    small_in,
    small_all,
    w_gate_ref,
    w_conv_ref,
    branch_grad_ref,
    w_out_ref,
    normed_out_ref,
    load_sem,
    local_sem,
    group_sem,
    share_send,
    share_recv,
    peer_send,
    peer_recv,
    mail_send,
    mail_recv,
    swap_send,
    swap_recv,
    line_send,
    line_recv,
    side_send,
    side_recv,
    cross_send,
    cross_recv,
    pair_send,
    pair_recv,
    branch_send,
    branch_recv,
    rep_send,
    rep_recv,
    all_send,
    all_recv,
):
    reps, shards = LINE * PLANE, lax.axis_size("shard")
    mine, rep = lax.axis_index("shard"), lax.axis_index("rep")
    y, c = mine // 2, lax.rem(mine, 2)
    z, x = rep // PLANE, lax.rem(rep, PLANE)
    beside = z * PLANE + (1 - x)
    rows, length = x_ref.shape[0], values_ref.shape[0]
    width, depth = values_ref.shape[1], own_columns.shape[1]
    half = D // 2
    sibling, peer = y * 2 + (1 - c), (1 - y) * 2 + c

    def other(step):
        return lax.rem(z + step // PLANE, LINE) * PLANE + lax.rem(x + step % PLANE, PLANE)

    def before(step):
        return lax.rem(z + LINE - step // PLANE, LINE) * PLANE + lax.rem(
            x + PLANE - step % PLANE, PLANE
        )

    def shard_at(step):
        return lax.rem(mine + step, shards)

    def each(count, body):
        def step(i, unused):
            body(i)
            return unused

        lax.fori_loop(0, count, step, 0)

    meet(
        [(other(step), mine) for step in range(1, reps)]
        + [(rep, shard_at(step)) for step in range(1, shards)]
    )

    loads = [
        pltpu.make_async_copy(far_ref, near_ref, load_sem.at[i])
        for i, (far_ref, near_ref) in enumerate(
            [
                (w_gate_hbm, w_gate_ref),
                (w_conv_hbm, w_conv_ref),
                (branch_grad_hbm, branch_grad_ref),
                (w_out_hbm, w_out_ref),
                (normed_out_hbm, normed_out_ref),
            ]
        )
    ]

    def group_copy(part, step):
        at = along_line(step)[1]
        return pltpu.make_async_copy(
            line_ref.at[part // 2, at], group_rows.at[step], group_sem.at[step]
        )

    def peer_copy(part, at):
        return remote(
            taken.at[part, at],
            taken_peer.at[part, at],
            peer_send.at[part, at],
            peer_recv.at[part, at],
            (rep, peer),
        )

    own_part = pltpu.make_async_copy(
        normed_ref.at[:, pl.ds(pl.multiple_of(mine * depth, depth), depth)],
        own_columns,
        local_sem.at[4],
    )
    own_part.start()
    gate_load = pltpu.make_async_copy(gate_taken_hbm, taken.at[0], local_sem.at[0])
    gate_load.start()
    peer_load = pltpu.make_async_copy(gate_peer_hbm, taken_peer.at[0], local_sem.at[7])
    peer_load.start()
    out_load = pltpu.make_async_copy(out_taken_hbm, taken.at[2], local_sem.at[5])
    out_load.start()
    for step in range(LINE):
        group_copy(0, step).start()
    out_load.wait()
    for at in range(LINE):
        peer_copy(2, at).start()

    for load in loads[::-1]:
        load.start()

    rows_sum = RowSum(partial, pair_in, row_out, row_in, pair_send, pair_recv)
    branch_sum = RowSum(partial, branch_pair, branch_out, branch_in, branch_send, branch_recv)

    def swap_copy(part):
        if part == 2:
            return remote(
                low.at[2, pl.ds(pl.multiple_of((1 - y) * 128, 128), 128), :],
                w_out_grad_ref.at[rep, :, pl.ds(pl.multiple_of(y * half, 128), half)],
                swap_send.at[2],
                swap_recv.at[2],
                (rep, peer),
            )
        return remote(
            low.at[part, :, pl.ds(pl.multiple_of((1 - c) * depth, depth), depth)],
            parts_ref.at[rep, part, c],
            swap_send.at[part],
            swap_recv.at[part],
            (rep, sibling),
        )

    def swap_own(part):
        if part == 2:
            return pltpu.make_async_copy(
                low.at[2, pl.ds(pl.multiple_of(y * 128, 128), 128), :],
                w_out_grad_ref.at[rep, :, pl.ds(pl.multiple_of(y * half, 128), half)],
                local_sem.at[6],
            )
        return pltpu.make_async_copy(
            low.at[part, :, pl.ds(pl.multiple_of(c * depth, depth), depth)],
            parts_ref.at[rep, part, c],
            local_sem.at[2 + part],
        )

    def mail_copy(part):
        return remote(
            mail_out.at[part],
            mail_in.at[part],
            mail_send.at[part],
            mail_recv.at[part],
            (beside, mine),
        )

    def sum_groups(part, then=None):
        for step in range(LINE):
            at = along_line(step)[1]
            if part > 0:
                peer_copy(part, at).wait_recv()
            elif step == 0:
                gate_load.wait()
                peer_load.wait()
            group_copy(part, step).wait()
            both = jnp.concatenate([taken[part, at], taken_peer[part, at]], axis=1)
            for lanes in (slice(0, half // 2), slice(half // 2, half)):
                term = dot_tn(both, group_rows[step, :, lanes])
                if step == 0:
                    total[:, lanes] = term
                else:
                    total[:, lanes] += term
            if then is not None:
                group_copy(then, step).start()
        for source, place in ((0, y), (256, 1 - y)):
            rows_kept = pl.ds(pl.multiple_of(source + x * 128, 128), 128)
            rows_sent = pl.ds(pl.multiple_of(source + (1 - x) * 128, 128), 128)
            there = pl.ds(pl.multiple_of(place * 128, 128), 128)
            sum_kept[there, :] = total[rows_kept, :]
            mail_out[part, there, :] = total[rows_sent, :].astype(BF)
        mail_copy(part).start()

    def close_sum(part):
        gains = gain_ref[:, pl.ds(pl.multiple_of(y * half, 128), half)] if part < 2 else 1.0
        mail_copy(part).wait_recv()
        low[part] = ((sum_kept[...] + mail_in[part].astype(F32)) * gains).astype(BF)
        swap_own(part).start()
        swap_copy(part).start()

    def sum_block(part, owner):
        return w_out_grad_ref.at[owner, 0:64] if part == 2 else parts_ref.at[owner, part]

    def cross_block(origin, column):
        owner = origin * PLANE + (x if column == 0 else 1 - x)
        return w_out_grad_ref.at[owner, 64:128]

    def cross_side(column):
        block = cross_block(z, column)
        return remote(
            block, block, cross_send.at[0, 2, 0], cross_recv.at[2, 0], (beside, mine)
        )

    def cross_copy(column, origin, toward):
        block = cross_block(origin, column)
        return remote(
            block,
            block,
            cross_send.at[column, (1 - toward) // 2, origin],
            cross_recv.at[column, origin],
            ((z + toward) * PLANE + x, mine),
        )

    def inner(toward):
        return z < LINE - 1 if toward > 0 else z > 0

    def cross_start(column):
        for toward in (1, -1):

            @pl.when(inner(toward))
            def _(toward=toward):
                cross_copy(column, z, toward).start()

    def cross_pass(step):
        for column in range(PLANE):
            for toward in (1, -1):
                origin = z - toward * step

                @pl.when(origin >= 0 if toward > 0 else origin < LINE)
                def _(column=column, origin=origin, toward=toward):
                    cross_copy(column, origin, toward).wait_recv()

                    @pl.when(inner(toward))
                    def _():
                        cross_copy(column, origin, toward).start()

    def cross_finish():
        cross_side(0).wait_send()
        for column in range(PLANE):
            for toward in (1, -1):
                for origin in range(LINE):
                    passed = origin <= z if toward > 0 else origin >= z

                    @pl.when(passed & inner(toward))
                    def _(column=column, origin=origin, toward=toward):
                        cross_copy(column, origin, toward).wait_send()

    def line_copy(part, origin, toward, lane):
        block = sum_block(part, origin * PLANE + x)
        return remote(
            block,
            block,
            line_send.at[part, lane, origin],
            line_recv.at[part, origin],
            ((z + toward) * PLANE + x, mine),
        )

    def side_copy(part, origin, from_x):
        block = sum_block(part, origin * PLANE + from_x)
        return remote(
            block, block, side_send.at[part, origin], side_recv.at[part, origin], (beside, mine)
        )

    def spread_own(part):
        swap_own(part).wait()
        swap_copy(part).wait_recv()
        side_copy(part, z, x).start()

        @pl.when(z < LINE - 1)
        def _():
            line_copy(part, z, 1, 0).start()

        @pl.when(z > 0)
        def _():
            line_copy(part, z, -1, 1).start()

    def pass_on(part, step):
        @pl.when(z - step >= 0)
        def _():
            origin = z - step
            line_copy(part, origin, 1, 0).wait_recv()

            @pl.when(z < LINE - 1)
            def _():
                line_copy(part, origin, 1, 0).start()

            side_copy(part, origin, x).start()

        @pl.when(z + step < LINE)
        def _():
            origin = z + step
            line_copy(part, origin, -1, 1).wait_recv()

            @pl.when(z > 0)
            def _():
                line_copy(part, origin, -1, 1).start()

            side_copy(part, origin, x).start()

    in_given_order(back_ref, inverse_ref, values_ref, values_given_ref, scaled_ref)
    own_share = share_own(scaled_ref, taken.at[1], local_sem.at[1])
    share_start(scaled_ref, taken.at[1], share_send, share_recv, own_share)
    sum_groups(0, 2)
    close_sum(0)
    spread_own(0)
    loads[3].wait()
    loads[4].wait()
    branch_sum.fill(lambda span: dot_nn(normed_out_ref[span, :], w_out_ref[...]))
    sum_groups(2, 1)
    branch_sum.join()
    close_sum(2)
    pass_on(0, 1)
    spread_own(2)
    cross_side(0).start()
    cross_start(0)

    branch = branch_sum.result()
    branch_sum.finish()
    whole = resid_ref[...].astype(F32) + branch
    block_out_ref[...] = whole.astype(BF)
    counts = valid_ref[...].astype(F32)
    square_total = jnp.sum(
        counts * jnp.sum(whole * whole, axis=1, keepdims=True), axis=0, keepdims=True
    )
    square_branch = jnp.sum(
        counts * jnp.sum(branch * branch, axis=1, keepdims=True), axis=0, keepdims=True
    )
    count = jnp.sum(counts, axis=0, keepdims=True)
    pass_on(0, 2)

    heads, share = H // shards, 2 * N // shards
    lane = lax.broadcasted_iota(jnp.int32, (rows, TAIL_PAD), 1)
    owned = ((lane >= mine * share) & (lane < (mine + 1) * share)) | (
        (lane >= 2 * N + mine * heads) & (lane < 2 * N + (mine + 1) * heads)
    )

    def grad_rows(span):
        tail = dot_nn(back_ref[span, :], tail_low[...])
        tail = jnp.where(owned, tail, 0.0).astype(BF)
        return (
            dot_nn(gate_given_ref[span, :], w_gate_ref[...])
            + dot_nn(values_given_ref[span, :], w_conv_ref[0:width, :])
            + dot_nn(tail, w_conv_ref[width:, :])
        )

    loads[0].wait()
    loads[1].wait()
    rows_sum.fill(grad_rows)

    share_rows = TAIL_PAD // reps

    def tail_rows(ref, owner):
        return ref.at[pl.ds(pl.multiple_of(owner * share_rows, 16), share_rows)]

    def tail_part_copy(step):
        to = other(step)
        return remote(
            tail_rows(tail_sum, to),
            tail_parts.at[step],
            rep_send.at[0, step],
            rep_recv.at[0, step],
            (to, mine),
        )

    def tail_spread_copy(step):
        return remote(
            tail_rows(tails_ref, rep),
            tail_rows(tails_ref, rep),
            rep_send.at[1, step],
            rep_recv.at[1, step],
            (other(step), mine),
        )

    own_part.wait()
    tail_own[...] = dot_tn(tail_low[...], own_columns[...])
    tail_sum[...] = tail_own[...].astype(BF)
    for step in range(1, reps):
        tail_part_copy(step).start()

    for step in range(LINE):
        at = share_arrival(taken.at[1], share_recv, own_share, step)
        peer_copy(1, at).start()
    rows_sum.join()
    pass_on(0, 3)

    pass_on(2, 1)
    cross_side(1).wait_recv()
    cross_start(1)
    for step in range(1, reps):
        tail_part_copy(step).wait_recv()
    span = pl.ds(pl.multiple_of(rep * share_rows, 16), share_rows)
    piece = tail_own[span, :]
    for step in range(1, reps):
        piece = piece + tail_parts[step].astype(F32)
    tails_ref[span, :] = piece.astype(BF)
    for step in range(1, reps):
        tail_spread_copy(step).start()

    grad_normed = rows_sum.result()
    given = x_ref[...].astype(F32)
    inverse = lax.rsqrt(jnp.mean(given * given, axis=1, keepdims=True) + EPSILON)
    grad_norm_gain = jnp.sum(grad_normed * (given * inverse), axis=0, keepdims=True)
    scaled = grad_normed * gain_ref[...]
    pull = inverse * inverse * inverse * jnp.mean(scaled * given, axis=1, keepdims=True)
    span = pl.ds(pl.multiple_of(mine * rows, rows), rows)
    loads[2].wait()
    kept = dot_nn(back_ref[span, :], branch_grad_ref[...])
    grad_in_ref[...] = (scaled * inverse - given * pull + kept).astype(BF)
    pass_on(2, 2)

    lane = lax.broadcasted_iota(jnp.int32, (1, 128), 1)
    at = 0
    for i in range(D // 128):
        small[at : at + 1, :] = grad_norm_gain[:, 128 * i : 128 * i + 128]
        at += 1
    channels = (width + 2 * N) // 128
    for tap in range(KW):
        for i in range(channels):
            small[at : at + 1, :] = grad_conv_w_ref[tap : tap + 1, 128 * i : 128 * i + 128]
            at += 1
    for i in range(channels):
        small[at : at + 1, :] = grad_conv_b_ref[:, 128 * i : 128 * i + 128]
        at += 1
    for i in range(width // 128):
        small[at : at + 1, :] = grad_gain_ref[:, 128 * i : 128 * i + 128]
        at += 1
    small[at : at + 3, :] = grad_head_ref[0:3, :]
    small[at + 3 : at + 4, :] = jnp.where(
        lane == 0,
        spread(square_total),
        jnp.where(lane == 1, spread(square_branch), jnp.where(lane == 2, spread(count), 0.0)),
    )
    small[at + 4 :, :] = jnp.zeros((small.shape[0] - at - 4, 128), F32)

    def small_rep_copy(step):
        return remote(
            small, small_in.at[rep], rep_send.at[2, step], rep_recv.at[2, step], (other(step), mine)
        )

    def small_rep_arrival(step):
        return remote(
            small,
            small_in.at[before(step)],
            rep_send.at[2, step],
            rep_recv.at[2, step],
            (other(step), mine),
        )

    def small_shard_copy(step):
        return remote(
            small_all.at[mine],
            small_all.at[mine],
            all_send.at[step],
            all_recv.at[step],
            (rep, shard_at(step)),
        )

    for step in range(1, reps):
        small_rep_copy(step).start()
    small_in[rep] = small[...]
    sum_groups(1)
    pass_on(2, 3)
    cross_pass(1)
    close_sum(1)
    spread_own(1)
    for step in range(1, reps):
        small_rep_arrival(step).wait_recv()
    added = small_in[0]
    for i in range(1, reps):
        added = added + small_in[i]
    small_all[mine] = added
    for step in range(1, shards):
        small_shard_copy(step).start()
    pass_on(1, 1)
    cross_pass(2)
    for step in range(1, shards):
        small_shard_copy(step).wait_recv()

    def over_shards(row):
        value = small_all[0, row : row + 1, :]
        for i in range(1, shards):
            value = value + small_all[i, row : row + 1, :]
        return value

    at = 0
    for i in range(D // 128):
        out_norm_ref[:, 128 * i : 128 * i + 128] = over_shards(at)
        at += 1
    for tap in range(KW + 1):
        ref, row = (out_conv_w_ref, tap) if tap < KW else (out_conv_b_ref, 0)
        for i in range(channels):
            if i < width // 128:
                for shard in range(shards):
                    to = shard * width + 128 * i
                    ref[row : row + 1, to : to + 128] = small_all[shard, at : at + 1, :]
            else:
                to = DI + 128 * i - width
                ref[row : row + 1, to : to + 128] = over_shards(at)
            at += 1
    for i in range(width // 128):
        for shard in range(shards):
            to = shard * width + 128 * i
            out_gain_ref[:, to : to + 128] = small_all[shard, at : at + 1, :]
        at += 1
    for i in range(3):
        out_head_ref[i : i + 1, :] = over_shards(at + i)
    stats = over_shards(at + 3)
    per = jnp.maximum(stats[:, 2:3], 1.0) * D
    out_head_ref[3:4, :] = jnp.sqrt(stats / spread(per))
    out_head_ref[4:8, :] = jnp.zeros((4, 128), F32)

    pass_on(1, 2)
    cross_pass(3)
    pass_on(1, 3)

    cross_finish()
    for step in range(1, reps):
        tail_spread_copy(step).wait_recv()
    for part in range(3):
        for origin in range(LINE):
            side_copy(part, origin, 1 - x).wait_recv()
            side_copy(part, origin, x).wait_send()

            @pl.when((origin <= z) & (z < LINE - 1))
            def _(part=part, origin=origin):
                line_copy(part, origin, 1, 0).wait_send()

            @pl.when((origin >= z) & (z > 0))
            def _(part=part, origin=origin):
                line_copy(part, origin, -1, 1).wait_send()

        swap_copy(part).wait_send()
        mail_copy(part).wait_send()
        if part > 0:
            for at in range(LINE):
                peer_copy(part, at).wait_send()
    share_sent(scaled_ref, taken.at[1], share_send, share_recv)
    rows_sum.finish()
    for step in range(1, shards):
        small_shard_copy(step).wait_send()
    for step in range(1, reps):
        tail_part_copy(step).wait_send()
        tail_spread_copy(step).wait_send()
        small_rep_copy(step).wait_send()


def run_end(operands, shards):
    reps = LINE * PLANE
    length, width = operands[4].shape
    rows, depth = length // shards, D // shards
    dma = pltpu.SemaphoreType.DMA
    vector = pl.BlockSpec(memory_space=pltpu.VMEM)
    anywhere = pl.BlockSpec(memory_space=pl.ANY)
    shape = jax.ShapeDtypeStruct
    channels = width + 2 * N
    small = -(-(D + 5 * channels + width + 4 * 128) // 1024) * 8
    return pl.pallas_call(
        end_kernel,
        out_shape=(
            shape((reps, 2, 2, 256, depth), BF),
            shape((reps, 128, D), BF),
            shape((TAIL_PAD, depth), BF),
            shape((rows, D), BF),
            shape((rows, D), BF),
            shape((1, D), F32),
            shape((KW, CONVW), F32),
            shape((1, CONVW), F32),
            shape((8, 128), F32),
            shape((1, DI), F32),
        ),
        in_specs=[anywhere] * 3 + [vector] * 3 + [anywhere] * 2 + [vector] + [anywhere] * 4 + [vector] + [anywhere] + [vector] * 8,
        out_specs=(anywhere,) * 2 + (vector,) * 8,
        scratch_shapes=[
            pltpu.VMEM((3, LINE, length, 256), BF),
            pltpu.VMEM((3, LINE, length, 256), BF),
            pltpu.VMEM((length, width), BF),
            pltpu.VMEM((length, width), BF),
            pltpu.VMEM((LINE, length, D // 2), BF),
            pltpu.VMEM((length, depth), BF),
            pltpu.VMEM((512, D // 2), F32),
            pltpu.VMEM((256, D // 2), F32),
            pltpu.VMEM((3, 256, D // 2), BF),
            pltpu.VMEM((3, 256, D // 2), BF),
            pltpu.VMEM((3, 256, D // 2), BF),
            pltpu.VMEM((length, D), F32),
            pltpu.VMEM((2, rows, D), F32),
            pltpu.VMEM((rows, D), BF),
            pltpu.VMEM((rows, D), BF),
            pltpu.VMEM((2, rows, D), F32),
            pltpu.VMEM((rows, D), BF),
            pltpu.VMEM((rows, D), BF),
            pltpu.VMEM((TAIL_PAD, depth), BF),
            pltpu.VMEM((TAIL_PAD, depth), F32),
            pltpu.VMEM((reps, TAIL_PAD // reps, depth), BF),
            pltpu.VMEM((small, 128), F32),
            pltpu.VMEM((reps, small, 128), F32),
            pltpu.VMEM((shards, small, 128), F32),
            pltpu.VMEM((width, D), BF),
            pltpu.VMEM((width + TAIL_PAD, D), BF),
            pltpu.VMEM((length, D), BF),
            pltpu.VMEM((width, D), BF),
            pltpu.VMEM((length, width), BF),
            dma((5,)),
            dma((8,)),
            dma((LINE,)),
            dma((LINE,)),
            dma((LINE,)),
            dma((3, LINE)),
            dma((3, LINE)),
            dma((3,)),
            dma((3,)),
            dma((3,)),
            dma((3,)),
            dma((3, 2, LINE)),
            dma((3, LINE)),
            dma((3, LINE)),
            dma((3, LINE)),
            dma((PLANE, 3, LINE)),
            dma((PLANE + 1, LINE)),
            dma((3,)),
            dma((3,)),
            dma((3,)),
            dma((3,)),
            dma((3, reps)),
            dma((3, reps)),
            dma((shards,)),
            dma((shards,)),
        ],
        compiler_params=pltpu.CompilerParams(
            vmem_limit_bytes=VMEM_BYTES, collective_id=3, has_side_effects=True
        ),
        cost_estimate=pl.CostEstimate(
            flops=2 * reps * length * D * 256, bytes_accessed=96 << 20, transcendentals=0
        ),
        name="weight_gradient",
    )(*operands)


def assemble_kernel(parts_ref, tail_ref, out_ref):
    step, steps = pl.program_id(0), pl.num_programs(0)
    reps = parts_ref.shape[0]

    @pl.when(step < steps - 1)
    def _():
        for rep in range(reps):
            out_ref[128 * rep : 128 * rep + 128, :] = parts_ref[rep, 0, 0].astype(F32)

    @pl.when(step == steps - 1)
    def _():
        out_ref[0:TAIL, :] = tail_ref[0:TAIL, :].astype(F32)


def run_assemble(parts, tail):
    reps, unused, cores, stack, depth = parts.shape
    shards = cores * stack // 128
    steps = 2 * shards

    def place(i):
        at = jnp.minimum(i, steps - 1)
        shard = lax.rem(at, shards)
        return (0, at // shards, lax.rem(shard, cores), shard // cores, 0)

    return pl.pallas_call(
        assemble_kernel,
        grid=(steps + 1,),
        out_shape=jax.ShapeDtypeStruct((PROJ, depth), F32),
        in_specs=[
            pl.BlockSpec((reps, 1, 1, 128, depth), place),
            pl.BlockSpec((TAIL_PAD, depth), lambda i: (0, 0)),
        ],
        out_specs=pl.BlockSpec((reps * 128, depth), lambda i: (i, 0)),
        compiler_params=params(),
        name="assemble",
    )(parts, tail)


def exchange(pieces, axis, mine):
    count = lax.axis_size(axis)
    own = pieces(mine)
    gathered = jnp.zeros((count,) + own.shape, own.dtype)
    gathered = lax.dynamic_update_index_in_dim(gathered, own, mine, 0)
    for other in range(1, count):
        arrived = lax.ppermute(
            pieces(mine ^ other), axis, [(i, i ^ other) for i in range(count)]
        )
        gathered = lax.dynamic_update_index_in_dim(gathered, arrived, mine ^ other, 0)
    return gathered


def columns_at(array, start, width):
    return lax.dynamic_slice_in_dim(array, start, width, axis=1)


def plain_device(
    x_in,
    cotangent,
    seq_lengths,
    seq_order,
    valid,
    norm_gain,
    w_in,
    conv_w,
    conv_b,
    head_rows,
    gain_row,
    w_out,
):
    shards, mine = lax.axis_size("shard"), lax.axis_index("shard")
    rows = x_in.shape[0]
    length = rows * shards
    depth = w_in.shape[0]
    heads = H // shards
    width = DI // shards
    share = 2 * N // shards
    w_tail = w_in[:, 2 * DI :]

    def conv_piece(d):
        return jnp.concatenate([columns_at(w_in, DI + d * width, width), w_tail], axis=1)

    x_group = lax.all_gather(x_in, "shard", axis=0, tiled=True)
    w_conv = exchange(conv_piece, "shard", mine).reshape(D, width + TAIL)
    w_gate = exchange(lambda d: columns_at(w_in, d * width, width), "shard", mine).reshape(D, width)
    branch_grad = lax.all_gather(
        jnp.where(valid[:, None] > 0, cotangent, jnp.zeros_like(cotangent)),
        "shard",
        axis=0,
        tiled=True,
    )
    slot_ids = jnp.arange(length, dtype=jnp.int32)
    source, target, position = slot_tables(seq_lengths[0], seq_order[0], slot_ids)
    resid = dot_nn((source[:, None] == slot_ids[None, :]).astype(BF), x_group)
    inverse_rms = lax.rsqrt(jnp.mean(resid * resid, axis=1, keepdims=True) + EPSILON)
    normed = (resid * inverse_rms * norm_gain[None, :]).astype(BF)
    resid_mine = lax.dynamic_slice_in_dim(resid, mine * rows, rows, axis=0)
    gate = dot_nn(normed, w_gate).astype(BF)
    conv_in = jnp.pad(dot_nn(normed, w_conv).astype(BF), ((0, 0), (0, TAIL_PAD - TAIL)))
    place = jnp.broadcast_to(position[:, None], (length, 128))
    (
        normed_out,
        grad_gate,
        grad_gain,
        grad_values,
        grad_tail,
        grad_conv_w,
        grad_conv_b,
        grad_head,
    ) = run_mixer(
        (conv_in, gate, branch_grad, w_out, place, conv_w, conv_b, head_rows, gain_row), shards, False
    )
    branch = lax.psum_scatter(dot_nn(normed_out, w_out), "shard", scatter_dimension=0, tiled=True)
    total_rows = resid_mine + branch
    weights_valid = valid.astype(F32)
    square_total = jnp.sum(weights_valid * jnp.sum(total_rows * total_rows, axis=1))
    square_branch = jnp.sum(weights_valid * jnp.sum(branch * branch, axis=1))
    grad_w_out = lax.psum(dot_tn(normed_out, branch_grad), "rep")
    grad_tail = lax.psum(grad_tail, "shard").astype(BF)
    lane = jnp.arange(TAIL, dtype=jnp.int32)
    owned = ((lane >= mine * share) & (lane < (mine + 1) * share)) | (
        (lane >= 2 * N + mine * heads) & (lane < 2 * N + (mine + 1) * heads)
    )
    kept_tail = jnp.where(owned[None, :], grad_tail[:, :TAIL], jnp.zeros((), BF))
    back = (target[:, None] == slot_ids[None, :]).astype(BF)

    def returned(grad):
        return dot_nn(back, grad).astype(BF)

    grad_normed = lax.psum_scatter(
        dot_nt(returned(grad_gate), w_gate)
        + dot_nt(returned(grad_values), w_conv[:, :width])
        + dot_nt(returned(kept_tail), w_conv[:, width:]),
        "shard",
        scatter_dimension=0,
        tiled=True,
    )
    given = x_in.astype(F32)
    given_rms = lax.rsqrt(jnp.mean(given * given, axis=1, keepdims=True) + EPSILON)
    grad_norm_gain = jnp.sum(grad_normed * (given * given_rms), axis=0)
    scaled = grad_normed * norm_gain[None, :]
    grad_resid = scaled * given_rms - given * (
        given_rms**3 * jnp.mean(scaled * given, axis=1, keepdims=True)
    )
    back_mine = lax.dynamic_slice_in_dim(back, mine * rows, rows, axis=0)
    grad_in = (grad_resid + dot_nn(back_mine, branch_grad)).astype(BF)

    def to_owners(columns):
        part = dot_tn(normed, columns).reshape(shards, depth, columns.shape[1])
        swapped = lax.all_to_all(part, "shard", split_axis=0, concat_axis=0, tiled=True)
        summed = lax.psum(swapped, "rep")
        return summed.transpose(1, 0, 2).reshape(depth, shards * columns.shape[1])

    grad_w_tail = lax.psum(
        dot_tn(columns_at(normed, mine * depth, depth), grad_tail[:, :TAIL]), "rep"
    )
    grad_w_in = jnp.concatenate([to_owners(grad_gate), to_owners(grad_values), grad_w_tail], axis=1)

    def placed(part):
        own = lax.dynamic_update_slice_in_dim(
            jnp.zeros((part.shape[0], DI), F32), part[:, :width], mine * width, axis=1
        )
        return jnp.concatenate([own, part[:, width:]], axis=1)

    summed = lax.psum(
        (
            grad_norm_gain,
            placed(grad_conv_w),
            placed(grad_conv_b)[0],
            grad_head,
            placed(grad_gain)[0],
            jnp.stack([square_total, square_branch, jnp.sum(weights_valid)]),
        ),
        ALL,
    )
    roots = jnp.sqrt(summed[5] / (jnp.maximum(summed[5][2], 1.0) * D))
    return (
        total_rows.astype(BF),
        grad_in,
        summed[0],
        grad_w_in,
        summed[1],
        summed[2],
        summed[3][0, :H],
        summed[3][1, :H],
        summed[3][2, :H],
        summed[4],
        grad_w_out,
        roots[0],
        roots[1],
    )


def on_device(
    x_in,
    cotangent,
    seq_lengths,
    seq_order,
    valid,
    norm_gain,
    w_in,
    conv_w,
    conv_b,
    dt_bias,
    a_log,
    d_skip,
    gated_gain,
    w_out,
):
    shards, mine = lax.axis_size("shard"), lax.axis_index("shard")
    reps = lax.axis_size("rep")
    rows = x_in.shape[0]
    length = rows * shards
    depth = w_in.shape[0]
    heads = H // shards
    width = DI // shards

    head_rows = jnp.pad(jnp.stack([dt_bias, a_log, d_skip]), ((0, 5), (0, 128 - H)))
    bias_row, gain_row = conv_b[None, :], gated_gain[None, :]
    spans = reps == LINE * PLANE and shards == 4 and width == reps * 128 and rows == 128
    if not spans:
        return plain_device(
            x_in,
            cotangent,
            seq_lengths,
            seq_order,
            valid,
            norm_gain,
            w_in,
            conv_w,
            bias_row,
            head_rows,
            gain_row,
            w_out,
        )
    norm_row, valid_column = norm_gain[None, :], valid[:, None]
    (
        normed,
        w_gate,
        w_conv,
        branch_grad,
        back,
        resid,
        inverse,
        line,
        normed_out,
        grad_gain,
        grad_values,
        grad_conv_w,
        grad_conv_b,
        grad_head,
        gate_taken,
        out_taken,
        gate_peer,
        gate_given,
        tail,
    ) = run_mixer(
        (
            seq_lengths,
            seq_order,
            x_in,
            cotangent,
            valid_column,
            norm_row,
            w_in.T,
            w_out,
            conv_w,
            bias_row,
            head_rows,
            gain_row,
        ),
        shards,
        True,
    )
    operands = (
        gate_taken,
        gate_peer,
        out_taken,
        gate_given,
        grad_values,
        tail,
        normed,
        line,
        inverse,
        w_gate,
        w_conv,
        w_out,
        normed_out,
        back,
        branch_grad,
        x_in,
        resid,
        valid_column,
        norm_row,
        grad_conv_w,
        grad_conv_b,
        grad_head,
        grad_gain,
    )
    (
        parts,
        w_out_parts,
        tails,
        block_out,
        grad_in,
        out_norm,
        out_conv_w,
        out_conv_b,
        out_head,
        out_gain,
    ) = run_end(operands, shards)
    grad_w_out = w_out_parts.reshape(width, D).astype(F32)
    grad_w_in = run_assemble(parts, tails).T
    return (
        block_out,
        grad_in,
        out_norm[0],
        grad_w_in,
        out_conv_w,
        out_conv_b[0],
        out_head[0, :H],
        out_head[1, :H],
        out_head[2, :H],
        out_gain[0],
        grad_w_out,
        out_head[3, 0],
        out_head[3, 1],
    )


def solution(mesh):
    in_specs = (
        P(ALL, None),
        P(ALL, None),
        P("rep", None),
        P("rep", None),
        P(ALL),
        P(),
        P("shard", None),
        P(),
        P(),
        P(),
        P(),
        P(),
        P(),
        P("shard", None),
    )
    out_specs = (
        P(ALL, None),
        P(ALL, None),
        P(),
        P("shard", None),
        P(),
        P(),
        P(),
        P(),
        P(),
        P(),
        P("shard", None),
        P(),
        P(),
    )
    return jax.shard_map(
        on_device, mesh=mesh, in_specs=in_specs, out_specs=out_specs, check_vma=False
    )
```

```python
import functools

import jax
import jax.numpy as jnp
from jax import lax
from jax.experimental import pallas as pl
from jax.experimental.pallas import tpu as pltpu
from jax.sharding import PartitionSpec as P

D = 2048
H = 64
P_SIZE = 64
N = 128
KW = 4
SPAN = 128
DI = 4096
CONVW = 4352
PROJ = 8512
TAIL = PROJ - 2 * DI

EPSILON = 1e-05
ALL = ("rep", "shard")
VMEM_BYTES = 58 * 1024 * 1024
BF = jnp.bfloat16
F32 = jnp.float32


def dot_nn(a, b):
    return lax.dot_general(a, b, (((1,), (0,)), ((), ())), preferred_element_type=F32)


def dot_nt(a, b):
    return lax.dot_general(a, b, (((1,), (1,)), ((), ())), preferred_element_type=F32)


def dot_tn(a, b):
    return lax.dot_general(a, b, (((0,), (0,)), ((), ())), preferred_element_type=F32)


def halves(a):
    high = a.astype(BF)
    return high, (a - high.astype(F32)).astype(BF)


def slot_tables(seq_lengths, seq_order, slot_ids):
    seq_count = seq_lengths.shape[0]
    numbers = jnp.arange(seq_count, dtype=jnp.int32)
    chosen = (seq_order[:, None] == numbers[None, :]).astype(jnp.int32)
    given_start = jnp.cumsum(seq_lengths) - seq_lengths
    owner_length = jnp.sum(chosen * seq_lengths[None, :], axis=1)
    owner_start = jnp.cumsum(owner_length) - owner_length
    owner_from = jnp.sum(chosen * given_start[None, :], axis=1)
    placed_at = jnp.sum(chosen * owner_start[:, None], axis=0)
    column = slot_ids[:, None]
    within = (column >= owner_start[None, :]) & (column < (owner_start + owner_length)[None, :])
    offset = column - owner_start[None, :]
    source = jnp.sum(jnp.where(within, offset + owner_from[None, :], 0), axis=1)
    position = jnp.sum(jnp.where(within, offset, 0), axis=1)
    given_within = (column >= given_start[None, :]) & (
        column < (given_start + seq_lengths)[None, :]
    )
    target = jnp.sum(
        jnp.where(given_within, column - given_start[None, :] + placed_at[None, :], 0), axis=1
    )
    return (source, target, position)


def params():
    return pltpu.CompilerParams(vmem_limit_bytes=VMEM_BYTES)


def spread_rows(row):
    return jnp.broadcast_to(row, (16, row.shape[1]))


def sigmoid(v):
    return 1.0 / (1.0 + jnp.exp(-v))


def spread(column, lanes=128):
    return jnp.broadcast_to(column, (column.shape[0], lanes))


MESH = pl.DeviceIdType.MESH
LINE, PLANE = 4, 2
CHUNK = 256
TAIL_PAD = 384


def remote(src, dst, send_sem, recv_sem, device):
    return pltpu.make_async_remote_copy(
        src_ref=src,
        dst_ref=dst,
        send_sem=send_sem,
        recv_sem=recv_sem,
        device_id=device,
        device_id_type=MESH,
    )


def meet(devices):
    barrier = pltpu.get_barrier_semaphore()
    for device in devices:
        pl.semaphore_signal(barrier, inc=1, device_id=device, device_id_type=MESH)
    pl.semaphore_wait(barrier, len(devices))


class Line:
    def __init__(self, store, first, share, send_sem, recv_sem):
        self.store, self.first, self.share = store, first, share
        self.send_sem, self.recv_sem = send_sem, recv_sem
        self.mine, self.rep = lax.axis_index("shard"), lax.axis_index("rep")
        self.z, self.x = self.rep // PLANE, lax.rem(self.rep, PLANE)
        self.sibling = self.mine // 2 * 2 + (1 - lax.rem(self.mine, 2))

    def along(self, origin, toward, first=False):
        block = self.store.at[origin, self.share]
        lane = (toward + 1) // 2
        return remote(
            self.first if first else block,
            block,
            self.send_sem.at[lane, origin],
            self.recv_sem.at[0, origin],
            ((self.z + toward) * PLANE + self.x, self.mine),
        )

    def inward(self, origin):
        block = self.store.at[origin, self.share]
        return remote(
            block,
            block,
            self.send_sem.at[2, origin],
            self.recv_sem.at[1, origin],
            (self.rep, self.sibling),
        )

    def start(self):
        for toward in (1, -1):
            self.guarded(toward, lambda: self.along(self.z, toward, True).start())

    def guarded(self, toward, act):
        pl.when(self.z < LINE - 1 if toward > 0 else self.z > 0)(act)

    def step(self, distance):
        for toward in (1, -1):
            origin = self.z - toward * distance

            @pl.when(origin >= 0 if toward > 0 else origin < LINE)
            def _():
                self.along(origin, toward).wait_recv()
                self.guarded(toward, lambda: self.along(origin, toward).start())
                self.inward(origin).start()

    def finish(self):
        for origin in range(LINE):

            @pl.when(origin != self.z)
            def _():
                self.inward(origin).wait_recv()
                self.inward(origin).wait_send()

            for toward in (1, -1):
                passed = origin <= self.z if toward > 0 else origin >= self.z
                pl.when(passed)(
                    lambda: self.guarded(toward, lambda: self.along(origin, toward).wait_send())
                )


def meet_with_line(devices):
    mine, rep = lax.axis_index("shard"), lax.axis_index("rep")
    z, x = rep // PLANE, lax.rem(rep, PLANE)
    barrier = pltpu.get_barrier_semaphore()
    for device in devices:
        pl.semaphore_signal(barrier, inc=1, device_id=device, device_id_type=MESH)
    for toward, there in ((1, z < LINE - 1), (-1, z > 0)):

        @pl.when(there)
        def _():
            pl.semaphore_signal(
                barrier, inc=1, device_id=((z + toward) * PLANE + x, mine), device_id_type=MESH
            )

    beyond = (z + LINE - 1) // LINE + (2 * (LINE - 1) - z) // LINE
    pl.semaphore_wait(barrier, len(devices) + beyond)


def tables_in_kernel(lengths_ref, order_ref, slots):
    count = lengths_ref.shape[1]
    lengths = [lengths_ref[0, i] for i in range(count)]
    order = [order_ref[0, i] for i in range(count)]
    given_start, at = [], jnp.int32(0)
    for i in range(count):
        given_start.append(at)
        at = at + lengths[i]
    source = jnp.zeros_like(slots)
    position = jnp.zeros_like(slots)
    placed_at = [jnp.int32(0)] * count
    at = jnp.int32(0)
    for k in range(count):
        length, start = jnp.int32(0), jnp.int32(0)
        for i in range(count):
            chosen = order[k] == i
            length = length + jnp.where(chosen, lengths[i], 0)
            start = start + jnp.where(chosen, given_start[i], 0)
            placed_at[i] = placed_at[i] + jnp.where(chosen, at, 0)
        within = (slots >= at) & (slots < at + length)
        source = source + jnp.where(within, slots - at + start, 0)
        position = position + jnp.where(within, slots - at, 0)
        at = at + length
    target = jnp.zeros_like(slots)
    for i in range(count):
        within = (slots >= given_start[i]) & (slots < given_start[i] + lengths[i])
        target = target + jnp.where(within, slots - given_start[i] + placed_at[i], 0)
    return source, target, position


def start_phases(
    lengths_ref,
    order_ref,
    x_ref,
    cotangent_ref,
    valid_ref,
    gain_ref,
    w_ref,
    normed_out_ref,
    w_gate_out_ref,
    w_conv_out_ref,
    branch_grad_out_ref,
    back_ref,
    resid_ref,
    inverse_ref,
    line_ref,
    conv_in_ref,
    gate_ref,
    grads,
    place_ref,
    x_all,
    normed,
    w_gate,
    w_conv,
    local_sem,
    row_send,
    row_recv,
    w_send,
    w_recv,
    w_local,
    line_send,
    line_recv,
):
    mine, rep = lax.axis_index("shard"), lax.axis_index("rep")
    y, c = mine // 2, lax.rem(mine, 2)
    z, x = rep // PLANE, lax.rem(rep, PLANE)
    sibling, peer, far = y * 2 + (1 - c), (1 - y) * 2 + c, (1 - y) * 2 + (1 - c)
    beside = z * PLANE + (1 - x)
    rows, length = x_ref.shape[0], x_all.shape[0]
    depth, width = w_ref.shape[1], gate_ref.shape[1]
    chunks = width // CHUNK
    tail_half = TAIL // 2

    part = pl.ds(pl.multiple_of(y * (D // 2), 128), D // 2)
    share = pl.ds(pl.multiple_of(c * (length // 2), 16), length // 2)
    wholes = (x_all, grads)

    lines = [
        Line(
            line_ref.at[kind],
            wholes[kind].at[share, part],
            share,
            line_send.at[kind],
            line_recv.at[kind],
        )
        for kind in range(2)
    ]

    def line_own(kind):
        return pltpu.make_async_copy(
            wholes[kind].at[:, part], line_ref.at[kind, z], local_sem.at[4 + kind]
        )

    def block(ref, shard):
        return ref.at[pl.ds(pl.multiple_of(shard * rows, rows), rows)]

    def row_copies(kind, own, store):
        return (
            remote(own, block(store, mine), row_send.at[kind, 0], row_recv.at[kind, 0], (rep, peer)),
            remote(own, block(store, mine), row_send.at[kind, 1], row_recv.at[kind, 1], (rep, sibling)),
            remote(
                block(store, peer),
                block(store, peer),
                row_send.at[kind, 2],
                row_recv.at[kind, 2],
                (rep, sibling),
            ),
        )

    def lanes(shard):
        return pl.ds(pl.multiple_of(shard * depth, depth), depth)

    def weight_copies(store, index, base, stride, at, half):
        share = pl.ds(pl.multiple_of(at + half * x, 16), half)
        both = pl.ds(pl.multiple_of((1 - y) * 2 * depth, 128), 2 * depth)

        def source(shard, start, count):
            return w_ref.at[pl.ds(pl.multiple_of(base + stride * shard + start, 16), count)]

        def sems(way):
            return w_send.at[way, index], w_recv.at[way, index]

        whole = pl.ds(pl.multiple_of(at, 16), 2 * half)
        near = at if stride else 0
        return (
            lambda: remote(
                source(peer, near + half * x, half), store.at[share, lanes(mine)], *sems(0), (rep, peer)
            ),
            lambda: remote(
                source(far, near + half * x, half), store.at[share, lanes(mine)], *sems(1), (rep, far)
            ),
            lambda: remote(store.at[share, both], store.at[share, both], *sems(2), (beside, mine)),
            lambda: remote(
                source(sibling, near, 2 * half), store.at[whole, lanes(mine)], *sems(3), (rep, sibling)
            ),
            lambda: pltpu.make_async_copy(
                source(mine, near, 2 * half), store.at[whole, lanes(mine)], w_local.at[index]
            ),
        )

    def conv_copies(q):
        return weight_copies(w_conv, q, DI, width, q * CHUNK, CHUNK // 2)

    def tail_copies():
        return weight_copies(w_conv, chunks, 2 * DI, 0, width, tail_half)

    def gate_copies(q):
        return weight_copies(w_gate, chunks + 1 + q, 0, width, q * CHUNK, CHUNK // 2)

    def send_near(copies):
        copies[3]().start()
        copies[4]().start()

    def send_far(copies):
        copies[0]().start()
        copies[1]().start()

    def pass_on(copies):
        copies[0]().wait_recv()
        copies[1]().wait_recv()
        copies[2]().start()
        copies[0]().wait_send()
        copies[1]().wait_send()

    def arrived(copies):
        copies[2]().wait_recv()
        copies[3]().wait_recv()
        copies[4]().wait()

    def each(count, body):
        def step(i, unused):
            body(i)
            return unused

        lax.fori_loop(0, count, step, 0)

    x_copies = row_copies(0, x_ref, x_all)
    grad_copies = row_copies(1, block(grads, mine), grads)
    own_rows = pltpu.make_async_copy(x_ref, block(x_all, mine), local_sem.at[0])
    convs = [conv_copies(q) for q in range(chunks)]
    gates = [gate_copies(q) for q in range(chunks)]
    tail = tail_copies()
    x_copies[0].start()
    x_copies[1].start()
    own_rows.start()
    for copies in convs + [tail] + gates:
        send_near(copies)
    grads[pl.ds(pl.multiple_of(mine * rows, rows), rows), :] = jnp.where(
        spread(valid_ref[...], D) > 0, cotangent_ref[...].astype(F32), 0.0
    ).astype(BF)
    grad_copies[0].start()
    grad_copies[1].start()
    w_conv[width + TAIL :, :] = jnp.zeros((TAIL_PAD - TAIL, D), BF)

    def table_block(i):
        span = pl.ds(pl.multiple_of(i * rows, rows), rows)
        slots = lax.broadcasted_iota(jnp.int32, (rows, length), 0) + i * rows
        across = lax.broadcasted_iota(jnp.int32, (rows, length), 1)
        target = tables_in_kernel(lengths_ref, order_ref, slots)[1]
        back_ref[span, :] = (target == across).astype(F32).astype(BF)
        few_slots = lax.broadcasted_iota(jnp.int32, (rows, 128), 0) + i * rows
        place_ref[span, :] = tables_in_kernel(lengths_ref, order_ref, few_slots)[2]

    each(length // rows, table_block)
    x_copies[0].wait_recv()
    x_copies[2].start()
    x_copies[0].wait_send()
    send_far(convs[0])
    send_far(convs[1])
    own_rows.wait()
    x_copies[1].wait_recv()
    x_copies[2].wait_recv()
    line_own(0).start()
    lines[0].start()

    def picked(i):
        slots = lax.broadcasted_iota(jnp.int32, (rows, length), 0) + i * rows
        across = lax.broadcasted_iota(jnp.int32, (rows, length), 1)
        source = tables_in_kernel(lengths_ref, order_ref, slots)[0]
        return dot_nn((source == across).astype(F32).astype(BF), x_all[...])

    def norm_block(i):
        span = pl.ds(pl.multiple_of(i * rows, rows), rows)
        resid = picked(i)
        inverse = lax.rsqrt(jnp.mean(resid * resid, axis=1, keepdims=True) + EPSILON)
        normed[span, :] = (resid * inverse * gain_ref[...]).astype(BF)

    each(length // rows // 2, norm_block)
    grad_copies[0].wait_recv()
    grad_copies[2].start()
    grad_copies[0].wait_send()
    send_far(convs[2])
    each(length // rows // 2, lambda i: norm_block(i + length // rows // 2))
    grad_copies[1].wait_recv()
    grad_copies[2].wait_recv()
    line_own(1).start()
    lines[1].start()
    pass_on(convs[0])
    send_far(convs[3])
    resid_ref[...] = picked(mine).astype(BF)
    normed_store = pltpu.make_async_copy(normed, normed_out_ref, local_sem.at[1])
    normed_store.start()

    def inverse_block(i):
        span = pl.ds(pl.multiple_of(i * rows, rows), rows)
        given = x_all[span, :].astype(F32)
        inverse_ref[span, :] = spread(
            lax.rsqrt(jnp.mean(given * given, axis=1, keepdims=True) + EPSILON)
        )

    def project(store, target, at, count):
        span = pl.ds(at, count)
        target[:, span] = dot_nt(normed[...], store[span, :]).astype(BF)

    def conv_chunk(q):
        arrived(convs[q])
        project(w_conv, conv_in_ref, q * CHUNK, CHUNK)

    def gate_chunk(q):
        arrived(gates[q])
        project(w_gate, gate_ref, q * CHUNK, CHUNK)

    pass_on(convs[1])
    send_far(tail)
    lines[0].step(1)
    each(length // rows, inverse_block)
    pass_on(convs[2])
    send_far(gates[0])
    conv_chunk(0)
    pass_on(convs[3])
    send_far(gates[1])
    lines[0].step(2)
    conv_chunk(1)
    pass_on(tail)
    send_far(gates[2])
    conv_chunk(2)
    send_far(gates[3])
    conv_chunk(3)
    arrived(tail)
    project(w_conv, conv_in_ref, width, TAIL_PAD)
    conv_store = pltpu.make_async_copy(w_conv, w_conv_out_ref, local_sem.at[2])
    conv_store.start()
    lines[1].step(1)
    yield
    pass_on(gates[0])
    lines[0].step(3)
    yield
    pass_on(gates[1])
    lines[1].step(2)
    gate_chunk(0)
    yield
    pass_on(gates[2])
    gate_chunk(1)
    pass_on(gates[3])
    gate_chunk(2)
    gate_chunk(3)
    gate_store = pltpu.make_async_copy(w_gate, w_gate_out_ref, local_sem.at[3])
    gate_store.start()
    grads_store = pltpu.make_async_copy(grads, branch_grad_out_ref, local_sem.at[6])
    grads_store.start()
    lines[1].step(3)
    yield
    for copies in convs + [tail] + gates:
        copies[2]().wait_send()
        copies[3]().wait_send()
    x_copies[1].wait_send()
    x_copies[2].wait_send()
    grad_copies[1].wait_send()
    grad_copies[2].wait_send()
    normed_store.wait()
    conv_store.wait()
    gate_store.wait()
    grads_store.wait()
    for kind in range(2):
        line_own(kind).wait()
        lines[kind].finish()
    yield


def conv_pre(x, conv_w, conv_b, place):
    pre = conv_b + conv_w[KW - 1 : KW] * x
    for back in range(1, KW):
        moved = pltpu.roll(x, back, 0)
        pre = pre + jnp.where(place >= back, conv_w[KW - 1 - back : KW - back] * moved, 0.0)
    return pre


def conv_lanes(chunk, width, mine):
    if 128 * chunk < width:
        return pl.ds(pl.multiple_of(mine * width + 128 * chunk, 128), 128)
    return pl.ds(DI + 128 * chunk - width, 128)


def block_terms(place):
    local = lax.broadcasted_iota(jnp.int32, (SPAN, 128), 0)
    across = lax.broadcasted_iota(jnp.int32, (SPAN, 128), 1)
    begins = local - place
    causal = (across <= local) & (across >= begins)
    reach_end = local >= begins[SPAN - 1 : SPAN, :]
    entered = place >= local + 1
    carries = place[SPAN - 1 : SPAN, :] >= SPAN
    return causal, reach_end, entered, carries


def pair_terms(pair, run, run_t, step, causal, reach_end, entered, carries):
    left = lax.broadcasted_iota(jnp.int32, (SPAN, 128), 1) < P_SIZE
    runs = [spread(run[:, 2 * pair + i : 2 * pair + i + 1]) for i in range(2)]
    decays = []
    for i in range(2):
        gap = runs[i] - run_t[2 * pair + i : 2 * pair + i + 1, :]
        decays.append(jnp.exp(jnp.where(causal, gap, -jnp.inf)))
    both = jnp.where(left, runs[0], runs[1])
    end = both[SPAN - 1 : SPAN, :]
    entering = jnp.where(entered, jnp.exp(both), 0.0)
    tail = jnp.where(reach_end, jnp.exp(jnp.where(reach_end, end - both, 0.0)), 0.0)
    carried = jnp.where(carries, jnp.exp(end), 0.0)
    size = jnp.where(
        left,
        spread(step[:, 2 * pair : 2 * pair + 1]),
        spread(step[:, 2 * pair + 1 : 2 * pair + 2]),
    )
    return left, decays, entering, tail, carried, size


def stacked(value, left):
    zero = jnp.zeros_like(value)
    return jnp.concatenate([jnp.where(left, value, zero), jnp.where(left, zero, value)], axis=0)


def own_lanes(row, mine, heads):
    return pltpu.roll(row, lax.rem(128 - mine * heads, 128), 1)


def skip_lanes(row, pair):
    left = lax.broadcasted_iota(jnp.int32, (1, 128), 1) < P_SIZE
    return jnp.where(
        left,
        spread(row[:, 2 * pair : 2 * pair + 1]),
        spread(row[:, 2 * pair + 1 : 2 * pair + 2]),
    )


def step_and_run(conv_in_ref, heads_ref, run_ref, step_ref, width, mine):
    length = run_ref.shape[0]
    heads = width // P_SIZE
    lower = (
        lax.broadcasted_iota(jnp.int32, (SPAN, SPAN), 0)
        >= lax.broadcasted_iota(jnp.int32, (SPAN, SPAN), 1)
    ).astype(F32)
    bias = heads_ref[0:1, :]
    rate = jnp.exp(own_lanes(heads_ref[...], mine, heads)[1:2, :])

    def block(b, unused):
        rows = pl.ds(pl.multiple_of(b * SPAN, SPAN), SPAN)
        raw = conv_in_ref[rows, width + 2 * N : width + 2 * N + 128].astype(F32)
        step = own_lanes(jax.nn.softplus(raw + bias), mine, heads)
        step_ref[rows, :] = step
        run_ref[rows, :] = jnp.dot(
            lower, -step * rate, precision=lax.Precision.HIGHEST, preferred_element_type=F32
        )
        return unused

    lax.fori_loop(0, length // SPAN, block, 0)


def along_line(step):
    rep = lax.axis_index("rep")
    there = lax.rem(rep // PLANE + step, LINE)
    return there * PLANE + lax.rem(rep, PLANE), there


def share_copy(source, taken, send_sem, recv_sem, step):
    to, there = along_line(step)
    z, wide = lax.axis_index("rep") // PLANE, taken.shape[2]
    return remote(
        source.at[:, pl.ds(pl.multiple_of(there * wide, 128), wide)],
        taken.at[z],
        send_sem.at[step],
        recv_sem.at[z],
        (to, lax.axis_index("shard")),
    )


def share_own(source, taken, sem):
    z, wide = lax.axis_index("rep") // PLANE, taken.shape[2]
    return pltpu.make_async_copy(
        source.at[:, pl.ds(pl.multiple_of(z * wide, 128), wide)], taken.at[z], sem
    )


def share_start(source, taken, send_sem, recv_sem, own):
    own.start()
    for step in range(1, LINE):
        share_copy(source, taken, send_sem, recv_sem, step).start()


def share_arrival(taken, recv_sem, own, step):
    to, there = along_line(step)
    if step == 0:
        own.wait()
    else:
        block, sem = taken.at[there], recv_sem.at[there]
        remote(block, block, sem, sem, (to, lax.axis_index("shard"))).wait_recv()
    return there


def share_sent(source, taken, send_sem, recv_sem):
    for step in range(1, LINE):
        share_copy(source, taken, send_sem, recv_sem, step).wait_send()


def in_given_order(back_ref, inverse_ref, grad_ref, given_ref, scaled_ref):
    length, width = grad_ref.shape

    def block(i, unused):
        span = pl.ds(pl.multiple_of(i * SPAN, SPAN), SPAN)
        moved = dot_nn(back_ref[span, :], grad_ref[...])
        if given_ref is not None:
            given_ref[span, :] = moved.astype(BF)
        for c in range(width // 128):
            lanes = slice(128 * c, 128 * c + 128)
            scaled_ref[span, lanes] = (moved[:, lanes] * inverse_ref[span, :]).astype(BF)
        return unused

    lax.fori_loop(0, length // SPAN, block, 0)


class RowSum:
    def __init__(self, partial, pair_in, row_out, row_in, send_sem, recv_sem):
        self.partial, self.pair_in, self.row_out, self.row_in = partial, pair_in, row_out, row_in
        self.rows = row_in.shape[0]
        mine, rep = lax.axis_index("shard"), lax.axis_index("rep")
        self.y, self.core = mine // 2, lax.rem(mine, 2)
        sibling, peer = self.y * 2 + (1 - self.core), (1 - self.y) * 2 + self.core
        self.pairs = [
            remote(
                partial.at[self.span(2 * side + (1 - self.core))],
                pair_in.at[side],
                send_sem.at[side],
                recv_sem.at[side],
                (rep, sibling),
            )
            for side in range(2)
        ]
        self.across = remote(row_out, row_in, send_sem.at[2], recv_sem.at[2], (rep, peer))

    def span(self, shard):
        return pl.ds(pl.multiple_of(shard * self.rows, self.rows), self.rows)

    def fill(self, rows_of):
        def block(i, unused):
            span = self.span(i)
            self.partial[span, :] = rows_of(span)
            return unused

        lax.fori_loop(0, self.partial.shape[0] // self.rows, block, 0)
        for copy in self.pairs:
            copy.start()

    def join(self):
        for copy in self.pairs:
            copy.wait_recv()
        there = self.span(2 * (1 - self.y) + self.core)
        self.row_out[...] = (self.pair_in[1 - self.y] + self.partial[there, :]).astype(BF)
        self.across.start()

    def result(self):
        self.across.wait_recv()
        here = self.partial[self.span(2 * self.y + self.core), :]
        return self.pair_in[self.y] + here + self.row_in[...].astype(F32)

    def finish(self):
        for copy in self.pairs + [self.across]:
            copy.wait_send()


def mixer_kernel(spans, *refs):
    refs = list(refs)

    def take(count):
        taken, refs[:] = refs[:count], refs[count:]
        return taken

    if spans:
        start_in = take(7)
        w_out_hbm, conv_w_ref, conv_b_ref, heads_ref, gain_ref = take(5)
        start_out = take(8)
        normed_out_ref, grad_gain_ref, grad_values_ref = take(3)
    else:
        conv_in_ref, gate_ref, branch_grad_ref, w_out_ref, place_ref = take(5)
        conv_w_ref, conv_b_ref, heads_ref, gain_ref = take(4)
        normed_out_ref, grad_gate_ref, grad_gain_ref, grad_values_ref, grad_tail_ref = take(5)
    grad_conv_w_ref, grad_conv_b_ref, grad_head_ref = take(3)
    if spans:
        taken_ref, taken_out_ref, gate_peer_ref = take(3)
        gate_given_ref, tail_ref = take(2)
    (
        mixed_ref,
        starts_ref,
        grad_mixed_ref,
        act_ref,
        pre_ref,
        step_ref,
        run_ref,
        state_ref,
        gno_ref,
        sums,
        grad_act_ref,
        joined_ref,
        join_ref,
        send_sem,
        recv_sem,
    ) = take(15)
    if spans:
        start_scratch = take(8)
        start_sems = take(8)
        conv_in_ref, gate_ref, branch_grad_ref, place_ref = start_scratch[:4]
        back_ref, inverse_ref = start_out[4], start_out[6]
        w_out_ref, grad_gate_ref, grad_tail_ref, scaled_ref, tail_in = take(5)
        share_send, share_recv, own_sem, peer_send, peer_recv, tail_send, tail_recv = take(7)
    length, width = gate_ref.shape
    mine, rep, shards = lax.axis_index("shard"), lax.axis_index("rep"), lax.axis_size("shard")
    heads = width // P_SIZE
    peers = [(rep, lax.rem(mine + step, shards)) for step in range(1, shards)]
    if spans:
        y, core = mine // 2, lax.rem(mine, 2)
        sibling, peer = y * 2 + (1 - core), (1 - y) * 2 + core
        others = [lax.rem(mine + step, shards) for step in range(1, shards)]
        rows = length // shards
        beside = rep // PLANE * PLANE + (1 - lax.rem(rep, PLANE))
        meet([(along_line(step)[0], mine) for step in range(1, LINE)] + [(beside, mine)] + peers)
        w_out_load = pltpu.make_async_copy(w_out_hbm, w_out_ref, own_sem.at[2])
        w_out_load.start()
        start = start_phases(*start_in, *start_out, *start_scratch, *start_sems)
        next(start)
    else:
        meet(peers)
    for c in range((width + 2 * N) // 128):
        lanes = slice(128 * c, 128 * c + 128)
        there = conv_lanes(c, width, mine)
        pre = conv_pre(
            conv_in_ref[:, lanes].astype(F32),
            conv_w_ref[:, there],
            conv_b_ref[:, there],
            place_ref[...],
        )
        pre_ref[:, lanes] = pre
        act_ref[:, lanes] = (pre * sigmoid(pre)).astype(BF)
    step_and_run(conv_in_ref, heads_ref, run_ref, step_ref, width, mine)
    if spans:
        next(start)
    state_ref[...] = jnp.zeros_like(state_ref)
    skips = own_lanes(heads_ref[...], mine, heads)[2:3, :]

    def forward_block(b, unused):
        row = pl.multiple_of(b * SPAN, SPAN)
        rows = pl.ds(row, SPAN)
        starts_ref[pl.ds(pl.multiple_of(b * N, N), N), :] = state_ref[...]
        run = run_ref[rows, :]
        run_t = run.T
        step = step_ref[rows, :]
        masks = block_terms(place_ref[rows, :])
        in_map = act_ref[rows, width : width + N]
        out_map = act_ref[rows, width + N : width + 2 * N]
        products = dot_nt(out_map, in_map)
        in_map_t = in_map.T
        for pair in range(width // 128):
            lanes = slice(128 * pair, 128 * pair + 128)
            left, decays, entering, tail, carried, size = pair_terms(
                pair, run, run_t, step, *masks
            )
            values = act_ref[rows, lanes].astype(F32)
            scaled = values * size
            weights = jnp.concatenate([(d * products).astype(BF) for d in decays], axis=1)
            out = dot_nn(weights, stacked(scaled.astype(BF), left))
            state = state_ref[:, lanes]
            high, low = halves(state)
            out += entering * (dot_nn(out_map, high) + dot_nn(out_map, low))
            mixed_ref[rows, lanes] = out + skip_lanes(skips, pair) * values
            high, low = halves(tail * scaled)
            fresh = dot_nn(in_map_t, high) + dot_nn(in_map_t, low)
            state_ref[:, lanes] = carried * state + fresh
        return unused

    halfway = length // SPAN // 2
    lax.fori_loop(0, halfway, forward_block, 0)
    if spans:
        next(start)
    lax.fori_loop(halfway, length // SPAN, forward_block, 0)
    if spans:
        next(start)
        w_out_load.wait()

    lane = lax.broadcasted_iota(jnp.int32, (SPAN, 128), 1)

    def gated(rows, c):
        lanes = slice(128 * c, 128 * c + 128)
        gate = gate_ref[rows, lanes].astype(F32)
        opened = sigmoid(gate)
        mixed = mixed_ref[rows, lanes]
        back = gno_ref[rows, lanes]
        gain = gain_ref[:, pl.ds(pl.multiple_of(mine * width + 128 * c, 128), 128)]
        return gate, opened, mixed, back, gain, mixed * (gate * opened), back * gain

    def measure(b, unused):
        rows = pl.ds(pl.multiple_of(b * SPAN, SPAN), SPAN)
        gno_ref[rows, :] = dot_nt(branch_grad_ref[rows, :], w_out_ref[...])
        squares = jnp.zeros((SPAN, 128), F32)
        crosses = jnp.zeros((SPAN, 128), F32)
        for c in range(width // 128):
            product, weighted = gated(rows, c)[5:]
            squares += product * product
            crosses += weighted * product
        squares = jnp.sum(squares, axis=1, keepdims=True)
        crosses = jnp.sum(crosses, axis=1, keepdims=True)
        both = jnp.where(lane == 0, spread(squares), jnp.where(lane == 1, spread(crosses), 0.0))
        sums[mine, :, rows] = both.T[0:8, :]
        return unused

    lax.fori_loop(0, length // SPAN, measure, 0)

    copies = [
        remote(sums.at[mine], sums.at[mine], send_sem.at[i], recv_sem.at[i], peer)
        for i, peer in enumerate(peers)
    ]
    for copy in copies:
        copy.start()
    for copy in copies:
        copy.wait_recv()
    grad_gain_ref[...] = jnp.zeros_like(grad_gain_ref)

    def finish(b, unused):
        rows = pl.ds(pl.multiple_of(b * SPAN, SPAN), SPAN)
        both = sums[0, :, rows]
        for shard in range(1, shards):
            both = both + sums[shard, :, rows]
        both = jnp.concatenate([both, jnp.zeros((SPAN - 8, SPAN), F32)], axis=0).T / DI
        inverse = lax.rsqrt(both[:, 0:1] + EPSILON)
        pull = spread(inverse * inverse * inverse * both[:, 1:2])
        inverse = spread(inverse)
        for c in range(width // 128):
            lanes = slice(128 * c, 128 * c + 128)
            gate, opened, mixed, back, gain, product, weighted = gated(rows, c)
            normalized = product * inverse
            normed_out_ref[rows, lanes] = (normalized * gain).astype(BF)
            grad_product = inverse * weighted - product * pull
            grad_gain_ref[:, lanes] += jnp.sum(back * normalized, axis=0, keepdims=True)
            grad_mixed_ref[rows, lanes] = grad_product * (gate * opened)
            grad_gate_ref[rows, lanes] = (
                grad_product * mixed * (opened * (1.0 + gate * (1.0 - opened)))
            ).astype(BF)
        return unused

    lax.fori_loop(0, length // SPAN, finish, 0)
    for copy in copies:
        copy.wait_send()
    if spans:
        exchanges = ((scaled_ref, taken_ref), (normed_out_ref, taken_out_ref))
        own_shares = [share_own(*pair, own_sem.at[i]) for i, pair in enumerate(exchanges)]

        def gate_peer_copy(at):
            return remote(
                taken_ref.at[at], gate_peer_ref.at[at], peer_send.at[at], peer_recv.at[at], (rep, peer)
            )

        def row_block(ref, shard):
            return ref.at[pl.ds(pl.multiple_of(shard * rows, rows), rows)]

        tail_out = [
            remote(
                row_block(grad_tail_ref, other),
                tail_in.at[i],
                tail_send.at[0, i],
                tail_recv.at[0, i],
                (rep, other),
            )
            for i, other in enumerate(others)
        ]
        tail_back = [
            remote(
                row_block(tail_ref, mine),
                row_block(tail_ref, mine),
                tail_send.at[1, i],
                tail_recv.at[1, i],
                (rep, other),
            )
            for i, other in enumerate(others)
        ]
        in_given_order(back_ref, inverse_ref, grad_gate_ref, gate_given_ref, scaled_ref)
        share_start(*exchanges[0], share_send.at[0], share_recv.at[0], own_shares[0])
    state_ref[...] = jnp.zeros_like(state_ref)
    grad_head_ref[...] = jnp.zeros_like(grad_head_ref)
    upper = (
        lax.broadcasted_iota(jnp.int32, (SPAN, SPAN), 0)
        <= lax.broadcasted_iota(jnp.int32, (SPAN, SPAN), 1)
    ).astype(F32)
    last_row = lax.broadcasted_iota(jnp.int32, (SPAN, 128), 0) == SPAN - 1
    join_ref[...] = (
        lax.broadcasted_iota(jnp.int32, (width, 128), 0) // P_SIZE + mine * heads
        == lax.broadcasted_iota(jnp.int32, (width, 128), 1)
    ).astype(F32).astype(BF)

    blocks = length // SPAN

    def backward_block(count, unused):
        b = blocks - 1 - count
        row = pl.multiple_of(b * SPAN, SPAN)
        rows = pl.ds(row, SPAN)
        start_rows = pl.ds(pl.multiple_of(b * N, N), N)
        run = run_ref[rows, :]
        run_t = run.T
        step = step_ref[rows, :]
        masks = block_terms(place_ref[rows, :])
        in_map = act_ref[rows, width : width + N]
        out_map = act_ref[rows, width + N : width + 2 * N]
        out_map_t = out_map.T
        products = dot_nt(out_map, in_map)
        grad_products = jnp.zeros((SPAN, SPAN), F32)
        grad_out_map = jnp.zeros((SPAN, N), F32)
        grad_in_map = jnp.zeros((SPAN, N), F32)
        for pair in range(width // 128):
            lanes = slice(128 * pair, 128 * pair + 128)
            left, decays, entering, tail, carried, size = pair_terms(
                pair, run, run_t, step, *masks
            )
            values = act_ref[rows, lanes].astype(F32)
            grad = grad_mixed_ref[rows, lanes]
            start = starts_ref[start_rows, lanes]
            later = state_ref[:, lanes]
            scaled = values * size
            scaled_low = scaled.astype(BF)
            grad_low = grad.astype(BF)
            weights = jnp.concatenate([(d * products).astype(BF) for d in decays], axis=0)
            grad_scaled = dot_tn(weights, stacked(grad_low, left))
            grad_pairs = dot_nt(grad_low, stacked(scaled_low, left))
            grad_products += (
                grad_pairs[:, :SPAN] * decays[0] + grad_pairs[:, SPAN:] * decays[1]
            )
            later_high, later_low = halves(later)
            from_later = tail * (dot_nn(in_map, later_high) + dot_nn(in_map, later_low))
            grad_scaled += from_later
            entering_high, entering_low = halves(entering * grad)
            grad_out_map += dot_nt(entering_high, start.astype(BF))
            grad_in_map += dot_nt((tail * scaled).astype(BF), later_high)
            ending = jnp.sum(scaled * from_later, axis=0, keepdims=True) + carried * jnp.sum(
                start * later, axis=0, keepdims=True
            )
            state_ref[:, lanes] = (
                carried * later + dot_nn(out_map_t, entering_high) + dot_nn(out_map_t, entering_low)
            )
            skip = skip_lanes(skips, pair)
            inner = mixed_ref[rows, lanes] - skip * values
            joined_ref[0:SPAN, lanes] = (
                grad_low.astype(F32) * inner
                - scaled_low.astype(F32) * (grad_scaled - from_later)
                - scaled * from_later
                + jnp.where(last_row, ending, 0.0)
            )
            joined_ref[SPAN : 2 * SPAN, lanes] = grad_scaled * values
            joined_ref[2 * SPAN : 2 * SPAN + 16, lanes] = spread_rows(
                jnp.sum(grad * values, axis=0, keepdims=True)
            )
            grad_act_ref[rows, lanes] = grad_scaled * size + skip * grad
        grad_products = grad_products.astype(BF)
        grad_act_ref[rows, width : width + N] = grad_in_map + dot_tn(grad_products, out_map)
        grad_act_ref[rows, width + N : width + 2 * N] = grad_out_map + dot_nn(
            grad_products, in_map
        )
        joined = joined_ref[...]
        first = joined.astype(BF)
        second, third = halves(joined - first.astype(F32))
        join = join_ref[...]
        by_head = dot_nn(first, join) + dot_nn(second, join) + dot_nn(third, join)
        grad_log = jnp.dot(
            upper, by_head[:SPAN], precision=lax.Precision.HIGHEST, preferred_element_type=F32
        )
        rate = jnp.exp(heads_ref[1:2, :])
        raw = conv_in_ref[rows, width + 2 * N : width + 2 * N + 128].astype(F32) + heads_ref[0:1, :]
        grad_dt = (by_head[SPAN : 2 * SPAN] - grad_log * rate) * sigmoid(raw)
        grad_tail_ref[rows, 2 * N : 2 * N + 128] = grad_dt
        grad_head_ref[0:1, :] += jnp.sum(grad_dt, axis=0, keepdims=True)
        grad_head_ref[1:2, :] += jnp.sum(
            -grad_log * jax.nn.softplus(raw) * rate, axis=0, keepdims=True
        )
        grad_head_ref[2:3, :] += by_head[2 * SPAN : 2 * SPAN + 1]
        return unused

    if spans:
        lax.fori_loop(0, blocks - 1, backward_block, 0)
        for step in range(LINE):
            at = share_arrival(taken_ref, share_recv.at[0], own_shares[0], step)
            gate_peer_copy(at).start()
        lax.fori_loop(blocks - 1, blocks, backward_block, 0)
        share_start(*exchanges[1], share_send.at[1], share_recv.at[1], own_shares[1])
    else:
        lax.fori_loop(0, blocks, backward_block, 0)

    place = place_ref[...]
    own_chunks = width // 128
    for c in [own_chunks, own_chunks + 1] + list(range(own_chunks)):
        lanes = slice(128 * c, 128 * c + 128)
        x = conv_in_ref[:, lanes].astype(F32)
        conv_w = conv_w_ref[:, conv_lanes(c, width, mine)]
        pre = pre_ref[:, lanes]
        gain = sigmoid(pre)
        grad_pre = grad_act_ref[:, lanes] * (gain * (1.0 + pre * (1.0 - gain)))
        grad_conv_b_ref[:, lanes] = jnp.sum(grad_pre, axis=0, keepdims=True)
        grad_conv_w_ref[KW - 1 : KW, lanes] = jnp.sum(grad_pre * x, axis=0, keepdims=True)
        grad_x = conv_w[KW - 1 : KW] * grad_pre
        for back in range(1, KW):
            tap = KW - 1 - back
            kept = jnp.where(place >= back, grad_pre, 0.0)
            grad_conv_w_ref[tap : tap + 1, lanes] = jnp.sum(
                kept * pltpu.roll(x, back, 0), axis=0, keepdims=True
            )
            grad_x += conv_w[tap : tap + 1] * pltpu.roll(kept, length - back, 0)
        if c < width // 128:
            grad_values_ref[:, lanes] = grad_x.astype(BF)
        else:
            grad_tail_ref[:, 128 * c - width : 128 * c - width + 128] = grad_x
        if spans and c == own_chunks + 1:
            for copy in tail_out:
                copy.start()
    if spans:
        span = pl.ds(pl.multiple_of(mine * rows, rows), rows)
        tail = grad_tail_ref[span, :]
        for i, copy in enumerate(tail_out):
            copy.wait_recv()
            tail = tail + tail_in[i]
        tail_ref[span, :] = tail.astype(BF)
        for copy in tail_back:
            copy.start()
        for step in range(LINE):
            share_arrival(taken_out_ref, share_recv.at[1], own_shares[1], step)
        for i, pair in enumerate(exchanges):
            share_sent(*pair, share_send.at[i], share_recv.at[i])
        for at in range(LINE):
            gate_peer_copy(at).wait()
        for copy in tail_out:
            copy.wait_send()
        for copy in tail_back:
            copy.wait()
        next(start)


def run_mixer(operands, shards, spans):
    if spans:
        rows = operands[2].shape[0]
        length, width = rows * shards, DI // shards
    else:
        length, width = operands[1].shape
        rows = length // shards
    blocks, chunks = length // SPAN, width // CHUNK
    shape = jax.ShapeDtypeStruct
    vector = pl.BlockSpec(memory_space=pltpu.VMEM)
    anywhere = pl.BlockSpec(memory_space=pl.ANY)
    scalars = pl.BlockSpec(memory_space=pltpu.SMEM)
    dma = pltpu.SemaphoreType.DMA
    small = [
        shape((KW, width + 2 * N), F32),
        shape((1, width + 2 * N), F32),
        shape((8, 128), F32),
    ]
    scratch = [
        pltpu.VMEM((length, width), F32),
        pltpu.VMEM((blocks * N, width), F32),
        pltpu.VMEM((length, width), F32),
        pltpu.VMEM((length, width + 2 * N), BF),
        pltpu.VMEM((length, width + 2 * N), F32),
        pltpu.VMEM((length, 128), F32),
        pltpu.VMEM((length, 128), F32),
        pltpu.VMEM((N, width), F32),
        pltpu.VMEM((length, width), F32),
        pltpu.VMEM((shards, 8, length), F32),
        pltpu.VMEM((length, width + 2 * N), F32),
        pltpu.VMEM((2 * SPAN + 16, width), F32),
        pltpu.VMEM((width, 128), BF),
        dma((shards - 1,)),
        dma((shards - 1,)),
    ]
    if spans:
        taken = shape((LINE, length, 2 * 128), BF)
        outs = [
            (shape((length, D), BF), anywhere),
            (shape((width, D), BF), anywhere),
            (shape((width + TAIL_PAD, D), BF), anywhere),
            (shape((length, D), BF), anywhere),
            (shape((length, length), BF), vector),
            (shape((rows, D), BF), vector),
            (shape((length, 128), F32), vector),
            (shape((2, LINE, length, D // 2), BF), anywhere),
            (shape((length, width), BF), vector),
            (shape((1, width), F32), vector),
            (shape((length, width), BF), vector),
            *[(one, vector) for one in small],
            (taken, anywhere),
            (taken, anywhere),
            (taken, anywhere),
            (shape((length, width), BF), vector),
            (shape((length, TAIL_PAD), BF), vector),
        ]
        in_specs = [scalars, scalars, anywhere, vector, vector, vector, anywhere, anywhere]
        in_specs += [vector] * 4
        weights = 2 * chunks + 1
        scratch += [
            pltpu.VMEM((length, width + TAIL_PAD), BF),
            pltpu.VMEM((length, width), BF),
            pltpu.VMEM((length, D), BF),
            pltpu.VMEM((length, 128), jnp.int32),
            pltpu.VMEM((length, D), BF),
            pltpu.VMEM((length, D), BF),
            pltpu.VMEM((width, D), BF),
            pltpu.VMEM((width + TAIL_PAD, D), BF),
            dma((7,)),
            dma((2, 3)),
            dma((2, 3)),
            dma((4, weights)),
            dma((4, weights)),
            dma((weights,)),
            dma((2, 3, LINE)),
            dma((2, 2, LINE)),
            pltpu.VMEM((width, D), BF),
            pltpu.VMEM((length, width), BF),
            pltpu.VMEM((length, TAIL_PAD), F32),
            pltpu.VMEM((length, width), BF),
            pltpu.VMEM((shards - 1, rows, TAIL_PAD), F32),
            dma((2, LINE)),
            dma((2, LINE)),
            dma((3,)),
            dma((LINE,)),
            dma((LINE,)),
            dma((2, shards - 1)),
            dma((2, shards - 1)),
        ]
    else:
        wide = shape((length, width), BF)
        outs = [wide, wide, shape((1, width), F32), wide, shape((length, TAIL_PAD), F32), *small]
        outs = [(one, vector) for one in outs]
        in_specs = [vector] * 9
    return pl.pallas_call(
        functools.partial(mixer_kernel, spans),
        out_shape=tuple(out for out, spec in outs),
        in_specs=in_specs,
        out_specs=tuple(spec for out, spec in outs),
        scratch_shapes=scratch,
        compiler_params=pltpu.CompilerParams(
            vmem_limit_bytes=VMEM_BYTES, collective_id=2, has_side_effects=True
        ),
        cost_estimate=pl.CostEstimate(
            flops=60 * length * width * 128, bytes_accessed=32 * length * width, transcendentals=0
        ),
        name="mixer",
    )(*operands)


def end_kernel(
    gate_taken_hbm,
    gate_peer_hbm,
    out_taken_hbm,
    gate_given_ref,
    values_ref,
    tail_low,
    normed_ref,
    line_ref,
    inverse_ref,
    w_gate_hbm,
    w_conv_hbm,
    w_out_hbm,
    normed_out_hbm,
    back_ref,
    branch_grad_hbm,
    x_ref,
    resid_ref,
    valid_ref,
    gain_ref,
    grad_conv_w_ref,
    grad_conv_b_ref,
    grad_head_ref,
    grad_gain_ref,
    parts_ref,
    w_out_grad_ref,
    tails_ref,
    block_out_ref,
    grad_in_ref,
    out_norm_ref,
    out_conv_w_ref,
    out_conv_b_ref,
    out_head_ref,
    out_gain_ref,
    taken,
    taken_peer,
    values_given_ref,
    scaled_ref,
    group_rows,
    own_columns,
    total,
    sum_kept,
    mail_out,
    mail_in,
    low,
    partial,
    pair_in,
    row_out,
    row_in,
    branch_pair,
    branch_out,
    branch_in,
    tail_sum,
    tail_own,
    tail_parts,
    small,
    small_in,
    small_all,
    w_gate_ref,
    w_conv_ref,
    branch_grad_ref,
    w_out_ref,
    normed_out_ref,
    load_sem,
    local_sem,
    group_sem,
    share_send,
    share_recv,
    peer_send,
    peer_recv,
    mail_send,
    mail_recv,
    swap_send,
    swap_recv,
    line_send,
    line_recv,
    side_send,
    side_recv,
    cross_send,
    cross_recv,
    pair_send,
    pair_recv,
    branch_send,
    branch_recv,
    rep_send,
    rep_recv,
    all_send,
    all_recv,
):
    reps, shards = LINE * PLANE, lax.axis_size("shard")
    mine, rep = lax.axis_index("shard"), lax.axis_index("rep")
    y, c = mine // 2, lax.rem(mine, 2)
    z, x = rep // PLANE, lax.rem(rep, PLANE)
    beside = z * PLANE + (1 - x)
    rows, length = x_ref.shape[0], values_ref.shape[0]
    width, depth = values_ref.shape[1], own_columns.shape[1]
    half = D // 2
    sibling, peer = y * 2 + (1 - c), (1 - y) * 2 + c

    def other(step):
        return lax.rem(z + step // PLANE, LINE) * PLANE + lax.rem(x + step % PLANE, PLANE)

    def before(step):
        return lax.rem(z + LINE - step // PLANE, LINE) * PLANE + lax.rem(
            x + PLANE - step % PLANE, PLANE
        )

    def shard_at(step):
        return lax.rem(mine + step, shards)

    def each(count, body):
        def step(i, unused):
            body(i)
            return unused

        lax.fori_loop(0, count, step, 0)

    meet(
        [(other(step), mine) for step in range(1, reps)]
        + [(rep, shard_at(step)) for step in range(1, shards)]
    )

    loads = [
        pltpu.make_async_copy(far_ref, near_ref, load_sem.at[i])
        for i, (far_ref, near_ref) in enumerate(
            [
                (w_gate_hbm, w_gate_ref),
                (w_conv_hbm, w_conv_ref),
                (branch_grad_hbm, branch_grad_ref),
                (w_out_hbm, w_out_ref),
                (normed_out_hbm, normed_out_ref),
            ]
        )
    ]

    def group_copy(part, step):
        at = along_line(step)[1]
        return pltpu.make_async_copy(
            line_ref.at[part // 2, at], group_rows.at[step], group_sem.at[step]
        )

    def peer_copy(part, at):
        return remote(
            taken.at[part, at],
            taken_peer.at[part, at],
            peer_send.at[part, at],
            peer_recv.at[part, at],
            (rep, peer),
        )

    own_part = pltpu.make_async_copy(
        normed_ref.at[:, pl.ds(pl.multiple_of(mine * depth, depth), depth)],
        own_columns,
        local_sem.at[4],
    )
    own_part.start()
    gate_load = pltpu.make_async_copy(gate_taken_hbm, taken.at[0], local_sem.at[0])
    gate_load.start()
    peer_load = pltpu.make_async_copy(gate_peer_hbm, taken_peer.at[0], local_sem.at[7])
    peer_load.start()
    out_load = pltpu.make_async_copy(out_taken_hbm, taken.at[2], local_sem.at[5])
    out_load.start()
    for step in range(LINE):
        group_copy(0, step).start()
    out_load.wait()
    for at in range(LINE):
        peer_copy(2, at).start()

    for load in loads[::-1]:
        load.start()

    rows_sum = RowSum(partial, pair_in, row_out, row_in, pair_send, pair_recv)
    branch_sum = RowSum(partial, branch_pair, branch_out, branch_in, branch_send, branch_recv)

    def swap_copy(part):
        if part == 2:
            return remote(
                low.at[2, pl.ds(pl.multiple_of((1 - y) * 128, 128), 128), :],
                w_out_grad_ref.at[rep, :, pl.ds(pl.multiple_of(y * half, 128), half)],
                swap_send.at[2],
                swap_recv.at[2],
                (rep, peer),
            )
        return remote(
            low.at[part, :, pl.ds(pl.multiple_of((1 - c) * depth, depth), depth)],
            parts_ref.at[rep, part, c],
            swap_send.at[part],
            swap_recv.at[part],
            (rep, sibling),
        )

    def swap_own(part):
        if part == 2:
            return pltpu.make_async_copy(
                low.at[2, pl.ds(pl.multiple_of(y * 128, 128), 128), :],
                w_out_grad_ref.at[rep, :, pl.ds(pl.multiple_of(y * half, 128), half)],
                local_sem.at[6],
            )
        return pltpu.make_async_copy(
            low.at[part, :, pl.ds(pl.multiple_of(c * depth, depth), depth)],
            parts_ref.at[rep, part, c],
            local_sem.at[2 + part],
        )

    def mail_copy(part):
        return remote(
            mail_out.at[part],
            mail_in.at[part],
            mail_send.at[part],
            mail_recv.at[part],
            (beside, mine),
        )

    def sum_groups(part, then=None):
        for step in range(LINE):
            at = along_line(step)[1]
            if part > 0:
                peer_copy(part, at).wait_recv()
            elif step == 0:
                gate_load.wait()
                peer_load.wait()
            group_copy(part, step).wait()
            both = jnp.concatenate([taken[part, at], taken_peer[part, at]], axis=1)
            for lanes in (slice(0, half // 2), slice(half // 2, half)):
                term = dot_tn(both, group_rows[step, :, lanes])
                if step == 0:
                    total[:, lanes] = term
                else:
                    total[:, lanes] += term
            if then is not None:
                group_copy(then, step).start()
        for source, place in ((0, y), (256, 1 - y)):
            rows_kept = pl.ds(pl.multiple_of(source + x * 128, 128), 128)
            rows_sent = pl.ds(pl.multiple_of(source + (1 - x) * 128, 128), 128)
            there = pl.ds(pl.multiple_of(place * 128, 128), 128)
            sum_kept[there, :] = total[rows_kept, :]
            mail_out[part, there, :] = total[rows_sent, :].astype(BF)
        mail_copy(part).start()

    def close_sum(part):
        gains = gain_ref[:, pl.ds(pl.multiple_of(y * half, 128), half)] if part < 2 else 1.0
        mail_copy(part).wait_recv()
        low[part] = ((sum_kept[...] + mail_in[part].astype(F32)) * gains).astype(BF)
        swap_own(part).start()
        swap_copy(part).start()

    def sum_block(part, owner):
        return w_out_grad_ref.at[owner, 0:64] if part == 2 else parts_ref.at[owner, part]

    def cross_block(origin, column):
        owner = origin * PLANE + (x if column == 0 else 1 - x)
        return w_out_grad_ref.at[owner, 64:128]

    def cross_side(column):
        block = cross_block(z, column)
        return remote(
            block, block, cross_send.at[0, 2, 0], cross_recv.at[2, 0], (beside, mine)
        )

    def cross_copy(column, origin, toward):
        block = cross_block(origin, column)
        return remote(
            block,
            block,
            cross_send.at[column, (1 - toward) // 2, origin],
            cross_recv.at[column, origin],
            ((z + toward) * PLANE + x, mine),
        )

    def inner(toward):
        return z < LINE - 1 if toward > 0 else z > 0

    def cross_start(column):
        for toward in (1, -1):

            @pl.when(inner(toward))
            def _(toward=toward):
                cross_copy(column, z, toward).start()

    def cross_pass(step):
        for column in range(PLANE):
            for toward in (1, -1):
                origin = z - toward * step

                @pl.when(origin >= 0 if toward > 0 else origin < LINE)
                def _(column=column, origin=origin, toward=toward):
                    cross_copy(column, origin, toward).wait_recv()

                    @pl.when(inner(toward))
                    def _():
                        cross_copy(column, origin, toward).start()

    def cross_finish():
        cross_side(0).wait_send()
        for column in range(PLANE):
            for toward in (1, -1):
                for origin in range(LINE):
                    passed = origin <= z if toward > 0 else origin >= z

                    @pl.when(passed & inner(toward))
                    def _(column=column, origin=origin, toward=toward):
                        cross_copy(column, origin, toward).wait_send()

    def line_copy(part, origin, toward, lane):
        block = sum_block(part, origin * PLANE + x)
        return remote(
            block,
            block,
            line_send.at[part, lane, origin],
            line_recv.at[part, origin],
            ((z + toward) * PLANE + x, mine),
        )

    def side_copy(part, origin, from_x):
        block = sum_block(part, origin * PLANE + from_x)
        return remote(
            block, block, side_send.at[part, origin], side_recv.at[part, origin], (beside, mine)
        )

    def spread_own(part):
        swap_own(part).wait()
        swap_copy(part).wait_recv()
        side_copy(part, z, x).start()

        @pl.when(z < LINE - 1)
        def _():
            line_copy(part, z, 1, 0).start()

        @pl.when(z > 0)
        def _():
            line_copy(part, z, -1, 1).start()

    def pass_on(part, step):
        @pl.when(z - step >= 0)
        def _():
            origin = z - step
            line_copy(part, origin, 1, 0).wait_recv()

            @pl.when(z < LINE - 1)
            def _():
                line_copy(part, origin, 1, 0).start()

            side_copy(part, origin, x).start()

        @pl.when(z + step < LINE)
        def _():
            origin = z + step
            line_copy(part, origin, -1, 1).wait_recv()

            @pl.when(z > 0)
            def _():
                line_copy(part, origin, -1, 1).start()

            side_copy(part, origin, x).start()

    in_given_order(back_ref, inverse_ref, values_ref, values_given_ref, scaled_ref)
    own_share = share_own(scaled_ref, taken.at[1], local_sem.at[1])
    share_start(scaled_ref, taken.at[1], share_send, share_recv, own_share)
    sum_groups(0, 2)
    close_sum(0)
    spread_own(0)
    loads[3].wait()
    loads[4].wait()
    branch_sum.fill(lambda span: dot_nn(normed_out_ref[span, :], w_out_ref[...]))
    sum_groups(2, 1)
    branch_sum.join()
    close_sum(2)
    pass_on(0, 1)
    spread_own(2)
    cross_side(0).start()
    cross_start(0)

    branch = branch_sum.result()
    branch_sum.finish()
    whole = resid_ref[...].astype(F32) + branch
    block_out_ref[...] = whole.astype(BF)
    counts = valid_ref[...].astype(F32)
    square_total = jnp.sum(
        counts * jnp.sum(whole * whole, axis=1, keepdims=True), axis=0, keepdims=True
    )
    square_branch = jnp.sum(
        counts * jnp.sum(branch * branch, axis=1, keepdims=True), axis=0, keepdims=True
    )
    count = jnp.sum(counts, axis=0, keepdims=True)
    pass_on(0, 2)

    heads, share = H // shards, 2 * N // shards
    lane = lax.broadcasted_iota(jnp.int32, (rows, TAIL_PAD), 1)
    owned = ((lane >= mine * share) & (lane < (mine + 1) * share)) | (
        (lane >= 2 * N + mine * heads) & (lane < 2 * N + (mine + 1) * heads)
    )

    def grad_rows(span):
        tail = dot_nn(back_ref[span, :], tail_low[...])
        tail = jnp.where(owned, tail, 0.0).astype(BF)
        return (
            dot_nn(gate_given_ref[span, :], w_gate_ref[...])
            + dot_nn(values_given_ref[span, :], w_conv_ref[0:width, :])
            + dot_nn(tail, w_conv_ref[width:, :])
        )

    loads[0].wait()
    loads[1].wait()
    rows_sum.fill(grad_rows)

    share_rows = TAIL_PAD // reps

    def tail_rows(ref, owner):
        return ref.at[pl.ds(pl.multiple_of(owner * share_rows, 16), share_rows)]

    def tail_part_copy(step):
        to = other(step)
        return remote(
            tail_rows(tail_sum, to),
            tail_parts.at[step],
            rep_send.at[0, step],
            rep_recv.at[0, step],
            (to, mine),
        )

    def tail_spread_copy(step):
        return remote(
            tail_rows(tails_ref, rep),
            tail_rows(tails_ref, rep),
            rep_send.at[1, step],
            rep_recv.at[1, step],
            (other(step), mine),
        )

    own_part.wait()
    tail_own[...] = dot_tn(tail_low[...], own_columns[...])
    tail_sum[...] = tail_own[...].astype(BF)
    for step in range(1, reps):
        tail_part_copy(step).start()

    for step in range(LINE):
        at = share_arrival(taken.at[1], share_recv, own_share, step)
        peer_copy(1, at).start()
    rows_sum.join()
    pass_on(0, 3)

    pass_on(2, 1)
    cross_side(1).wait_recv()
    cross_start(1)
    for step in range(1, reps):
        tail_part_copy(step).wait_recv()
    span = pl.ds(pl.multiple_of(rep * share_rows, 16), share_rows)
    piece = tail_own[span, :]
    for step in range(1, reps):
        piece = piece + tail_parts[step].astype(F32)
    tails_ref[span, :] = piece.astype(BF)
    for step in range(1, reps):
        tail_spread_copy(step).start()

    grad_normed = rows_sum.result()
    given = x_ref[...].astype(F32)
    inverse = lax.rsqrt(jnp.mean(given * given, axis=1, keepdims=True) + EPSILON)
    grad_norm_gain = jnp.sum(grad_normed * (given * inverse), axis=0, keepdims=True)
    scaled = grad_normed * gain_ref[...]
    pull = inverse * inverse * inverse * jnp.mean(scaled * given, axis=1, keepdims=True)
    span = pl.ds(pl.multiple_of(mine * rows, rows), rows)
    loads[2].wait()
    kept = dot_nn(back_ref[span, :], branch_grad_ref[...])
    grad_in_ref[...] = (scaled * inverse - given * pull + kept).astype(BF)
    pass_on(2, 2)

    lane = lax.broadcasted_iota(jnp.int32, (1, 128), 1)
    at = 0
    for i in range(D // 128):
        small[at : at + 1, :] = grad_norm_gain[:, 128 * i : 128 * i + 128]
        at += 1
    channels = (width + 2 * N) // 128
    for tap in range(KW):
        for i in range(channels):
            small[at : at + 1, :] = grad_conv_w_ref[tap : tap + 1, 128 * i : 128 * i + 128]
            at += 1
    for i in range(channels):
        small[at : at + 1, :] = grad_conv_b_ref[:, 128 * i : 128 * i + 128]
        at += 1
    for i in range(width // 128):
        small[at : at + 1, :] = grad_gain_ref[:, 128 * i : 128 * i + 128]
        at += 1
    small[at : at + 3, :] = grad_head_ref[0:3, :]
    small[at + 3 : at + 4, :] = jnp.where(
        lane == 0,
        spread(square_total),
        jnp.where(lane == 1, spread(square_branch), jnp.where(lane == 2, spread(count), 0.0)),
    )
    small[at + 4 :, :] = jnp.zeros((small.shape[0] - at - 4, 128), F32)

    def small_rep_copy(step):
        return remote(
            small, small_in.at[rep], rep_send.at[2, step], rep_recv.at[2, step], (other(step), mine)
        )

    def small_rep_arrival(step):
        return remote(
            small,
            small_in.at[before(step)],
            rep_send.at[2, step],
            rep_recv.at[2, step],
            (other(step), mine),
        )

    def small_shard_copy(step):
        return remote(
            small_all.at[mine],
            small_all.at[mine],
            all_send.at[step],
            all_recv.at[step],
            (rep, shard_at(step)),
        )

    for step in range(1, reps):
        small_rep_copy(step).start()
    small_in[rep] = small[...]
    sum_groups(1)
    pass_on(2, 3)
    cross_pass(1)
    close_sum(1)
    spread_own(1)
    for step in range(1, reps):
        small_rep_arrival(step).wait_recv()
    added = small_in[0]
    for i in range(1, reps):
        added = added + small_in[i]
    small_all[mine] = added
    for step in range(1, shards):
        small_shard_copy(step).start()
    pass_on(1, 1)
    cross_pass(2)
    for step in range(1, shards):
        small_shard_copy(step).wait_recv()

    def over_shards(row):
        value = small_all[0, row : row + 1, :]
        for i in range(1, shards):
            value = value + small_all[i, row : row + 1, :]
        return value

    at = 0
    for i in range(D // 128):
        out_norm_ref[:, 128 * i : 128 * i + 128] = over_shards(at)
        at += 1
    for tap in range(KW + 1):
        ref, row = (out_conv_w_ref, tap) if tap < KW else (out_conv_b_ref, 0)
        for i in range(channels):
            if i < width // 128:
                for shard in range(shards):
                    to = shard * width + 128 * i
                    ref[row : row + 1, to : to + 128] = small_all[shard, at : at + 1, :]
            else:
                to = DI + 128 * i - width
                ref[row : row + 1, to : to + 128] = over_shards(at)
            at += 1
    for i in range(width // 128):
        for shard in range(shards):
            to = shard * width + 128 * i
            out_gain_ref[:, to : to + 128] = small_all[shard, at : at + 1, :]
        at += 1
    for i in range(3):
        out_head_ref[i : i + 1, :] = over_shards(at + i)
    stats = over_shards(at + 3)
    per = jnp.maximum(stats[:, 2:3], 1.0) * D
    out_head_ref[3:4, :] = jnp.sqrt(stats / spread(per))
    out_head_ref[4:8, :] = jnp.zeros((4, 128), F32)

    pass_on(1, 2)
    cross_pass(3)
    pass_on(1, 3)

    cross_finish()
    for step in range(1, reps):
        tail_spread_copy(step).wait_recv()
    for part in range(3):
        for origin in range(LINE):
            side_copy(part, origin, 1 - x).wait_recv()
            side_copy(part, origin, x).wait_send()

            @pl.when((origin <= z) & (z < LINE - 1))
            def _(part=part, origin=origin):
                line_copy(part, origin, 1, 0).wait_send()

            @pl.when((origin >= z) & (z > 0))
            def _(part=part, origin=origin):
                line_copy(part, origin, -1, 1).wait_send()

        swap_copy(part).wait_send()
        mail_copy(part).wait_send()
        if part > 0:
            for at in range(LINE):
                peer_copy(part, at).wait_send()
    share_sent(scaled_ref, taken.at[1], share_send, share_recv)
    rows_sum.finish()
    for step in range(1, shards):
        small_shard_copy(step).wait_send()
    for step in range(1, reps):
        tail_part_copy(step).wait_send()
        tail_spread_copy(step).wait_send()
        small_rep_copy(step).wait_send()


def run_end(operands, shards):
    reps = LINE * PLANE
    length, width = operands[4].shape
    rows, depth = length // shards, D // shards
    dma = pltpu.SemaphoreType.DMA
    vector = pl.BlockSpec(memory_space=pltpu.VMEM)
    anywhere = pl.BlockSpec(memory_space=pl.ANY)
    shape = jax.ShapeDtypeStruct
    channels = width + 2 * N
    small = -(-(D + 5 * channels + width + 4 * 128) // 1024) * 8
    return pl.pallas_call(
        end_kernel,
        out_shape=(
            shape((reps, 2, 2, 256, depth), BF),
            shape((reps, 128, D), BF),
            shape((TAIL_PAD, depth), BF),
            shape((rows, D), BF),
            shape((rows, D), BF),
            shape((1, D), F32),
            shape((KW, CONVW), F32),
            shape((1, CONVW), F32),
            shape((8, 128), F32),
            shape((1, DI), F32),
        ),
        in_specs=[anywhere] * 3 + [vector] * 3 + [anywhere] * 2 + [vector] + [anywhere] * 4 + [vector] + [anywhere] + [vector] * 8,
        out_specs=(anywhere,) * 2 + (vector,) * 8,
        scratch_shapes=[
            pltpu.VMEM((3, LINE, length, 256), BF),
            pltpu.VMEM((3, LINE, length, 256), BF),
            pltpu.VMEM((length, width), BF),
            pltpu.VMEM((length, width), BF),
            pltpu.VMEM((LINE, length, D // 2), BF),
            pltpu.VMEM((length, depth), BF),
            pltpu.VMEM((512, D // 2), F32),
            pltpu.VMEM((256, D // 2), F32),
            pltpu.VMEM((3, 256, D // 2), BF),
            pltpu.VMEM((3, 256, D // 2), BF),
            pltpu.VMEM((3, 256, D // 2), BF),
            pltpu.VMEM((length, D), F32),
            pltpu.VMEM((2, rows, D), F32),
            pltpu.VMEM((rows, D), BF),
            pltpu.VMEM((rows, D), BF),
            pltpu.VMEM((2, rows, D), F32),
            pltpu.VMEM((rows, D), BF),
            pltpu.VMEM((rows, D), BF),
            pltpu.VMEM((TAIL_PAD, depth), BF),
            pltpu.VMEM((TAIL_PAD, depth), F32),
            pltpu.VMEM((reps, TAIL_PAD // reps, depth), BF),
            pltpu.VMEM((small, 128), F32),
            pltpu.VMEM((reps, small, 128), F32),
            pltpu.VMEM((shards, small, 128), F32),
            pltpu.VMEM((width, D), BF),
            pltpu.VMEM((width + TAIL_PAD, D), BF),
            pltpu.VMEM((length, D), BF),
            pltpu.VMEM((width, D), BF),
            pltpu.VMEM((length, width), BF),
            dma((5,)),
            dma((8,)),
            dma((LINE,)),
            dma((LINE,)),
            dma((LINE,)),
            dma((3, LINE)),
            dma((3, LINE)),
            dma((3,)),
            dma((3,)),
            dma((3,)),
            dma((3,)),
            dma((3, 2, LINE)),
            dma((3, LINE)),
            dma((3, LINE)),
            dma((3, LINE)),
            dma((PLANE, 3, LINE)),
            dma((PLANE + 1, LINE)),
            dma((3,)),
            dma((3,)),
            dma((3,)),
            dma((3,)),
            dma((3, reps)),
            dma((3, reps)),
            dma((shards,)),
            dma((shards,)),
        ],
        compiler_params=pltpu.CompilerParams(
            vmem_limit_bytes=VMEM_BYTES, collective_id=3, has_side_effects=True
        ),
        cost_estimate=pl.CostEstimate(
            flops=2 * reps * length * D * 256, bytes_accessed=96 << 20, transcendentals=0
        ),
        name="weight_gradient",
    )(*operands)


def assemble_kernel(parts_ref, tail_ref, rows_ref, out_ref, rows_out_ref):
    step, steps = pl.program_id(0), pl.num_programs(0)
    reps = parts_ref.shape[0]

    @pl.when(step < steps - 1)
    def _():
        for rep in range(reps):
            out_ref[128 * rep : 128 * rep + 128, :] = parts_ref[rep, 0, 0].astype(F32)
        rows_out_ref[...] = rows_ref[...].astype(F32)

    @pl.when(step == steps - 1)
    def _():
        out_ref[0:TAIL, :] = tail_ref[0:TAIL, :].astype(F32)


def run_assemble(parts, tail, rows):
    reps, unused, cores, stack, depth = parts.shape
    shards = cores * stack // 128
    steps = 2 * shards

    def place(i):
        at = jnp.minimum(i, steps - 1)
        shard = lax.rem(at, shards)
        return (0, at // shards, lax.rem(shard, cores), shard // cores, 0)

    height = rows.shape[0] // steps

    def row_place(i):
        return (jnp.minimum(i, steps - 1), 0)

    return pl.pallas_call(
        assemble_kernel,
        grid=(steps + 1,),
        out_shape=(
            jax.ShapeDtypeStruct((PROJ, depth), F32),
            jax.ShapeDtypeStruct(rows.shape, F32),
        ),
        in_specs=[
            pl.BlockSpec((reps, 1, 1, 128, depth), place),
            pl.BlockSpec((TAIL_PAD, depth), lambda i: (0, 0)),
            pl.BlockSpec((height, D), row_place),
        ],
        out_specs=(
            pl.BlockSpec((reps * 128, depth), lambda i: (i, 0)),
            pl.BlockSpec((height, D), row_place),
        ),
        compiler_params=params(),
        name="assemble",
    )(parts, tail, rows)


def exchange(pieces, axis, mine):
    count = lax.axis_size(axis)
    own = pieces(mine)
    gathered = jnp.zeros((count,) + own.shape, own.dtype)
    gathered = lax.dynamic_update_index_in_dim(gathered, own, mine, 0)
    for other in range(1, count):
        arrived = lax.ppermute(
            pieces(mine ^ other), axis, [(i, i ^ other) for i in range(count)]
        )
        gathered = lax.dynamic_update_index_in_dim(gathered, arrived, mine ^ other, 0)
    return gathered


def columns_at(array, start, width):
    return lax.dynamic_slice_in_dim(array, start, width, axis=1)


def plain_device(
    x_in,
    cotangent,
    seq_lengths,
    seq_order,
    valid,
    norm_gain,
    w_in,
    conv_w,
    conv_b,
    head_rows,
    gain_row,
    w_out,
):
    shards, mine = lax.axis_size("shard"), lax.axis_index("shard")
    rows = x_in.shape[0]
    length = rows * shards
    depth = w_in.shape[0]
    heads = H // shards
    width = DI // shards
    share = 2 * N // shards
    w_tail = w_in[:, 2 * DI :]

    def conv_piece(d):
        return jnp.concatenate([columns_at(w_in, DI + d * width, width), w_tail], axis=1)

    x_group = lax.all_gather(x_in, "shard", axis=0, tiled=True)
    w_conv = exchange(conv_piece, "shard", mine).reshape(D, width + TAIL)
    w_gate = exchange(lambda d: columns_at(w_in, d * width, width), "shard", mine).reshape(D, width)
    branch_grad = lax.all_gather(
        jnp.where(valid[:, None] > 0, cotangent, jnp.zeros_like(cotangent)),
        "shard",
        axis=0,
        tiled=True,
    )
    slot_ids = jnp.arange(length, dtype=jnp.int32)
    source, target, position = slot_tables(seq_lengths[0], seq_order[0], slot_ids)
    resid = dot_nn((source[:, None] == slot_ids[None, :]).astype(BF), x_group)
    inverse_rms = lax.rsqrt(jnp.mean(resid * resid, axis=1, keepdims=True) + EPSILON)
    normed = (resid * inverse_rms * norm_gain[None, :]).astype(BF)
    resid_mine = lax.dynamic_slice_in_dim(resid, mine * rows, rows, axis=0)
    gate = dot_nn(normed, w_gate).astype(BF)
    conv_in = jnp.pad(dot_nn(normed, w_conv).astype(BF), ((0, 0), (0, TAIL_PAD - TAIL)))
    place = jnp.broadcast_to(position[:, None], (length, 128))
    (
        normed_out,
        grad_gate,
        grad_gain,
        grad_values,
        grad_tail,
        grad_conv_w,
        grad_conv_b,
        grad_head,
    ) = run_mixer(
        (conv_in, gate, branch_grad, w_out, place, conv_w, conv_b, head_rows, gain_row), shards, False
    )
    branch = lax.psum_scatter(dot_nn(normed_out, w_out), "shard", scatter_dimension=0, tiled=True)
    total_rows = resid_mine + branch
    weights_valid = valid.astype(F32)
    square_total = jnp.sum(weights_valid * jnp.sum(total_rows * total_rows, axis=1))
    square_branch = jnp.sum(weights_valid * jnp.sum(branch * branch, axis=1))
    grad_w_out = lax.psum(dot_tn(normed_out, branch_grad), "rep")
    grad_tail = lax.psum(grad_tail, "shard").astype(BF)
    lane = jnp.arange(TAIL, dtype=jnp.int32)
    owned = ((lane >= mine * share) & (lane < (mine + 1) * share)) | (
        (lane >= 2 * N + mine * heads) & (lane < 2 * N + (mine + 1) * heads)
    )
    kept_tail = jnp.where(owned[None, :], grad_tail[:, :TAIL], jnp.zeros((), BF))
    back = (target[:, None] == slot_ids[None, :]).astype(BF)

    def returned(grad):
        return dot_nn(back, grad).astype(BF)

    grad_normed = lax.psum_scatter(
        dot_nt(returned(grad_gate), w_gate)
        + dot_nt(returned(grad_values), w_conv[:, :width])
        + dot_nt(returned(kept_tail), w_conv[:, width:]),
        "shard",
        scatter_dimension=0,
        tiled=True,
    )
    given = x_in.astype(F32)
    given_rms = lax.rsqrt(jnp.mean(given * given, axis=1, keepdims=True) + EPSILON)
    grad_norm_gain = jnp.sum(grad_normed * (given * given_rms), axis=0)
    scaled = grad_normed * norm_gain[None, :]
    grad_resid = scaled * given_rms - given * (
        given_rms**3 * jnp.mean(scaled * given, axis=1, keepdims=True)
    )
    back_mine = lax.dynamic_slice_in_dim(back, mine * rows, rows, axis=0)
    grad_in = (grad_resid + dot_nn(back_mine, branch_grad)).astype(BF)

    def to_owners(columns):
        part = dot_tn(normed, columns).reshape(shards, depth, columns.shape[1])
        swapped = lax.all_to_all(part, "shard", split_axis=0, concat_axis=0, tiled=True)
        summed = lax.psum(swapped, "rep")
        return summed.transpose(1, 0, 2).reshape(depth, shards * columns.shape[1])

    grad_w_tail = lax.psum(
        dot_tn(columns_at(normed, mine * depth, depth), grad_tail[:, :TAIL]), "rep"
    )
    grad_w_in = jnp.concatenate([to_owners(grad_gate), to_owners(grad_values), grad_w_tail], axis=1)

    def placed(part):
        own = lax.dynamic_update_slice_in_dim(
            jnp.zeros((part.shape[0], DI), F32), part[:, :width], mine * width, axis=1
        )
        return jnp.concatenate([own, part[:, width:]], axis=1)

    summed = lax.psum(
        (
            grad_norm_gain,
            placed(grad_conv_w),
            placed(grad_conv_b)[0],
            grad_head,
            placed(grad_gain)[0],
            jnp.stack([square_total, square_branch, jnp.sum(weights_valid)]),
        ),
        ALL,
    )
    roots = jnp.sqrt(summed[5] / (jnp.maximum(summed[5][2], 1.0) * D))
    return (
        total_rows.astype(BF),
        grad_in,
        summed[0],
        grad_w_in,
        summed[1],
        summed[2],
        summed[3][0, :H],
        summed[3][1, :H],
        summed[3][2, :H],
        summed[4],
        grad_w_out,
        roots[0],
        roots[1],
    )


def on_device(
    x_in,
    cotangent,
    seq_lengths,
    seq_order,
    valid,
    norm_gain,
    w_in,
    conv_w,
    conv_b,
    dt_bias,
    a_log,
    d_skip,
    gated_gain,
    w_out,
):
    shards, mine = lax.axis_size("shard"), lax.axis_index("shard")
    reps = lax.axis_size("rep")
    rows = x_in.shape[0]
    length = rows * shards
    depth = w_in.shape[0]
    heads = H // shards
    width = DI // shards

    head_rows = jnp.pad(jnp.stack([dt_bias, a_log, d_skip]), ((0, 5), (0, 128 - H)))
    bias_row, gain_row = conv_b[None, :], gated_gain[None, :]
    spans = reps == LINE * PLANE and shards == 4 and width == reps * 128 and rows == 128
    if not spans:
        return plain_device(
            x_in,
            cotangent,
            seq_lengths,
            seq_order,
            valid,
            norm_gain,
            w_in,
            conv_w,
            bias_row,
            head_rows,
            gain_row,
            w_out,
        )
    norm_row, valid_column = norm_gain[None, :], valid[:, None]
    (
        normed,
        w_gate,
        w_conv,
        branch_grad,
        back,
        resid,
        inverse,
        line,
        normed_out,
        grad_gain,
        grad_values,
        grad_conv_w,
        grad_conv_b,
        grad_head,
        gate_taken,
        out_taken,
        gate_peer,
        gate_given,
        tail,
    ) = run_mixer(
        (
            seq_lengths,
            seq_order,
            x_in,
            cotangent,
            valid_column,
            norm_row,
            w_in.T,
            w_out,
            conv_w,
            bias_row,
            head_rows,
            gain_row,
        ),
        shards,
        True,
    )
    operands = (
        gate_taken,
        gate_peer,
        out_taken,
        gate_given,
        grad_values,
        tail,
        normed,
        line,
        inverse,
        w_gate,
        w_conv,
        w_out,
        normed_out,
        back,
        branch_grad,
        x_in,
        resid,
        valid_column,
        norm_row,
        grad_conv_w,
        grad_conv_b,
        grad_head,
        grad_gain,
    )
    (
        parts,
        w_out_parts,
        tails,
        block_out,
        grad_in,
        out_norm,
        out_conv_w,
        out_conv_b,
        out_head,
        out_gain,
    ) = run_end(operands, shards)
    grad_w_in, grad_w_out = run_assemble(parts, tails, w_out_parts.reshape(width, D))
    grad_w_in = grad_w_in.T
    return (
        block_out,
        grad_in,
        out_norm[0],
        grad_w_in,
        out_conv_w,
        out_conv_b[0],
        out_head[0, :H],
        out_head[1, :H],
        out_head[2, :H],
        out_gain[0],
        grad_w_out,
        out_head[3, 0],
        out_head[3, 1],
    )


def solution(mesh):
    in_specs = (
        P(ALL, None),
        P(ALL, None),
        P("rep", None),
        P("rep", None),
        P(ALL),
        P(),
        P("shard", None),
        P(),
        P(),
        P(),
        P(),
        P(),
        P(),
        P("shard", None),
    )
    out_specs = (
        P(ALL, None),
        P(ALL, None),
        P(),
        P("shard", None),
        P(),
        P(),
        P(),
        P(),
        P(),
        P(),
        P("shard", None),
        P(),
        P(),
    )
    return jax.shard_map(
        on_device, mesh=mesh, in_specs=in_specs, out_specs=out_specs, check_vma=False
    )
```

```python
import functools

import jax
import jax.numpy as jnp
from jax import lax
from jax.experimental import pallas as pl
from jax.experimental.pallas import tpu as pltpu
from jax.sharding import PartitionSpec as P

D = 2048
H = 64
P_SIZE = 64
N = 128
KW = 4
SPAN = 128
DI = 4096
CONVW = 4352
PROJ = 8512
TAIL = PROJ - 2 * DI

EPSILON = 1e-05
ALL = ("rep", "shard")
VMEM_BYTES = 58 * 1024 * 1024
BF = jnp.bfloat16
F32 = jnp.float32


def dot_nn(a, b):
    return lax.dot_general(a, b, (((1,), (0,)), ((), ())), preferred_element_type=F32)


def dot_nt(a, b):
    return lax.dot_general(a, b, (((1,), (1,)), ((), ())), preferred_element_type=F32)


def dot_tn(a, b):
    return lax.dot_general(a, b, (((0,), (0,)), ((), ())), preferred_element_type=F32)


def halves(a):
    high = a.astype(BF)
    return high, (a - high.astype(F32)).astype(BF)


def slot_tables(seq_lengths, seq_order, slot_ids):
    seq_count = seq_lengths.shape[0]
    numbers = jnp.arange(seq_count, dtype=jnp.int32)
    chosen = (seq_order[:, None] == numbers[None, :]).astype(jnp.int32)
    given_start = jnp.cumsum(seq_lengths) - seq_lengths
    owner_length = jnp.sum(chosen * seq_lengths[None, :], axis=1)
    owner_start = jnp.cumsum(owner_length) - owner_length
    owner_from = jnp.sum(chosen * given_start[None, :], axis=1)
    placed_at = jnp.sum(chosen * owner_start[:, None], axis=0)
    column = slot_ids[:, None]
    within = (column >= owner_start[None, :]) & (column < (owner_start + owner_length)[None, :])
    offset = column - owner_start[None, :]
    source = jnp.sum(jnp.where(within, offset + owner_from[None, :], 0), axis=1)
    position = jnp.sum(jnp.where(within, offset, 0), axis=1)
    given_within = (column >= given_start[None, :]) & (
        column < (given_start + seq_lengths)[None, :]
    )
    target = jnp.sum(
        jnp.where(given_within, column - given_start[None, :] + placed_at[None, :], 0), axis=1
    )
    return (source, target, position)


def params():
    return pltpu.CompilerParams(vmem_limit_bytes=VMEM_BYTES)


def spread_rows(row):
    return jnp.broadcast_to(row, (16, row.shape[1]))


def sigmoid(v):
    return 1.0 / (1.0 + jnp.exp(-v))


def spread(column, lanes=128):
    return jnp.broadcast_to(column, (column.shape[0], lanes))


MESH = pl.DeviceIdType.MESH
LINE, PLANE = 4, 2
CHUNK = 256
TAIL_PAD = 384


def remote(src, dst, send_sem, recv_sem, device):
    return pltpu.make_async_remote_copy(
        src_ref=src,
        dst_ref=dst,
        send_sem=send_sem,
        recv_sem=recv_sem,
        device_id=device,
        device_id_type=MESH,
    )


def meet(devices):
    barrier = pltpu.get_barrier_semaphore()
    for device in devices:
        pl.semaphore_signal(barrier, inc=1, device_id=device, device_id_type=MESH)
    pl.semaphore_wait(barrier, len(devices))


class Line:
    def __init__(self, store, first, share, send_sem, recv_sem):
        self.store, self.first, self.share = store, first, share
        self.send_sem, self.recv_sem = send_sem, recv_sem
        self.mine, self.rep = lax.axis_index("shard"), lax.axis_index("rep")
        self.z, self.x = self.rep // PLANE, lax.rem(self.rep, PLANE)
        self.sibling = self.mine // 2 * 2 + (1 - lax.rem(self.mine, 2))

    def along(self, origin, toward, first=False):
        block = self.store.at[origin, self.share]
        lane = (toward + 1) // 2
        return remote(
            self.first if first else block,
            block,
            self.send_sem.at[lane, origin],
            self.recv_sem.at[0, origin],
            ((self.z + toward) * PLANE + self.x, self.mine),
        )

    def inward(self, origin):
        block = self.store.at[origin, self.share]
        return remote(
            block,
            block,
            self.send_sem.at[2, origin],
            self.recv_sem.at[1, origin],
            (self.rep, self.sibling),
        )

    def start(self):
        for toward in (1, -1):
            self.guarded(toward, lambda: self.along(self.z, toward, True).start())

    def guarded(self, toward, act):
        pl.when(self.z < LINE - 1 if toward > 0 else self.z > 0)(act)

    def step(self, distance):
        for toward in (1, -1):
            origin = self.z - toward * distance

            @pl.when(origin >= 0 if toward > 0 else origin < LINE)
            def _():
                self.along(origin, toward).wait_recv()
                self.guarded(toward, lambda: self.along(origin, toward).start())
                self.inward(origin).start()

    def finish(self):
        for origin in range(LINE):

            @pl.when(origin != self.z)
            def _():
                self.inward(origin).wait_recv()
                self.inward(origin).wait_send()

            for toward in (1, -1):
                passed = origin <= self.z if toward > 0 else origin >= self.z
                pl.when(passed)(
                    lambda: self.guarded(toward, lambda: self.along(origin, toward).wait_send())
                )


def meet_with_line(devices):
    mine, rep = lax.axis_index("shard"), lax.axis_index("rep")
    z, x = rep // PLANE, lax.rem(rep, PLANE)
    barrier = pltpu.get_barrier_semaphore()
    for device in devices:
        pl.semaphore_signal(barrier, inc=1, device_id=device, device_id_type=MESH)
    for toward, there in ((1, z < LINE - 1), (-1, z > 0)):

        @pl.when(there)
        def _():
            pl.semaphore_signal(
                barrier, inc=1, device_id=((z + toward) * PLANE + x, mine), device_id_type=MESH
            )

    beyond = (z + LINE - 1) // LINE + (2 * (LINE - 1) - z) // LINE
    pl.semaphore_wait(barrier, len(devices) + beyond)


def tables_in_kernel(lengths_ref, order_ref, slots):
    count = lengths_ref.shape[1]
    lengths = [lengths_ref[0, i] for i in range(count)]
    order = [order_ref[0, i] for i in range(count)]
    given_start, at = [], jnp.int32(0)
    for i in range(count):
        given_start.append(at)
        at = at + lengths[i]
    source = jnp.zeros_like(slots)
    position = jnp.zeros_like(slots)
    placed_at = [jnp.int32(0)] * count
    at = jnp.int32(0)
    for k in range(count):
        length, start = jnp.int32(0), jnp.int32(0)
        for i in range(count):
            chosen = order[k] == i
            length = length + jnp.where(chosen, lengths[i], 0)
            start = start + jnp.where(chosen, given_start[i], 0)
            placed_at[i] = placed_at[i] + jnp.where(chosen, at, 0)
        within = (slots >= at) & (slots < at + length)
        source = source + jnp.where(within, slots - at + start, 0)
        position = position + jnp.where(within, slots - at, 0)
        at = at + length
    target = jnp.zeros_like(slots)
    for i in range(count):
        within = (slots >= given_start[i]) & (slots < given_start[i] + lengths[i])
        target = target + jnp.where(within, slots - given_start[i] + placed_at[i], 0)
    return source, target, position


def start_phases(
    lengths_ref,
    order_ref,
    x_ref,
    cotangent_ref,
    valid_ref,
    gain_ref,
    w_ref,
    normed_out_ref,
    w_gate_out_ref,
    w_conv_out_ref,
    branch_grad_out_ref,
    back_ref,
    resid_ref,
    inverse_ref,
    line_ref,
    conv_in_ref,
    gate_ref,
    grads,
    place_ref,
    x_all,
    normed,
    w_gate,
    w_conv,
    local_sem,
    row_send,
    row_recv,
    w_send,
    w_recv,
    w_local,
    line_send,
    line_recv,
):
    mine, rep = lax.axis_index("shard"), lax.axis_index("rep")
    y, c = mine // 2, lax.rem(mine, 2)
    z, x = rep // PLANE, lax.rem(rep, PLANE)
    sibling, peer, far = y * 2 + (1 - c), (1 - y) * 2 + c, (1 - y) * 2 + (1 - c)
    beside = z * PLANE + (1 - x)
    rows, length = x_ref.shape[0], x_all.shape[0]
    depth, width = w_ref.shape[1], gate_ref.shape[1]
    chunks = width // CHUNK
    tail_half = TAIL // 2

    part = pl.ds(pl.multiple_of(y * (D // 2), 128), D // 2)
    share = pl.ds(pl.multiple_of(c * (length // 2), 16), length // 2)
    wholes = (x_all, grads)

    lines = [
        Line(
            line_ref.at[kind],
            wholes[kind].at[share, part],
            share,
            line_send.at[kind],
            line_recv.at[kind],
        )
        for kind in range(2)
    ]

    def line_own(kind):
        return pltpu.make_async_copy(
            wholes[kind].at[:, part], line_ref.at[kind, z], local_sem.at[4 + kind]
        )

    def block(ref, shard):
        return ref.at[pl.ds(pl.multiple_of(shard * rows, rows), rows)]

    def row_copies(kind, own, store):
        return (
            remote(own, block(store, mine), row_send.at[kind, 0], row_recv.at[kind, 0], (rep, peer)),
            remote(own, block(store, mine), row_send.at[kind, 1], row_recv.at[kind, 1], (rep, sibling)),
            remote(
                block(store, peer),
                block(store, peer),
                row_send.at[kind, 2],
                row_recv.at[kind, 2],
                (rep, sibling),
            ),
        )

    def lanes(shard):
        return pl.ds(pl.multiple_of(shard * depth, depth), depth)

    def weight_copies(store, index, base, stride, at, half):
        share = pl.ds(pl.multiple_of(at + half * x, 16), half)
        both = pl.ds(pl.multiple_of((1 - y) * 2 * depth, 128), 2 * depth)

        def source(shard, start, count):
            return w_ref.at[pl.ds(pl.multiple_of(base + stride * shard + start, 16), count)]

        def sems(way):
            return w_send.at[way, index], w_recv.at[way, index]

        whole = pl.ds(pl.multiple_of(at, 16), 2 * half)
        near = at if stride else 0
        return (
            lambda: remote(
                source(peer, near + half * x, half), store.at[share, lanes(mine)], *sems(0), (rep, peer)
            ),
            lambda: remote(
                source(far, near + half * x, half), store.at[share, lanes(mine)], *sems(1), (rep, far)
            ),
            lambda: remote(store.at[share, both], store.at[share, both], *sems(2), (beside, mine)),
            lambda: remote(
                source(sibling, near, 2 * half), store.at[whole, lanes(mine)], *sems(3), (rep, sibling)
            ),
            lambda: pltpu.make_async_copy(
                source(mine, near, 2 * half), store.at[whole, lanes(mine)], w_local.at[index]
            ),
        )

    def conv_copies(q):
        return weight_copies(w_conv, q, DI, width, q * CHUNK, CHUNK // 2)

    def tail_copies():
        return weight_copies(w_conv, chunks, 2 * DI, 0, width, tail_half)

    def gate_copies(q):
        return weight_copies(w_gate, chunks + 1 + q, 0, width, q * CHUNK, CHUNK // 2)

    def send_near(copies):
        copies[3]().start()
        copies[4]().start()

    def send_far(copies):
        copies[0]().start()
        copies[1]().start()

    def pass_on(copies):
        copies[0]().wait_recv()
        copies[1]().wait_recv()
        copies[2]().start()
        copies[0]().wait_send()
        copies[1]().wait_send()

    def arrived(copies):
        copies[2]().wait_recv()
        copies[3]().wait_recv()
        copies[4]().wait()

    def each(count, body):
        def step(i, unused):
            body(i)
            return unused

        lax.fori_loop(0, count, step, 0)

    x_copies = row_copies(0, x_ref, x_all)
    grad_copies = row_copies(1, block(grads, mine), grads)
    own_rows = pltpu.make_async_copy(x_ref, block(x_all, mine), local_sem.at[0])
    convs = [conv_copies(q) for q in range(chunks)]
    gates = [gate_copies(q) for q in range(chunks)]
    tail = tail_copies()
    x_copies[0].start()
    x_copies[1].start()
    own_rows.start()
    for copies in convs + [tail] + gates:
        send_near(copies)
    grads[pl.ds(pl.multiple_of(mine * rows, rows), rows), :] = jnp.where(
        spread(valid_ref[...], D) > 0, cotangent_ref[...].astype(F32), 0.0
    ).astype(BF)
    grad_copies[0].start()
    grad_copies[1].start()
    w_conv[width + TAIL :, :] = jnp.zeros((TAIL_PAD - TAIL, D), BF)

    def table_block(i):
        span = pl.ds(pl.multiple_of(i * rows, rows), rows)
        slots = lax.broadcasted_iota(jnp.int32, (rows, length), 0) + i * rows
        across = lax.broadcasted_iota(jnp.int32, (rows, length), 1)
        target = tables_in_kernel(lengths_ref, order_ref, slots)[1]
        back_ref[span, :] = (target == across).astype(F32).astype(BF)
        few_slots = lax.broadcasted_iota(jnp.int32, (rows, 128), 0) + i * rows
        place_ref[span, :] = tables_in_kernel(lengths_ref, order_ref, few_slots)[2]

    each(length // rows, table_block)
    x_copies[0].wait_recv()
    x_copies[2].start()
    x_copies[0].wait_send()
    send_far(convs[0])
    send_far(convs[1])
    own_rows.wait()
    x_copies[1].wait_recv()
    x_copies[2].wait_recv()
    line_own(0).start()
    lines[0].start()

    def picked(i):
        slots = lax.broadcasted_iota(jnp.int32, (rows, length), 0) + i * rows
        across = lax.broadcasted_iota(jnp.int32, (rows, length), 1)
        source = tables_in_kernel(lengths_ref, order_ref, slots)[0]
        return dot_nn((source == across).astype(F32).astype(BF), x_all[...])

    def norm_block(i):
        span = pl.ds(pl.multiple_of(i * rows, rows), rows)
        resid = picked(i)
        inverse = lax.rsqrt(jnp.mean(resid * resid, axis=1, keepdims=True) + EPSILON)
        normed[span, :] = (resid * inverse * gain_ref[...]).astype(BF)

    each(length // rows // 2, norm_block)
    grad_copies[0].wait_recv()
    grad_copies[2].start()
    grad_copies[0].wait_send()
    send_far(convs[2])
    each(length // rows // 2, lambda i: norm_block(i + length // rows // 2))
    grad_copies[1].wait_recv()
    grad_copies[2].wait_recv()
    line_own(1).start()
    lines[1].start()
    pass_on(convs[0])
    send_far(convs[3])
    resid_ref[...] = picked(mine).astype(BF)
    normed_store = pltpu.make_async_copy(normed, normed_out_ref, local_sem.at[1])
    normed_store.start()

    def inverse_block(i):
        span = pl.ds(pl.multiple_of(i * rows, rows), rows)
        given = x_all[span, :].astype(F32)
        inverse_ref[span, :] = spread(
            lax.rsqrt(jnp.mean(given * given, axis=1, keepdims=True) + EPSILON)
        )

    def project(store, target, at, count):
        span = pl.ds(at, count)
        target[:, span] = dot_nt(normed[...], store[span, :]).astype(BF)

    def conv_chunk(q):
        arrived(convs[q])
        project(w_conv, conv_in_ref, q * CHUNK, CHUNK)

    def gate_chunk(q):
        arrived(gates[q])
        project(w_gate, gate_ref, q * CHUNK, CHUNK)

    pass_on(convs[1])
    send_far(tail)
    lines[0].step(1)
    each(length // rows, inverse_block)
    pass_on(convs[2])
    send_far(gates[0])
    conv_chunk(0)
    pass_on(convs[3])
    send_far(gates[1])
    lines[0].step(2)
    conv_chunk(1)
    pass_on(tail)
    send_far(gates[2])
    conv_chunk(2)
    send_far(gates[3])
    conv_chunk(3)
    arrived(tail)
    project(w_conv, conv_in_ref, width, TAIL_PAD)
    conv_store = pltpu.make_async_copy(w_conv, w_conv_out_ref, local_sem.at[2])
    conv_store.start()
    lines[1].step(1)
    yield
    pass_on(gates[0])
    lines[0].step(3)
    yield
    pass_on(gates[1])
    lines[1].step(2)
    gate_chunk(0)
    yield
    pass_on(gates[2])
    gate_chunk(1)
    pass_on(gates[3])
    gate_chunk(2)
    gate_chunk(3)
    gate_store = pltpu.make_async_copy(w_gate, w_gate_out_ref, local_sem.at[3])
    gate_store.start()
    grads_store = pltpu.make_async_copy(grads, branch_grad_out_ref, local_sem.at[6])
    grads_store.start()
    lines[1].step(3)
    yield
    for copies in convs + [tail] + gates:
        copies[2]().wait_send()
        copies[3]().wait_send()
    x_copies[1].wait_send()
    x_copies[2].wait_send()
    grad_copies[1].wait_send()
    grad_copies[2].wait_send()
    normed_store.wait()
    conv_store.wait()
    gate_store.wait()
    grads_store.wait()
    for kind in range(2):
        line_own(kind).wait()
        lines[kind].finish()
    yield


def conv_pre(x, conv_w, conv_b, place):
    pre = conv_b + conv_w[KW - 1 : KW] * x
    for back in range(1, KW):
        moved = pltpu.roll(x, back, 0)
        pre = pre + jnp.where(place >= back, conv_w[KW - 1 - back : KW - back] * moved, 0.0)
    return pre


def conv_lanes(chunk, width, mine):
    if 128 * chunk < width:
        return pl.ds(pl.multiple_of(mine * width + 128 * chunk, 128), 128)
    return pl.ds(DI + 128 * chunk - width, 128)


def block_terms(place):
    local = lax.broadcasted_iota(jnp.int32, (SPAN, 128), 0)
    across = lax.broadcasted_iota(jnp.int32, (SPAN, 128), 1)
    begins = local - place
    causal = (across <= local) & (across >= begins)
    reach_end = local >= begins[SPAN - 1 : SPAN, :]
    entered = place >= local + 1
    carries = place[SPAN - 1 : SPAN, :] >= SPAN
    return causal, reach_end, entered, carries


def pair_terms(pair, run, run_t, step, causal, reach_end, entered, carries):
    left = lax.broadcasted_iota(jnp.int32, (SPAN, 128), 1) < P_SIZE
    runs = [spread(run[:, 2 * pair + i : 2 * pair + i + 1]) for i in range(2)]
    decays = []
    for i in range(2):
        gap = runs[i] - run_t[2 * pair + i : 2 * pair + i + 1, :]
        decays.append(jnp.exp(jnp.where(causal, gap, -jnp.inf)))
    both = jnp.where(left, runs[0], runs[1])
    end = both[SPAN - 1 : SPAN, :]
    entering = jnp.where(entered, jnp.exp(both), 0.0)
    tail = jnp.where(reach_end, jnp.exp(jnp.where(reach_end, end - both, 0.0)), 0.0)
    carried = jnp.where(carries, jnp.exp(end), 0.0)
    size = jnp.where(
        left,
        spread(step[:, 2 * pair : 2 * pair + 1]),
        spread(step[:, 2 * pair + 1 : 2 * pair + 2]),
    )
    return left, decays, entering, tail, carried, size


def stacked(value, left):
    zero = jnp.zeros_like(value)
    return jnp.concatenate([jnp.where(left, value, zero), jnp.where(left, zero, value)], axis=0)


def own_lanes(row, mine, heads):
    return pltpu.roll(row, lax.rem(128 - mine * heads, 128), 1)


def skip_lanes(row, pair):
    left = lax.broadcasted_iota(jnp.int32, (1, 128), 1) < P_SIZE
    return jnp.where(
        left,
        spread(row[:, 2 * pair : 2 * pair + 1]),
        spread(row[:, 2 * pair + 1 : 2 * pair + 2]),
    )


def step_and_run(conv_in_ref, heads_ref, run_ref, step_ref, width, mine):
    length = run_ref.shape[0]
    heads = width // P_SIZE
    lower = (
        lax.broadcasted_iota(jnp.int32, (SPAN, SPAN), 0)
        >= lax.broadcasted_iota(jnp.int32, (SPAN, SPAN), 1)
    ).astype(F32)
    bias = heads_ref[0:1, :]
    rate = jnp.exp(own_lanes(heads_ref[...], mine, heads)[1:2, :])

    def block(b, unused):
        rows = pl.ds(pl.multiple_of(b * SPAN, SPAN), SPAN)
        raw = conv_in_ref[rows, width + 2 * N : width + 2 * N + 128].astype(F32)
        step = own_lanes(jax.nn.softplus(raw + bias), mine, heads)
        step_ref[rows, :] = step
        run_ref[rows, :] = jnp.dot(
            lower, -step * rate, precision=lax.Precision.HIGHEST, preferred_element_type=F32
        )
        return unused

    lax.fori_loop(0, length // SPAN, block, 0)


def along_line(step):
    rep = lax.axis_index("rep")
    there = lax.rem(rep // PLANE + step, LINE)
    return there * PLANE + lax.rem(rep, PLANE), there


def share_copy(source, taken, send_sem, recv_sem, step):
    to, there = along_line(step)
    z, wide = lax.axis_index("rep") // PLANE, taken.shape[2]
    return remote(
        source.at[:, pl.ds(pl.multiple_of(there * wide, 128), wide)],
        taken.at[z],
        send_sem.at[step],
        recv_sem.at[z],
        (to, lax.axis_index("shard")),
    )


def share_own(source, taken, sem):
    z, wide = lax.axis_index("rep") // PLANE, taken.shape[2]
    return pltpu.make_async_copy(
        source.at[:, pl.ds(pl.multiple_of(z * wide, 128), wide)], taken.at[z], sem
    )


def share_start(source, taken, send_sem, recv_sem, own):
    own.start()
    for step in range(1, LINE):
        share_copy(source, taken, send_sem, recv_sem, step).start()


def share_arrival(taken, recv_sem, own, step):
    to, there = along_line(step)
    if step == 0:
        own.wait()
    else:
        block, sem = taken.at[there], recv_sem.at[there]
        remote(block, block, sem, sem, (to, lax.axis_index("shard"))).wait_recv()
    return there


def share_sent(source, taken, send_sem, recv_sem):
    for step in range(1, LINE):
        share_copy(source, taken, send_sem, recv_sem, step).wait_send()


def in_given_order(back_ref, inverse_ref, grad_ref, given_ref, scaled_ref):
    length, width = grad_ref.shape

    def block(i, unused):
        span = pl.ds(pl.multiple_of(i * SPAN, SPAN), SPAN)
        moved = dot_nn(back_ref[span, :], grad_ref[...])
        if given_ref is not None:
            given_ref[span, :] = moved.astype(BF)
        for c in range(width // 128):
            lanes = slice(128 * c, 128 * c + 128)
            scaled_ref[span, lanes] = (moved[:, lanes] * inverse_ref[span, :]).astype(BF)
        return unused

    lax.fori_loop(0, length // SPAN, block, 0)


class RowSum:
    def __init__(self, partial, pair_in, row_out, row_in, send_sem, recv_sem):
        self.partial, self.pair_in, self.row_out, self.row_in = partial, pair_in, row_out, row_in
        self.rows = row_in.shape[0]
        mine, rep = lax.axis_index("shard"), lax.axis_index("rep")
        self.y, self.core = mine // 2, lax.rem(mine, 2)
        sibling, peer = self.y * 2 + (1 - self.core), (1 - self.y) * 2 + self.core
        self.pairs = [
            remote(
                partial.at[self.span(2 * side + (1 - self.core))],
                pair_in.at[side],
                send_sem.at[side],
                recv_sem.at[side],
                (rep, sibling),
            )
            for side in range(2)
        ]
        self.across = remote(row_out, row_in, send_sem.at[2], recv_sem.at[2], (rep, peer))

    def span(self, shard):
        return pl.ds(pl.multiple_of(shard * self.rows, self.rows), self.rows)

    def fill(self, rows_of):
        def block(i, unused):
            span = self.span(i)
            self.partial[span, :] = rows_of(span)
            return unused

        lax.fori_loop(0, self.partial.shape[0] // self.rows, block, 0)
        for copy in self.pairs:
            copy.start()

    def join(self):
        for copy in self.pairs:
            copy.wait_recv()
        there = self.span(2 * (1 - self.y) + self.core)
        self.row_out[...] = (self.pair_in[1 - self.y] + self.partial[there, :]).astype(BF)
        self.across.start()

    def result(self):
        self.across.wait_recv()
        here = self.partial[self.span(2 * self.y + self.core), :]
        return self.pair_in[self.y] + here + self.row_in[...].astype(F32)

    def finish(self):
        for copy in self.pairs + [self.across]:
            copy.wait_send()


def mixer_kernel(spans, *refs):
    refs = list(refs)

    def take(count):
        taken, refs[:] = refs[:count], refs[count:]
        return taken

    if spans:
        start_in = take(7)
        w_out_hbm, conv_w_ref, conv_b_ref, heads_ref, gain_ref = take(5)
        start_out = take(8)
        normed_out_ref, grad_gain_ref, grad_values_ref = take(3)
    else:
        conv_in_ref, gate_ref, branch_grad_ref, w_out_ref, place_ref = take(5)
        conv_w_ref, conv_b_ref, heads_ref, gain_ref = take(4)
        normed_out_ref, grad_gate_ref, grad_gain_ref, grad_values_ref, grad_tail_ref = take(5)
    grad_conv_w_ref, grad_conv_b_ref, grad_head_ref = take(3)
    if spans:
        taken_ref, taken_out_ref, gate_peer_ref = take(3)
        gate_given_ref, tail_ref = take(2)
    (
        mixed_ref,
        starts_ref,
        grad_mixed_ref,
        act_ref,
        pre_ref,
        step_ref,
        run_ref,
        state_ref,
        gno_ref,
        sums,
        grad_act_ref,
        joined_ref,
        join_ref,
        send_sem,
        recv_sem,
    ) = take(15)
    if spans:
        start_scratch = take(8)
        start_sems = take(8)
        conv_in_ref, gate_ref, branch_grad_ref, place_ref = start_scratch[:4]
        back_ref, inverse_ref = start_out[4], start_out[6]
        w_out_ref, grad_gate_ref, grad_tail_ref, scaled_ref, tail_in = take(5)
        share_send, share_recv, own_sem, peer_send, peer_recv, tail_send, tail_recv = take(7)
    length, width = gate_ref.shape
    mine, rep, shards = lax.axis_index("shard"), lax.axis_index("rep"), lax.axis_size("shard")
    heads = width // P_SIZE
    peers = [(rep, lax.rem(mine + step, shards)) for step in range(1, shards)]
    if spans:
        y, core = mine // 2, lax.rem(mine, 2)
        sibling, peer = y * 2 + (1 - core), (1 - y) * 2 + core
        others = [lax.rem(mine + step, shards) for step in range(1, shards)]
        rows = length // shards
        beside = rep // PLANE * PLANE + (1 - lax.rem(rep, PLANE))
        meet([(along_line(step)[0], mine) for step in range(1, LINE)] + [(beside, mine)] + peers)
        w_out_load = pltpu.make_async_copy(w_out_hbm, w_out_ref, own_sem.at[2])
        w_out_load.start()
        start = start_phases(*start_in, *start_out, *start_scratch, *start_sems)
        next(start)
    else:
        meet(peers)
    for c in range((width + 2 * N) // 128):
        lanes = slice(128 * c, 128 * c + 128)
        there = conv_lanes(c, width, mine)
        pre = conv_pre(
            conv_in_ref[:, lanes].astype(F32),
            conv_w_ref[:, there],
            conv_b_ref[:, there],
            place_ref[...],
        )
        pre_ref[:, lanes] = pre
        act_ref[:, lanes] = (pre * sigmoid(pre)).astype(BF)
    step_and_run(conv_in_ref, heads_ref, run_ref, step_ref, width, mine)
    if spans:
        next(start)
    state_ref[...] = jnp.zeros_like(state_ref)
    skips = own_lanes(heads_ref[...], mine, heads)[2:3, :]

    def forward_block(b, unused):
        row = pl.multiple_of(b * SPAN, SPAN)
        rows = pl.ds(row, SPAN)
        starts_ref[pl.ds(pl.multiple_of(b * N, N), N), :] = state_ref[...]
        run = run_ref[rows, :]
        run_t = run.T
        step = step_ref[rows, :]
        masks = block_terms(place_ref[rows, :])
        in_map = act_ref[rows, width : width + N]
        out_map = act_ref[rows, width + N : width + 2 * N]
        products = dot_nt(out_map, in_map)
        in_map_t = in_map.T
        for pair in range(width // 128):
            lanes = slice(128 * pair, 128 * pair + 128)
            left, decays, entering, tail, carried, size = pair_terms(
                pair, run, run_t, step, *masks
            )
            values = act_ref[rows, lanes].astype(F32)
            scaled = values * size
            weights = jnp.concatenate([(d * products).astype(BF) for d in decays], axis=1)
            out = dot_nn(weights, stacked(scaled.astype(BF), left))
            state = state_ref[:, lanes]
            high, low = halves(state)
            out += entering * (dot_nn(out_map, high) + dot_nn(out_map, low))
            mixed_ref[rows, lanes] = out + skip_lanes(skips, pair) * values
            high, low = halves(tail * scaled)
            fresh = dot_nn(in_map_t, high) + dot_nn(in_map_t, low)
            state_ref[:, lanes] = carried * state + fresh
        return unused

    halfway = length // SPAN // 2
    lax.fori_loop(0, halfway, forward_block, 0)
    if spans:
        next(start)
    lax.fori_loop(halfway, length // SPAN, forward_block, 0)
    if spans:
        next(start)
        w_out_load.wait()

    lane = lax.broadcasted_iota(jnp.int32, (SPAN, 128), 1)

    def gated(rows, c):
        lanes = slice(128 * c, 128 * c + 128)
        gate = gate_ref[rows, lanes].astype(F32)
        opened = sigmoid(gate)
        mixed = mixed_ref[rows, lanes]
        back = gno_ref[rows, lanes]
        gain = gain_ref[:, pl.ds(pl.multiple_of(mine * width + 128 * c, 128), 128)]
        return gate, opened, mixed, back, gain, mixed * (gate * opened), back * gain

    def measure(b, unused):
        rows = pl.ds(pl.multiple_of(b * SPAN, SPAN), SPAN)
        gno_ref[rows, :] = dot_nt(branch_grad_ref[rows, :], w_out_ref[...])
        squares = jnp.zeros((SPAN, 128), F32)
        crosses = jnp.zeros((SPAN, 128), F32)
        for c in range(width // 128):
            product, weighted = gated(rows, c)[5:]
            squares += product * product
            crosses += weighted * product
        squares = jnp.sum(squares, axis=1, keepdims=True)
        crosses = jnp.sum(crosses, axis=1, keepdims=True)
        both = jnp.where(lane == 0, spread(squares), jnp.where(lane == 1, spread(crosses), 0.0))
        sums[mine, :, rows] = both.T[0:8, :]
        return unused

    lax.fori_loop(0, length // SPAN, measure, 0)

    copies = [
        remote(sums.at[mine], sums.at[mine], send_sem.at[i], recv_sem.at[i], peer)
        for i, peer in enumerate(peers)
    ]
    for copy in copies:
        copy.start()
    for copy in copies:
        copy.wait_recv()
    grad_gain_ref[...] = jnp.zeros_like(grad_gain_ref)

    def finish(b, unused):
        rows = pl.ds(pl.multiple_of(b * SPAN, SPAN), SPAN)
        both = sums[0, :, rows]
        for shard in range(1, shards):
            both = both + sums[shard, :, rows]
        both = jnp.concatenate([both, jnp.zeros((SPAN - 8, SPAN), F32)], axis=0).T / DI
        inverse = lax.rsqrt(both[:, 0:1] + EPSILON)
        pull = spread(inverse * inverse * inverse * both[:, 1:2])
        inverse = spread(inverse)
        for c in range(width // 128):
            lanes = slice(128 * c, 128 * c + 128)
            gate, opened, mixed, back, gain, product, weighted = gated(rows, c)
            normalized = product * inverse
            normed_out_ref[rows, lanes] = (normalized * gain).astype(BF)
            grad_product = inverse * weighted - product * pull
            grad_gain_ref[:, lanes] += jnp.sum(back * normalized, axis=0, keepdims=True)
            grad_mixed_ref[rows, lanes] = grad_product * (gate * opened)
            grad_gate_ref[rows, lanes] = (
                grad_product * mixed * (opened * (1.0 + gate * (1.0 - opened)))
            ).astype(BF)
        return unused

    lax.fori_loop(0, length // SPAN, finish, 0)
    for copy in copies:
        copy.wait_send()
    if spans:
        exchanges = ((scaled_ref, taken_ref), (normed_out_ref, taken_out_ref))
        own_shares = [share_own(*pair, own_sem.at[i]) for i, pair in enumerate(exchanges)]

        def gate_peer_copy(at):
            return remote(
                taken_ref.at[at], gate_peer_ref.at[at], peer_send.at[at], peer_recv.at[at], (rep, peer)
            )

        def row_block(ref, shard):
            return ref.at[pl.ds(pl.multiple_of(shard * rows, rows), rows)]

        tail_out = [
            remote(
                row_block(grad_tail_ref, other),
                tail_in.at[i],
                tail_send.at[0, i],
                tail_recv.at[0, i],
                (rep, other),
            )
            for i, other in enumerate(others)
        ]
        tail_back = [
            remote(
                row_block(tail_ref, mine),
                row_block(tail_ref, mine),
                tail_send.at[1, i],
                tail_recv.at[1, i],
                (rep, other),
            )
            for i, other in enumerate(others)
        ]
        in_given_order(back_ref, inverse_ref, grad_gate_ref, gate_given_ref, scaled_ref)
        share_start(*exchanges[0], share_send.at[0], share_recv.at[0], own_shares[0])
    state_ref[...] = jnp.zeros_like(state_ref)
    grad_head_ref[...] = jnp.zeros_like(grad_head_ref)
    upper = (
        lax.broadcasted_iota(jnp.int32, (SPAN, SPAN), 0)
        <= lax.broadcasted_iota(jnp.int32, (SPAN, SPAN), 1)
    ).astype(F32)
    last_row = lax.broadcasted_iota(jnp.int32, (SPAN, 128), 0) == SPAN - 1
    join_ref[...] = (
        lax.broadcasted_iota(jnp.int32, (width, 128), 0) // P_SIZE + mine * heads
        == lax.broadcasted_iota(jnp.int32, (width, 128), 1)
    ).astype(F32).astype(BF)

    blocks = length // SPAN

    def backward_block(count, unused):
        b = blocks - 1 - count
        row = pl.multiple_of(b * SPAN, SPAN)
        rows = pl.ds(row, SPAN)
        start_rows = pl.ds(pl.multiple_of(b * N, N), N)
        run = run_ref[rows, :]
        run_t = run.T
        step = step_ref[rows, :]
        masks = block_terms(place_ref[rows, :])
        in_map = act_ref[rows, width : width + N]
        out_map = act_ref[rows, width + N : width + 2 * N]
        out_map_t = out_map.T
        products = dot_nt(out_map, in_map)
        grad_products = jnp.zeros((SPAN, SPAN), F32)
        grad_out_map = jnp.zeros((SPAN, N), F32)
        grad_in_map = jnp.zeros((SPAN, N), F32)
        for pair in range(width // 128):
            lanes = slice(128 * pair, 128 * pair + 128)
            left, decays, entering, tail, carried, size = pair_terms(
                pair, run, run_t, step, *masks
            )
            values = act_ref[rows, lanes].astype(F32)
            grad = grad_mixed_ref[rows, lanes]
            start = starts_ref[start_rows, lanes]
            later = state_ref[:, lanes]
            scaled = values * size
            scaled_low = scaled.astype(BF)
            grad_low = grad.astype(BF)
            weights = jnp.concatenate([(d * products).astype(BF) for d in decays], axis=0)
            grad_scaled = dot_tn(weights, stacked(grad_low, left))
            grad_pairs = dot_nt(grad_low, stacked(scaled_low, left))
            grad_products += (
                grad_pairs[:, :SPAN] * decays[0] + grad_pairs[:, SPAN:] * decays[1]
            )
            later_high, later_low = halves(later)
            from_later = tail * (dot_nn(in_map, later_high) + dot_nn(in_map, later_low))
            grad_scaled += from_later
            entering_high, entering_low = halves(entering * grad)
            grad_out_map += dot_nt(entering_high, start.astype(BF))
            grad_in_map += dot_nt((tail * scaled).astype(BF), later_high)
            ending = jnp.sum(scaled * from_later, axis=0, keepdims=True) + carried * jnp.sum(
                start * later, axis=0, keepdims=True
            )
            state_ref[:, lanes] = (
                carried * later + dot_nn(out_map_t, entering_high) + dot_nn(out_map_t, entering_low)
            )
            skip = skip_lanes(skips, pair)
            inner = mixed_ref[rows, lanes] - skip * values
            joined_ref[0:SPAN, lanes] = (
                grad_low.astype(F32) * inner
                - scaled_low.astype(F32) * (grad_scaled - from_later)
                - scaled * from_later
                + jnp.where(last_row, ending, 0.0)
            )
            joined_ref[SPAN : 2 * SPAN, lanes] = grad_scaled * values
            joined_ref[2 * SPAN : 2 * SPAN + 16, lanes] = spread_rows(
                jnp.sum(grad * values, axis=0, keepdims=True)
            )
            grad_act_ref[rows, lanes] = grad_scaled * size + skip * grad
        grad_products = grad_products.astype(BF)
        grad_act_ref[rows, width : width + N] = grad_in_map + dot_tn(grad_products, out_map)
        grad_act_ref[rows, width + N : width + 2 * N] = grad_out_map + dot_nn(
            grad_products, in_map
        )
        joined = joined_ref[...]
        first = joined.astype(BF)
        second, third = halves(joined - first.astype(F32))
        join = join_ref[...]
        by_head = dot_nn(first, join) + dot_nn(second, join) + dot_nn(third, join)
        grad_log = jnp.dot(
            upper, by_head[:SPAN], precision=lax.Precision.HIGHEST, preferred_element_type=F32
        )
        rate = jnp.exp(heads_ref[1:2, :])
        raw = conv_in_ref[rows, width + 2 * N : width + 2 * N + 128].astype(F32) + heads_ref[0:1, :]
        grad_dt = (by_head[SPAN : 2 * SPAN] - grad_log * rate) * sigmoid(raw)
        grad_tail_ref[rows, 2 * N : 2 * N + 128] = grad_dt
        grad_head_ref[0:1, :] += jnp.sum(grad_dt, axis=0, keepdims=True)
        grad_head_ref[1:2, :] += jnp.sum(
            -grad_log * jax.nn.softplus(raw) * rate, axis=0, keepdims=True
        )
        grad_head_ref[2:3, :] += by_head[2 * SPAN : 2 * SPAN + 1]
        return unused

    if spans:
        lax.fori_loop(0, blocks - 1, backward_block, 0)
        for step in range(LINE):
            at = share_arrival(taken_ref, share_recv.at[0], own_shares[0], step)
            gate_peer_copy(at).start()
        lax.fori_loop(blocks - 1, blocks, backward_block, 0)
        share_start(*exchanges[1], share_send.at[1], share_recv.at[1], own_shares[1])
    else:
        lax.fori_loop(0, blocks, backward_block, 0)

    place = place_ref[...]
    own_chunks = width // 128
    for c in [own_chunks, own_chunks + 1] + list(range(own_chunks)):
        lanes = slice(128 * c, 128 * c + 128)
        x = conv_in_ref[:, lanes].astype(F32)
        conv_w = conv_w_ref[:, conv_lanes(c, width, mine)]
        pre = pre_ref[:, lanes]
        gain = sigmoid(pre)
        grad_pre = grad_act_ref[:, lanes] * (gain * (1.0 + pre * (1.0 - gain)))
        grad_conv_b_ref[:, lanes] = jnp.sum(grad_pre, axis=0, keepdims=True)
        grad_conv_w_ref[KW - 1 : KW, lanes] = jnp.sum(grad_pre * x, axis=0, keepdims=True)
        grad_x = conv_w[KW - 1 : KW] * grad_pre
        for back in range(1, KW):
            tap = KW - 1 - back
            kept = jnp.where(place >= back, grad_pre, 0.0)
            grad_conv_w_ref[tap : tap + 1, lanes] = jnp.sum(
                kept * pltpu.roll(x, back, 0), axis=0, keepdims=True
            )
            grad_x += conv_w[tap : tap + 1] * pltpu.roll(kept, length - back, 0)
        if c < width // 128:
            grad_values_ref[:, lanes] = grad_x.astype(BF)
        else:
            grad_tail_ref[:, 128 * c - width : 128 * c - width + 128] = grad_x
        if spans and c == own_chunks + 1:
            for copy in tail_out:
                copy.start()
    if spans:
        span = pl.ds(pl.multiple_of(mine * rows, rows), rows)
        tail = grad_tail_ref[span, :]
        for i, copy in enumerate(tail_out):
            copy.wait_recv()
            tail = tail + tail_in[i]
        tail_ref[span, :] = tail.astype(BF)
        for copy in tail_back:
            copy.start()
        for step in range(LINE):
            share_arrival(taken_out_ref, share_recv.at[1], own_shares[1], step)
        for i, pair in enumerate(exchanges):
            share_sent(*pair, share_send.at[i], share_recv.at[i])
        for at in range(LINE):
            gate_peer_copy(at).wait()
        for copy in tail_out:
            copy.wait_send()
        for copy in tail_back:
            copy.wait()
        next(start)


def run_mixer(operands, shards, spans):
    if spans:
        rows = operands[2].shape[0]
        length, width = rows * shards, DI // shards
    else:
        length, width = operands[1].shape
        rows = length // shards
    blocks, chunks = length // SPAN, width // CHUNK
    shape = jax.ShapeDtypeStruct
    vector = pl.BlockSpec(memory_space=pltpu.VMEM)
    anywhere = pl.BlockSpec(memory_space=pl.ANY)
    scalars = pl.BlockSpec(memory_space=pltpu.SMEM)
    dma = pltpu.SemaphoreType.DMA
    small = [
        shape((KW, width + 2 * N), F32),
        shape((1, width + 2 * N), F32),
        shape((8, 128), F32),
    ]
    scratch = [
        pltpu.VMEM((length, width), F32),
        pltpu.VMEM((blocks * N, width), F32),
        pltpu.VMEM((length, width), F32),
        pltpu.VMEM((length, width + 2 * N), BF),
        pltpu.VMEM((length, width + 2 * N), F32),
        pltpu.VMEM((length, 128), F32),
        pltpu.VMEM((length, 128), F32),
        pltpu.VMEM((N, width), F32),
        pltpu.VMEM((length, width), F32),
        pltpu.VMEM((shards, 8, length), F32),
        pltpu.VMEM((length, width + 2 * N), F32),
        pltpu.VMEM((2 * SPAN + 16, width), F32),
        pltpu.VMEM((width, 128), BF),
        dma((shards - 1,)),
        dma((shards - 1,)),
    ]
    if spans:
        taken = shape((LINE, length, 2 * 128), BF)
        outs = [
            (shape((length, D), BF), anywhere),
            (shape((width, D), BF), anywhere),
            (shape((width + TAIL_PAD, D), BF), anywhere),
            (shape((length, D), BF), anywhere),
            (shape((length, length), BF), vector),
            (shape((rows, D), BF), vector),
            (shape((length, 128), F32), vector),
            (shape((2, LINE, length, D // 2), BF), anywhere),
            (shape((length, width), BF), vector),
            (shape((1, width), F32), vector),
            (shape((length, width), BF), vector),
            *[(one, vector) for one in small],
            (taken, anywhere),
            (taken, anywhere),
            (taken, anywhere),
            (shape((length, width), BF), vector),
            (shape((length, TAIL_PAD), BF), vector),
        ]
        in_specs = [scalars, scalars, anywhere, vector, vector, vector, anywhere, anywhere]
        in_specs += [vector] * 4
        weights = 2 * chunks + 1
        scratch += [
            pltpu.VMEM((length, width + TAIL_PAD), BF),
            pltpu.VMEM((length, width), BF),
            pltpu.VMEM((length, D), BF),
            pltpu.VMEM((length, 128), jnp.int32),
            pltpu.VMEM((length, D), BF),
            pltpu.VMEM((length, D), BF),
            pltpu.VMEM((width, D), BF),
            pltpu.VMEM((width + TAIL_PAD, D), BF),
            dma((7,)),
            dma((2, 3)),
            dma((2, 3)),
            dma((4, weights)),
            dma((4, weights)),
            dma((weights,)),
            dma((2, 3, LINE)),
            dma((2, 2, LINE)),
            pltpu.VMEM((width, D), BF),
            pltpu.VMEM((length, width), BF),
            pltpu.VMEM((length, TAIL_PAD), F32),
            pltpu.VMEM((length, width), BF),
            pltpu.VMEM((shards - 1, rows, TAIL_PAD), F32),
            dma((2, LINE)),
            dma((2, LINE)),
            dma((3,)),
            dma((LINE,)),
            dma((LINE,)),
            dma((2, shards - 1)),
            dma((2, shards - 1)),
        ]
    else:
        wide = shape((length, width), BF)
        outs = [wide, wide, shape((1, width), F32), wide, shape((length, TAIL_PAD), F32), *small]
        outs = [(one, vector) for one in outs]
        in_specs = [vector] * 9
    return pl.pallas_call(
        functools.partial(mixer_kernel, spans),
        out_shape=tuple(out for out, spec in outs),
        in_specs=in_specs,
        out_specs=tuple(spec for out, spec in outs),
        scratch_shapes=scratch,
        compiler_params=pltpu.CompilerParams(
            vmem_limit_bytes=VMEM_BYTES, collective_id=2, has_side_effects=True
        ),
        cost_estimate=pl.CostEstimate(
            flops=60 * length * width * 128, bytes_accessed=32 * length * width, transcendentals=0
        ),
        name="mixer",
    )(*operands)


def end_kernel(
    gate_taken_hbm,
    gate_peer_hbm,
    out_taken_hbm,
    gate_given_ref,
    values_ref,
    tail_low,
    normed_ref,
    line_ref,
    inverse_ref,
    w_gate_hbm,
    w_conv_hbm,
    w_out_hbm,
    normed_out_hbm,
    back_ref,
    branch_grad_hbm,
    x_ref,
    resid_ref,
    valid_ref,
    gain_ref,
    grad_conv_w_ref,
    grad_conv_b_ref,
    grad_head_ref,
    grad_gain_ref,
    parts_ref,
    w_out_grad_ref,
    tails_ref,
    block_out_ref,
    grad_in_ref,
    out_norm_ref,
    out_conv_w_ref,
    out_conv_b_ref,
    out_head_ref,
    out_gain_ref,
    taken,
    taken_peer,
    values_given_ref,
    scaled_ref,
    group_rows,
    own_columns,
    total,
    sum_kept,
    mail_out,
    mail_in,
    low,
    partial,
    pair_in,
    row_out,
    row_in,
    branch_pair,
    branch_out,
    branch_in,
    tail_sum,
    tail_own,
    tail_parts,
    small,
    small_in,
    small_all,
    w_gate_ref,
    w_conv_ref,
    branch_grad_ref,
    w_out_ref,
    normed_out_ref,
    load_sem,
    local_sem,
    group_sem,
    share_send,
    share_recv,
    peer_send,
    peer_recv,
    mail_send,
    mail_recv,
    swap_send,
    swap_recv,
    line_send,
    line_recv,
    side_send,
    side_recv,
    cross_send,
    cross_recv,
    pair_send,
    pair_recv,
    branch_send,
    branch_recv,
    rep_send,
    rep_recv,
    all_send,
    all_recv,
):
    reps, shards = LINE * PLANE, lax.axis_size("shard")
    mine, rep = lax.axis_index("shard"), lax.axis_index("rep")
    y, c = mine // 2, lax.rem(mine, 2)
    z, x = rep // PLANE, lax.rem(rep, PLANE)
    beside = z * PLANE + (1 - x)
    rows, length = x_ref.shape[0], values_ref.shape[0]
    width, depth = values_ref.shape[1], own_columns.shape[1]
    half = D // 2
    sibling, peer = y * 2 + (1 - c), (1 - y) * 2 + c

    def other(step):
        return lax.rem(z + step // PLANE, LINE) * PLANE + lax.rem(x + step % PLANE, PLANE)

    def before(step):
        return lax.rem(z + LINE - step // PLANE, LINE) * PLANE + lax.rem(
            x + PLANE - step % PLANE, PLANE
        )

    def shard_at(step):
        return lax.rem(mine + step, shards)

    def each(count, body):
        def step(i, unused):
            body(i)
            return unused

        lax.fori_loop(0, count, step, 0)

    meet(
        [(other(step), mine) for step in range(1, reps)]
        + [(rep, shard_at(step)) for step in range(1, shards)]
    )

    loads = [
        pltpu.make_async_copy(far_ref, near_ref, load_sem.at[i])
        for i, (far_ref, near_ref) in enumerate(
            [
                (w_gate_hbm, w_gate_ref),
                (w_conv_hbm, w_conv_ref),
                (branch_grad_hbm, branch_grad_ref),
                (w_out_hbm, w_out_ref),
                (normed_out_hbm, normed_out_ref),
            ]
        )
    ]

    def group_copy(part, step):
        at = along_line(step)[1]
        return pltpu.make_async_copy(
            line_ref.at[part // 2, at], group_rows.at[step], group_sem.at[step]
        )

    def peer_copy(part, at):
        return remote(
            taken.at[part, at],
            taken_peer.at[part, at],
            peer_send.at[part, at],
            peer_recv.at[part, at],
            (rep, peer),
        )

    own_part = pltpu.make_async_copy(
        normed_ref.at[:, pl.ds(pl.multiple_of(mine * depth, depth), depth)],
        own_columns,
        local_sem.at[4],
    )
    own_part.start()
    gate_load = pltpu.make_async_copy(gate_taken_hbm, taken.at[0], local_sem.at[0])
    gate_load.start()
    peer_load = pltpu.make_async_copy(gate_peer_hbm, taken_peer.at[0], local_sem.at[7])
    peer_load.start()
    out_load = pltpu.make_async_copy(out_taken_hbm, taken.at[2], local_sem.at[5])
    out_load.start()
    for step in range(LINE):
        group_copy(0, step).start()
    out_load.wait()
    for at in range(LINE):
        peer_copy(2, at).start()

    for load in loads[::-1]:
        load.start()

    rows_sum = RowSum(partial, pair_in, row_out, row_in, pair_send, pair_recv)
    branch_sum = RowSum(partial, branch_pair, branch_out, branch_in, branch_send, branch_recv)

    def swap_copy(part):
        if part == 2:
            return remote(
                low.at[2, pl.ds(pl.multiple_of((1 - y) * 128, 128), 128), :],
                w_out_grad_ref.at[rep, :, pl.ds(pl.multiple_of(y * half, 128), half)],
                swap_send.at[2],
                swap_recv.at[2],
                (rep, peer),
            )
        return remote(
            low.at[part, :, pl.ds(pl.multiple_of((1 - c) * depth, depth), depth)],
            parts_ref.at[rep, part, c],
            swap_send.at[part],
            swap_recv.at[part],
            (rep, sibling),
        )

    def swap_own(part):
        if part == 2:
            return pltpu.make_async_copy(
                low.at[2, pl.ds(pl.multiple_of(y * 128, 128), 128), :],
                w_out_grad_ref.at[rep, :, pl.ds(pl.multiple_of(y * half, 128), half)],
                local_sem.at[6],
            )
        return pltpu.make_async_copy(
            low.at[part, :, pl.ds(pl.multiple_of(c * depth, depth), depth)],
            parts_ref.at[rep, part, c],
            local_sem.at[2 + part],
        )

    def mail_copy(part):
        return remote(
            mail_out.at[part],
            mail_in.at[part],
            mail_send.at[part],
            mail_recv.at[part],
            (beside, mine),
        )

    def sum_groups(part, then=None):
        for step in range(LINE):
            at = along_line(step)[1]
            if part > 0:
                peer_copy(part, at).wait_recv()
            elif step == 0:
                gate_load.wait()
                peer_load.wait()
            group_copy(part, step).wait()
            both = jnp.concatenate([taken[part, at], taken_peer[part, at]], axis=1)
            for lanes in (slice(0, half // 2), slice(half // 2, half)):
                term = dot_tn(both, group_rows[step, :, lanes])
                if step == 0:
                    total[:, lanes] = term
                else:
                    total[:, lanes] += term
            if then is not None:
                group_copy(then, step).start()
        for source, place in ((0, y), (256, 1 - y)):
            rows_kept = pl.ds(pl.multiple_of(source + x * 128, 128), 128)
            rows_sent = pl.ds(pl.multiple_of(source + (1 - x) * 128, 128), 128)
            there = pl.ds(pl.multiple_of(place * 128, 128), 128)
            sum_kept[there, :] = total[rows_kept, :]
            mail_out[part, there, :] = total[rows_sent, :].astype(BF)
        mail_copy(part).start()

    def close_sum(part):
        gains = gain_ref[:, pl.ds(pl.multiple_of(y * half, 128), half)] if part < 2 else 1.0
        mail_copy(part).wait_recv()
        low[part] = ((sum_kept[...] + mail_in[part].astype(F32)) * gains).astype(BF)
        swap_own(part).start()
        swap_copy(part).start()

    def sum_block(part, owner):
        return w_out_grad_ref.at[owner, 0:64] if part == 2 else parts_ref.at[owner, part]

    def cross_block(origin, column):
        owner = origin * PLANE + (x if column == 0 else 1 - x)
        return w_out_grad_ref.at[owner, 64:128]

    def cross_side(column):
        block = cross_block(z, column)
        return remote(
            block, block, cross_send.at[0, 2, 0], cross_recv.at[2, 0], (beside, mine)
        )

    def cross_copy(column, origin, toward):
        block = cross_block(origin, column)
        return remote(
            block,
            block,
            cross_send.at[column, (1 - toward) // 2, origin],
            cross_recv.at[column, origin],
            ((z + toward) * PLANE + x, mine),
        )

    def inner(toward):
        return z < LINE - 1 if toward > 0 else z > 0

    def cross_start(column):
        for toward in (1, -1):

            @pl.when(inner(toward))
            def _(toward=toward):
                cross_copy(column, z, toward).start()

    def cross_pass(step):
        for column in range(PLANE):
            for toward in (1, -1):
                origin = z - toward * step

                @pl.when(origin >= 0 if toward > 0 else origin < LINE)
                def _(column=column, origin=origin, toward=toward):
                    cross_copy(column, origin, toward).wait_recv()

                    @pl.when(inner(toward))
                    def _():
                        cross_copy(column, origin, toward).start()

    def cross_finish():
        cross_side(0).wait_send()
        for column in range(PLANE):
            for toward in (1, -1):
                for origin in range(LINE):
                    passed = origin <= z if toward > 0 else origin >= z

                    @pl.when(passed & inner(toward))
                    def _(column=column, origin=origin, toward=toward):
                        cross_copy(column, origin, toward).wait_send()

    def line_copy(part, origin, toward, lane):
        block = sum_block(part, origin * PLANE + x)
        return remote(
            block,
            block,
            line_send.at[part, lane, origin],
            line_recv.at[part, origin],
            ((z + toward) * PLANE + x, mine),
        )

    def side_copy(part, origin, from_x):
        block = sum_block(part, origin * PLANE + from_x)
        return remote(
            block, block, side_send.at[part, origin], side_recv.at[part, origin], (beside, mine)
        )

    def spread_own(part):
        swap_own(part).wait()
        swap_copy(part).wait_recv()
        side_copy(part, z, x).start()

        @pl.when(z < LINE - 1)
        def _():
            line_copy(part, z, 1, 0).start()

        @pl.when(z > 0)
        def _():
            line_copy(part, z, -1, 1).start()

    def pass_on(part, step):
        @pl.when(z - step >= 0)
        def _():
            origin = z - step
            line_copy(part, origin, 1, 0).wait_recv()

            @pl.when(z < LINE - 1)
            def _():
                line_copy(part, origin, 1, 0).start()

            side_copy(part, origin, x).start()

        @pl.when(z + step < LINE)
        def _():
            origin = z + step
            line_copy(part, origin, -1, 1).wait_recv()

            @pl.when(z > 0)
            def _():
                line_copy(part, origin, -1, 1).start()

            side_copy(part, origin, x).start()

    in_given_order(back_ref, inverse_ref, values_ref, values_given_ref, scaled_ref)
    own_share = share_own(scaled_ref, taken.at[1], local_sem.at[1])
    share_start(scaled_ref, taken.at[1], share_send, share_recv, own_share)
    sum_groups(0, 2)
    close_sum(0)
    spread_own(0)
    loads[3].wait()
    loads[4].wait()
    branch_sum.fill(lambda span: dot_nn(normed_out_ref[span, :], w_out_ref[...]))
    sum_groups(2, 1)
    branch_sum.join()
    close_sum(2)
    pass_on(0, 1)
    spread_own(2)
    cross_side(0).start()
    cross_start(0)

    branch = branch_sum.result()
    branch_sum.finish()
    whole = resid_ref[...].astype(F32) + branch
    block_out_ref[...] = whole.astype(BF)
    counts = valid_ref[...].astype(F32)
    square_total = jnp.sum(
        counts * jnp.sum(whole * whole, axis=1, keepdims=True), axis=0, keepdims=True
    )
    square_branch = jnp.sum(
        counts * jnp.sum(branch * branch, axis=1, keepdims=True), axis=0, keepdims=True
    )
    count = jnp.sum(counts, axis=0, keepdims=True)
    pass_on(0, 2)

    heads, share = H // shards, 2 * N // shards
    lane = lax.broadcasted_iota(jnp.int32, (rows, TAIL_PAD), 1)
    owned = ((lane >= mine * share) & (lane < (mine + 1) * share)) | (
        (lane >= 2 * N + mine * heads) & (lane < 2 * N + (mine + 1) * heads)
    )

    def grad_rows(span):
        tail = dot_nn(back_ref[span, :], tail_low[...])
        tail = jnp.where(owned, tail, 0.0).astype(BF)
        return (
            dot_nn(gate_given_ref[span, :], w_gate_ref[...])
            + dot_nn(values_given_ref[span, :], w_conv_ref[0:width, :])
            + dot_nn(tail, w_conv_ref[width:, :])
        )

    loads[0].wait()
    loads[1].wait()
    rows_sum.fill(grad_rows)

    share_rows = TAIL_PAD // reps

    def tail_rows(ref, owner):
        return ref.at[pl.ds(pl.multiple_of(owner * share_rows, 16), share_rows)]

    def tail_part_copy(step):
        to = other(step)
        return remote(
            tail_rows(tail_sum, to),
            tail_parts.at[step],
            rep_send.at[0, step],
            rep_recv.at[0, step],
            (to, mine),
        )

    def tail_spread_copy(step):
        return remote(
            tail_rows(tails_ref, rep),
            tail_rows(tails_ref, rep),
            rep_send.at[1, step],
            rep_recv.at[1, step],
            (other(step), mine),
        )

    own_part.wait()
    tail_own[...] = dot_tn(tail_low[...], own_columns[...])
    tail_sum[...] = tail_own[...].astype(BF)
    for step in range(1, reps):
        tail_part_copy(step).start()

    for step in range(LINE):
        at = share_arrival(taken.at[1], share_recv, own_share, step)
        peer_copy(1, at).start()
    rows_sum.join()
    pass_on(0, 3)

    pass_on(2, 1)
    cross_side(1).wait_recv()
    cross_start(1)
    for step in range(1, reps):
        tail_part_copy(step).wait_recv()
    span = pl.ds(pl.multiple_of(rep * share_rows, 16), share_rows)
    piece = tail_own[span, :]
    for step in range(1, reps):
        piece = piece + tail_parts[step].astype(F32)
    tails_ref[span, :] = piece.astype(BF)
    for step in range(1, reps):
        tail_spread_copy(step).start()

    sum_groups(1)

    grad_normed = rows_sum.result()
    given = x_ref[...].astype(F32)
    inverse = lax.rsqrt(jnp.mean(given * given, axis=1, keepdims=True) + EPSILON)
    grad_norm_gain = jnp.sum(grad_normed * (given * inverse), axis=0, keepdims=True)
    scaled = grad_normed * gain_ref[...]
    pull = inverse * inverse * inverse * jnp.mean(scaled * given, axis=1, keepdims=True)
    span = pl.ds(pl.multiple_of(mine * rows, rows), rows)
    loads[2].wait()
    kept = dot_nn(back_ref[span, :], branch_grad_ref[...])
    grad_in_ref[...] = (scaled * inverse - given * pull + kept).astype(BF)
    pass_on(2, 2)

    lane = lax.broadcasted_iota(jnp.int32, (1, 128), 1)
    at = 0
    for i in range(D // 128):
        small[at : at + 1, :] = grad_norm_gain[:, 128 * i : 128 * i + 128]
        at += 1
    channels = (width + 2 * N) // 128
    for tap in range(KW):
        for i in range(channels):
            small[at : at + 1, :] = grad_conv_w_ref[tap : tap + 1, 128 * i : 128 * i + 128]
            at += 1
    for i in range(channels):
        small[at : at + 1, :] = grad_conv_b_ref[:, 128 * i : 128 * i + 128]
        at += 1
    for i in range(width // 128):
        small[at : at + 1, :] = grad_gain_ref[:, 128 * i : 128 * i + 128]
        at += 1
    small[at : at + 3, :] = grad_head_ref[0:3, :]
    small[at + 3 : at + 4, :] = jnp.where(
        lane == 0,
        spread(square_total),
        jnp.where(lane == 1, spread(square_branch), jnp.where(lane == 2, spread(count), 0.0)),
    )
    small[at + 4 :, :] = jnp.zeros((small.shape[0] - at - 4, 128), F32)

    def small_rep_copy(step):
        return remote(
            small, small_in.at[rep], rep_send.at[2, step], rep_recv.at[2, step], (other(step), mine)
        )

    def small_rep_arrival(step):
        return remote(
            small,
            small_in.at[before(step)],
            rep_send.at[2, step],
            rep_recv.at[2, step],
            (other(step), mine),
        )

    def small_shard_copy(step):
        return remote(
            small_all.at[mine],
            small_all.at[mine],
            all_send.at[step],
            all_recv.at[step],
            (rep, shard_at(step)),
        )

    for step in range(1, reps):
        small_rep_copy(step).start()
    small_in[rep] = small[...]
    pass_on(2, 3)
    cross_pass(1)
    close_sum(1)
    spread_own(1)
    for step in range(1, reps):
        small_rep_arrival(step).wait_recv()
    added = small_in[0]
    for i in range(1, reps):
        added = added + small_in[i]
    small_all[mine] = added
    for step in range(1, shards):
        small_shard_copy(step).start()
    pass_on(1, 1)
    cross_pass(2)
    for step in range(1, shards):
        small_shard_copy(step).wait_recv()

    def over_shards(row):
        value = small_all[0, row : row + 1, :]
        for i in range(1, shards):
            value = value + small_all[i, row : row + 1, :]
        return value

    at = 0
    for i in range(D // 128):
        out_norm_ref[:, 128 * i : 128 * i + 128] = over_shards(at)
        at += 1
    for tap in range(KW + 1):
        ref, row = (out_conv_w_ref, tap) if tap < KW else (out_conv_b_ref, 0)
        for i in range(channels):
            if i < width // 128:
                for shard in range(shards):
                    to = shard * width + 128 * i
                    ref[row : row + 1, to : to + 128] = small_all[shard, at : at + 1, :]
            else:
                to = DI + 128 * i - width
                ref[row : row + 1, to : to + 128] = over_shards(at)
            at += 1
    for i in range(width // 128):
        for shard in range(shards):
            to = shard * width + 128 * i
            out_gain_ref[:, to : to + 128] = small_all[shard, at : at + 1, :]
        at += 1
    for i in range(3):
        out_head_ref[i : i + 1, :] = over_shards(at + i)
    stats = over_shards(at + 3)
    per = jnp.maximum(stats[:, 2:3], 1.0) * D
    out_head_ref[3:4, :] = jnp.sqrt(stats / spread(per))
    out_head_ref[4:8, :] = jnp.zeros((4, 128), F32)

    pass_on(1, 2)
    cross_pass(3)
    pass_on(1, 3)

    cross_finish()
    for step in range(1, reps):
        tail_spread_copy(step).wait_recv()
    for part in range(3):
        for origin in range(LINE):
            side_copy(part, origin, 1 - x).wait_recv()
            side_copy(part, origin, x).wait_send()

            @pl.when((origin <= z) & (z < LINE - 1))
            def _(part=part, origin=origin):
                line_copy(part, origin, 1, 0).wait_send()

            @pl.when((origin >= z) & (z > 0))
            def _(part=part, origin=origin):
                line_copy(part, origin, -1, 1).wait_send()

        swap_copy(part).wait_send()
        mail_copy(part).wait_send()
        if part > 0:
            for at in range(LINE):
                peer_copy(part, at).wait_send()
    share_sent(scaled_ref, taken.at[1], share_send, share_recv)
    rows_sum.finish()
    for step in range(1, shards):
        small_shard_copy(step).wait_send()
    for step in range(1, reps):
        tail_part_copy(step).wait_send()
        tail_spread_copy(step).wait_send()
        small_rep_copy(step).wait_send()


def run_end(operands, shards):
    reps = LINE * PLANE
    length, width = operands[4].shape
    rows, depth = length // shards, D // shards
    dma = pltpu.SemaphoreType.DMA
    vector = pl.BlockSpec(memory_space=pltpu.VMEM)
    anywhere = pl.BlockSpec(memory_space=pl.ANY)
    shape = jax.ShapeDtypeStruct
    channels = width + 2 * N
    small = -(-(D + 5 * channels + width + 4 * 128) // 1024) * 8
    return pl.pallas_call(
        end_kernel,
        out_shape=(
            shape((reps, 2, 2, 256, depth), BF),
            shape((reps, 128, D), BF),
            shape((TAIL_PAD, depth), BF),
            shape((rows, D), BF),
            shape((rows, D), BF),
            shape((1, D), F32),
            shape((KW, CONVW), F32),
            shape((1, CONVW), F32),
            shape((8, 128), F32),
            shape((1, DI), F32),
        ),
        in_specs=[anywhere] * 3 + [vector] * 3 + [anywhere] * 2 + [vector] + [anywhere] * 4 + [vector] + [anywhere] + [vector] * 8,
        out_specs=(anywhere,) * 2 + (vector,) * 8,
        scratch_shapes=[
            pltpu.VMEM((3, LINE, length, 256), BF),
            pltpu.VMEM((3, LINE, length, 256), BF),
            pltpu.VMEM((length, width), BF),
            pltpu.VMEM((length, width), BF),
            pltpu.VMEM((LINE, length, D // 2), BF),
            pltpu.VMEM((length, depth), BF),
            pltpu.VMEM((512, D // 2), F32),
            pltpu.VMEM((256, D // 2), F32),
            pltpu.VMEM((3, 256, D // 2), BF),
            pltpu.VMEM((3, 256, D // 2), BF),
            pltpu.VMEM((3, 256, D // 2), BF),
            pltpu.VMEM((length, D), F32),
            pltpu.VMEM((2, rows, D), F32),
            pltpu.VMEM((rows, D), BF),
            pltpu.VMEM((rows, D), BF),
            pltpu.VMEM((2, rows, D), F32),
            pltpu.VMEM((rows, D), BF),
            pltpu.VMEM((rows, D), BF),
            pltpu.VMEM((TAIL_PAD, depth), BF),
            pltpu.VMEM((TAIL_PAD, depth), F32),
            pltpu.VMEM((reps, TAIL_PAD // reps, depth), BF),
            pltpu.VMEM((small, 128), F32),
            pltpu.VMEM((reps, small, 128), F32),
            pltpu.VMEM((shards, small, 128), F32),
            pltpu.VMEM((width, D), BF),
            pltpu.VMEM((width + TAIL_PAD, D), BF),
            pltpu.VMEM((length, D), BF),
            pltpu.VMEM((width, D), BF),
            pltpu.VMEM((length, width), BF),
            dma((5,)),
            dma((8,)),
            dma((LINE,)),
            dma((LINE,)),
            dma((LINE,)),
            dma((3, LINE)),
            dma((3, LINE)),
            dma((3,)),
            dma((3,)),
            dma((3,)),
            dma((3,)),
            dma((3, 2, LINE)),
            dma((3, LINE)),
            dma((3, LINE)),
            dma((3, LINE)),
            dma((PLANE, 3, LINE)),
            dma((PLANE + 1, LINE)),
            dma((3,)),
            dma((3,)),
            dma((3,)),
            dma((3,)),
            dma((3, reps)),
            dma((3, reps)),
            dma((shards,)),
            dma((shards,)),
        ],
        compiler_params=pltpu.CompilerParams(
            vmem_limit_bytes=VMEM_BYTES, collective_id=3, has_side_effects=True
        ),
        cost_estimate=pl.CostEstimate(
            flops=2 * reps * length * D * 256, bytes_accessed=96 << 20, transcendentals=0
        ),
        name="weight_gradient",
    )(*operands)


def assemble_kernel(parts_ref, tail_ref, rows_ref, out_ref, rows_out_ref):
    step, steps = pl.program_id(0), pl.num_programs(0)
    reps = parts_ref.shape[0]

    @pl.when(step < steps - 1)
    def _():
        for rep in range(reps):
            out_ref[128 * rep : 128 * rep + 128, :] = parts_ref[rep, 0, 0].astype(F32)
        rows_out_ref[...] = rows_ref[...].astype(F32)

    @pl.when(step == steps - 1)
    def _():
        out_ref[0:TAIL, :] = tail_ref[0:TAIL, :].astype(F32)


def run_assemble(parts, tail, rows):
    reps, unused, cores, stack, depth = parts.shape
    shards = cores * stack // 128
    steps = 2 * shards

    def place(i):
        at = jnp.minimum(i, steps - 1)
        shard = lax.rem(at, shards)
        return (0, at // shards, lax.rem(shard, cores), shard // cores, 0)

    height = rows.shape[0] // steps

    def row_place(i):
        return (jnp.minimum(i, steps - 1), 0)

    return pl.pallas_call(
        assemble_kernel,
        grid=(steps + 1,),
        out_shape=(
            jax.ShapeDtypeStruct((PROJ, depth), F32),
            jax.ShapeDtypeStruct(rows.shape, F32),
        ),
        in_specs=[
            pl.BlockSpec((reps, 1, 1, 128, depth), place),
            pl.BlockSpec((TAIL_PAD, depth), lambda i: (0, 0)),
            pl.BlockSpec((height, D), row_place),
        ],
        out_specs=(
            pl.BlockSpec((reps * 128, depth), lambda i: (i, 0)),
            pl.BlockSpec((height, D), row_place),
        ),
        compiler_params=params(),
        name="assemble",
    )(parts, tail, rows)


def exchange(pieces, axis, mine):
    count = lax.axis_size(axis)
    own = pieces(mine)
    gathered = jnp.zeros((count,) + own.shape, own.dtype)
    gathered = lax.dynamic_update_index_in_dim(gathered, own, mine, 0)
    for other in range(1, count):
        arrived = lax.ppermute(
            pieces(mine ^ other), axis, [(i, i ^ other) for i in range(count)]
        )
        gathered = lax.dynamic_update_index_in_dim(gathered, arrived, mine ^ other, 0)
    return gathered


def columns_at(array, start, width):
    return lax.dynamic_slice_in_dim(array, start, width, axis=1)


def plain_device(
    x_in,
    cotangent,
    seq_lengths,
    seq_order,
    valid,
    norm_gain,
    w_in,
    conv_w,
    conv_b,
    head_rows,
    gain_row,
    w_out,
):
    shards, mine = lax.axis_size("shard"), lax.axis_index("shard")
    rows = x_in.shape[0]
    length = rows * shards
    depth = w_in.shape[0]
    heads = H // shards
    width = DI // shards
    share = 2 * N // shards
    w_tail = w_in[:, 2 * DI :]

    def conv_piece(d):
        return jnp.concatenate([columns_at(w_in, DI + d * width, width), w_tail], axis=1)

    x_group = lax.all_gather(x_in, "shard", axis=0, tiled=True)
    w_conv = exchange(conv_piece, "shard", mine).reshape(D, width + TAIL)
    w_gate = exchange(lambda d: columns_at(w_in, d * width, width), "shard", mine).reshape(D, width)
    branch_grad = lax.all_gather(
        jnp.where(valid[:, None] > 0, cotangent, jnp.zeros_like(cotangent)),
        "shard",
        axis=0,
        tiled=True,
    )
    slot_ids = jnp.arange(length, dtype=jnp.int32)
    source, target, position = slot_tables(seq_lengths[0], seq_order[0], slot_ids)
    resid = dot_nn((source[:, None] == slot_ids[None, :]).astype(BF), x_group)
    inverse_rms = lax.rsqrt(jnp.mean(resid * resid, axis=1, keepdims=True) + EPSILON)
    normed = (resid * inverse_rms * norm_gain[None, :]).astype(BF)
    resid_mine = lax.dynamic_slice_in_dim(resid, mine * rows, rows, axis=0)
    gate = dot_nn(normed, w_gate).astype(BF)
    conv_in = jnp.pad(dot_nn(normed, w_conv).astype(BF), ((0, 0), (0, TAIL_PAD - TAIL)))
    place = jnp.broadcast_to(position[:, None], (length, 128))
    (
        normed_out,
        grad_gate,
        grad_gain,
        grad_values,
        grad_tail,
        grad_conv_w,
        grad_conv_b,
        grad_head,
    ) = run_mixer(
        (conv_in, gate, branch_grad, w_out, place, conv_w, conv_b, head_rows, gain_row), shards, False
    )
    branch = lax.psum_scatter(dot_nn(normed_out, w_out), "shard", scatter_dimension=0, tiled=True)
    total_rows = resid_mine + branch
    weights_valid = valid.astype(F32)
    square_total = jnp.sum(weights_valid * jnp.sum(total_rows * total_rows, axis=1))
    square_branch = jnp.sum(weights_valid * jnp.sum(branch * branch, axis=1))
    grad_w_out = lax.psum(dot_tn(normed_out, branch_grad), "rep")
    grad_tail = lax.psum(grad_tail, "shard").astype(BF)
    lane = jnp.arange(TAIL, dtype=jnp.int32)
    owned = ((lane >= mine * share) & (lane < (mine + 1) * share)) | (
        (lane >= 2 * N + mine * heads) & (lane < 2 * N + (mine + 1) * heads)
    )
    kept_tail = jnp.where(owned[None, :], grad_tail[:, :TAIL], jnp.zeros((), BF))
    back = (target[:, None] == slot_ids[None, :]).astype(BF)

    def returned(grad):
        return dot_nn(back, grad).astype(BF)

    grad_normed = lax.psum_scatter(
        dot_nt(returned(grad_gate), w_gate)
        + dot_nt(returned(grad_values), w_conv[:, :width])
        + dot_nt(returned(kept_tail), w_conv[:, width:]),
        "shard",
        scatter_dimension=0,
        tiled=True,
    )
    given = x_in.astype(F32)
    given_rms = lax.rsqrt(jnp.mean(given * given, axis=1, keepdims=True) + EPSILON)
    grad_norm_gain = jnp.sum(grad_normed * (given * given_rms), axis=0)
    scaled = grad_normed * norm_gain[None, :]
    grad_resid = scaled * given_rms - given * (
        given_rms**3 * jnp.mean(scaled * given, axis=1, keepdims=True)
    )
    back_mine = lax.dynamic_slice_in_dim(back, mine * rows, rows, axis=0)
    grad_in = (grad_resid + dot_nn(back_mine, branch_grad)).astype(BF)

    def to_owners(columns):
        part = dot_tn(normed, columns).reshape(shards, depth, columns.shape[1])
        swapped = lax.all_to_all(part, "shard", split_axis=0, concat_axis=0, tiled=True)
        summed = lax.psum(swapped, "rep")
        return summed.transpose(1, 0, 2).reshape(depth, shards * columns.shape[1])

    grad_w_tail = lax.psum(
        dot_tn(columns_at(normed, mine * depth, depth), grad_tail[:, :TAIL]), "rep"
    )
    grad_w_in = jnp.concatenate([to_owners(grad_gate), to_owners(grad_values), grad_w_tail], axis=1)

    def placed(part):
        own = lax.dynamic_update_slice_in_dim(
            jnp.zeros((part.shape[0], DI), F32), part[:, :width], mine * width, axis=1
        )
        return jnp.concatenate([own, part[:, width:]], axis=1)

    summed = lax.psum(
        (
            grad_norm_gain,
            placed(grad_conv_w),
            placed(grad_conv_b)[0],
            grad_head,
            placed(grad_gain)[0],
            jnp.stack([square_total, square_branch, jnp.sum(weights_valid)]),
        ),
        ALL,
    )
    roots = jnp.sqrt(summed[5] / (jnp.maximum(summed[5][2], 1.0) * D))
    return (
        total_rows.astype(BF),
        grad_in,
        summed[0],
        grad_w_in,
        summed[1],
        summed[2],
        summed[3][0, :H],
        summed[3][1, :H],
        summed[3][2, :H],
        summed[4],
        grad_w_out,
        roots[0],
        roots[1],
    )


def on_device(
    x_in,
    cotangent,
    seq_lengths,
    seq_order,
    valid,
    norm_gain,
    w_in,
    conv_w,
    conv_b,
    dt_bias,
    a_log,
    d_skip,
    gated_gain,
    w_out,
):
    shards, mine = lax.axis_size("shard"), lax.axis_index("shard")
    reps = lax.axis_size("rep")
    rows = x_in.shape[0]
    length = rows * shards
    depth = w_in.shape[0]
    heads = H // shards
    width = DI // shards

    head_rows = jnp.pad(jnp.stack([dt_bias, a_log, d_skip]), ((0, 5), (0, 128 - H)))
    bias_row, gain_row = conv_b[None, :], gated_gain[None, :]
    spans = reps == LINE * PLANE and shards == 4 and width == reps * 128 and rows == 128
    if not spans:
        return plain_device(
            x_in,
            cotangent,
            seq_lengths,
            seq_order,
            valid,
            norm_gain,
            w_in,
            conv_w,
            bias_row,
            head_rows,
            gain_row,
            w_out,
        )
    norm_row, valid_column = norm_gain[None, :], valid[:, None]
    (
        normed,
        w_gate,
        w_conv,
        branch_grad,
        back,
        resid,
        inverse,
        line,
        normed_out,
        grad_gain,
        grad_values,
        grad_conv_w,
        grad_conv_b,
        grad_head,
        gate_taken,
        out_taken,
        gate_peer,
        gate_given,
        tail,
    ) = run_mixer(
        (
            seq_lengths,
            seq_order,
            x_in,
            cotangent,
            valid_column,
            norm_row,
            w_in.T,
            w_out,
            conv_w,
            bias_row,
            head_rows,
            gain_row,
        ),
        shards,
        True,
    )
    operands = (
        gate_taken,
        gate_peer,
        out_taken,
        gate_given,
        grad_values,
        tail,
        normed,
        line,
        inverse,
        w_gate,
        w_conv,
        w_out,
        normed_out,
        back,
        branch_grad,
        x_in,
        resid,
        valid_column,
        norm_row,
        grad_conv_w,
        grad_conv_b,
        grad_head,
        grad_gain,
    )
    (
        parts,
        w_out_parts,
        tails,
        block_out,
        grad_in,
        out_norm,
        out_conv_w,
        out_conv_b,
        out_head,
        out_gain,
    ) = run_end(operands, shards)
    grad_w_in, grad_w_out = run_assemble(parts, tails, w_out_parts.reshape(width, D))
    grad_w_in = grad_w_in.T
    return (
        block_out,
        grad_in,
        out_norm[0],
        grad_w_in,
        out_conv_w,
        out_conv_b[0],
        out_head[0, :H],
        out_head[1, :H],
        out_head[2, :H],
        out_gain[0],
        grad_w_out,
        out_head[3, 0],
        out_head[3, 1],
    )


def solution(mesh):
    in_specs = (
        P(ALL, None),
        P(ALL, None),
        P("rep", None),
        P("rep", None),
        P(ALL),
        P(),
        P("shard", None),
        P(),
        P(),
        P(),
        P(),
        P(),
        P(),
        P("shard", None),
    )
    out_specs = (
        P(ALL, None),
        P(ALL, None),
        P(),
        P("shard", None),
        P(),
        P(),
        P(),
        P(),
        P(),
        P(),
        P("shard", None),
        P(),
        P(),
    )
    return jax.shard_map(
        on_device, mesh=mesh, in_specs=in_specs, out_specs=out_specs, check_vma=False
    )
```
